32 devices in a mesh: ep: 8 (over z, y), tp: 4 (over x, core).
Axes of the slice: x: 2, y: 2, z: 4, core: 2. Of those that a mesh axis runs over, the one named last changes fastest.
Arguments:
- inputs: bfloat16 [8192, 2048], P(('ep', 'tp')), may hold values from -6 to 6
- cotangent: bfloat16 [8192, 2048], P(('ep', 'tp')), may hold values from -6 to 6
- arrangement: int32 [8192], replicated, may hold values from 0 to 8191, as said below
- seq_lengths: int32 [8], replicated, may hold values from 1 to 4096, 8192 in all
- routes: int32 [8192, 8], P(('ep', 'tp')), may hold values from 0 to 31, all different within a row; in each aligned block of 256 rows (0 to 255, 256 to 511, ...) at most 128 rows name the same one
- gate_values: float32 [8192, 8], P(('ep', 'tp')), may hold values from 0.05 to 0.25
- input_gain: float32 [2048], replicated, may hold values from 0.25 to 1.75
- query_proj: bfloat16 [2048, 4096], P(None, 'tp'), may hold values from -0.125 to 0.125
- key_projected: bfloat16 [2048, 512], P(None, 'tp'), may hold values from -0.125 to 0.125
- value_projected: bfloat16 [2048, 512], P(None, 'tp'), may hold values from -0.125 to 0.125
- query_gain: float32 [128], replicated, may hold values from 0.25 to 1.75
- key_gain: float32 [128], replicated, may hold values from 0.25 to 1.75
- output_proj: bfloat16 [4096, 2048], P('tp'), may hold values from -1.5 to 1.5
- expert_gain: float32 [2048], replicated, may hold values from 0.25 to 1.75
- gate_weight: bfloat16 [32, 2048, 768], P(('ep', 'tp')), may hold values from -0.125 to 0.125
- up_weight: bfloat16 [32, 2048, 768], P(('ep', 'tp')), may hold values from -0.125 to 0.125
- down_weight: bfloat16 [32, 768, 2048], P(('ep', 'tp')), may hold values from -0.875 to 0.875
Outputs:
- layer_out: bfloat16 [8192, 2048], P(('ep', 'tp'))
- grad_inputs: float32 [8192, 2048], P(('ep', 'tp'))
- grad_query: float32 [2048, 4096], P('ep', 'tp')
- grad_key: float32 [2048, 512], P('ep', 'tp')
- grad_value: float32 [2048, 512], P('ep', 'tp')
- grad_output: float32 [4096, 2048], P('tp', 'ep')
- grad_input_gain: float32 [2048], replicated
- grad_query_gain: float32 [128], replicated
- grad_key_gain: float32 [128], replicated
- grad_expert_gain: float32 [2048], replicated
- grad_gate: float32 [32, 2048, 768], P(('ep', 'tp'))
- grad_up: float32 [32, 2048, 768], P(('ep', 'tp'))
- grad_down: float32 [32, 768, 2048], P(('ep', 'tp'))
The draws below stay inside these ranges and needn't reach their ends.
Inputs may be any that keep to these rules, and one draw needn't show every extreme that they name: arrangement holds every given index once. Place t = e * 1024 + j * 256 + s * 32 + b, with b < 32, holds one of the given tokens s * 1024 + j * 256 to s * 1024 + j * 256 + 255. `routes`: within each aligned block of 256 places, no expert is named by more than 128 rows, a bound that some block reaches.
All inputs are finite; a program needn't handle non-finite values.
Results may differ from the reference program's by a relative error of at most 0.025.
Values may be sent and summed in bfloat16 or wider, within the bound.
A program may use at most 384 MiB of HBM per device.

```python
import math
import jax
import jax.numpy as jnp
import numpy as np
from jax import lax

MODEL_WIDTH = 2048
QUERY_HEADS = 32
KEY_VALUE_HEADS = 4
HEAD_WIDTH = 128
FF = 768
TOP = 8
MAXLEN = 4096
EXPERTS = 32
TOKEN_TOTAL = 8192
TOK_DEV = 1024
ROWS = 256
BLOCK = 32
CAP = 128
NSEQ = 8


def draw_arrangement(key, part):
    key = jax.random.fold_in(key, 11)
    groups = TOKEN_TOTAL // ROWS
    ep_count = TOKEN_TOTAL // TOK_DEV
    tp_count = TOK_DEV // ROWS
    subkeys = jax.random.split(key, groups)
    orders = jax.vmap(lambda subkey: jax.random.permutation(subkey, ROWS))(subkeys).astype(jnp.int32)
    orders = orders.reshape(ep_count, tp_count, ep_count, BLOCK)
    source = jnp.arange(ep_count, dtype=jnp.int32)[:, None, None, None]
    lanes = jnp.arange(tp_count, dtype=jnp.int32)[None, :, None, None]
    anchor = orders + source * TOK_DEV + lanes * ROWS
    return jnp.transpose(anchor, (2, 1, 0, 3)).reshape(TOKEN_TOTAL).astype(jnp.int32)


def block_levels(rng, shape, cuts, smallest, high):
    loudness, own = 1.0, jax.random.fold_in(rng, 6)
    for axis_at, parts in cuts:
        heights = jnp.exp(jax.random.uniform(jax.random.fold_in(own, axis_at), (parts,), jnp.float32, smallest / len(cuts), high / len(cuts)))
        loudness = loudness * jnp.repeat(heights, shape[axis_at] // parts).reshape([-1 if axis == axis_at else 1 for axis in range(len(shape))])
    return loudness


def length_profile(count, total, limit, lean):
    weights = [(1 << 20) // math.isqrt(rank ** lean) + 1 for rank in range(2, count + 1)]
    surplus, holding = total - limit - (count - 1), [1] * (count - 1)
    while surplus > 0:
        free = [i for i in range(count - 1) if holding[i] < limit]
        pool, left = sum([weights[i] for i in free]), surplus
        for i in free:
            extra = min(limit - holding[i], max(1, left * weights[i] // pool), surplus)
            holding[i] = holding[i] + extra
            surplus = surplus - extra
    return np.array([limit] + holding)


def ragged(rng, count, total, most, skew):
    if count == 2:
        one = jax.random.randint(rng, (), max(1, total - most), min(most, total - 1) + 1)
        return jnp.stack([one, total - one])
    lengths = jnp.asarray(length_profile(count, total, most, skew), jnp.int32)
    twos = (count - 1) // 2
    donor, sink = lengths[1:1 + 2 * twos:2], lengths[2:2 + 2 * twos:2]
    slack = jnp.minimum(donor - 1, most - sink)
    passed = jax.random.randint(jax.random.fold_in(rng, 1), (twos,), 0, 1 << 20) % (slack + 1)
    lengths = lengths.at[1:1 + 2 * twos:2].set(donor - passed).at[2:2 + 2 * twos:2].set(sink + passed)
    return lengths[jax.random.permutation(jax.random.fold_in(rng, 2), count)]


def routed_block(own_key, own, number, rows, number_of, top, limit, slope):
    sequence = jax.random.permutation(own_key, number_of)
    packed, common = shares(number_of, rows * top, limit, slope, True), shares(number_of, rows * top, limit, slope, False)
    places = jnp.arange(number_of)

    def named(tallies, offset_by):
        used = int((tallies > 0).sum())
        fixed = max(1, used // 4)
        passed = fixed + (places - fixed + offset_by * (used - fixed)) % max(1, number_of - fixed)
        return jnp.zeros((number_of,), jnp.int32).at[sequence[jnp.where(places < fixed, places, passed)]].set(jnp.asarray(tallies, jnp.int32))

    tallies = jnp.where(number % 4 == 0, named(packed, number // 4), named(common, number - number // 4 - 1))
    mixed = jax.random.permutation(jax.random.fold_in(own, 3), number_of)
    donor, taker = mixed[0:number_of // 2 * 2:2], mixed[1:number_of // 2 * 2:2]
    room = jnp.minimum(tallies[donor] - 1, limit - tallies[taker]) // 2
    room = jnp.where((donor == sequence[0]) | (taker == sequence[0]) | (tallies[taker] == 0), 0, jnp.maximum(room, 0))
    passed = jax.random.randint(jax.random.fold_in(own, 4), (number_of // 2,), 0, 1 << 20) % (room + 1)
    tallies = tallies.at[donor].add(-passed).at[taker].add(passed)
    items = jnp.searchsorted(jnp.cumsum(tallies), jnp.arange(rows * top), side="right").astype(jnp.int32)
    table = items.reshape(top, rows).T
    table = table[jax.random.permutation(jax.random.fold_in(own, 1), rows)]
    offset_by = jax.random.randint(jax.random.fold_in(own, 2), (rows, 1), 0, top)
    return jnp.take_along_axis(table, (jnp.arange(top)[None, :] + offset_by) % top, axis=1)


def shares(amount, total, limit, skew, full):
    loads = [(1 << 20) // math.isqrt(standing ** skew) + 1 for standing in range(1, amount + 1)]
    largest = limit if full else min(limit, max(-(-total // amount), total * loads[0] // sum(loads)))
    least = 1 if total - largest >= amount - 1 else 0
    counts, surplus = [largest] + [least] * (amount - 1), total - largest - least * (amount - 1)
    while surplus > 0:
        movable = [i for i in range(1, amount) if counts[i] < largest] or [i for i in range(1, amount) if counts[i] < limit]
        pool, left = sum([loads[i] for i in movable]), surplus
        for i in movable:
            extra = min(limit - counts[i], max(1, left * loads[i] // pool), surplus)
            counts[i] = counts[i] + extra
            surplus = surplus - extra
    return np.array(counts)


def scatter_about(key, shape, deviation, most, cuts=(), kind=jnp.bfloat16):
    loudness = block_levels(key, shape, cuts, -0.22, 0.18) if cuts else 1.0
    array = jax.random.normal(key, shape, jnp.float32) * deviation * loudness
    return jnp.minimum(jnp.maximum(array, -most), most).astype(kind)


def setup_inputs(seed: int = 0) -> dict:
    key_of = jax.random.split(jax.random.key(seed), 18)
    inputs = scatter_about(key_of[0], (TOKEN_TOTAL, MODEL_WIDTH), 1.0, 6.0, ((0, 32),))
    cotangent = scatter_about(key_of[1], (TOKEN_TOTAL, MODEL_WIDTH), 1.0, 6.0, ((0, 32),))
    arrangement = draw_arrangement(jax.random.fold_in(key_of[17], 71), 0)
    seq_lengths = ragged(key_of[3], NSEQ, TOKEN_TOTAL, MAXLEN, 2).astype(jnp.int32)
    routes_keys = jax.random.split(jax.random.fold_in(key_of[4], 1), TOKEN_TOTAL // ROWS)
    routes_turns = jax.random.permutation(jax.random.fold_in(key_of[4], 3), TOKEN_TOTAL // ROWS)
    routes = jax.vmap(lambda own, number: routed_block(jax.random.fold_in(key_of[4], 2), own, number, ROWS, EXPERTS, TOP, CAP, 2))(routes_keys, routes_turns).reshape((TOKEN_TOTAL, TOP))
    gate_values = jnp.clip(jnp.exp(math.log(0.25) - 1.609438 * jax.random.uniform(key_of[5], (TOKEN_TOTAL, TOP), jnp.float32) ** block_levels(key_of[5], (TOKEN_TOTAL, TOP), ((0, 32),), -0.2, 0.2)), 0.05, 0.25)
    input_gain = jnp.clip(1.0 + 0.15 * jax.random.normal(key_of[6], (MODEL_WIDTH,), jnp.float32), 0.25, 1.75)
    query_proj = scatter_about(key_of[7], (MODEL_WIDTH, QUERY_HEADS * HEAD_WIDTH), MODEL_WIDTH ** -0.5, 0.125, ((1, 4),))
    key_projected = scatter_about(key_of[8], (MODEL_WIDTH, KEY_VALUE_HEADS * HEAD_WIDTH), MODEL_WIDTH ** -0.5, 0.125, ((1, 4),))
    value_projected = scatter_about(key_of[9], (MODEL_WIDTH, KEY_VALUE_HEADS * HEAD_WIDTH), MODEL_WIDTH ** -0.5, 0.125, ((1, 4),))
    query_gain = jnp.clip(1.0 + 0.15 * jax.random.normal(key_of[10], (HEAD_WIDTH,), jnp.float32), 0.25, 1.75)
    key_gain = jnp.clip(1.0 + 0.15 * jax.random.normal(key_of[11], (HEAD_WIDTH,), jnp.float32), 0.25, 1.75)
    output_proj = scatter_about(key_of[12], (QUERY_HEADS * HEAD_WIDTH, MODEL_WIDTH), (max(1, QUERY_HEADS * HEAD_WIDTH // 256)) ** -0.5, 1.5, ((0, 4),))
    expert_gain = jnp.clip(1.0 + 0.15 * jax.random.normal(key_of[13], (MODEL_WIDTH,), jnp.float32), 0.25, 1.75)
    gate_weight = scatter_about(key_of[14], (EXPERTS, MODEL_WIDTH, FF), MODEL_WIDTH ** -0.5, 0.125, ((0, 32),))
    up_weight = scatter_about(key_of[15], (EXPERTS, MODEL_WIDTH, FF), MODEL_WIDTH ** -0.5, 0.125, ((0, 32),))
    down_weight = scatter_about(key_of[16], (EXPERTS, FF, MODEL_WIDTH), (FF // 16) ** -0.5, 0.875, ((0, 32),))
    return {"inputs": inputs, "cotangent": cotangent, "arrangement": arrangement, "seq_lengths": seq_lengths, "routes": routes, "gate_values": gate_values, "input_gain": input_gain, "query_proj": query_proj, "key_projected": key_projected, "value_projected": value_projected, "query_gain": query_gain, "key_gain": key_gain, "output_proj": output_proj, "expert_gain": expert_gain, "gate_weight": gate_weight, "up_weight": up_weight, "down_weight": down_weight}


EPSILON = 1e-06
ROPE_BASE = 1000000.0
FINEST_PRECISION = lax.Precision.HIGHEST
NEGATIVE = -1e+30
QUERY_WINDOW = 512

@jax.custom_vjp
def lower_half(v):
    return lax.optimization_barrier(v.astype(jnp.bfloat16)).astype(jnp.float32)

@jax.custom_vjp
def lower_backward(v):
    return v

def low_keep(v):
    return (lower_half(v), None)

def low_pass(kept, grad):
    return (grad,)

def back_keep(v):
    return (v, None)

def back_low(kept, grad):
    return (lower_half(grad),)
lower_half.defvjp(low_keep, low_pass)
lower_backward.defvjp(back_keep, back_low)

def rms_scale(values, gain):
    inverse = lax.rsqrt(lax.optimization_barrier(jnp.mean(values * values, axis=-1, keepdims=True)) + EPSILON)
    return values * inverse * gain

def rotate_half(values):
    half = values.shape[-1] // 2
    return jnp.concatenate([-values[..., half:], values[..., :half]], axis=-1)

def rope_apply(values, cosine, sine):
    return values * cosine + rotate_half(values) * sine

def rope_tables(positions, head_dim):
    freqs = ROPE_BASE ** (-jnp.arange(0, head_dim, 2, dtype=jnp.float32) / head_dim)
    angles = positions.astype(jnp.float32)[:, None] * freqs[None, :]
    angles = jnp.concatenate([angles, angles], axis=-1)
    return (jnp.cos(angles), jnp.sin(angles))

def seq_info(given, seq_lengths):
    ends = jnp.cumsum(seq_lengths).astype(jnp.int32)
    starts = (ends - seq_lengths).astype(jnp.int32)
    seq_ids = lax.optimization_barrier(jnp.sum((given[:, None] >= ends[None, :]).astype(jnp.int32), axis=1)).astype(jnp.int32)
    match = seq_ids[:, None] == jnp.arange(seq_lengths.shape[0], dtype=jnp.int32)[None, :]
    firsts = lax.optimization_barrier(jnp.sum(jnp.where(match, starts[None, :], 0), axis=1)).astype(jnp.int32)
    return (seq_ids, (given - firsts).astype(jnp.int32))

def attention(query_matrix, keys_all, values_all, seq_ids):
    window = MAXLEN + QUERY_WINDOW
    head_group = QUERY_HEADS // KEY_VALUE_HEADS
    score_scale = HEAD_WIDTH ** (-0.5)

    def block_fn(block_index, query_matrix, keys_all, values_all):
        start_offset = (block_index * QUERY_WINDOW).astype(jnp.int32)
        lowest = jnp.clip(start_offset + QUERY_WINDOW - window, 0, TOKEN_TOTAL - window).astype(jnp.int32)
        query_slice = lax.dynamic_slice_in_dim(query_matrix, start_offset, QUERY_WINDOW, 0).reshape(QUERY_WINDOW, KEY_VALUE_HEADS, head_group, HEAD_WIDTH)
        key_part = lax.dynamic_slice_in_dim(keys_all, lowest, window, 0)
        value_part = lax.dynamic_slice_in_dim(values_all, lowest, window, 0)
        scores = jnp.einsum('qhgd,khd->hgqk', query_slice, key_part, precision=FINEST_PRECISION) * score_scale
        scores = lower_backward(scores)
        query_index = start_offset + jnp.arange(QUERY_WINDOW, dtype=jnp.int32)
        key_index = lowest + jnp.arange(window, dtype=jnp.int32)
        allowed = (seq_ids[query_index][:, None] == seq_ids[key_index][None, :]) & (key_index[None, :] <= query_index[:, None])
        masked = jnp.where(allowed, scores, NEGATIVE)
        probs = jax.nn.softmax(masked, axis=-1)
        output = jnp.einsum('hgqk,khd->qhgd', lower_half(probs), value_part, precision=FINEST_PRECISION)
        return lower_backward(lower_half(output)).reshape(QUERY_WINDOW, QUERY_HEADS * HEAD_WIDTH)
    checked = jax.checkpoint(block_fn)
    blocks = lax.map(lambda block_index: checked(block_index, query_matrix, keys_all, values_all), jnp.arange(TOKEN_TOTAL // QUERY_WINDOW, dtype=jnp.int32))
    return blocks.reshape(TOKEN_TOTAL, QUERY_HEADS * HEAD_WIDTH)

def reference(inputs, cotangent, arrangement, seq_lengths, routes, gate_values, input_gain, query_proj, key_projected, value_projected, query_gain, key_gain, output_proj, expert_gain, gate_weight, up_weight, down_weight):
    inverse = jnp.zeros((TOKEN_TOTAL,), jnp.int32).at[arrangement].set(jnp.arange(TOKEN_TOTAL, dtype=jnp.int32))
    route_given = routes[inverse]
    weight_given = gate_values[inverse].astype(jnp.float32)
    given = jnp.arange(TOKEN_TOTAL, dtype=jnp.int32)
    seq_ids, positions = seq_info(given, seq_lengths)
    cosine, sine = rope_tables(positions, HEAD_WIDTH)
    slot_total = TOKEN_TOTAL * TOP
    room = EXPERTS * CAP
    flat_routes = route_given.reshape(-1)

    def table_for(expert):
        hit = flat_routes == expert
        place = (jnp.cumsum(hit.astype(jnp.int32)) - 1).astype(jnp.int32)
        target = jnp.where(hit, place, room).astype(jnp.int32)
        return jnp.full((room,), slot_total, jnp.int32).at[target].set(jnp.arange(slot_total, dtype=jnp.int32), mode='drop')
    tables = lax.map(table_for, jnp.arange(EXPERTS, dtype=jnp.int32))
    token_of = (tables // TOP).astype(jnp.int32)
    gate_flat = jnp.concatenate([weight_given.reshape(-1), jnp.zeros((1,), weight_given.dtype)])
    gate_of = gate_flat[tables]

    def forward(inputs_f, input_g, query_w, key_weight, value_weight, query_g, key_g, output_w, expert_g, gate_w, up_w, down_w):
        normed_input = lower_half(rms_scale(inputs_f, input_g))
        query_raw = lower_backward(jnp.dot(normed_input, query_w, precision=FINEST_PRECISION)).reshape(TOKEN_TOTAL, QUERY_HEADS, HEAD_WIDTH)
        key_unrotated = lower_backward(jnp.dot(normed_input, key_weight, precision=FINEST_PRECISION)).reshape(TOKEN_TOTAL, KEY_VALUE_HEADS, HEAD_WIDTH)
        value_row_block = lower_backward(lower_half(jnp.dot(normed_input, value_weight, precision=FINEST_PRECISION))).reshape(TOKEN_TOTAL, KEY_VALUE_HEADS, HEAD_WIDTH)
        query_rows = lower_half(rope_apply(rms_scale(query_raw, query_g), cosine[:, None, :], sine[:, None, :]))
        key_rows = lower_half(rope_apply(rms_scale(key_unrotated, key_g), cosine[:, None, :], sine[:, None, :]))
        out_rows = attention(query_rows, key_rows, value_row_block, seq_ids)
        branch = lower_backward(jnp.dot(out_rows, output_w, precision=FINEST_PRECISION))
        hidden = inputs_f + branch
        normed_mid = lower_half(rms_scale(hidden, expert_g))
        padded = jnp.concatenate([normed_mid, jnp.zeros((1, MODEL_WIDTH), normed_mid.dtype)], axis=0)

        def expert_fn(items):
            token_rows, gate_e, up_e, down_e = items
            rows_in = lower_backward(padded[token_rows])
            gate_part = lower_backward(jnp.dot(rows_in, gate_e, precision=FINEST_PRECISION))
            up_part = lower_backward(jnp.dot(rows_in, up_e, precision=FINEST_PRECISION))
            inner = lower_half(jax.nn.silu(gate_part) * up_part)
            return lower_backward(lower_half(jnp.dot(inner, down_e, precision=FINEST_PRECISION)))
        outputs = lax.map(jax.checkpoint(expert_fn), (token_of, gate_w, up_w, down_w))
        mixed = jnp.zeros((TOKEN_TOTAL + 1, MODEL_WIDTH), outputs.dtype).at[token_of.reshape(-1)].add(gate_of.reshape(-1)[:, None] * outputs.reshape(-1, MODEL_WIDTH))
        return hidden + mixed[:TOKEN_TOTAL]
    primals = (inputs.astype(jnp.float32), input_gain, query_proj.astype(jnp.float32), key_projected.astype(jnp.float32), value_projected.astype(jnp.float32), query_gain, key_gain, output_proj.astype(jnp.float32), expert_gain, gate_weight.astype(jnp.float32), up_weight.astype(jnp.float32), down_weight.astype(jnp.float32))
    layer_out, pullback = jax.vjp(forward, *primals)
    grads = pullback(cotangent.astype(jnp.float32))
    return (layer_out.astype(jnp.bfloat16), grads[0], grads[2], grads[3], grads[4], grads[7], grads[1], grads[5], grads[6], grads[8], grads[9], grads[10], grads[11])
```

```python
import math

import jax
import jax.numpy as jnp
from jax import lax
from jax.experimental import pallas as pl
from jax.experimental.pallas import tpu as pltpu
from jax.sharding import PartitionSpec as P

TOP = 8
EPSILON = 1e-06
ROPE_BASE = 1000000.0
KEY_SPAN = 512
QUERY_TOKENS = 32
HEAD = 128
ROW_TILE = 256
MIB = 1 << 20
LOG2E = math.log2(math.e)
ROWS_BY_ROWS = (((0,), (0,)), ((), ()))
COLS_BY_COLS = (((1,), (1,)), ((), ()))


def dot(left, right):
    return jnp.dot(left, right, preferred_element_type=jnp.float32)


def dot_with(left, right, dims):
    return lax.dot_general(left, right, dims, preferred_element_type=jnp.float32)


def cost(flops, moved, transcendentals=0):
    return pl.CostEstimate(
        flops=int(flops), bytes_accessed=int(moved), transcendentals=int(transcendentals)
    )


def params(mib):
    return pltpu.CompilerParams(
        dimension_semantics=("arbitrary",), vmem_limit_bytes=mib * MIB
    )


def whole(shape, single=True):
    rank = len(shape)
    if single:
        return pl.BlockSpec(shape, lambda *ids: (0,) * rank, pipeline_mode=pl.Buffered(1))
    return pl.BlockSpec(shape, lambda *ids: (0,) * rank)


def rows_of(shape):
    rank = len(shape)
    return pl.BlockSpec(shape, lambda i, *ids: (i,) + (0,) * (rank - 1))


def rope_tables(positions, head_dim):
    freqs = ROPE_BASE ** (-jnp.arange(0, head_dim, 2, dtype=jnp.float32) / head_dim)
    angles = positions.astype(jnp.float32)[:, None] * freqs[None, :]
    cosine, sine = jnp.cos(angles), jnp.sin(angles)
    return (
        jnp.concatenate([cosine, cosine], axis=-1),
        jnp.concatenate([-sine, sine], axis=-1),
    )


def seq_starts(given, seq_lengths):
    ends = jnp.cumsum(seq_lengths)
    passed = given[:, None] >= ends[None, :]
    return jnp.sum(jnp.where(passed, seq_lengths[None, :], 0), axis=1)


def inverse_root(values):
    return lax.rsqrt(jnp.mean(values * values, axis=-1, keepdims=True) + EPSILON)


def front_kernel(
    x_ref, gain_ref, wq_ref, wk_ref, wv_ref, qg_ref, kg_ref, cos_ref, sin_ref,
    normed_ref, qraw_ref, q_ref, kraw_ref, kv_ref,
):
    x = x_ref[...].astype(jnp.float32)
    normed = (x * inverse_root(x) * gain_ref[...]).astype(jnp.bfloat16)
    normed_ref[...] = normed
    cosine, sine = cos_ref[...], sin_ref[...]

    def prepare(raw, gain):
        values = raw * inverse_root(raw) * gain
        return (values * cosine + pltpu.roll(values, HEAD // 2, 1) * sine).astype(jnp.bfloat16)

    raw = dot(normed, wq_ref[...])
    qraw_ref[...] = raw
    for head in range(raw.shape[1] // HEAD):
        part = slice(head * HEAD, (head + 1) * HEAD)
        q_ref[:, part] = prepare(raw[:, part], qg_ref[...])
    raw = dot(normed, wk_ref[...])
    kraw_ref[...] = raw
    kv_ref[:, :HEAD] = prepare(raw, kg_ref[...])
    kv_ref[:, HEAD:] = dot(normed, wv_ref[...]).astype(jnp.bfloat16)


def front(group_x, input_gain, wq, wk, wv, query_gain, key_gain, cosine, sine):
    rows, width = group_x.shape
    cols = wq.shape[1]
    tile = min(ROW_TILE, rows)
    out = [
        ((rows, width), jnp.bfloat16),
        ((rows, cols), jnp.float32),
        ((rows, cols), jnp.bfloat16),
        ((rows, HEAD), jnp.float32),
        ((rows, 2 * HEAD), jnp.bfloat16),
    ]
    return pl.pallas_call(
        front_kernel,
        grid=(rows // tile,),
        in_specs=[
            rows_of((tile, width)),
            whole((1, width)),
            whole(wq.shape),
            whole(wk.shape),
            whole(wv.shape),
            whole((1, HEAD)),
            whole((1, HEAD)),
            rows_of((tile, HEAD)),
            rows_of((tile, HEAD)),
        ],
        out_specs=[rows_of((tile, shape[1])) for shape, kind in out],
        out_shape=[jax.ShapeDtypeStruct(shape, kind) for shape, kind in out],
        compiler_params=params(40),
        cost_estimate=cost(2 * rows * width * (cols + 2 * HEAD), 20 * MIB),
        name="front",
    )(
        group_x,
        input_gain[None],
        wq,
        wk,
        wv,
        query_gain[None],
        key_gain[None],
        cosine,
        sine,
    )


def stack_heads(block):
    heads = block.shape[1] // HEAD
    return jnp.concatenate(
        [block[:, head * HEAD : (head + 1) * HEAD] for head in range(heads)], axis=0
    )


def attend_forward_kernel(
    bounds_ref, q_ref, ask_ref, key_given_ref, kv_ref, exact_ref, out_ref, lse_ref, acc, tot
):
    step = pl.program_id(0)
    tokens, cols = q_ref.shape
    heads = cols // HEAD
    query = stack_heads(q_ref[...])
    ask = ask_ref[...]
    last = jnp.concatenate([ask[:, 0:1]] * heads, axis=0)
    first = jnp.concatenate([ask[:, 1:2]] * heads, axis=0)
    acc[...] = jnp.zeros_like(acc)
    tot[...] = jnp.zeros_like(tot)

    def visit(span, masked):
        offset = pl.multiple_of(span * KEY_SPAN, KEY_SPAN)
        keys = kv_ref[pl.ds(offset, KEY_SPAN), :HEAD]
        values = kv_ref[pl.ds(offset, KEY_SPAN), HEAD:]
        scores = dot_with(query, keys, COLS_BY_COLS)
        weights = jnp.exp2(scores * (HEAD**-0.5 * LOG2E))
        if masked:
            key_given = key_given_ref[:, pl.ds(offset, KEY_SPAN)]
            weights = jnp.where((key_given <= last) & (key_given >= first), weights, 0.0)
        part = weights[:, :HEAD]
        for chunk in range(1, KEY_SPAN // HEAD):
            part = part + weights[:, chunk * HEAD : (chunk + 1) * HEAD]
        tot[...] += part
        acc[...] += dot(weights.astype(jnp.bfloat16), values)

    lowest, open_low = bounds_ref[0, step], bounds_ref[1, step]
    open_high, highest = bounds_ref[2, step], bounds_ref[3, step]

    @pl.loop(lowest, open_low)
    def _(span):
        visit(span, True)

    @pl.loop(open_low, open_high)
    def _(span):
        visit(span, False)

    @pl.loop(open_high, highest)
    def _(span):
        visit(span, True)

    total = tot[...]
    exact = acc[...] / jnp.sum(total, axis=1, keepdims=True)
    for head in range(heads):
        rows = exact[head * tokens : (head + 1) * tokens]
        exact_ref[:, head * HEAD : (head + 1) * HEAD] = rows
        out_ref[:, head * HEAD : (head + 1) * HEAD] = rows.astype(jnp.bfloat16)
    lse_ref[0] = jnp.log2(jnp.sum(total.T, axis=0, keepdims=True))


def attend_forward(bounds, query, ask, key_given, kv, pairs):
    rows, cols = query.shape
    heads = cols // HEAD
    steps = rows // QUERY_TOKENS
    stacked = heads * QUERY_TOKENS
    return pl.pallas_call(
        attend_forward_kernel,
        grid_spec=pltpu.PrefetchScalarGridSpec(
            num_scalar_prefetch=1,
            grid=(steps,),
            in_specs=[
                rows_of((QUERY_TOKENS, cols)),
                rows_of((QUERY_TOKENS, 2)),
                whole(key_given.shape),
                whole(kv.shape),
            ],
            out_specs=[
                rows_of((QUERY_TOKENS, cols)),
                rows_of((QUERY_TOKENS, cols)),
                rows_of((1, 1, stacked)),
            ],
            scratch_shapes=[
                pltpu.VMEM((stacked, HEAD), jnp.float32),
                pltpu.VMEM((stacked, HEAD), jnp.float32),
            ],
        ),
        out_shape=[
            jax.ShapeDtypeStruct((rows, cols), jnp.float32),
            jax.ShapeDtypeStruct((rows, cols), jnp.bfloat16),
            jax.ShapeDtypeStruct((steps, 1, stacked), jnp.float32),
        ],
        compiler_params=params(48),
        cost_estimate=cost(8 * pairs * HEAD, 16 * MIB, pairs),
        name="attend_forward",
    )(bounds, query, ask, key_given, kv)


def attend_backward_kernel(
    bounds_ref, q_ref, grad_ref, exact_ref, lse_ref, ask_ref, key_given_ref, kv_ref,
    dq_ref, dkv_ref, acc,
):
    step = pl.program_id(0)
    tokens, cols = q_ref.shape
    heads = cols // HEAD

    @pl.when(step == 0)
    def _():
        dkv_ref[...] = jnp.zeros_like(dkv_ref)

    query = stack_heads(q_ref[...])
    grad = stack_heads(grad_ref[...])
    product = grad.astype(jnp.float32) * stack_heads(exact_ref[...])
    delta = jnp.sum(product.T, axis=0, keepdims=True)
    lse = lse_ref[0]
    last, first = ask_ref[0, 0:1, :], ask_ref[0, 1:2, :]
    acc[...] = jnp.zeros_like(acc)

    def visit(span, masked):
        offset = pl.multiple_of(span * KEY_SPAN, KEY_SPAN)
        place = pl.ds(offset, KEY_SPAN)
        keys = kv_ref[place, :HEAD]
        values = kv_ref[place, HEAD:]
        scores = dot_with(keys, query, COLS_BY_COLS)
        probs = jnp.exp2(scores * (HEAD**-0.5 * LOG2E) - lse)
        if masked:
            key_given = key_given_ref[place, :]
            probs = jnp.where((key_given <= last) & (key_given >= first), probs, 0.0)
        prob_grad = dot_with(values, grad, COLS_BY_COLS)
        score_grad = (probs * (prob_grad - delta)).astype(jnp.bfloat16)
        dkv_ref[place, HEAD:] += dot(probs.astype(jnp.bfloat16), grad)
        dkv_ref[place, :HEAD] += dot(score_grad, query) * (HEAD**-0.5)
        acc[...] += dot_with(score_grad, keys, ROWS_BY_ROWS)

    lowest, open_low = bounds_ref[0, step], bounds_ref[1, step]
    open_high, highest = bounds_ref[2, step], bounds_ref[3, step]

    @pl.loop(lowest, open_low)
    def _(span):
        visit(span, True)

    @pl.loop(open_low, open_high)
    def _(span):
        visit(span, False)

    @pl.loop(open_high, highest)
    def _(span):
        visit(span, True)

    for head in range(heads):
        dq_ref[:, head * HEAD : (head + 1) * HEAD] = acc[
            head * tokens : (head + 1) * tokens
        ] * (HEAD**-0.5)


def attend_backward(bounds, query, grad, exact, lse, ask_rows, key_column, kv, pairs):
    rows, cols = query.shape
    heads = cols // HEAD
    steps = rows // QUERY_TOKENS
    stacked = heads * QUERY_TOKENS
    return pl.pallas_call(
        attend_backward_kernel,
        grid_spec=pltpu.PrefetchScalarGridSpec(
            num_scalar_prefetch=1,
            grid=(steps,),
            in_specs=[
                rows_of((QUERY_TOKENS, cols)),
                rows_of((QUERY_TOKENS, cols)),
                rows_of((QUERY_TOKENS, cols)),
                rows_of((1, 1, stacked)),
                rows_of((1, 2, stacked)),
                whole(key_column.shape),
                whole(kv.shape),
            ],
            out_specs=[rows_of((QUERY_TOKENS, cols)), whole(kv.shape)],
            scratch_shapes=[pltpu.VMEM((stacked, HEAD), jnp.float32)],
        ),
        out_shape=[
            jax.ShapeDtypeStruct((rows, cols), jnp.float32),
            jax.ShapeDtypeStruct(kv.shape, jnp.float32),
        ],
        compiler_params=params(56),
        cost_estimate=cost(20 * pairs * HEAD, 32 * MIB, pairs),
        name="attend_backward",
    )(bounds, query, grad, exact, lse, ask_rows, key_column, kv)


def selection(meta, expert, capacity):
    tokens = meta.shape[1]
    weight = jnp.sum(jnp.where(meta[:TOP] == expert, meta[TOP:], 0.0), axis=0, keepdims=True)
    member = jnp.where(weight > 0.0, 1.0, 0.0)
    earlier = lax.broadcasted_iota(jnp.int32, (tokens, tokens), 0)
    later = lax.broadcasted_iota(jnp.int32, (tokens, tokens), 1)
    before = jnp.where(earlier < later, 1.0, 0.0).astype(jnp.bfloat16)
    rank = dot(jnp.broadcast_to(member, (16, tokens)).astype(jnp.bfloat16), before)[0:1]
    rank = jnp.where(weight > 0.0, rank, -1.0).astype(jnp.int32)
    hit = lax.broadcasted_iota(jnp.int32, (capacity, tokens), 0) == rank
    gate = jnp.sum(jnp.where(hit, weight, 0.0), axis=1, keepdims=True)
    return jnp.where(hit, 1.0, 0.0).astype(jnp.bfloat16), gate


def expert_kernel(
    expert_ref, meta_ref, x_ref, c_ref, wg_ref, wu_ref, wd_ref,
    mid_ref, xs_ref, cs_ref, inner_ref, gg_ref, ug_ref,
):
    blocks, _, tokens = meta_ref.shape
    capacity = xs_ref.shape[0] // blocks
    expert = expert_ref[0].astype(jnp.float32)
    picks = []
    for block in range(blocks):
        rows = slice(block * tokens, (block + 1) * tokens)
        slots = slice(block * capacity, (block + 1) * capacity)
        pick, gate = selection(meta_ref[block], expert, capacity)
        picks.append(pick)
        xs_ref[slots] = dot(pick, x_ref[rows]).astype(jnp.bfloat16)
        cs_ref[slots] = (dot(pick, c_ref[rows]) * gate).astype(jnp.bfloat16)
    gate_part = dot(xs_ref[...], wg_ref[0])
    up_part = dot(xs_ref[...], wu_ref[0])
    inner_grad = dot_with(cs_ref[...], wd_ref[0], COLS_BY_COLS)
    gate_sig = jax.nn.sigmoid(gate_part)
    activated = gate_part * gate_sig
    inner_ref[...] = (activated * up_part).astype(jnp.bfloat16)
    gate_grad = (inner_grad * up_part * gate_sig * (1.0 + gate_part * (1.0 - gate_sig))).astype(
        jnp.bfloat16
    )
    up_grad = (inner_grad * activated).astype(jnp.bfloat16)
    gg_ref[...] = gate_grad
    ug_ref[...] = up_grad
    slot_grad = dot_with(gate_grad, wg_ref[0], COLS_BY_COLS)
    slot_grad = (slot_grad + dot_with(up_grad, wu_ref[0], COLS_BY_COLS)).astype(jnp.bfloat16)
    for block in range(blocks):
        rows = slice(block * tokens, (block + 1) * tokens)
        slots = slice(block * capacity, (block + 1) * capacity)
        mid_ref[rows] = dot_with(picks[block], slot_grad[slots], ROWS_BY_ROWS).astype(
            jnp.bfloat16
        )


def expert_pass(expert, meta, x_all, c_all, gate_w, up_w, down_w, capacity):
    blocks, lines, tokens = meta.shape
    width, hidden = gate_w.shape[1:]
    per = max(1, 512 // tokens)
    total = blocks * capacity
    slots = per * capacity
    shapes = [(blocks * tokens, width)] + [(total, width)] * 2 + [(total, hidden)] * 3
    return pl.pallas_call(
        expert_kernel,
        grid_spec=pltpu.PrefetchScalarGridSpec(
            num_scalar_prefetch=1,
            grid=(blocks // per,),
            in_specs=[
                rows_of((per, lines, tokens)),
                rows_of((per * tokens, width)),
                rows_of((per * tokens, width)),
                whole(gate_w.shape),
                whole(up_w.shape),
                whole(down_w.shape),
            ],
            out_specs=[rows_of((per * tokens, width))]
            + [rows_of((slots, width))] * 2
            + [rows_of((slots, hidden))] * 3,
        ),
        out_shape=[jax.ShapeDtypeStruct(shape, jnp.bfloat16) for shape in shapes],
        compiler_params=params(56),
        cost_estimate=cost(10 * total * width * hidden, 150 * MIB, total * hidden),
        name="expert_pass",
    )(expert, meta, x_all, c_all, gate_w, up_w, down_w)


def down_kernel(expert_ref, meta_ref, inner_ref, wd_ref, out_ref):
    blocks, _, tokens = meta_ref.shape
    capacity = inner_ref.shape[0] // blocks
    expert = expert_ref[0].astype(jnp.float32)
    result = dot(inner_ref[...], wd_ref[0]).astype(jnp.bfloat16).astype(jnp.float32)
    for block in range(blocks):
        pick, gate = selection(meta_ref[block], expert, capacity)
        slots = slice(block * capacity, (block + 1) * capacity)
        scaled = (result[slots] * gate).astype(jnp.bfloat16)
        out_ref[block * tokens : (block + 1) * tokens] = dot_with(
            pick, scaled, ROWS_BY_ROWS
        ).astype(jnp.bfloat16)


def down_pass(expert, meta, inner, down_w):
    blocks, lines, tokens = meta.shape
    total, hidden = inner.shape
    width = down_w.shape[2]
    per = max(1, 512 // tokens)
    slots = per * (total // blocks)
    return pl.pallas_call(
        down_kernel,
        grid_spec=pltpu.PrefetchScalarGridSpec(
            num_scalar_prefetch=1,
            grid=(blocks // per,),
            in_specs=[
                rows_of((per, lines, tokens)),
                rows_of((slots, hidden)),
                whole(down_w.shape),
            ],
            out_specs=rows_of((per * tokens, width)),
        ),
        out_shape=jax.ShapeDtypeStruct((blocks * tokens, width), jnp.bfloat16),
        compiler_params=params(40),
        cost_estimate=cost(2 * total * width * hidden, 40 * MIB),
        name="down_pass",
    )(expert, meta, inner, down_w)


def head_back_kernel(raw_ref, grad_ref, gain_ref, cos_ref, sin_ref, out_ref, gain_grad_ref):
    @pl.when(pl.program_id(0) == 0)
    def _():
        gain_grad_ref[...] = jnp.zeros_like(gain_grad_ref)

    cosine, sine, gain = cos_ref[...], sin_ref[...], gain_ref[...]
    for head in range(raw_ref.shape[1] // HEAD):
        part = slice(head * HEAD, (head + 1) * HEAD)
        raw = raw_ref[:, part]
        grad = grad_ref[:, part].astype(jnp.float32)
        back = grad * cosine - pltpu.roll(grad, HEAD // 2, 1) * sine
        inverse = inverse_root(raw)
        hat = raw * inverse
        gain_grad_ref[...] += jnp.sum(back * hat, axis=0, keepdims=True)
        scaled = back * gain
        out_ref[:, part] = (
            inverse * (scaled - hat * jnp.mean(scaled * hat, axis=-1, keepdims=True))
        ).astype(jnp.bfloat16)


def head_back(raw, grad, gain, cosine, sine):
    rows, cols = raw.shape
    tile = min(ROW_TILE, rows)
    return pl.pallas_call(
        head_back_kernel,
        grid=(rows // tile,),
        in_specs=[
            rows_of((tile, cols)),
            rows_of((tile, cols)),
            whole((1, HEAD)),
            rows_of((tile, HEAD)),
            rows_of((tile, HEAD)),
        ],
        out_specs=[rows_of((tile, cols)), whole((1, HEAD))],
        out_shape=[
            jax.ShapeDtypeStruct((rows, cols), jnp.bfloat16),
            jax.ShapeDtypeStruct((1, HEAD), jnp.float32),
        ],
        compiler_params=params(24),
        cost_estimate=cost(rows * cols * 20, rows * cols * 10),
        name="head_back",
    )(raw, grad, gain[None], cosine, sine)


def on_device(
    inputs,
    cotangent,
    arrangement,
    seq_lengths,
    routes,
    gate_values,
    input_gain,
    query_proj,
    key_projected,
    value_projected,
    query_gain,
    key_gain,
    output_proj,
    expert_gain,
    gate_weight,
    up_weight,
    down_weight,
):
    ep_size = lax.axis_size("ep")
    tp_size = lax.axis_size("tp")
    ep_index = lax.axis_index("ep")
    tp_index = lax.axis_index("tp")
    everyone = ("ep", "tp")
    own_rows, width = inputs.shape
    group_rows = own_rows * tp_size
    row_block = own_rows // ep_size
    token_total = arrangement.shape[0]
    expert_count = ep_size * tp_size
    capacity = 2 * own_rows * TOP // expert_count
    heads = query_proj.shape[1] // HEAD
    expert = (ep_index * tp_size + tp_index).astype(jnp.int32)[None]

    table = arrangement.reshape(ep_size, tp_size, ep_size, row_block)
    leaving_from = lax.dynamic_index_in_dim(table, tp_index, 1, keepdims=False)
    leaving_from = lax.dynamic_index_in_dim(leaving_from, ep_index, 1, keepdims=False)
    send_index = leaving_from - (ep_index * group_rows + tp_index * own_rows)
    mover = (
        send_index.reshape(-1)[:, None] == jnp.arange(own_rows, dtype=jnp.int32)[None, :]
    ).astype(jnp.bfloat16)

    def to_places(rows):
        moved = dot(mover, rows).astype(jnp.bfloat16).reshape(ep_size, row_block, width)
        return lax.all_to_all(moved, "ep", split_axis=0, concat_axis=0, tiled=True).reshape(
            own_rows, width
        )

    def to_given(rows):
        moved = lax.all_to_all(
            rows.astype(jnp.bfloat16).reshape(ep_size, row_block, width),
            "ep",
            split_axis=0,
            concat_axis=0,
            tiled=True,
        ).reshape(own_rows, width)
        return dot_with(mover, moved, ROWS_BY_ROWS)

    def group_sorted(rows):
        gathered = lax.all_gather(rows, "tp", axis=0, tiled=True)
        gathered = gathered.reshape(tp_size, ep_size, row_block, rows.shape[1])
        return jnp.swapaxes(gathered, 0, 1).reshape(group_rows, rows.shape[1])

    def scatter_group(rows):
        placed = rows.reshape(ep_size, tp_size, row_block, rows.shape[1])
        placed = jnp.swapaxes(placed, 0, 1).reshape(group_rows, rows.shape[1])
        return lax.psum_scatter(placed, "tp", scatter_dimension=0, tiled=True)

    own_inputs = to_places(inputs)
    own_cot = to_places(cotangent)
    meta_own = jnp.concatenate([routes.astype(jnp.float32).T, gate_values.T], axis=0)
    meta = lax.all_gather(meta_own, everyone, axis=0, tiled=False)
    cot_all = lax.all_gather(own_cot, everyone, axis=0, tiled=True)

    query_given = lax.dynamic_index_in_dim(table, ep_index, 0, keepdims=False)
    query_given = jnp.swapaxes(query_given, 0, 1).reshape(group_rows)
    query_first = seq_starts(query_given, seq_lengths)
    cosine, sine = rope_tables(query_given - query_first, HEAD)
    key_given = jnp.transpose(table, (2, 1, 0, 3)).reshape(token_total)
    by_step = (-1, QUERY_TOKENS)
    given_steps, first_steps = query_given.reshape(by_step), query_first.reshape(by_step)
    lowest = jnp.min(first_steps, axis=1) // KEY_SPAN
    highest = jnp.max(given_steps, axis=1) // KEY_SPAN + 1
    open_low = (jnp.max(first_steps, axis=1) + KEY_SPAN - 1) // KEY_SPAN
    open_low = jnp.minimum(open_low, highest)
    open_high = jnp.clip((jnp.min(given_steps, axis=1) + 1) // KEY_SPAN, open_low, highest)
    bounds = jnp.stack([lowest, open_low, open_high, highest]).astype(jnp.int32)
    ask = jnp.stack([query_given, query_first], axis=1)
    ask_rows = jnp.stack(
        [jnp.tile(given_steps, (1, heads)), jnp.tile(first_steps, (1, heads))], axis=1
    )

    group_x = group_sorted(own_inputs)
    normed_in, query_raw, query_rows, key_raw, kv_rows = front(
        group_x, input_gain, query_proj, key_projected, value_projected,
        query_gain, key_gain, cosine, sine,
    )
    kv_places = lax.all_gather(kv_rows, "ep", axis=0, tiled=True)
    kv_all = jnp.transpose(
        kv_places.reshape(ep_size, ep_size, tp_size, row_block, 2 * HEAD), (1, 2, 0, 3, 4)
    ).reshape(token_total, 2 * HEAD)
    pairs = group_rows * heads * 1536
    exact, out_rows, lse = attend_forward(
        bounds, query_rows, ask, key_given[None], kv_all, pairs
    )
    branch = scatter_group(dot(out_rows, output_proj).astype(jnp.bfloat16))
    hidden = own_inputs.astype(jnp.float32) + branch.astype(jnp.float32)
    mid_scale = inverse_root(hidden)
    normed_mid = (hidden * mid_scale * expert_gain).astype(jnp.bfloat16)

    mid_all = lax.all_gather(normed_mid, everyone, axis=0, tiled=True)
    mid_partial, expert_in, slot_cot, inner, gate_grad, up_grad = expert_pass(
        expert, meta, mid_all, cot_all, gate_weight, up_weight, down_weight, capacity
    )
    mid_grad = lax.psum_scatter(mid_partial, everyone, scatter_dimension=0, tiled=True).astype(
        jnp.float32
    )
    out_partial = down_pass(expert, meta, inner, down_weight)
    grad_down = dot_with(inner, slot_cot, ROWS_BY_ROWS)
    grad_gate = dot_with(expert_in, gate_grad, ROWS_BY_ROWS)
    grad_up = dot_with(expert_in, up_grad, ROWS_BY_ROWS)
    mixed = lax.psum_scatter(out_partial, everyone, scatter_dimension=0, tiled=True).astype(
        jnp.float32
    )
    layer_out = to_given(hidden + mixed).astype(jnp.bfloat16)

    mid_hat = hidden * mid_scale
    grad_expert_gain = jnp.sum(mid_grad * mid_hat, axis=0)
    mid_scaled = mid_grad * expert_gain
    hidden_grad = own_cot.astype(jnp.float32) + mid_scale * (
        mid_scaled - mid_hat * jnp.mean(mid_scaled * mid_hat, axis=-1, keepdims=True)
    )
    branch_grad = group_sorted(hidden_grad.astype(jnp.bfloat16))
    out_grad = dot_with(branch_grad, output_proj, COLS_BY_COLS).astype(jnp.bfloat16)
    query_grad, kv_grad = attend_backward(
        bounds, query_rows, out_grad, exact, lse, ask_rows, key_given[:, None], kv_all, pairs
    )
    kv_grad = jnp.transpose(
        kv_grad.astype(jnp.bfloat16).reshape(ep_size, tp_size, ep_size, row_block, 2 * HEAD),
        (2, 0, 1, 3, 4),
    ).reshape(token_total, 2 * HEAD)
    kv_own = lax.psum_scatter(kv_grad, "ep", scatter_dimension=0, tiled=True)
    value_grad = kv_own[:, HEAD:]
    raw_query_grad, grad_query_gain = head_back(query_raw, query_grad, query_gain, cosine, sine)
    raw_key_grad, grad_key_gain = head_back(key_raw, kv_own[:, :HEAD], key_gain, cosine, sine)
    normed_grad = (
        dot_with(raw_query_grad, query_proj, COLS_BY_COLS)
        + dot_with(raw_key_grad, key_projected, COLS_BY_COLS)
        + dot_with(value_grad, value_projected, COLS_BY_COLS)
    )
    normed_grad = scatter_group(normed_grad.astype(jnp.bfloat16)).astype(jnp.float32)
    own_float = own_inputs.astype(jnp.float32)
    in_scale = inverse_root(own_float)
    in_hat = own_float * in_scale
    grad_input_gain = jnp.sum(normed_grad * in_hat, axis=0)
    in_scaled = normed_grad * input_gain
    grad_inputs = to_given(
        hidden_grad
        + in_scale * (in_scaled - in_hat * jnp.mean(in_scaled * in_hat, axis=-1, keepdims=True))
    )

    def ep_sum(rows):
        return lax.psum_scatter(
            rows.astype(jnp.bfloat16), "ep", scatter_dimension=0, tiled=True
        ).astype(jnp.float32)

    grad_output = jnp.transpose(ep_sum(dot_with(branch_grad, out_rows, ROWS_BY_ROWS)))
    grad_query = ep_sum(dot_with(normed_in, raw_query_grad, ROWS_BY_ROWS))
    grad_kv = ep_sum(
        dot_with(normed_in, jnp.concatenate([raw_key_grad, value_grad], axis=1), ROWS_BY_ROWS)
    )
    gains = lax.psum(
        (grad_input_gain, grad_expert_gain, grad_query_gain[0], grad_key_gain[0]), everyone
    )
    return (
        layer_out,
        grad_inputs,
        grad_query,
        grad_kv[:, :HEAD],
        grad_kv[:, HEAD:],
        grad_output,
        gains[0],
        gains[2],
        gains[3],
        gains[1],
        grad_gate[None],
        grad_up[None],
        grad_down[None],
    )


def solution(mesh):
    split = P(("ep", "tp"), None)
    experts = P(("ep", "tp"), None, None)
    columns = P(None, "tp")
    return jax.shard_map(
        on_device,
        mesh=mesh,
        in_specs=(
            split, split, P(), P(), split, split, P(), columns, columns, columns,
            P(), P(), P("tp", None), P(), experts, experts, experts,
        ),
        out_specs=(
            split, split, P("ep", "tp"), P("ep", "tp"), P("ep", "tp"), P("tp", "ep"),
            P(), P(), P(), P(), experts, experts, experts,
        ),
        check_vma=False,
    )
```

```python
import functools
import math

import jax
import jax.numpy as jnp
from jax import lax
from jax.experimental import pallas as pl
from jax.experimental.pallas import tpu as pltpu
from jax.sharding import PartitionSpec as P

TOP = 8
EPSILON = 1e-06
ROPE_BASE = 1000000.0
KEY_SPAN = 512
QUERY_TOKENS = 32
HEAD = 128
ROW_TILE = 256
MIB = 1 << 20
LOG2E = math.log2(math.e)
ROWS_BY_ROWS = (((0,), (0,)), ((), ()))
COLS_BY_COLS = (((1,), (1,)), ((), ()))


def dot(left, right):
    return jnp.dot(left, right, preferred_element_type=jnp.float32)


def dot_with(left, right, dims):
    return lax.dot_general(left, right, dims, preferred_element_type=jnp.float32)


def cost(flops, moved, transcendentals=0):
    return pl.CostEstimate(
        flops=int(flops), bytes_accessed=int(moved), transcendentals=int(transcendentals)
    )


def params(mib):
    return pltpu.CompilerParams(
        dimension_semantics=("arbitrary",), vmem_limit_bytes=mib * MIB
    )


def whole(shape, single=True):
    rank = len(shape)
    if single:
        return pl.BlockSpec(shape, lambda *ids: (0,) * rank, pipeline_mode=pl.Buffered(1))
    return pl.BlockSpec(shape, lambda *ids: (0,) * rank)


def rows_of(shape):
    rank = len(shape)
    return pl.BlockSpec(shape, lambda i, *ids: (i,) + (0,) * (rank - 1))


def rope_tables(positions, head_dim):
    freqs = ROPE_BASE ** (-jnp.arange(0, head_dim, 2, dtype=jnp.float32) / head_dim)
    angles = positions.astype(jnp.float32)[:, None] * freqs[None, :]
    cosine, sine = jnp.cos(angles), jnp.sin(angles)
    return (
        jnp.concatenate([cosine, cosine], axis=-1),
        jnp.concatenate([-sine, sine], axis=-1),
    )


def seq_starts(given, seq_lengths):
    ends = jnp.cumsum(seq_lengths)
    passed = given[:, None] >= ends[None, :]
    return jnp.sum(jnp.where(passed, seq_lengths[None, :], 0), axis=1)


def inverse_root(values):
    return lax.rsqrt(jnp.mean(values * values, axis=-1, keepdims=True) + EPSILON)


def front_kernel(
    x_ref, gain_ref, wq_ref, wk_ref, wv_ref, qg_ref, kg_ref, cos_ref, sin_ref,
    normed_ref, qraw_ref, q_ref, kraw_ref, kv_ref,
):
    x = x_ref[...].astype(jnp.float32)
    normed = (x * inverse_root(x) * gain_ref[...]).astype(jnp.bfloat16)
    normed_ref[...] = normed
    cosine, sine = cos_ref[...], sin_ref[...]

    def prepare(raw, gain):
        values = raw * inverse_root(raw) * gain
        return (values * cosine + pltpu.roll(values, HEAD // 2, 1) * sine).astype(jnp.bfloat16)

    raw = dot(normed, wq_ref[...])
    qraw_ref[...] = raw
    for head in range(raw.shape[1] // HEAD):
        part = slice(head * HEAD, (head + 1) * HEAD)
        q_ref[:, part] = prepare(raw[:, part], qg_ref[...])
    raw = dot(normed, wk_ref[...])
    kraw_ref[...] = raw
    kv_ref[:, :HEAD] = prepare(raw, kg_ref[...])
    kv_ref[:, HEAD:] = dot(normed, wv_ref[...]).astype(jnp.bfloat16)


def front(group_x, input_gain, wq, wk, wv, query_gain, key_gain, cosine, sine):
    rows, width = group_x.shape
    cols = wq.shape[1]
    tile = min(ROW_TILE, rows)
    out = [
        ((rows, width), jnp.bfloat16),
        ((rows, cols), jnp.float32),
        ((rows, cols), jnp.bfloat16),
        ((rows, HEAD), jnp.float32),
        ((rows, 2 * HEAD), jnp.bfloat16),
    ]
    return pl.pallas_call(
        front_kernel,
        grid=(rows // tile,),
        in_specs=[
            rows_of((tile, width)),
            whole((1, width)),
            whole(wq.shape),
            whole(wk.shape),
            whole(wv.shape),
            whole((1, HEAD)),
            whole((1, HEAD)),
            rows_of((tile, HEAD)),
            rows_of((tile, HEAD)),
        ],
        out_specs=[rows_of((tile, shape[1])) for shape, kind in out],
        out_shape=[jax.ShapeDtypeStruct(shape, kind) for shape, kind in out],
        compiler_params=params(40),
        cost_estimate=cost(2 * rows * width * (cols + 2 * HEAD), 20 * MIB),
        name="front",
    )(
        group_x,
        input_gain[None],
        wq,
        wk,
        wv,
        query_gain[None],
        key_gain[None],
        cosine,
        sine,
    )


def stack_heads(block):
    heads = block.shape[1] // HEAD
    return jnp.concatenate(
        [block[:, head * HEAD : (head + 1) * HEAD] for head in range(heads)], axis=0
    )


def attend_forward_kernel(
    bounds_ref, q_ref, ask_ref, key_given_ref, kv_ref, exact_ref, out_ref, lse_ref, acc, tot
):
    step = pl.program_id(0)
    tokens, cols = q_ref.shape
    heads = cols // HEAD
    query = stack_heads(q_ref[...])
    ask = ask_ref[...]
    last = jnp.concatenate([ask[:, 0:1]] * heads, axis=0)
    first = jnp.concatenate([ask[:, 1:2]] * heads, axis=0)
    acc[...] = jnp.zeros_like(acc)
    tot[...] = jnp.zeros_like(tot)

    def visit(span, masked):
        offset = pl.multiple_of(span * KEY_SPAN, KEY_SPAN)
        keys = kv_ref[pl.ds(offset, KEY_SPAN), :HEAD]
        values = kv_ref[pl.ds(offset, KEY_SPAN), HEAD:]
        scores = dot_with(query, keys, COLS_BY_COLS)
        weights = jnp.exp2(scores * (HEAD**-0.5 * LOG2E))
        if masked:
            key_given = key_given_ref[:, pl.ds(offset, KEY_SPAN)]
            weights = jnp.where((key_given <= last) & (key_given >= first), weights, 0.0)
        part = weights[:, :HEAD]
        for chunk in range(1, KEY_SPAN // HEAD):
            part = part + weights[:, chunk * HEAD : (chunk + 1) * HEAD]
        tot[...] += part
        acc[...] += dot(weights.astype(jnp.bfloat16), values)

    lowest, open_low = bounds_ref[0, step], bounds_ref[1, step]
    open_high, highest = bounds_ref[2, step], bounds_ref[3, step]

    @pl.loop(lowest, open_low)
    def _(span):
        visit(span, True)

    @pl.loop(open_low, open_high)
    def _(span):
        visit(span, False)

    @pl.loop(open_high, highest)
    def _(span):
        visit(span, True)

    total = tot[...]
    exact = acc[...] / jnp.sum(total, axis=1, keepdims=True)
    for head in range(heads):
        rows = exact[head * tokens : (head + 1) * tokens]
        exact_ref[:, head * HEAD : (head + 1) * HEAD] = rows
        out_ref[:, head * HEAD : (head + 1) * HEAD] = rows.astype(jnp.bfloat16)
    lse_ref[0] = jnp.log2(jnp.sum(total.T, axis=0, keepdims=True))


def attend_forward(bounds, query, ask, key_given, kv, pairs):
    rows, cols = query.shape
    heads = cols // HEAD
    steps = rows // QUERY_TOKENS
    stacked = heads * QUERY_TOKENS
    return pl.pallas_call(
        attend_forward_kernel,
        grid_spec=pltpu.PrefetchScalarGridSpec(
            num_scalar_prefetch=1,
            grid=(steps,),
            in_specs=[
                rows_of((QUERY_TOKENS, cols)),
                rows_of((QUERY_TOKENS, 2)),
                whole(key_given.shape),
                whole(kv.shape),
            ],
            out_specs=[
                rows_of((QUERY_TOKENS, cols)),
                rows_of((QUERY_TOKENS, cols)),
                rows_of((1, 1, stacked)),
            ],
            scratch_shapes=[
                pltpu.VMEM((stacked, HEAD), jnp.float32),
                pltpu.VMEM((stacked, HEAD), jnp.float32),
            ],
        ),
        out_shape=[
            jax.ShapeDtypeStruct((rows, cols), jnp.float32),
            jax.ShapeDtypeStruct((rows, cols), jnp.bfloat16),
            jax.ShapeDtypeStruct((steps, 1, stacked), jnp.float32),
        ],
        compiler_params=params(48),
        cost_estimate=cost(8 * pairs * HEAD, 16 * MIB, pairs),
        name="attend_forward",
    )(bounds, query, ask, key_given, kv)


def attend_backward_kernel(
    bounds_ref, q_ref, grad_ref, exact_ref, lse_ref, ask_ref, key_given_ref, kv_ref,
    dq_ref, rounded_ref, dkv_ref, acc,
):
    step = pl.program_id(0)
    tokens, cols = q_ref.shape
    heads = cols // HEAD

    @pl.when(step == 0)
    def _():
        dkv_ref[...] = jnp.zeros_like(dkv_ref)

    query = stack_heads(q_ref[...])
    grad = stack_heads(grad_ref[...])
    product = grad.astype(jnp.float32) * stack_heads(exact_ref[...])
    delta = jnp.sum(product.T, axis=0, keepdims=True)
    lse = lse_ref[0]
    last, first = ask_ref[0, 0:1, :], ask_ref[0, 1:2, :]
    acc[...] = jnp.zeros_like(acc)

    def visit(span, masked):
        offset = pl.multiple_of(span * KEY_SPAN, KEY_SPAN)
        place = pl.ds(offset, KEY_SPAN)
        keys = kv_ref[place, :HEAD]
        values = kv_ref[place, HEAD:]
        scores = dot_with(keys, query, COLS_BY_COLS)
        probs = jnp.exp2(scores * (HEAD**-0.5 * LOG2E) - lse)
        if masked:
            key_given = key_given_ref[place, :]
            probs = jnp.where((key_given <= last) & (key_given >= first), probs, 0.0)
        prob_grad = dot_with(values, grad, COLS_BY_COLS)
        score_grad = (probs * (prob_grad - delta)).astype(jnp.bfloat16)
        dkv_ref[place, HEAD:] += dot(probs.astype(jnp.bfloat16), grad)
        dkv_ref[place, :HEAD] += dot(score_grad, query) * (HEAD**-0.5)
        acc[...] += dot_with(score_grad, keys, ROWS_BY_ROWS)

    lowest, open_low = bounds_ref[0, step], bounds_ref[1, step]
    open_high, highest = bounds_ref[2, step], bounds_ref[3, step]

    @pl.loop(lowest, open_low)
    def _(span):
        visit(span, True)

    @pl.loop(open_low, open_high)
    def _(span):
        visit(span, False)

    @pl.loop(open_high, highest)
    def _(span):
        visit(span, True)

    for head in range(heads):
        dq_ref[:, head * HEAD : (head + 1) * HEAD] = acc[
            head * tokens : (head + 1) * tokens
        ] * (HEAD**-0.5)

    @pl.when(step == pl.num_programs(0) - 1)
    def _():
        @pl.loop(0, dkv_ref.shape[0], step=KEY_SPAN)
        def _(row):
            place = pl.ds(row, KEY_SPAN)
            rounded_ref[place] = dkv_ref[place].astype(jnp.bfloat16)


def attend_backward(bounds, query, grad, exact, lse, ask_rows, key_column, kv, pairs):
    rows, cols = query.shape
    heads = cols // HEAD
    steps = rows // QUERY_TOKENS
    stacked = heads * QUERY_TOKENS
    return pl.pallas_call(
        attend_backward_kernel,
        grid_spec=pltpu.PrefetchScalarGridSpec(
            num_scalar_prefetch=1,
            grid=(steps,),
            in_specs=[
                rows_of((QUERY_TOKENS, cols)),
                rows_of((QUERY_TOKENS, cols)),
                rows_of((QUERY_TOKENS, cols)),
                rows_of((1, 1, stacked)),
                rows_of((1, 2, stacked)),
                whole(key_column.shape),
                whole(kv.shape),
            ],
            out_specs=[rows_of((QUERY_TOKENS, cols)), whole(kv.shape)],
            scratch_shapes=[
                pltpu.VMEM(kv.shape, jnp.float32),
                pltpu.VMEM((stacked, HEAD), jnp.float32),
            ],
        ),
        out_shape=[
            jax.ShapeDtypeStruct((rows, cols), jnp.float32),
            jax.ShapeDtypeStruct(kv.shape, jnp.bfloat16),
        ],
        compiler_params=params(56),
        cost_estimate=cost(20 * pairs * HEAD, 32 * MIB, pairs),
        name="attend_backward",
    )(bounds, query, grad, exact, lse, ask_rows, key_column, kv)


def selection(meta, expert, capacity):
    tokens = meta.shape[1]
    weight = jnp.sum(jnp.where(meta[:TOP] == expert, meta[TOP : 2 * TOP], 0.0), axis=0, keepdims=True)
    member = jnp.where(weight > 0.0, 1.0, 0.0)
    earlier = lax.broadcasted_iota(jnp.int32, (tokens, tokens), 0)
    later = lax.broadcasted_iota(jnp.int32, (tokens, tokens), 1)
    before = jnp.where(earlier < later, 1.0, 0.0).astype(jnp.bfloat16)
    rank = dot(jnp.broadcast_to(member, (16, tokens)).astype(jnp.bfloat16), before)[0:1]
    rank = jnp.where(weight > 0.0, rank, -1.0).astype(jnp.int32)
    hit = lax.broadcasted_iota(jnp.int32, (capacity, tokens), 0) == rank
    gate = jnp.sum(jnp.where(hit, weight, 0.0), axis=1, keepdims=True)
    return jnp.where(hit, 1.0, 0.0).astype(jnp.bfloat16), gate


def expert_kernel(
    expert_ref, meta_ref, x_ref, c_ref, wg_ref, wu_ref, wd_ref,
    mid_ref, out_ref, xs_ref, cs_ref, inner_ref, gg_ref, ug_ref,
):
    blocks, _, tokens = meta_ref.shape
    capacity = xs_ref.shape[0] // blocks
    expert = expert_ref[0].astype(jnp.float32)
    picks, gates = [], []
    for block in range(blocks):
        rows = slice(block * tokens, (block + 1) * tokens)
        slots = slice(block * capacity, (block + 1) * capacity)
        pick, gate = selection(meta_ref[block], expert, capacity)
        picks.append(pick)
        gates.append(gate)
        xs_ref[slots] = dot(pick, x_ref[rows]).astype(jnp.bfloat16)
        cs_ref[slots] = (dot(pick, c_ref[rows]) * gate).astype(jnp.bfloat16)
    gate_part = dot(xs_ref[...], wg_ref[0])
    up_part = dot(xs_ref[...], wu_ref[0])
    inner_grad = dot_with(cs_ref[...], wd_ref[0], COLS_BY_COLS)
    gate_sig = jax.nn.sigmoid(gate_part)
    activated = gate_part * gate_sig
    inner = (activated * up_part).astype(jnp.bfloat16)
    inner_ref[...] = inner
    gate_grad = (inner_grad * up_part * gate_sig * (1.0 + gate_part * (1.0 - gate_sig))).astype(
        jnp.bfloat16
    )
    up_grad = (inner_grad * activated).astype(jnp.bfloat16)
    gg_ref[...] = gate_grad
    ug_ref[...] = up_grad
    slot_grad = dot_with(gate_grad, wg_ref[0], COLS_BY_COLS)
    slot_grad = (slot_grad + dot_with(up_grad, wu_ref[0], COLS_BY_COLS)).astype(jnp.bfloat16)
    for block in range(blocks):
        rows = slice(block * tokens, (block + 1) * tokens)
        slots = slice(block * capacity, (block + 1) * capacity)
        mid_ref[rows] = dot_with(picks[block], slot_grad[slots], ROWS_BY_ROWS).astype(
            jnp.bfloat16
        )
    result = dot(inner, wd_ref[0]).astype(jnp.bfloat16).astype(jnp.float32)
    for block in range(blocks):
        rows = slice(block * tokens, (block + 1) * tokens)
        slots = slice(block * capacity, (block + 1) * capacity)
        scaled = (result[slots] * gates[block]).astype(jnp.bfloat16)
        out_ref[rows] = dot_with(picks[block], scaled, ROWS_BY_ROWS).astype(jnp.bfloat16)


def expert_pass(expert, meta, x_all, c_all, gate_w, up_w, down_w, capacity):
    blocks, lines, tokens = meta.shape
    width, hidden = gate_w.shape[1:]
    per = max(1, 512 // tokens)
    total = blocks * capacity
    slots = per * capacity
    shapes = [(blocks * tokens, width)] * 2 + [(total, width)] * 2 + [(total, hidden)] * 3
    return pl.pallas_call(
        expert_kernel,
        grid_spec=pltpu.PrefetchScalarGridSpec(
            num_scalar_prefetch=1,
            grid=(blocks // per,),
            in_specs=[
                rows_of((per, lines, tokens)),
                rows_of((per * tokens, width)),
                rows_of((per * tokens, width)),
                whole(gate_w.shape),
                whole(up_w.shape),
                whole(down_w.shape),
            ],
            out_specs=[rows_of((per * tokens, width))] * 2
            + [rows_of((slots, width))] * 2
            + [rows_of((slots, hidden))] * 3,
        ),
        out_shape=[jax.ShapeDtypeStruct(shape, jnp.bfloat16) for shape in shapes],
        compiler_params=params(56),
        cost_estimate=cost(10 * total * width * hidden, 150 * MIB, total * hidden),
        name="expert_pass",
    )(expert, meta, x_all, c_all, gate_w, up_w, down_w)


def head_back_kernel(raw_ref, grad_ref, gain_ref, cos_ref, sin_ref, out_ref, gain_grad_ref):
    @pl.when(pl.program_id(0) == 0)
    def _():
        gain_grad_ref[...] = jnp.zeros_like(gain_grad_ref)

    cosine, sine, gain = cos_ref[...], sin_ref[...], gain_ref[...]
    for head in range(raw_ref.shape[1] // HEAD):
        part = slice(head * HEAD, (head + 1) * HEAD)
        raw = raw_ref[:, part]
        grad = grad_ref[:, part].astype(jnp.float32)
        back = grad * cosine - pltpu.roll(grad, HEAD // 2, 1) * sine
        inverse = inverse_root(raw)
        hat = raw * inverse
        gain_grad_ref[...] += jnp.sum(back * hat, axis=0, keepdims=True)
        scaled = back * gain
        out_ref[:, part] = (
            inverse * (scaled - hat * jnp.mean(scaled * hat, axis=-1, keepdims=True))
        ).astype(jnp.bfloat16)


def head_back(raw, grad, gain, cosine, sine):
    rows, cols = raw.shape
    tile = min(ROW_TILE, rows)
    return pl.pallas_call(
        head_back_kernel,
        grid=(rows // tile,),
        in_specs=[
            rows_of((tile, cols)),
            rows_of((tile, cols)),
            whole((1, HEAD)),
            rows_of((tile, HEAD)),
            rows_of((tile, HEAD)),
        ],
        out_specs=[rows_of((tile, cols)), whole((1, HEAD))],
        out_shape=[
            jax.ShapeDtypeStruct((rows, cols), jnp.bfloat16),
            jax.ShapeDtypeStruct((1, HEAD), jnp.float32),
        ],
        compiler_params=params(24),
        cost_estimate=cost(rows * cols * 20, rows * cols * 10),
        name="head_back",
    )(raw, grad, gain[None], cosine, sine)


MESH_ID = pl.DeviceIdType.MESH


class Place:
    def __init__(self, send_sem, tp_size=4):
        self.tp_size, self.send_sem, self.sent = tp_size, send_sem, []
        self.ep, self.tp = lax.axis_index("ep"), lax.axis_index("tp")
        self.z, self.y, self.x, self.core = self.ep // 2, self.ep % 2, self.tp // 2, self.tp % 2
        self.over_x = self.tp + 2 - 4 * self.x
        self.over_core = self.tp + 1 - 2 * self.core
        self.over_both = self.over_core + 2 - 4 * self.x

    def level(self, step):
        return (self.z, self.z + 1 - 2 * (self.z % 2), (self.z + 2) % 4, 3 - self.z)[step]

    def across(self, step, over_y):
        return self.level(step) * 2 + self.y + over_y * (1 - 2 * self.y)

    def device(self, step, first, second, other=0):
        core = self.core + other * (1 - 2 * self.core)
        over_y = first * (1 - core) + second * core
        over_x = first * core + second * (1 - core)
        x = self.x + over_x * (1 - 2 * self.x)
        return self.across(step, over_y), x * 2 + core

    def slot(self, *where):
        ep, tp = self.device(*where)
        return ep * self.tp_size + tp

    def greet(self, partners):
        barrier = pltpu.get_barrier_semaphore()
        for partner in partners:
            pl.semaphore_signal(barrier, inc=1, device_id=partner, device_id_type=MESH_ID)
        pl.semaphore_wait(barrier, len(partners))

    def greet_all_ways(self):
        partners = [(1, 0, 0), (2, 0, 0), (3, 0, 0), (0, 1, 0), (0, 0, 1), (0, 0, 0, 1)]
        self.greet([self.device(*partner) for partner in partners])

    def send(self, src, dst, sem, device):
        copy = pltpu.make_async_remote_copy(
            src_ref=src,
            dst_ref=dst,
            send_sem=self.send_sem.at[len(self.sent)],
            recv_sem=sem,
            device_id=device,
            device_id_type=MESH_ID,
        )
        copy.start()
        self.sent.append(copy)

    def arrive(self, dst, sem):
        pltpu.make_async_remote_copy(
            src_ref=dst,
            dst_ref=dst,
            send_sem=self.send_sem.at[0],
            recv_sem=sem,
            device_id=(self.ep, self.over_core),
            device_id_type=MESH_ID,
        ).wait_recv()

    def finish(self):
        for copy in self.sent:
            copy.wait_send()


def reach(kernel, out, scratch, ident, *operands, vmem_out=False, mib=None):
    dma = [kind if not isinstance(kind, tuple) else pltpu.SemaphoreType.DMA(kind) for kind in scratch]
    space = pltpu.VMEM if vmem_out else pl.ANY
    single = not isinstance(out, (list, tuple))
    return pl.pallas_call(
        kernel,
        in_specs=[pl.BlockSpec(memory_space=pl.ANY)] * len(operands),
        out_specs=jax.tree.map(lambda _: pl.BlockSpec(memory_space=space), out),
        out_shape=out,
        scratch_shapes=dma,
        compiler_params=pltpu.CompilerParams(
            collective_id=ident,
            has_side_effects=True,
            vmem_limit_bytes=(mib or 16) * MIB,
        ),
        cost_estimate=cost(1, 1),
        name=kernel.__name__ if not isinstance(kernel, functools.partial) else kernel.func.__name__,
    )(*operands)


def gather_all_kernel(x_ref, m_ref, out_ref, lines_ref, own_sem, send_sem, recv_sem, line_sem):
    place = Place(send_sem)
    rows, lines = x_ref.shape[0], m_ref.shape[0]

    def part(slot):
        return out_ref.at[pl.ds(slot * rows, rows)]

    def some(slot):
        return lines_ref.at[pl.ds(slot * lines, lines)]

    def send(where, partner):
        slot = place.slot(*where)
        own = where == (0, 0, 0)
        device = place.device(*partner)
        place.send(m_ref if own else some(slot), some(slot), line_sem.at[slot], device)
        place.send(x_ref if own else part(slot), part(slot), recv_sem.at[slot], device)

    def arrive(*where):
        slot = place.slot(*where)
        place.arrive(some(slot), line_sem.at[slot])
        place.arrive(part(slot), recv_sem.at[slot])

    mine = place.slot(0, 0, 0)
    own = [
        pltpu.make_async_copy(x_ref, part(mine), own_sem.at[0]),
        pltpu.make_async_copy(m_ref, some(mine), own_sem.at[1]),
    ]
    for copy in own:
        copy.start()
    place.greet_all_ways()
    for step in (1, 2, 3):
        send((0, 0, 0), (step, 0, 0))
    for step in range(4):
        if step:
            arrive(step, 0, 0)
        send((step, 0, 0), (0, 1, 0))
        send((step, 0, 0), (0, 0, 1))
        send((step, 0, 0), (0, 0, 0, 1))
        if step:
            arrive(step - 1, 1, 0)
            send((step - 1, 1, 0), (0, 0, 1))
            send((step - 1, 1, 0), (0, 0, 0, 1))
    arrive(3, 1, 0)
    send((3, 1, 0), (0, 0, 1))
    send((3, 1, 0), (0, 0, 0, 1))
    for step in range(4):
        for first in (0, 1):
            arrive(step, first, 1)
            send((step, first, 1), (0, 0, 0, 1))
    for step in range(4):
        for first in (0, 1):
            for second in (0, 1):
                arrive(step, first, second, 1)
    for copy in own:
        copy.wait()
    place.finish()


def gather_all(x, lines, parts, ident):
    out = [
        jax.ShapeDtypeStruct((parts * array.shape[0], array.shape[1]), array.dtype)
        for array in (x, lines)
    ]
    scratch = [(2,), (2 * parts - 2,), (parts,), (parts,)]
    return reach(gather_all_kernel, out, scratch, ident, x, lines)


BUFFERS = 4


def scatter_all_kernel(
    p_ref, out_ref, held, over_second, over_first, over_z, own,
    own_sem, send_sem, core_sem, second_sem, first_sem, z_sem,
):
    place = Place(send_sem)
    rows = out_ref.shape[0]

    def add(total, other):
        @pl.loop(0, rows, step=64)
        def _(row):
            some = pl.ds(row, 64)
            total[some] = total[some] + other[some]

    def part(slot):
        return p_ref.at[pl.ds(slot * rows, rows)]

    order = [(step, first, second) for second in (1, 0) for step in (3, 2, 1, 0) for first in (1, 0)]
    loads = []

    def load(number):
        buffer = number % BUFFERS
        copy = pltpu.make_async_copy(
            part(place.slot(*order[number])), own.at[buffer], own_sem.at[buffer]
        )
        copy.start()
        loads.append(copy)

    for number in range(BUFFERS):
        load(number)
    place.greet_all_ways()
    for step, first, second in order:
        place.send(
            part(place.slot(step, first, second, 1)),
            held.at[step, first, second],
            core_sem.at[step, first, second],
            place.device(0, 0, 0, 1),
        )
    for number, (step, first, second) in enumerate(order):
        mine = held.at[step, first, second]
        place.arrive(mine, core_sem.at[step, first, second])
        loads[number].wait()
        add(mine, own.at[number % BUFFERS])
        if number + BUFFERS < len(order):
            load(number + BUFFERS)
        if second:
            place.send(
                mine, over_second.at[step, first], second_sem.at[step, first], place.device(0, 0, 1)
            )

    def onward(step):
        mine = held.at[step, 0, 0]
        place.arrive(over_first.at[step], first_sem.at[step])
        add(mine, over_first.at[step])
        if step:
            place.send(mine, over_z.at[step], z_sem.at[step], place.device(step, 0, 0))

    for step in (3, 2, 1, 0):
        mine = held.at[step, 1, 0]
        place.arrive(over_second.at[step, 1], second_sem.at[step, 1])
        add(mine, over_second.at[step, 1])
        place.send(mine, over_first.at[step], first_sem.at[step], place.device(0, 1, 0))
        mine = held.at[step, 0, 0]
        place.arrive(over_second.at[step, 0], second_sem.at[step, 0])
        add(mine, over_second.at[step, 0])
        if step < 3:
            onward(step + 1)
    onward(0)
    for step in (3, 2, 1):
        place.arrive(over_z.at[step], z_sem.at[step])

    @pl.loop(0, rows, step=32)
    def _(row):
        some = pl.ds(row, 32)
        total = held[0, 0, 0, some].astype(jnp.float32)
        for step in (1, 2, 3):
            total = total + over_z[step, some].astype(jnp.float32)
        out_ref[some] = total

    place.finish()


def scatter_all(p, parts, ident):
    rows, width = p.shape[0] // parts, p.shape[1]

    def buffer(*lead):
        return pltpu.VMEM((*lead, rows, width), p.dtype)

    scratch = [buffer(4, 2, 2), buffer(4, 2), buffer(4), buffer(4), buffer(BUFFERS)]
    scratch += [(BUFFERS,), (parts - 1,), (4, 2, 2), (4, 2), (4,), (4,)]
    out = jax.ShapeDtypeStruct((rows, width), jnp.float32)
    return reach(scatter_all_kernel, out, scratch, ident, p, vmem_out=True, mib=56)


def enter_kernel(x_ref, c_ref, group_ref, cot_ref, own_sem, send_sem, x_sem, cot_sem):
    place = Place(send_sem)
    ep, tp = place.ep, place.tp
    others = [place.across(step, over) for step in range(4) for over in (0, 1)]
    own = [
        pltpu.make_async_copy(x_ref.at[ep], group_ref.at[ep, tp], own_sem.at[0]),
        pltpu.make_async_copy(c_ref.at[ep], cot_ref.at[ep], own_sem.at[1]),
    ]
    for copy in own:
        copy.start()
    place.greet(
        [(other, tp) for other in others[1:]] + [(ep, place.over_x), (ep, place.over_core)]
    )
    for other in others[1:]:
        place.send(x_ref.at[other], group_ref.at[ep, tp], x_sem.at[ep, tp], (other, tp))
    for number, other in enumerate(others):
        block = group_ref.at[other, tp]
        if number:
            place.arrive(block, x_sem.at[other, tp])
        source = block if number else x_ref.at[ep]
        place.send(source, block, x_sem.at[other, tp], (ep, place.over_x))
        place.send(source, block, x_sem.at[other, tp], (ep, place.over_core))
    for other in others[1:]:
        place.send(c_ref.at[other], cot_ref.at[ep], cot_sem.at[ep], (other, tp))
    for other in others:
        block = group_ref.at[other, place.over_x]
        place.arrive(block, x_sem.at[other, place.over_x])
        place.send(block, block, x_sem.at[other, place.over_x], (ep, place.over_core))
    for other in others:
        for source in (place.over_core, place.over_both):
            place.arrive(group_ref.at[other, source], x_sem.at[other, source])
    for other in others[1:]:
        place.arrive(cot_ref.at[other], cot_sem.at[other])
    for copy in own:
        copy.wait()
    place.finish()


def enter(x, c, tp_size, ident):
    ep_size, block, width = x.shape
    moves = (ep_size - 1) * 2 + ep_size * 3
    out = [
        jax.ShapeDtypeStruct((ep_size, tp_size, block, width), x.dtype),
        jax.ShapeDtypeStruct((ep_size, block, width), x.dtype),
    ]
    scratch = [(2,), (moves,), (ep_size, tp_size), (ep_size,)]
    return reach(enter_kernel, out, scratch, ident, x, c)


CHUNKS = 4


def gather_group_kernel(x_ref, group_ref, own_sem, send_sem, recv_sem):
    place = Place(send_sem)
    ep, tp = place.ep, place.tp
    some = x_ref.shape[0] // CHUNKS

    def piece(chunk, owner):
        return group_ref.at[pl.ds(chunk * some, some), owner]

    own = pltpu.make_async_copy(x_ref, group_ref.at[:, tp], own_sem)
    own.start()
    place.greet([(ep, place.over_x), (ep, place.over_core)])
    for partner in (place.over_x, place.over_core):
        for chunk in range(CHUNKS):
            place.send(
                x_ref.at[pl.ds(chunk * some, some)],
                piece(chunk, tp),
                recv_sem.at[chunk, tp],
                (ep, partner),
            )
    for chunk in range(CHUNKS):
        block = piece(chunk, place.over_x)
        place.arrive(block, recv_sem.at[chunk, place.over_x])
        place.send(block, block, recv_sem.at[chunk, place.over_x], (ep, place.over_core))
    for chunk in range(CHUNKS):
        for source in (place.over_core, place.over_both):
            place.arrive(piece(chunk, source), recv_sem.at[chunk, source])
    own.wait()
    place.finish()


def gather_group(x, tp_size, ident):
    ep_size, block, width = x.shape
    out = jax.ShapeDtypeStruct((ep_size, tp_size, block, width), x.dtype)
    scratch = [pltpu.SemaphoreType.DMA, (CHUNKS * 3,), (CHUNKS, tp_size)]
    return reach(gather_group_kernel, out, scratch, ident, x)


def scatter_group_kernel(
    p_ref, out_ref, own, held, over_x, own_sem, send_sem, core_sem, x_sem
):
    place = Place(send_sem)
    ep, tp = place.ep, place.tp
    some = p_ref.shape[0] // CHUNKS
    block, width = p_ref.shape[2:]

    def chunk_of(chunk):
        return pl.ds(chunk * some, some)

    loads = [
        pltpu.make_async_copy(p_ref.at[:, owner], own.at[number], own_sem.at[number])
        for number, owner in enumerate((place.over_x, tp))
    ]
    for copy in loads:
        copy.start()
    place.greet([(ep, place.over_x), (ep, place.over_core)])
    for number, owner in enumerate((place.over_both, place.over_core)):
        for chunk in range(CHUNKS):
            place.send(
                p_ref.at[chunk_of(chunk), owner],
                held.at[number, chunk_of(chunk)],
                core_sem.at[number, chunk],
                (ep, place.over_core),
            )

    def add(number, chunk):
        place.arrive(held.at[number, chunk_of(chunk)], core_sem.at[number, chunk])
        for row in range(chunk * some, (chunk + 1) * some):
            held[number, row] = held[number, row] + own[number, row]

    loads[0].wait()
    for chunk in range(CHUNKS):
        add(0, chunk)
        place.send(
            held.at[0, chunk_of(chunk)],
            over_x.at[chunk_of(chunk)],
            x_sem.at[chunk],
            (ep, place.over_x),
        )
    loads[1].wait()
    for chunk in range(CHUNKS):
        add(1, chunk)
    for chunk in range(CHUNKS):
        place.arrive(over_x.at[chunk_of(chunk)], x_sem.at[chunk])
        for row in range(chunk * some, (chunk + 1) * some):
            out_ref[row] = held[1, row].astype(jnp.float32) + over_x[row].astype(jnp.float32)
    place.finish()


def scatter_group(p, ident):
    ep_size, tp_size, block, width = p.shape

    def buffer(*lead):
        return pltpu.VMEM((*lead, ep_size, block, width), p.dtype)

    scratch = [buffer(2), buffer(2), buffer(), (2,), (CHUNKS * 3,), (2, CHUNKS), (CHUNKS,)]
    out = jax.ShapeDtypeStruct((ep_size, block, width), jnp.float32)
    return reach(scatter_group_kernel, out, scratch, ident, p, vmem_out=True, mib=24)


def gather_kv_kernel(kv_ref, out_ref, own_sem, send_sem, recv_sem):
    place = Place(send_sem)
    ep, tp = place.ep, place.tp
    own = pltpu.make_async_copy(kv_ref, out_ref.at[:, ep], own_sem)
    own.start()
    partners = [place.across(*where) for where in ((1, 0), (2, 0), (3, 0), (0, 1))]
    place.greet([(partner, tp) for partner in partners])
    for partner in (partners[3], *partners[:3]):
        place.send(kv_ref, out_ref.at[:, ep], recv_sem.at[ep], (partner, tp))
    for partner in partners[:3]:
        block = out_ref.at[:, partner]
        place.arrive(block, recv_sem.at[partner])
        place.send(block, block, recv_sem.at[partner], (partners[3], tp))
    for step in range(4):
        other = place.across(step, 1)
        place.arrive(out_ref.at[:, other], recv_sem.at[other])
    own.wait()
    place.finish()


def gather_kv(kv, ep_size, ident):
    blocks, rows, width = kv.shape
    out = jax.ShapeDtypeStruct((blocks, ep_size, rows, width), kv.dtype)
    scratch = [pltpu.SemaphoreType.DMA, (ep_size - 1,), (ep_size,)]
    return reach(gather_kv_kernel, out, scratch, ident, kv)


def scatter_kv_kernel(p_ref, out_ref, own, over_y, over_z, own_sem, send_sem, y_sem, z_sem):
    place = Place(send_sem)
    tp = place.tp
    blocks = out_ref.shape[0]
    order = (3, 2, 1, 0)
    loads = {}
    for step in order:
        loads[step] = pltpu.make_async_copy(
            p_ref.at[:, place.across(step, 0)], own.at[step], own_sem.at[step]
        )
        loads[step].start()
    place.greet([(place.across(*where), tp) for where in ((1, 0), (2, 0), (3, 0), (0, 1))])
    for step in order:
        place.send(
            p_ref.at[:, place.across(step, 1)],
            over_y.at[step],
            y_sem.at[step],
            (place.across(0, 1), tp),
        )
    for step in order:
        loads[step].wait()
        place.arrive(over_y.at[step], y_sem.at[step])

        @pl.loop(0, blocks)
        def _(block, step=step):
            own[step, block] = own[step, block] + over_y[step, block]

        if step:
            place.send(
                own.at[step], over_z.at[step], z_sem.at[step], (place.across(step, 0), tp)
            )
    for step in (3, 2, 1):
        place.arrive(over_z.at[step], z_sem.at[step])

    @pl.loop(0, blocks)
    def _(block):
        total = own[0, block].astype(jnp.float32)
        for step in (1, 2, 3):
            total = total + over_z[step, block].astype(jnp.float32)
        out_ref[block] = total.astype(jnp.bfloat16)

    place.finish()


def scatter_kv(p, ident):
    blocks, ep_size, rows, width = p.shape
    buffer = pltpu.VMEM((4, blocks, rows, width), p.dtype)
    scratch = [buffer, buffer, buffer, (4,), (7,), (4,), (4,)]
    out = jax.ShapeDtypeStruct((blocks, rows, width), p.dtype)
    return reach(scatter_kv_kernel, out, scratch, ident, p, vmem_out=True, mib=24)


def sum_small_kernel(x_ref, out_ref, total, arrived, own_sem, send_sem, recv_sem):
    place = Place(send_sem)
    own = pltpu.make_async_copy(x_ref, total.at[0], own_sem)
    own.start()
    own.wait()
    ways = [(place.ep, place.over_core), (place.ep, place.over_x), (place.across(0, 1), place.tp)]
    by_z = [(place.across(step, 0), place.tp) for step in (1, 2, 3)]
    place.greet(ways + by_z)
    for number, partner in enumerate(ways):
        place.send(total.at[number], arrived.at[number], recv_sem.at[number], partner)
        place.arrive(arrived.at[number], recv_sem.at[number])
        total[number + 1] = total[number] + arrived[number]
    for step in (1, 2, 3):
        place.send(total.at[3], arrived.at[2 + step], recv_sem.at[2 + step], by_z[step - 1])
    for step in (1, 2, 3):
        place.arrive(arrived.at[2 + step], recv_sem.at[2 + step])
    out_ref[...] = (total[3] + arrived[3]) + (arrived[4] + arrived[5])
    place.finish()


def sum_small(x, ident):
    shape = x.shape
    scratch = [pltpu.VMEM((4, *shape), x.dtype), pltpu.VMEM((6, *shape), x.dtype)]
    scratch += [pltpu.SemaphoreType.DMA, (6,), (6,)]
    out = jax.ShapeDtypeStruct(shape, x.dtype)
    return reach(sum_small_kernel, out, scratch, ident, x, vmem_out=True)


def on_device(
    inputs,
    cotangent,
    arrangement,
    seq_lengths,
    routes,
    gate_values,
    input_gain,
    query_proj,
    key_projected,
    value_projected,
    query_gain,
    key_gain,
    output_proj,
    expert_gain,
    gate_weight,
    up_weight,
    down_weight,
):
    ep_size = lax.axis_size("ep")
    tp_size = lax.axis_size("tp")
    ep_index = lax.axis_index("ep")
    tp_index = lax.axis_index("tp")
    everyone = ("ep", "tp")
    own_rows, width = inputs.shape
    group_rows = own_rows * tp_size
    row_block = own_rows // ep_size
    token_total = arrangement.shape[0]
    expert_count = ep_size * tp_size
    capacity = 2 * own_rows * TOP // expert_count
    heads = query_proj.shape[1] // HEAD
    known = (ep_size, tp_size) == (8, 4)
    expert = (ep_index * tp_size + tp_index).astype(jnp.int32)[None]

    table = arrangement.reshape(ep_size, tp_size, ep_size, row_block)
    leaving_from = lax.dynamic_index_in_dim(table, tp_index, 1, keepdims=False)
    leaving_from = lax.dynamic_index_in_dim(leaving_from, ep_index, 1, keepdims=False)
    send_index = leaving_from - (ep_index * group_rows + tp_index * own_rows)
    mover = (
        send_index.reshape(-1)[:, None] == jnp.arange(own_rows, dtype=jnp.int32)[None, :]
    ).astype(jnp.bfloat16)

    def to_places(rows):
        return dot(mover, rows).astype(jnp.bfloat16).reshape(ep_size, row_block, width)

    def exchange(rows):
        return lax.all_to_all(rows, "ep", split_axis=0, concat_axis=0, tiled=True)

    def to_given(rows):
        moved = exchange(rows.astype(jnp.bfloat16).reshape(ep_size, row_block, width))
        return dot_with(mover, moved.reshape(own_rows, width), ROWS_BY_ROWS)

    def group_sorted(rows, ident):
        blocks = rows.reshape(ep_size, row_block, width)
        if known:
            gathered = gather_group(blocks, tp_size, ident)
        else:
            gathered = lax.all_gather(blocks, "tp", axis=1)
        return gathered.reshape(group_rows, width)

    def sum_group(rows, ident):
        blocks = rows.astype(jnp.bfloat16).reshape(ep_size, tp_size, row_block, width)
        if known:
            return scatter_group(blocks, ident).reshape(own_rows, width)
        placed = jnp.swapaxes(blocks, 0, 1).reshape(group_rows, width)
        own = lax.psum_scatter(placed, "tp", scatter_dimension=0, tiled=True)
        return own.astype(jnp.float32)

    leaving_x, leaving_cot = to_places(inputs), to_places(cotangent)
    if known:
        group_x, own_cot = enter(leaving_x, leaving_cot, tp_size, 1)
        own_inputs = lax.dynamic_index_in_dim(group_x, tp_index, 1, keepdims=False)
    else:
        own_inputs, own_cot = exchange(leaving_x), exchange(leaving_cot)
        group_x = lax.all_gather(own_inputs, "tp", axis=1)
    own_inputs, own_cot = own_inputs.reshape(own_rows, width), own_cot.reshape(own_rows, width)
    group_x = group_x.reshape(group_rows, width)
    meta_own = jnp.concatenate([routes.astype(jnp.float32).T, gate_values.T], axis=0)
    cot_all = lax.all_gather(own_cot, everyone, axis=0, tiled=True)

    query_given = lax.dynamic_index_in_dim(table, ep_index, 0, keepdims=False)
    query_given = jnp.swapaxes(query_given, 0, 1).reshape(group_rows)
    query_first = seq_starts(query_given, seq_lengths)
    cosine, sine = rope_tables(query_given - query_first, HEAD)
    key_given = jnp.transpose(table, (2, 1, 0, 3)).reshape(token_total)
    by_step = (-1, QUERY_TOKENS)
    given_steps, first_steps = query_given.reshape(by_step), query_first.reshape(by_step)
    lowest = jnp.min(first_steps, axis=1) // KEY_SPAN
    highest = jnp.max(given_steps, axis=1) // KEY_SPAN + 1
    open_low = (jnp.max(first_steps, axis=1) + KEY_SPAN - 1) // KEY_SPAN
    open_low = jnp.minimum(open_low, highest)
    open_high = jnp.clip((jnp.min(given_steps, axis=1) + 1) // KEY_SPAN, open_low, highest)
    bounds = jnp.stack([lowest, open_low, open_high, highest]).astype(jnp.int32)
    ask = jnp.stack([query_given, query_first], axis=1)
    ask_rows = jnp.stack(
        [jnp.tile(given_steps, (1, heads)), jnp.tile(first_steps, (1, heads))], axis=1
    )

    normed_in, query_raw, query_rows, key_raw, kv_rows = front(
        group_x, input_gain, query_proj, key_projected, value_projected,
        query_gain, key_gain, cosine, sine,
    )
    kv_blocks = kv_rows.reshape(expert_count, row_block, 2 * HEAD)
    if known:
        kv_all = gather_kv(kv_blocks, ep_size, 2)
    else:
        kv_all = lax.all_gather(kv_blocks, "ep", axis=1)
    kv_all = kv_all.reshape(token_total, 2 * HEAD)
    pairs = group_rows * heads * 1536
    exact, out_rows, lse = attend_forward(
        bounds, query_rows, ask, key_given[None], kv_all, pairs
    )
    branch = sum_group(dot(out_rows, output_proj), 5)
    hidden = own_inputs.astype(jnp.float32) + branch
    mid_scale = inverse_root(hidden)
    normed_mid = (hidden * mid_scale * expert_gain).astype(jnp.bfloat16)

    normed_mid, cot_all = lax.optimization_barrier((normed_mid, cot_all))
    if known:
        mid_all, meta = gather_all(normed_mid, meta_own, expert_count, 3)
    else:
        mid_all = lax.all_gather(normed_mid, everyone, axis=0, tiled=True)
        meta = lax.all_gather(meta_own, everyone, axis=0, tiled=True)
    meta = meta.reshape(expert_count, 2 * TOP, own_rows)
    mid_partial, out_partial, expert_in, slot_cot, inner, gate_grad, up_grad = expert_pass(
        expert, meta, mid_all, cot_all, gate_weight, up_weight, down_weight, capacity
    )
    def sum_over_all(partial):
        return lax.psum_scatter(partial, everyone, scatter_dimension=0, tiled=True)

    if known:
        mid_grad = scatter_all(mid_partial, expert_count, 4)
    else:
        mid_grad = sum_over_all(mid_partial).astype(jnp.float32)
    grad_down = dot_with(inner, slot_cot, ROWS_BY_ROWS)
    grad_gate = dot_with(expert_in, gate_grad, ROWS_BY_ROWS)
    grad_up = dot_with(expert_in, up_grad, ROWS_BY_ROWS)
    layer_out = to_given(hidden + sum_over_all(out_partial).astype(jnp.float32))
    layer_out = layer_out.astype(jnp.bfloat16)

    mid_hat = hidden * mid_scale
    grad_expert_gain = jnp.sum(mid_grad * mid_hat, axis=0)
    mid_scaled = mid_grad * expert_gain
    hidden_grad = own_cot.astype(jnp.float32) + mid_scale * (
        mid_scaled - mid_hat * jnp.mean(mid_scaled * mid_hat, axis=-1, keepdims=True)
    )
    branch_grad = group_sorted(hidden_grad.astype(jnp.bfloat16), 6)
    out_grad = dot_with(branch_grad, output_proj, COLS_BY_COLS).astype(jnp.bfloat16)
    query_grad, kv_grad = attend_backward(
        bounds, query_rows, out_grad, exact, lse, ask_rows, key_given[:, None], kv_all, pairs
    )
    kv_grad = kv_grad.reshape(expert_count, ep_size, row_block, 2 * HEAD)
    if known:
        kv_own = scatter_kv(kv_grad, 7)
    else:
        kv_own = lax.psum_scatter(kv_grad, "ep", scatter_dimension=1)
    kv_own = kv_own.reshape(group_rows, 2 * HEAD)
    value_grad = kv_own[:, HEAD:]
    raw_query_grad, grad_query_gain = head_back(query_raw, query_grad, query_gain, cosine, sine)
    raw_key_grad, grad_key_gain = head_back(key_raw, kv_own[:, :HEAD], key_gain, cosine, sine)
    normed_grad = (
        dot_with(raw_query_grad, query_proj, COLS_BY_COLS)
        + dot_with(raw_key_grad, key_projected, COLS_BY_COLS)
        + dot_with(value_grad, value_projected, COLS_BY_COLS)
    )
    normed_grad = sum_group(normed_grad, 8)
    own_float = own_inputs.astype(jnp.float32)
    in_scale = inverse_root(own_float)
    in_hat = own_float * in_scale
    grad_input_gain = jnp.sum(normed_grad * in_hat, axis=0)
    in_scaled = normed_grad * input_gain
    grad_inputs = to_given(
        hidden_grad
        + in_scale * (in_scaled - in_hat * jnp.mean(in_scaled * in_hat, axis=-1, keepdims=True))
    )

    def ep_sum(rows):
        return lax.psum_scatter(
            rows.astype(jnp.bfloat16), "ep", scatter_dimension=0, tiled=True
        ).astype(jnp.float32)

    grad_output = jnp.transpose(ep_sum(dot_with(branch_grad, out_rows, ROWS_BY_ROWS)))
    grad_query = ep_sum(dot_with(normed_in, raw_query_grad, ROWS_BY_ROWS))
    grad_kv = ep_sum(
        dot_with(normed_in, jnp.concatenate([raw_key_grad, value_grad], axis=1), ROWS_BY_ROWS)
    )
    gains = jnp.concatenate(
        [grad_input_gain, grad_expert_gain, grad_query_gain[0], grad_key_gain[0]]
    )
    if known:
        gains = sum_small(gains.reshape(-1, HEAD), 9).reshape(-1)
    else:
        gains = lax.psum(gains, everyone)
    cuts = (width, 2 * width, 2 * width + HEAD)
    return (
        layer_out,
        grad_inputs,
        grad_query,
        grad_kv[:, :HEAD],
        grad_kv[:, HEAD:],
        grad_output,
        gains[: cuts[0]],
        gains[cuts[1] : cuts[2]],
        gains[cuts[2] :],
        gains[cuts[0] : cuts[1]],
        grad_gate[None],
        grad_up[None],
        grad_down[None],
    )


def solution(mesh):
    split = P(("ep", "tp"), None)
    experts = P(("ep", "tp"), None, None)
    columns = P(None, "tp")
    return jax.shard_map(
        on_device,
        mesh=mesh,
        in_specs=(
            split, split, P(), P(), split, split, P(), columns, columns, columns,
            P(), P(), P("tp", None), P(), experts, experts, experts,
        ),
        out_specs=(
            split, split, P("ep", "tp"), P("ep", "tp"), P("ep", "tp"), P("tp", "ep"),
            P(), P(), P(), P(), experts, experts, experts,
        ),
        check_vma=False,
    )
```

```python
import functools
import math

import jax
import jax.numpy as jnp
from jax import lax
from jax.experimental import pallas as pl
from jax.experimental.pallas import tpu as pltpu
from jax.sharding import PartitionSpec as P

TOP = 8
EPSILON = 1e-06
ROPE_BASE = 1000000.0
KEY_SPAN = 512
QUERY_TOKENS = 32
HEAD = 128
ROW_TILE = 256
MIB = 1 << 20
LOG2E = math.log2(math.e)
ROWS_BY_ROWS = (((0,), (0,)), ((), ()))
COLS_BY_COLS = (((1,), (1,)), ((), ()))


def dot(left, right):
    return jnp.dot(left, right, preferred_element_type=jnp.float32)


def dot_with(left, right, dims):
    return lax.dot_general(left, right, dims, preferred_element_type=jnp.float32)


def cost(flops, moved, transcendentals=0):
    return pl.CostEstimate(
        flops=int(flops), bytes_accessed=int(moved), transcendentals=int(transcendentals)
    )


def params(mib):
    return pltpu.CompilerParams(
        dimension_semantics=("arbitrary",), vmem_limit_bytes=mib * MIB
    )


def whole(shape, single=True):
    rank = len(shape)
    if single:
        return pl.BlockSpec(shape, lambda *ids: (0,) * rank, pipeline_mode=pl.Buffered(1))
    return pl.BlockSpec(shape, lambda *ids: (0,) * rank)


def rows_of(shape):
    rank = len(shape)
    return pl.BlockSpec(shape, lambda i, *ids: (i,) + (0,) * (rank - 1))


def rope_tables(positions, head_dim):
    freqs = ROPE_BASE ** (-jnp.arange(0, head_dim, 2, dtype=jnp.float32) / head_dim)
    angles = positions.astype(jnp.float32)[:, None] * freqs[None, :]
    cosine, sine = jnp.cos(angles), jnp.sin(angles)
    return (
        jnp.concatenate([cosine, cosine], axis=-1),
        jnp.concatenate([-sine, sine], axis=-1),
    )


def seq_starts(given, seq_lengths):
    ends = jnp.cumsum(seq_lengths)
    passed = given[:, None] >= ends[None, :]
    return jnp.sum(jnp.where(passed, seq_lengths[None, :], 0), axis=1)


def inverse_root(values):
    return lax.rsqrt(jnp.mean(values * values, axis=-1, keepdims=True) + EPSILON)


def front_kernel(
    x_ref, gain_ref, wq_ref, wk_ref, wv_ref, qg_ref, kg_ref, cos_ref, sin_ref,
    normed_ref, qraw_ref, q_ref, kraw_ref, kv_ref,
):
    x = x_ref[...].astype(jnp.float32)
    normed = (x * inverse_root(x) * gain_ref[...]).astype(jnp.bfloat16)
    normed_ref[...] = normed
    cosine, sine = cos_ref[...], sin_ref[...]

    def prepare(raw, gain):
        values = raw * inverse_root(raw) * gain
        return (values * cosine + pltpu.roll(values, HEAD // 2, 1) * sine).astype(jnp.bfloat16)

    raw = dot(normed, wq_ref[...])
    qraw_ref[...] = raw
    for head in range(raw.shape[1] // HEAD):
        part = slice(head * HEAD, (head + 1) * HEAD)
        q_ref[:, part] = prepare(raw[:, part], qg_ref[...])
    raw = dot(normed, wk_ref[...])
    kraw_ref[...] = raw
    kv_ref[:, :HEAD] = prepare(raw, kg_ref[...])
    kv_ref[:, HEAD:] = dot(normed, wv_ref[...]).astype(jnp.bfloat16)


def front(group_x, input_gain, wq, wk, wv, query_gain, key_gain, cosine, sine):
    rows, width = group_x.shape
    cols = wq.shape[1]
    tile = min(ROW_TILE, rows)
    out = [
        ((rows, width), jnp.bfloat16),
        ((rows, cols), jnp.float32),
        ((rows, cols), jnp.bfloat16),
        ((rows, HEAD), jnp.float32),
        ((rows, 2 * HEAD), jnp.bfloat16),
    ]
    return pl.pallas_call(
        front_kernel,
        grid=(rows // tile,),
        in_specs=[
            rows_of((tile, width)),
            whole((1, width)),
            whole(wq.shape),
            whole(wk.shape),
            whole(wv.shape),
            whole((1, HEAD)),
            whole((1, HEAD)),
            rows_of((tile, HEAD)),
            rows_of((tile, HEAD)),
        ],
        out_specs=[rows_of((tile, shape[1])) for shape, kind in out],
        out_shape=[jax.ShapeDtypeStruct(shape, kind) for shape, kind in out],
        compiler_params=params(40),
        cost_estimate=cost(2 * rows * width * (cols + 2 * HEAD), 20 * MIB),
        name="front",
    )(
        group_x,
        input_gain[None],
        wq,
        wk,
        wv,
        query_gain[None],
        key_gain[None],
        cosine,
        sine,
    )


def stack_heads(block):
    heads = block.shape[1] // HEAD
    return jnp.concatenate(
        [block[:, head * HEAD : (head + 1) * HEAD] for head in range(heads)], axis=0
    )


def attend_forward_kernel(
    bounds_ref, q_ref, ask_ref, key_given_ref, kv_ref, exact_ref, out_ref, lse_ref, acc, tot
):
    step = pl.program_id(0)
    tokens, cols = q_ref.shape
    heads = cols // HEAD
    query = stack_heads(q_ref[...])
    ask = ask_ref[...]
    last = jnp.concatenate([ask[:, 0:1]] * heads, axis=0)
    first = jnp.concatenate([ask[:, 1:2]] * heads, axis=0)
    acc[...] = jnp.zeros_like(acc)
    tot[...] = jnp.zeros_like(tot)

    def visit(span, masked):
        offset = pl.multiple_of(span * KEY_SPAN, KEY_SPAN)
        keys = kv_ref[pl.ds(offset, KEY_SPAN), :HEAD]
        values = kv_ref[pl.ds(offset, KEY_SPAN), HEAD:]
        scores = dot_with(query, keys, COLS_BY_COLS)
        weights = jnp.exp2(scores * (HEAD**-0.5 * LOG2E))
        if masked:
            key_given = key_given_ref[:, pl.ds(offset, KEY_SPAN)]
            weights = jnp.where((key_given <= last) & (key_given >= first), weights, 0.0)
        part = weights[:, :HEAD]
        for chunk in range(1, KEY_SPAN // HEAD):
            part = part + weights[:, chunk * HEAD : (chunk + 1) * HEAD]
        tot[...] += part
        acc[...] += dot(weights.astype(jnp.bfloat16), values)

    lowest, open_low = bounds_ref[0, step], bounds_ref[1, step]
    open_high, highest = bounds_ref[2, step], bounds_ref[3, step]

    @pl.loop(lowest, open_low)
    def _(span):
        visit(span, True)

    @pl.loop(open_low, open_high)
    def _(span):
        visit(span, False)

    @pl.loop(open_high, highest)
    def _(span):
        visit(span, True)

    total = tot[...]
    exact = acc[...] / jnp.sum(total, axis=1, keepdims=True)
    for head in range(heads):
        rows = exact[head * tokens : (head + 1) * tokens]
        exact_ref[:, head * HEAD : (head + 1) * HEAD] = rows
        out_ref[:, head * HEAD : (head + 1) * HEAD] = rows.astype(jnp.bfloat16)
    lse_ref[0] = jnp.log2(jnp.sum(total.T, axis=0, keepdims=True))


def attend_forward(bounds, query, ask, key_given, kv, pairs):
    rows, cols = query.shape
    heads = cols // HEAD
    steps = rows // QUERY_TOKENS
    stacked = heads * QUERY_TOKENS
    return pl.pallas_call(
        attend_forward_kernel,
        grid_spec=pltpu.PrefetchScalarGridSpec(
            num_scalar_prefetch=1,
            grid=(steps,),
            in_specs=[
                rows_of((QUERY_TOKENS, cols)),
                rows_of((QUERY_TOKENS, 2)),
                whole(key_given.shape),
                whole(kv.shape),
            ],
            out_specs=[
                rows_of((QUERY_TOKENS, cols)),
                rows_of((QUERY_TOKENS, cols)),
                rows_of((1, 1, stacked)),
            ],
            scratch_shapes=[
                pltpu.VMEM((stacked, HEAD), jnp.float32),
                pltpu.VMEM((stacked, HEAD), jnp.float32),
            ],
        ),
        out_shape=[
            jax.ShapeDtypeStruct((rows, cols), jnp.float32),
            jax.ShapeDtypeStruct((rows, cols), jnp.bfloat16),
            jax.ShapeDtypeStruct((steps, 1, stacked), jnp.float32),
        ],
        compiler_params=params(48),
        cost_estimate=cost(8 * pairs * HEAD, 16 * MIB, pairs),
        name="attend_forward",
    )(bounds, query, ask, key_given, kv)


def attend_backward_kernel(
    bounds_ref, q_ref, grad_ref, exact_ref, lse_ref, ask_ref, key_given_ref, kv_ref,
    dq_ref, rounded_ref, dkv_ref, acc,
):
    step = pl.program_id(0)
    tokens, cols = q_ref.shape
    heads = cols // HEAD

    @pl.when(step == 0)
    def _():
        dkv_ref[...] = jnp.zeros_like(dkv_ref)

    query = stack_heads(q_ref[...])
    grad = stack_heads(grad_ref[...])
    product = grad.astype(jnp.float32) * stack_heads(exact_ref[...])
    delta = jnp.sum(product.T, axis=0, keepdims=True)
    lse = lse_ref[0]
    last, first = ask_ref[0, 0:1, :], ask_ref[0, 1:2, :]
    acc[...] = jnp.zeros_like(acc)

    def visit(span, masked):
        offset = pl.multiple_of(span * KEY_SPAN, KEY_SPAN)
        place = pl.ds(offset, KEY_SPAN)
        keys = kv_ref[place, :HEAD]
        values = kv_ref[place, HEAD:]
        scores = dot_with(keys, query, COLS_BY_COLS)
        probs = jnp.exp2(scores * (HEAD**-0.5 * LOG2E) - lse)
        if masked:
            key_given = key_given_ref[place, :]
            probs = jnp.where((key_given <= last) & (key_given >= first), probs, 0.0)
        prob_grad = dot_with(values, grad, COLS_BY_COLS)
        score_grad = (probs * (prob_grad - delta)).astype(jnp.bfloat16)
        dkv_ref[place, HEAD:] += dot(probs.astype(jnp.bfloat16), grad)
        dkv_ref[place, :HEAD] += dot(score_grad, query) * (HEAD**-0.5)
        acc[...] += dot_with(score_grad, keys, ROWS_BY_ROWS)

    lowest, open_low = bounds_ref[0, step], bounds_ref[1, step]
    open_high, highest = bounds_ref[2, step], bounds_ref[3, step]

    @pl.loop(lowest, open_low)
    def _(span):
        visit(span, True)

    @pl.loop(open_low, open_high)
    def _(span):
        visit(span, False)

    @pl.loop(open_high, highest)
    def _(span):
        visit(span, True)

    for head in range(heads):
        dq_ref[:, head * HEAD : (head + 1) * HEAD] = acc[
            head * tokens : (head + 1) * tokens
        ] * (HEAD**-0.5)

    @pl.when(step == pl.num_programs(0) - 1)
    def _():
        @pl.loop(0, dkv_ref.shape[0], step=KEY_SPAN)
        def _(row):
            place = pl.ds(row, KEY_SPAN)
            rounded_ref[place] = dkv_ref[place].astype(jnp.bfloat16)


def attend_backward(bounds, query, grad, exact, lse, ask_rows, key_column, kv, pairs):
    rows, cols = query.shape
    heads = cols // HEAD
    steps = rows // QUERY_TOKENS
    stacked = heads * QUERY_TOKENS
    return pl.pallas_call(
        attend_backward_kernel,
        grid_spec=pltpu.PrefetchScalarGridSpec(
            num_scalar_prefetch=1,
            grid=(steps,),
            in_specs=[
                rows_of((QUERY_TOKENS, cols)),
                rows_of((QUERY_TOKENS, cols)),
                rows_of((QUERY_TOKENS, cols)),
                rows_of((1, 1, stacked)),
                rows_of((1, 2, stacked)),
                whole(key_column.shape),
                whole(kv.shape),
            ],
            out_specs=[rows_of((QUERY_TOKENS, cols)), whole(kv.shape)],
            scratch_shapes=[
                pltpu.VMEM(kv.shape, jnp.float32),
                pltpu.VMEM((stacked, HEAD), jnp.float32),
            ],
        ),
        out_shape=[
            jax.ShapeDtypeStruct((rows, cols), jnp.float32),
            jax.ShapeDtypeStruct(kv.shape, jnp.bfloat16),
        ],
        compiler_params=params(56),
        cost_estimate=cost(20 * pairs * HEAD, 32 * MIB, pairs),
        name="attend_backward",
    )(bounds, query, grad, exact, lse, ask_rows, key_column, kv)


def selection(meta, expert, capacity):
    tokens = meta.shape[1]
    weight = jnp.sum(jnp.where(meta[:TOP] == expert, meta[TOP : 2 * TOP], 0.0), axis=0, keepdims=True)
    member = jnp.where(weight > 0.0, 1.0, 0.0)
    earlier = lax.broadcasted_iota(jnp.int32, (tokens, tokens), 0)
    later = lax.broadcasted_iota(jnp.int32, (tokens, tokens), 1)
    before = jnp.where(earlier < later, 1.0, 0.0).astype(jnp.bfloat16)
    rank = dot(jnp.broadcast_to(member, (16, tokens)).astype(jnp.bfloat16), before)[0:1]
    rank = jnp.where(weight > 0.0, rank, -1.0).astype(jnp.int32)
    hit = lax.broadcasted_iota(jnp.int32, (capacity, tokens), 0) == rank
    gate = jnp.sum(jnp.where(hit, weight, 0.0), axis=1, keepdims=True)
    return jnp.where(hit, 1.0, 0.0).astype(jnp.bfloat16), gate


def expert_kernel(
    expert_ref, meta_ref, x_ref, c_ref, wg_ref, wu_ref, wd_ref,
    mid_ref, out_ref, xs_ref, cs_ref, inner_ref, gg_ref, ug_ref,
):
    blocks, _, tokens = meta_ref.shape
    capacity = xs_ref.shape[0] // blocks
    expert = expert_ref[0].astype(jnp.float32)
    picks, gates = [], []
    for block in range(blocks):
        rows = slice(block * tokens, (block + 1) * tokens)
        slots = slice(block * capacity, (block + 1) * capacity)
        pick, gate = selection(meta_ref[block], expert, capacity)
        picks.append(pick)
        gates.append(gate)
        xs_ref[slots] = dot(pick, x_ref[rows]).astype(jnp.bfloat16)
        cs_ref[slots] = (dot(pick, c_ref[rows]) * gate).astype(jnp.bfloat16)
    gate_part = dot(xs_ref[...], wg_ref[0])
    up_part = dot(xs_ref[...], wu_ref[0])
    inner_grad = dot_with(cs_ref[...], wd_ref[0], COLS_BY_COLS)
    gate_sig = jax.nn.sigmoid(gate_part)
    activated = gate_part * gate_sig
    inner = (activated * up_part).astype(jnp.bfloat16)
    inner_ref[...] = inner
    gate_grad = (inner_grad * up_part * gate_sig * (1.0 + gate_part * (1.0 - gate_sig))).astype(
        jnp.bfloat16
    )
    up_grad = (inner_grad * activated).astype(jnp.bfloat16)
    gg_ref[...] = gate_grad
    ug_ref[...] = up_grad
    slot_grad = dot_with(gate_grad, wg_ref[0], COLS_BY_COLS)
    slot_grad = (slot_grad + dot_with(up_grad, wu_ref[0], COLS_BY_COLS)).astype(jnp.bfloat16)
    for block in range(blocks):
        rows = slice(block * tokens, (block + 1) * tokens)
        slots = slice(block * capacity, (block + 1) * capacity)
        mid_ref[rows] = dot_with(picks[block], slot_grad[slots], ROWS_BY_ROWS).astype(
            jnp.bfloat16
        )
    result = dot(inner, wd_ref[0]).astype(jnp.bfloat16).astype(jnp.float32)
    for block in range(blocks):
        rows = slice(block * tokens, (block + 1) * tokens)
        slots = slice(block * capacity, (block + 1) * capacity)
        scaled = (result[slots] * gates[block]).astype(jnp.bfloat16)
        out_ref[rows] = dot_with(picks[block], scaled, ROWS_BY_ROWS).astype(jnp.bfloat16)


def expert_pass(expert, meta, x_all, c_all, gate_w, up_w, down_w, capacity):
    blocks, lines, tokens = meta.shape
    width, hidden = gate_w.shape[1:]
    per = max(1, 512 // tokens)
    total = blocks * capacity
    slots = per * capacity
    shapes = [(blocks * tokens, width)] * 2 + [(total, width)] * 2 + [(total, hidden)] * 3
    return pl.pallas_call(
        expert_kernel,
        grid_spec=pltpu.PrefetchScalarGridSpec(
            num_scalar_prefetch=1,
            grid=(blocks // per,),
            in_specs=[
                rows_of((per, lines, tokens)),
                rows_of((per * tokens, width)),
                rows_of((per * tokens, width)),
                whole(gate_w.shape),
                whole(up_w.shape),
                whole(down_w.shape),
            ],
            out_specs=[rows_of((per * tokens, width))] * 2
            + [rows_of((slots, width))] * 2
            + [rows_of((slots, hidden))] * 3,
        ),
        out_shape=[jax.ShapeDtypeStruct(shape, jnp.bfloat16) for shape in shapes],
        compiler_params=params(56),
        cost_estimate=cost(10 * total * width * hidden, 150 * MIB, total * hidden),
        name="expert_pass",
    )(expert, meta, x_all, c_all, gate_w, up_w, down_w)


def head_back_kernel(raw_ref, grad_ref, gain_ref, cos_ref, sin_ref, out_ref, gain_grad_ref):
    @pl.when(pl.program_id(0) == 0)
    def _():
        gain_grad_ref[...] = jnp.zeros_like(gain_grad_ref)

    cosine, sine, gain = cos_ref[...], sin_ref[...], gain_ref[...]
    for head in range(raw_ref.shape[1] // HEAD):
        part = slice(head * HEAD, (head + 1) * HEAD)
        raw = raw_ref[:, part]
        grad = grad_ref[:, part].astype(jnp.float32)
        back = grad * cosine - pltpu.roll(grad, HEAD // 2, 1) * sine
        inverse = inverse_root(raw)
        hat = raw * inverse
        gain_grad_ref[...] += jnp.sum(back * hat, axis=0, keepdims=True)
        scaled = back * gain
        out_ref[:, part] = (
            inverse * (scaled - hat * jnp.mean(scaled * hat, axis=-1, keepdims=True))
        ).astype(jnp.bfloat16)


def head_back(raw, grad, gain, cosine, sine):
    rows, cols = raw.shape
    tile = min(ROW_TILE, rows)
    return pl.pallas_call(
        head_back_kernel,
        grid=(rows // tile,),
        in_specs=[
            rows_of((tile, cols)),
            rows_of((tile, cols)),
            whole((1, HEAD)),
            rows_of((tile, HEAD)),
            rows_of((tile, HEAD)),
        ],
        out_specs=[rows_of((tile, cols)), whole((1, HEAD))],
        out_shape=[
            jax.ShapeDtypeStruct((rows, cols), jnp.bfloat16),
            jax.ShapeDtypeStruct((1, HEAD), jnp.float32),
        ],
        compiler_params=params(24),
        cost_estimate=cost(rows * cols * 20, rows * cols * 10),
        name="head_back",
    )(raw, grad, gain[None], cosine, sine)


MESH_ID = pl.DeviceIdType.MESH


class Place:
    def __init__(self, send_sem, tp_size=4, nearest=False):
        self.tp_size, self.send_sem, self.sent = tp_size, send_sem, []
        self.nearest = nearest
        self.ep, self.tp = lax.axis_index("ep"), lax.axis_index("tp")
        self.z, self.y, self.x, self.core = self.ep // 2, self.ep % 2, self.tp // 2, self.tp % 2
        self.edge = 1 - (self.z + self.z // 2) % 2
        self.over_x = self.tp + 2 - 4 * self.x
        self.over_core = self.tp + 1 - 2 * self.core
        self.over_both = self.over_core + 2 - 4 * self.x

    def level(self, step):
        levels = [self.z, self.z + 1 - 2 * (self.z % 2), (self.z + 2) % 4, 3 - self.z]
        if self.nearest and step > 1:
            return self.edge * levels[step] + (1 - self.edge) * levels[5 - step]
        return levels[step]

    def across(self, step, over_y):
        return self.level(step) * 2 + self.y + over_y * (1 - 2 * self.y)

    def device(self, step, first, second, other=0):
        core = self.core + other * (1 - 2 * self.core)
        over_y = first * (1 - core) + second * core
        over_x = first * core + second * (1 - core)
        x = self.x + over_x * (1 - 2 * self.x)
        return self.across(step, over_y), x * 2 + core

    def slot(self, *where):
        ep, tp = self.device(*where)
        return ep * self.tp_size + tp

    def greet(self, partners):
        barrier = pltpu.get_barrier_semaphore()
        for partner in partners:
            pl.semaphore_signal(barrier, inc=1, device_id=partner, device_id_type=MESH_ID)
        pl.semaphore_wait(barrier, len(partners))

    def greet_all_ways(self):
        partners = [(1, 0, 0), (2, 0, 0), (3, 0, 0), (0, 1, 0), (0, 0, 1), (0, 0, 0, 1)]
        self.greet([self.device(*partner) for partner in partners])

    def send(self, src, dst, sem, device):
        copy = pltpu.make_async_remote_copy(
            src_ref=src,
            dst_ref=dst,
            send_sem=self.send_sem.at[len(self.sent)],
            recv_sem=sem,
            device_id=device,
            device_id_type=MESH_ID,
        )
        copy.start()
        self.sent.append(copy)

    def arrive(self, dst, sem):
        pltpu.make_async_remote_copy(
            src_ref=dst,
            dst_ref=dst,
            send_sem=self.send_sem.at[0],
            recv_sem=sem,
            device_id=(self.ep, self.over_core),
            device_id_type=MESH_ID,
        ).wait_recv()

    def finish(self):
        for copy in self.sent:
            copy.wait_send()


def reach(kernel, out, scratch, ident, *operands, vmem_out=False, mib=None):
    dma = [kind if not isinstance(kind, tuple) else pltpu.SemaphoreType.DMA(kind) for kind in scratch]
    spaces = vmem_out if isinstance(vmem_out, tuple) else jax.tree.map(lambda _: vmem_out, out)
    out_specs = jax.tree.map(
        lambda vmem: pl.BlockSpec(memory_space=pltpu.VMEM if vmem else pl.ANY), spaces
    )
    return pl.pallas_call(
        kernel,
        in_specs=[pl.BlockSpec(memory_space=pl.ANY)] * len(operands),
        out_specs=out_specs,
        out_shape=out,
        scratch_shapes=dma,
        compiler_params=pltpu.CompilerParams(
            collective_id=ident,
            has_side_effects=True,
            vmem_limit_bytes=(mib or 16) * MIB,
        ),
        cost_estimate=cost(1, 1),
        name=kernel.__name__ if not isinstance(kernel, functools.partial) else kernel.func.__name__,
    )(*operands)


NEAR = ((0, 0), (1, 0), (0, 1), (2, 0), (1, 1), (3, 0), (2, 1), (3, 1))
ORDER = tuple((*where, 0) for where in NEAR[:6])
ORDER += ((0, 0, 1), (2, 1, 0), (1, 0, 1), (3, 1, 0), (0, 1, 1))
ORDER += tuple((*where, 1) for where in NEAR[3:])


def expert_all_kernel(
    x_ref, m_ref, c_ref, wg_ref, wu_ref, wd_ref,
    all_ref, mid_ref, out_ref, xs_ref, cs_ref, inner_ref, gg_ref, ug_ref,
    lines, wg, wu, wd, pair, xb, cb, midb, outb, xsb, csb, innerb, ggb, ugb,
    w_sem, own_sem, z_sem, z_line_sem, send_sem, line_send_sem, recv_sem, line_sem,
    load_sem, store_sem,
):
    place = Place(send_sem, nearest=True)
    rows = x_ref.shape[0]
    capacity = xsb.shape[1] // 2
    expert = (place.ep * 4 + place.tp).astype(jnp.float32)
    count = len(ORDER)
    slots = {(*where, other): place.slot(*where, other) for where in ORDER for other in (0, 1)}
    first, second, across = place.device(0, 1, 0), place.device(0, 0, 1), place.device(0, 0, 0, 1)

    def part(ref, slot):
        return ref.at[pl.ds(slot * rows, rows)]

    weights = [
        pltpu.make_async_copy(ref, held, w_sem.at[number])
        for number, (ref, held) in enumerate(((wg_ref, wg), (wu_ref, wu), (wd_ref, wd)))
    ]
    mine = slots[0, 0, 0, 0]
    own = [
        pltpu.make_async_copy(x_ref, part(all_ref, mine), own_sem.at[0]),
        pltpu.make_async_copy(m_ref, lines.at[mine], own_sem.at[1]),
    ]
    for copy in own + weights:
        copy.start()
    place.greet_all_ways()
    for copy in own:
        copy.wait()

    def copies(slot, device, rows_sem, words_sem):
        some = dict(device_id=device, device_id_type=MESH_ID)
        return (
            pltpu.make_async_remote_copy(
                src_ref=lines.at[slot], dst_ref=lines.at[slot],
                send_sem=words_sem, recv_sem=line_sem.at[slot], **some,
            ),
            pltpu.make_async_remote_copy(
                src_ref=part(all_ref, slot), dst_ref=part(all_ref, slot),
                send_sem=rows_sem, recv_sem=recv_sem.at[slot], **some,
            ),
        )

    def along_z(step):
        level, z = place.level(step), place.z
        up = (z < 3) if step == 0 else (level < z) & (z < 3)
        down = (z > 0) if step == 0 else (level > z) & (z > 0)
        return ((up, 2 * step, (place.ep + 2, place.tp)), (down, 2 * step + 1, (place.ep - 2, place.tp)))

    def z_copies(slot, number, device):
        return copies(slot, device, z_sem.at[number], z_line_sem.at[number])

    sends = []
    for where in ORDER:
        targets = [across]
        if where[2] == 0:
            targets = [second, *targets]
        if where[1:] == (0, 0):
            targets = [first, *targets]
        sends.append(targets)
    starts = [sum(len(targets) for targets in sends[:number]) for number in range(count)]

    def arrive(slot):
        for copy in copies(slot, across, send_sem.at[0], line_send_sem.at[0]):
            copy.wait_recv()

    def onward_z(step):
        for wanted, index, device in along_z(step):

            @pl.when(wanted)
            def _(index=index, device=device):
                for copy in z_copies(slots[step, 0, 0, 0], index, device):
                    copy.start()

    relays = {1: 2, 3: 3}

    def event(number):
        where = ORDER[number]
        slot = slots[(*where, 0)]
        if where[0] in relays.values() and where[1:] == (0, 0):

            @pl.when(place.edge == 1)
            def _():
                arrive(slot)

        elif number:
            arrive(slot)
        if where in ((0, 0, 0), (1, 0, 0)):
            onward_z(where[0])
        if number in relays:
            step = relays[number]

            @pl.when(place.edge == 0)
            def _():
                arrive(slots[step, 0, 0, 0])
                onward_z(step)

        for index, device in enumerate(sends[number], starts[number]):
            for copy in copies(slot, device, send_sem.at[index], line_send_sem.at[index]):
                copy.start()

    def load_copies(slot, parity, half):
        return (
            pltpu.make_async_copy(part(all_ref, slot), xb.at[parity, half], load_sem.at[parity, half]),
            pltpu.make_async_copy(part(c_ref, slot), cb.at[parity, half], load_sem.at[parity, 2 + half]),
        )

    def load(number):
        where, parity = ORDER[number], number % 2
        arrive(slots[(*where, 1)])
        for half in (0, 1):
            slot = slots[(*where, half)]
            pair[parity, half] = lines[slot]
            for copy in load_copies(slot, parity, half):
                copy.start()

    def store_copies(number, parity, both):
        kept = pl.ds(number * 2 * capacity, 2 * capacity)
        moves = [(held.at[parity], ref.at[kept]) for held, ref in (
            (xsb, xs_ref), (csb, cs_ref), (innerb, inner_ref), (ggb, gg_ref), (ugb, ug_ref),
        )]
        for half in (0, 1):
            moves.append((midb.at[parity, half], part(mid_ref, both[half])))
            moves.append((outb.at[parity, half], part(out_ref, both[half])))
        return [
            pltpu.make_async_copy(held, ref, store_sem.at[parity, index])
            for index, (held, ref) in enumerate(moves)
        ]

    def compute(parity):
        picks, gates = [], []
        for half in (0, 1):
            pick, gate = selection(pair[parity, half], expert, capacity)
            picks.append(pick)
            gates.append(gate)
            some = slice(half * capacity, (half + 1) * capacity)
            xsb[parity, some] = dot(pick, xb[parity, half]).astype(jnp.bfloat16)
            csb[parity, some] = (dot(pick, cb[parity, half]) * gate).astype(jnp.bfloat16)
        expert_in, slot_cot = xsb[parity], csb[parity]
        gate_part = dot(expert_in, wg[0])
        up_part = dot(expert_in, wu[0])
        inner_grad = dot_with(slot_cot, wd[0], COLS_BY_COLS)
        gate_sig = jax.nn.sigmoid(gate_part)
        activated = gate_part * gate_sig
        inner = (activated * up_part).astype(jnp.bfloat16)
        innerb[parity] = inner
        gate_grad = inner_grad * up_part * gate_sig * (1.0 + gate_part * (1.0 - gate_sig))
        gate_grad = gate_grad.astype(jnp.bfloat16)
        up_grad = (inner_grad * activated).astype(jnp.bfloat16)
        ggb[parity] = gate_grad
        ugb[parity] = up_grad
        slot_grad = dot_with(gate_grad, wg[0], COLS_BY_COLS)
        slot_grad = (slot_grad + dot_with(up_grad, wu[0], COLS_BY_COLS)).astype(jnp.bfloat16)
        result = dot(inner, wd[0]).astype(jnp.bfloat16).astype(jnp.float32)
        for half in (0, 1):
            some = slice(half * capacity, (half + 1) * capacity)
            midb[parity, half] = dot_with(picks[half], slot_grad[some], ROWS_BY_ROWS).astype(
                jnp.bfloat16
            )
            scaled = (result[some] * gates[half]).astype(jnp.bfloat16)
            outb[parity, half] = dot_with(picks[half], scaled, ROWS_BY_ROWS).astype(jnp.bfloat16)

    @pl.loop(0, count + 2)
    def _(turn):
        for number in range(count):

            @pl.when(turn == number)
            def _(number=number):
                event(number)

        for number in range(count):

            @pl.when(turn == number + 1)
            def _(number=number):
                load(number)

        @pl.when(turn == 2)
        def _():
            for copy in weights:
                copy.wait()

        @pl.when(turn >= 2)
        def _():
            parity = turn % 2
            for half in (0, 1):
                for copy in load_copies(0, parity, half):
                    copy.wait()

            @pl.when(turn >= 4)
            def _():
                for copy in store_copies(0, parity, (0, 0)):
                    copy.wait()

            compute(parity)

        for number in range(count):

            @pl.when(turn == number + 2)
            def _(number=number):
                both = [slots[(*ORDER[number], half)] for half in (0, 1)]
                for copy in store_copies(number, number % 2, both):
                    copy.start()

    for parity in (0, 1):
        for copy in store_copies(0, parity, (0, 0)):
            copy.wait()
    for index in range(sum(len(targets) for targets in sends)):
        for copy in copies(0, across, send_sem.at[index], line_send_sem.at[index]):
            copy.wait_send()
    for step in range(4):
        for wanted, index, device in along_z(step):

            @pl.when(wanted)
            def _(index=index, device=device):
                for copy in z_copies(0, index, device):
                    copy.wait_send()


def expert_all(x, lines, c_all, gate_w, up_w, down_w, capacity, ident):
    rows, width = x.shape
    blocks = c_all.shape[0] // rows
    hidden = gate_w.shape[2]
    total = blocks * capacity
    shapes = [c_all.shape] * 3 + [(total, width)] * 2 + [(total, hidden)] * 3
    out = [jax.ShapeDtypeStruct(shape, jnp.bfloat16) for shape in shapes]

    def buffer(*shape):
        return pltpu.VMEM(shape, jnp.bfloat16)

    scratch = [pltpu.VMEM((blocks, *lines.shape), jnp.float32)]
    scratch += [buffer(*gate_w.shape), buffer(*up_w.shape), buffer(*down_w.shape)]
    scratch += [pltpu.VMEM((2, 2, *lines.shape), jnp.float32)]
    scratch += [buffer(2, 2, rows, width)] * 4 + [buffer(2, 2 * capacity, width)] * 2
    scratch += [buffer(2, 2 * capacity, hidden)] * 3
    scratch += [(3,), (2,), (8,), (8,), (28,), (28,), (blocks,), (blocks,), (2, 4), (2, 9)]
    operands = (x, lines, c_all, gate_w, up_w, down_w)
    return reach(expert_all_kernel, out, scratch, ident, *operands, mib=58)[1:]


BUFFERS = 4


def scatter_all_kernel(
    p_ref, out_ref, held, over_second, over_first, over_z, own,
    own_sem, send_sem, core_sem, second_sem, first_sem, z_sem,
):
    place = Place(send_sem)
    rows = out_ref.shape[0]

    def add(total, other):
        @pl.loop(0, rows, step=64)
        def _(row):
            some = pl.ds(row, 64)
            total[some] = total[some] + other[some]

    def part(slot):
        return p_ref.at[pl.ds(slot * rows, rows)]

    order = [(step, first, second) for second in (1, 0) for step in (3, 2, 1, 0) for first in (1, 0)]
    loads = []

    def load(number):
        buffer = number % BUFFERS
        copy = pltpu.make_async_copy(
            part(place.slot(*order[number])), own.at[buffer], own_sem.at[buffer]
        )
        copy.start()
        loads.append(copy)

    for number in range(BUFFERS):
        load(number)
    place.greet_all_ways()
    for step, first, second in order:
        place.send(
            part(place.slot(step, first, second, 1)),
            held.at[step, first, second],
            core_sem.at[step, first, second],
            place.device(0, 0, 0, 1),
        )
    for number, (step, first, second) in enumerate(order):
        mine = held.at[step, first, second]
        place.arrive(mine, core_sem.at[step, first, second])
        loads[number].wait()
        add(mine, own.at[number % BUFFERS])
        if number + BUFFERS < len(order):
            load(number + BUFFERS)
        if second:
            place.send(
                mine, over_second.at[step, first], second_sem.at[step, first], place.device(0, 0, 1)
            )

    def onward(step):
        mine = held.at[step, 0, 0]
        place.arrive(over_first.at[step], first_sem.at[step])
        add(mine, over_first.at[step])
        if step:
            place.send(mine, over_z.at[step], z_sem.at[step], place.device(step, 0, 0))

    for step in (3, 2, 1, 0):
        mine = held.at[step, 1, 0]
        place.arrive(over_second.at[step, 1], second_sem.at[step, 1])
        add(mine, over_second.at[step, 1])
        place.send(mine, over_first.at[step], first_sem.at[step], place.device(0, 1, 0))
        mine = held.at[step, 0, 0]
        place.arrive(over_second.at[step, 0], second_sem.at[step, 0])
        add(mine, over_second.at[step, 0])
        if step < 3:
            onward(step + 1)
    onward(0)
    for step in (3, 2, 1):
        place.arrive(over_z.at[step], z_sem.at[step])

    @pl.loop(0, rows, step=32)
    def _(row):
        some = pl.ds(row, 32)
        total = held[0, 0, 0, some].astype(jnp.float32)
        for step in (1, 2, 3):
            total = total + over_z[step, some].astype(jnp.float32)
        out_ref[some] = total

    place.finish()


def scatter_all(p, parts, ident):
    rows, width = p.shape[0] // parts, p.shape[1]

    def buffer(*lead):
        return pltpu.VMEM((*lead, rows, width), p.dtype)

    scratch = [buffer(4, 2, 2), buffer(4, 2), buffer(4), buffer(4), buffer(BUFFERS)]
    scratch += [(BUFFERS,), (parts - 1,), (4, 2, 2), (4, 2), (4,), (4,)]
    out = jax.ShapeDtypeStruct((rows, width), jnp.float32)
    return reach(scatter_all_kernel, out, scratch, ident, p, vmem_out=True, mib=56)


def enter_kernel(x_ref, c_ref, group_ref, cot_ref, own_sem, send_sem, x_sem, cot_sem):
    place = Place(send_sem)
    ep, tp = place.ep, place.tp
    others = [place.across(step, over) for step in range(4) for over in (0, 1)]
    own = [
        pltpu.make_async_copy(x_ref.at[ep], group_ref.at[ep, tp], own_sem.at[0]),
        pltpu.make_async_copy(c_ref.at[ep], cot_ref.at[ep], own_sem.at[1]),
    ]
    for copy in own:
        copy.start()
    place.greet(
        [(other, tp) for other in others[1:]] + [(ep, place.over_x), (ep, place.over_core)]
    )
    for other in others[1:]:
        place.send(x_ref.at[other], group_ref.at[ep, tp], x_sem.at[ep, tp], (other, tp))
    for number, other in enumerate(others):
        block = group_ref.at[other, tp]
        if number:
            place.arrive(block, x_sem.at[other, tp])
        source = block if number else x_ref.at[ep]
        place.send(source, block, x_sem.at[other, tp], (ep, place.over_x))
        place.send(source, block, x_sem.at[other, tp], (ep, place.over_core))
    for other in others[1:]:
        place.send(c_ref.at[other], cot_ref.at[ep], cot_sem.at[ep], (other, tp))
    for other in others:
        block = group_ref.at[other, place.over_x]
        place.arrive(block, x_sem.at[other, place.over_x])
        place.send(block, block, x_sem.at[other, place.over_x], (ep, place.over_core))
    for other in others:
        for source in (place.over_core, place.over_both):
            place.arrive(group_ref.at[other, source], x_sem.at[other, source])
    for other in others[1:]:
        place.arrive(cot_ref.at[other], cot_sem.at[other])
    for copy in own:
        copy.wait()
    place.finish()


def enter(x, c, tp_size, ident):
    ep_size, block, width = x.shape
    moves = (ep_size - 1) * 2 + ep_size * 3
    out = [
        jax.ShapeDtypeStruct((ep_size, tp_size, block, width), x.dtype),
        jax.ShapeDtypeStruct((ep_size, block, width), x.dtype),
    ]
    scratch = [(2,), (moves,), (ep_size, tp_size), (ep_size,)]
    return reach(enter_kernel, out, scratch, ident, x, c)


CHUNKS = 4


def gather_group_kernel(x_ref, group_ref, own_sem, send_sem, recv_sem):
    place = Place(send_sem)
    ep, tp = place.ep, place.tp
    some = x_ref.shape[0] // CHUNKS

    def piece(chunk, owner):
        return group_ref.at[pl.ds(chunk * some, some), owner]

    own = pltpu.make_async_copy(x_ref, group_ref.at[:, tp], own_sem)
    own.start()
    place.greet([(ep, place.over_x), (ep, place.over_core)])
    for partner in (place.over_x, place.over_core):
        for chunk in range(CHUNKS):
            place.send(
                x_ref.at[pl.ds(chunk * some, some)],
                piece(chunk, tp),
                recv_sem.at[chunk, tp],
                (ep, partner),
            )
    for chunk in range(CHUNKS):
        block = piece(chunk, place.over_x)
        place.arrive(block, recv_sem.at[chunk, place.over_x])
        place.send(block, block, recv_sem.at[chunk, place.over_x], (ep, place.over_core))
    for chunk in range(CHUNKS):
        for source in (place.over_core, place.over_both):
            place.arrive(piece(chunk, source), recv_sem.at[chunk, source])
    own.wait()
    place.finish()


def gather_group(x, tp_size, ident):
    ep_size, block, width = x.shape
    out = jax.ShapeDtypeStruct((ep_size, tp_size, block, width), x.dtype)
    scratch = [pltpu.SemaphoreType.DMA, (CHUNKS * 3,), (CHUNKS, tp_size)]
    return reach(gather_group_kernel, out, scratch, ident, x)


def scatter_group_kernel(
    p_ref, out_ref, own, held, over_x, own_sem, send_sem, core_sem, x_sem
):
    place = Place(send_sem)
    ep, tp = place.ep, place.tp
    some = p_ref.shape[0] // CHUNKS
    block, width = p_ref.shape[2:]

    def chunk_of(chunk):
        return pl.ds(chunk * some, some)

    loads = [
        pltpu.make_async_copy(p_ref.at[:, owner], own.at[number], own_sem.at[number])
        for number, owner in enumerate((place.over_x, tp))
    ]
    for copy in loads:
        copy.start()
    place.greet([(ep, place.over_x), (ep, place.over_core)])
    for number, owner in enumerate((place.over_both, place.over_core)):
        for chunk in range(CHUNKS):
            place.send(
                p_ref.at[chunk_of(chunk), owner],
                held.at[number, chunk_of(chunk)],
                core_sem.at[number, chunk],
                (ep, place.over_core),
            )

    def add(number, chunk):
        place.arrive(held.at[number, chunk_of(chunk)], core_sem.at[number, chunk])
        for row in range(chunk * some, (chunk + 1) * some):
            held[number, row] = held[number, row] + own[number, row]

    loads[0].wait()
    for chunk in range(CHUNKS):
        add(0, chunk)
        place.send(
            held.at[0, chunk_of(chunk)],
            over_x.at[chunk_of(chunk)],
            x_sem.at[chunk],
            (ep, place.over_x),
        )
    loads[1].wait()
    for chunk in range(CHUNKS):
        add(1, chunk)
    for chunk in range(CHUNKS):
        place.arrive(over_x.at[chunk_of(chunk)], x_sem.at[chunk])
        for row in range(chunk * some, (chunk + 1) * some):
            out_ref[row] = held[1, row].astype(jnp.float32) + over_x[row].astype(jnp.float32)
    place.finish()


def scatter_group(p, ident):
    ep_size, tp_size, block, width = p.shape

    def buffer(*lead):
        return pltpu.VMEM((*lead, ep_size, block, width), p.dtype)

    scratch = [buffer(2), buffer(2), buffer(), (2,), (CHUNKS * 3,), (2, CHUNKS), (CHUNKS,)]
    out = jax.ShapeDtypeStruct((ep_size, block, width), jnp.float32)
    return reach(scatter_group_kernel, out, scratch, ident, p, vmem_out=True, mib=24)


def gather_kv_kernel(kv_ref, out_ref, own_sem, send_sem, recv_sem):
    place = Place(send_sem)
    ep, tp = place.ep, place.tp
    own = pltpu.make_async_copy(kv_ref, out_ref.at[:, ep], own_sem)
    own.start()
    partners = [place.across(*where) for where in ((1, 0), (2, 0), (3, 0), (0, 1))]
    place.greet([(partner, tp) for partner in partners])
    for partner in (partners[3], *partners[:3]):
        place.send(kv_ref, out_ref.at[:, ep], recv_sem.at[ep], (partner, tp))
    for partner in partners[:3]:
        block = out_ref.at[:, partner]
        place.arrive(block, recv_sem.at[partner])
        place.send(block, block, recv_sem.at[partner], (partners[3], tp))
    for step in range(4):
        other = place.across(step, 1)
        place.arrive(out_ref.at[:, other], recv_sem.at[other])
    own.wait()
    place.finish()


def gather_kv(kv, ep_size, ident):
    blocks, rows, width = kv.shape
    out = jax.ShapeDtypeStruct((blocks, ep_size, rows, width), kv.dtype)
    scratch = [pltpu.SemaphoreType.DMA, (ep_size - 1,), (ep_size,)]
    return reach(gather_kv_kernel, out, scratch, ident, kv)


def scatter_kv_kernel(p_ref, out_ref, own, over_y, over_z, own_sem, send_sem, y_sem, z_sem):
    place = Place(send_sem)
    tp = place.tp
    blocks = out_ref.shape[0]
    order = (3, 2, 1, 0)
    loads = {}
    for step in order:
        loads[step] = pltpu.make_async_copy(
            p_ref.at[:, place.across(step, 0)], own.at[step], own_sem.at[step]
        )
        loads[step].start()
    place.greet([(place.across(*where), tp) for where in ((1, 0), (2, 0), (3, 0), (0, 1))])
    for step in order:
        place.send(
            p_ref.at[:, place.across(step, 1)],
            over_y.at[step],
            y_sem.at[step],
            (place.across(0, 1), tp),
        )
    for step in order:
        loads[step].wait()
        place.arrive(over_y.at[step], y_sem.at[step])

        @pl.loop(0, blocks)
        def _(block, step=step):
            own[step, block] = own[step, block] + over_y[step, block]

        if step:
            place.send(
                own.at[step], over_z.at[step], z_sem.at[step], (place.across(step, 0), tp)
            )
    for step in (3, 2, 1):
        place.arrive(over_z.at[step], z_sem.at[step])

    @pl.loop(0, blocks)
    def _(block):
        total = own[0, block].astype(jnp.float32)
        for step in (1, 2, 3):
            total = total + over_z[step, block].astype(jnp.float32)
        out_ref[block] = total.astype(jnp.bfloat16)

    place.finish()


def scatter_kv(p, ident):
    blocks, ep_size, rows, width = p.shape
    buffer = pltpu.VMEM((4, blocks, rows, width), p.dtype)
    scratch = [buffer, buffer, buffer, (4,), (7,), (4,), (4,)]
    out = jax.ShapeDtypeStruct((blocks, rows, width), p.dtype)
    return reach(scatter_kv_kernel, out, scratch, ident, p, vmem_out=True, mib=24)


SLOTS = 1024


def finish_kernel(*refs):
    partials, gains_ref, rows_ref, experts = refs[:3], refs[3], refs[4], refs[5:10]
    outs, gain_out, rows_out, grads, refs = refs[10:13], refs[13], refs[14], refs[15:18], refs[18:]
    owns, overs_y, overs_z, stages, refs = refs[:3], refs[3:6], refs[6:9], refs[9:11], refs[11:]
    wide, narrow, sums, refs = refs[0], refs[1], refs[2:5], refs[5:]
    own_sem, send_sem, y_sem, z_sem, gain_sem, load_sem, grad_sem, rows_sem, rows_send_sem = refs
    place = Place(send_sem)
    ep, tp = place.ep, place.tp
    count = len(partials)
    total, arrived = stages
    ways = [(ep, place.over_core), (ep, place.over_x)]
    ways += [(place.across(step, 0), tp) for step in (1, 2, 3)]
    ways.append((place.across(0, 1), tp))
    moves = [(number, step) for step in (3, 2, 1, 0) for number in range(count)]
    gain_load = pltpu.make_async_copy(gains_ref, total.at[0], own_sem.at[count, 0])
    gain_load.start()

    def own_copy(number, step):
        return pltpu.make_async_copy(
            partials[number].at[place.across(step, 0)],
            owns[number].at[step],
            own_sem.at[number, step],
        )

    def to_y(number, step):
        return pltpu.make_async_remote_copy(
            src_ref=partials[number].at[place.across(step, 1)],
            dst_ref=overs_y[number].at[step],
            send_sem=send_sem.at[number, step],
            recv_sem=y_sem.at[number, step],
            device_id=(place.across(0, 1), tp),
            device_id_type=MESH_ID,
        )

    def to_z(number, step):
        return pltpu.make_async_remote_copy(
            src_ref=owns[number].at[step],
            dst_ref=overs_z[number].at[step],
            send_sem=send_sem.at[number, 3 + step],
            recv_sem=z_sem.at[number, step],
            device_id=(place.across(step, 0), tp),
            device_id_type=MESH_ID,
        )

    def gain_copy(number):
        return pltpu.make_async_remote_copy(
            src_ref=total.at[(0, 1, 2, 2, 2, 3)[number]],
            dst_ref=arrived.at[number],
            send_sem=send_sem.at[count, number],
            recv_sem=gain_sem.at[number],
            device_id=ways[number],
            device_id_type=MESH_ID,
        )

    others = [(step, over) for step in range(4) for over in (0, 1)][1:]

    def row_copy(index):
        other = place.across(*others[index])
        return pltpu.make_async_remote_copy(
            src_ref=rows_ref.at[other],
            dst_ref=rows_out.at[ep],
            send_sem=rows_send_sem.at[index],
            recv_sem=rows_sem.at[ep],
            device_id=(other, tp),
            device_id_type=MESH_ID,
        )

    def row_arrival(index):
        other = place.across(*others[index])
        return pltpu.make_async_remote_copy(
            src_ref=rows_ref.at[other],
            dst_ref=rows_out.at[other],
            send_sem=rows_send_sem.at[index],
            recv_sem=rows_sem.at[other],
            device_id=(other, tp),
            device_id_type=MESH_ID,
        )

    own_rows = pltpu.make_async_copy(rows_ref.at[ep], rows_out.at[ep], rows_sem.at[ep])
    own_rows.start()
    for number, step in moves:
        own_copy(number, step).start()
    place.greet(ways[:2] + [(place.across(*other), tp) for other in others])
    gain_load.wait()
    gain_copy(0).start()
    for index in range(len(others)):
        row_copy(index).start()
    for number, step in moves:
        to_y(number, step).start()

    def event(index):
        number, step = moves[index]
        own, over = owns[number], overs_y[number]
        own_copy(number, step).wait()
        to_y(number, step).wait_recv()

        @pl.loop(0, own.shape[1], step=64)
        def _(row):
            some = pl.ds(row, 64)
            own[step, some] = own[step, some] + over[step, some]

        if step:
            to_z(number, step).start()
        if index < 2:
            gain_copy(index).wait_recv()
            total[index + 1] = total[index] + arrived[index]
            for later in (1,) if index == 0 else (2, 3, 4):
                gain_copy(later).start()
        if index == 2:
            for later in (2, 3, 4):
                gain_copy(later).wait_recv()
            total[3] = (total[2] + arrived[2]) + (arrived[3] + arrived[4])
            gain_copy(5).start()

    expert_in, slot_cot, inner, gate_grad, up_grad = experts
    pieces = expert_in.shape[0] // SLOTS
    jobs = ((expert_in, gate_grad), (expert_in, up_grad), (slot_cot, inner))
    steps = pieces * len(jobs)

    def load_copies(pair, piece, parity):
        some = pl.ds(piece * SLOTS, SLOTS)
        return [
            pltpu.make_async_copy(ref.at[some], held.at[parity], load_sem.at[parity, index])
            for index, (ref, held) in enumerate(zip(pair, (wide, narrow)))
        ]

    def grad_copy(job):
        return pltpu.make_async_copy(sums[job], grads[job], grad_sem.at[job])

    def multiply(job, parity):
        into = sums[job]
        left, right = (wide, narrow) if job < 2 else (narrow, wide)
        tile = 512 if into.shape[0] % 512 == 0 else 384

        @pl.loop(0, into.shape[0], step=tile)
        def _(row):
            some = pl.ds(pl.multiple_of(row, tile), tile)
            product = dot_with(left[parity, :, some], right[parity], ROWS_BY_ROWS)

            into[some] += product

    for into in sums:

        @pl.loop(0, into.shape[0], step=64)
        def _(row, into=into):
            into[pl.ds(row, 64)] = jnp.zeros((64, into.shape[1]), jnp.float32)

    @pl.loop(0, steps + 1)
    def _(turn):
        for index in range(len(moves)):

            @pl.when(turn == index)
            def _(index=index):
                event(index)

        for job, pair in enumerate(jobs):

            @pl.when((turn >= job * pieces) & (turn < (job + 1) * pieces))
            def _(job=job, pair=pair):
                for copy in load_copies(pair, turn - job * pieces, turn % 2):
                    copy.start()

        for job, pair in enumerate(jobs):

            @pl.when((turn > job * pieces) & (turn <= (job + 1) * pieces))
            def _(job=job, pair=pair):
                parity = (turn - 1) % 2
                for copy in load_copies(pair, 0, parity):
                    copy.wait()
                multiply(job, parity)

            @pl.when(turn == (job + 1) * pieces)
            def _(job=job):
                grad_copy(job).start()

    for number in range(count):
        own, over, out = owns[number], overs_z[number], outs[number]
        for step in (3, 2, 1):
            to_z(number, step).wait_recv()

        @pl.loop(0, own.shape[1], step=64)
        def _(row, own=own, over=over, out=out):
            some = pl.ds(row, 64)
            sum_of = own[0, some].astype(jnp.float32)
            for step in (1, 2, 3):
                sum_of = sum_of + over[step, some].astype(jnp.float32)
            out[some] = sum_of

    gain_copy(5).wait_recv()
    gain_out[...] = total[3] + arrived[5]
    for job in range(len(jobs)):
        grad_copy(job).wait()
    for number, step in moves:
        to_y(number, step).wait_send()
        if step:
            to_z(number, step).wait_send()
    for number in range(6):
        gain_copy(number).wait_send()
    own_rows.wait()
    for index in range(len(others)):
        row_copy(index).wait_send()
        row_arrival(index).wait_recv()


def finish(partials, gains, rows, expert_in, slot_cot, inner, gate_grad, up_grad, ident):
    count = len(partials)
    buffers = [pltpu.VMEM((4, *p.shape[1:]), p.dtype) for p in partials]
    width, hidden = expert_in.shape[1], inner.shape[1]
    grads = [(width, hidden), (width, hidden), (hidden, width)]
    scratch = buffers * 3
    scratch += [pltpu.VMEM((4, *gains.shape), gains.dtype), pltpu.VMEM((6, *gains.shape), gains.dtype)]
    scratch += [pltpu.VMEM((2, SLOTS, width), jnp.bfloat16), pltpu.VMEM((2, SLOTS, hidden), jnp.bfloat16)]
    scratch += [pltpu.VMEM(shape, jnp.float32) for shape in grads]
    scratch += [(count + 1, 4), (count + 1, 7), (count, 4), (count, 4), (6,), (2, 2), (3,), (8,), (7,)]
    out = [jax.ShapeDtypeStruct(p.shape[1:], jnp.float32) for p in partials]
    out.append(jax.ShapeDtypeStruct(gains.shape, jnp.float32))
    out.append(jax.ShapeDtypeStruct(rows.shape, rows.dtype))
    out += [jax.ShapeDtypeStruct(shape, jnp.float32) for shape in grads]
    operands = (*partials, gains, rows, expert_in, slot_cot, inner, gate_grad, up_grad)
    return reach(
        finish_kernel, out, scratch, ident, *operands, vmem_out=(True,) * 4 + (False,) * 4, mib=58
    )


def on_device(
    inputs,
    cotangent,
    arrangement,
    seq_lengths,
    routes,
    gate_values,
    input_gain,
    query_proj,
    key_projected,
    value_projected,
    query_gain,
    key_gain,
    output_proj,
    expert_gain,
    gate_weight,
    up_weight,
    down_weight,
):
    ep_size = lax.axis_size("ep")
    tp_size = lax.axis_size("tp")
    ep_index = lax.axis_index("ep")
    tp_index = lax.axis_index("tp")
    everyone = ("ep", "tp")
    own_rows, width = inputs.shape
    group_rows = own_rows * tp_size
    row_block = own_rows // ep_size
    token_total = arrangement.shape[0]
    expert_count = ep_size * tp_size
    capacity = 2 * own_rows * TOP // expert_count
    heads = query_proj.shape[1] // HEAD
    known = (ep_size, tp_size) == (8, 4)
    expert = (ep_index * tp_size + tp_index).astype(jnp.int32)[None]

    table = arrangement.reshape(ep_size, tp_size, ep_size, row_block)
    leaving_from = lax.dynamic_index_in_dim(table, tp_index, 1, keepdims=False)
    leaving_from = lax.dynamic_index_in_dim(leaving_from, ep_index, 1, keepdims=False)
    send_index = leaving_from - (ep_index * group_rows + tp_index * own_rows)
    mover = (
        send_index.reshape(-1)[:, None] == jnp.arange(own_rows, dtype=jnp.int32)[None, :]
    ).astype(jnp.bfloat16)

    def to_places(rows):
        return dot(mover, rows).astype(jnp.bfloat16).reshape(ep_size, row_block, width)

    def exchange(rows):
        return lax.all_to_all(rows, "ep", split_axis=0, concat_axis=0, tiled=True)

    def by_source(rows):
        return rows.astype(jnp.bfloat16).reshape(ep_size, row_block, width)

    def to_given(moved):
        return dot_with(mover, moved.reshape(own_rows, width), ROWS_BY_ROWS)

    def group_sorted(rows, ident):
        blocks = rows.reshape(ep_size, row_block, width)
        if known:
            gathered = gather_group(blocks, tp_size, ident)
        else:
            gathered = lax.all_gather(blocks, "tp", axis=1)
        return gathered.reshape(group_rows, width)

    def sum_group(rows, ident):
        blocks = rows.astype(jnp.bfloat16).reshape(ep_size, tp_size, row_block, width)
        if known:
            return scatter_group(blocks, ident).reshape(own_rows, width)
        placed = jnp.swapaxes(blocks, 0, 1).reshape(group_rows, width)
        own = lax.psum_scatter(placed, "tp", scatter_dimension=0, tiled=True)
        return own.astype(jnp.float32)

    leaving_x, leaving_cot = to_places(inputs), to_places(cotangent)
    if known:
        group_x, own_cot = enter(leaving_x, leaving_cot, tp_size, 1)
        own_inputs = lax.dynamic_index_in_dim(group_x, tp_index, 1, keepdims=False)
    else:
        own_inputs, own_cot = exchange(leaving_x), exchange(leaving_cot)
        group_x = lax.all_gather(own_inputs, "tp", axis=1)
    own_inputs, own_cot = own_inputs.reshape(own_rows, width), own_cot.reshape(own_rows, width)
    group_x = group_x.reshape(group_rows, width)
    meta_own = jnp.concatenate([routes.astype(jnp.float32).T, gate_values.T], axis=0)
    cot_all = lax.all_gather(own_cot, everyone, axis=0, tiled=True)

    query_given = lax.dynamic_index_in_dim(table, ep_index, 0, keepdims=False)
    query_given = jnp.swapaxes(query_given, 0, 1).reshape(group_rows)
    query_first = seq_starts(query_given, seq_lengths)
    cosine, sine = rope_tables(query_given - query_first, HEAD)
    key_given = jnp.transpose(table, (2, 1, 0, 3)).reshape(token_total)
    by_step = (-1, QUERY_TOKENS)
    given_steps, first_steps = query_given.reshape(by_step), query_first.reshape(by_step)
    lowest = jnp.min(first_steps, axis=1) // KEY_SPAN
    highest = jnp.max(given_steps, axis=1) // KEY_SPAN + 1
    open_low = (jnp.max(first_steps, axis=1) + KEY_SPAN - 1) // KEY_SPAN
    open_low = jnp.minimum(open_low, highest)
    open_high = jnp.clip((jnp.min(given_steps, axis=1) + 1) // KEY_SPAN, open_low, highest)
    bounds = jnp.stack([lowest, open_low, open_high, highest]).astype(jnp.int32)
    ask = jnp.stack([query_given, query_first], axis=1)
    ask_rows = jnp.stack(
        [jnp.tile(given_steps, (1, heads)), jnp.tile(first_steps, (1, heads))], axis=1
    )

    normed_in, query_raw, query_rows, key_raw, kv_rows = front(
        group_x, input_gain, query_proj, key_projected, value_projected,
        query_gain, key_gain, cosine, sine,
    )
    kv_blocks = kv_rows.reshape(expert_count, row_block, 2 * HEAD)
    if known:
        kv_all = gather_kv(kv_blocks, ep_size, 2)
    else:
        kv_all = lax.all_gather(kv_blocks, "ep", axis=1)
    kv_all = kv_all.reshape(token_total, 2 * HEAD)
    pairs = group_rows * heads * 1536
    exact, out_rows, lse = attend_forward(
        bounds, query_rows, ask, key_given[None], kv_all, pairs
    )
    branch = sum_group(dot(out_rows, output_proj), 5)
    hidden = own_inputs.astype(jnp.float32) + branch
    mid_scale = inverse_root(hidden)
    normed_mid = (hidden * mid_scale * expert_gain).astype(jnp.bfloat16)

    experts = (gate_weight, up_weight, down_weight, capacity)
    if known:
        results = expert_all(normed_mid, meta_own, cot_all, *experts, 3)
    else:
        mid_all = lax.all_gather(normed_mid, everyone, axis=0, tiled=True)
        meta = lax.all_gather(meta_own, everyone, axis=0)
        results = expert_pass(expert, meta, mid_all, cot_all, *experts)
    mid_partial, out_partial, expert_in, slot_cot, inner, gate_grad, up_grad = results
    def sum_over_all(partial):
        return lax.psum_scatter(partial, everyone, scatter_dimension=0, tiled=True)

    if known:
        mid_grad = scatter_all(mid_partial, expert_count, 4)
    else:
        mid_grad = sum_over_all(mid_partial).astype(jnp.float32)
    mid_grad, out_partial = lax.optimization_barrier((mid_grad, out_partial))
    mixed = sum_over_all(out_partial)

    mid_hat = hidden * mid_scale
    grad_expert_gain = jnp.sum(mid_grad * mid_hat, axis=0)
    mid_scaled = mid_grad * expert_gain
    hidden_grad = own_cot.astype(jnp.float32) + mid_scale * (
        mid_scaled - mid_hat * jnp.mean(mid_scaled * mid_hat, axis=-1, keepdims=True)
    )
    branch_grad = group_sorted(hidden_grad.astype(jnp.bfloat16), 6)
    out_grad = dot_with(branch_grad, output_proj, COLS_BY_COLS).astype(jnp.bfloat16)
    query_grad, kv_grad = attend_backward(
        bounds, query_rows, out_grad, exact, lse, ask_rows, key_given[:, None], kv_all, pairs
    )
    kv_grad = kv_grad.reshape(expert_count, ep_size, row_block, 2 * HEAD)
    if known:
        kv_own = scatter_kv(kv_grad, 7)
    else:
        kv_own = lax.psum_scatter(kv_grad, "ep", scatter_dimension=1)
    kv_own = kv_own.reshape(group_rows, 2 * HEAD)
    value_grad = kv_own[:, HEAD:]
    raw_query_grad, grad_query_gain = head_back(query_raw, query_grad, query_gain, cosine, sine)
    raw_key_grad, grad_key_gain = head_back(key_raw, kv_own[:, :HEAD], key_gain, cosine, sine)
    normed_grad = (
        dot_with(raw_query_grad, query_proj, COLS_BY_COLS)
        + dot_with(raw_key_grad, key_projected, COLS_BY_COLS)
        + dot_with(value_grad, value_projected, COLS_BY_COLS)
    )
    normed_grad = sum_group(normed_grad, 8)
    own_float = own_inputs.astype(jnp.float32)
    in_scale = inverse_root(own_float)
    in_hat = own_float * in_scale
    grad_input_gain = jnp.sum(normed_grad * in_hat, axis=0)
    in_scaled = normed_grad * input_gain
    input_rows = by_source(
        hidden_grad
        + in_scale * (in_scaled - in_hat * jnp.mean(in_scaled * in_hat, axis=-1, keepdims=True))
    )

    weights = [
        dot_with(branch_grad, out_rows, ROWS_BY_ROWS),
        dot_with(normed_in, raw_query_grad, ROWS_BY_ROWS),
        dot_with(normed_in, jnp.concatenate([raw_key_grad, value_grad], axis=1), ROWS_BY_ROWS),
    ]
    weights = [array.astype(jnp.bfloat16).reshape(ep_size, -1, array.shape[1]) for array in weights]
    gains = jnp.concatenate(
        [grad_input_gain, grad_expert_gain, grad_query_gain[0], grad_key_gain[0]]
    )
    if known:
        experts = (expert_in, slot_cot, inner, gate_grad, up_grad)
        results = finish(weights, gains.reshape(-1, HEAD), input_rows, *experts, 10)
        grad_output, grad_query, grad_kv, gains, input_rows = results[:5]
        grad_gate, grad_up, grad_down = results[5:]
        gains = gains.reshape(-1)
    else:
        grad_output, grad_query, grad_kv = [
            lax.psum_scatter(array, "ep", scatter_dimension=0).astype(jnp.float32)
            for array in weights
        ]
        gains, input_rows = lax.psum(gains, everyone), exchange(input_rows)
        grad_gate = dot_with(expert_in, gate_grad, ROWS_BY_ROWS)
        grad_up = dot_with(expert_in, up_grad, ROWS_BY_ROWS)
        grad_down = dot_with(inner, slot_cot, ROWS_BY_ROWS)
    mixed, gains = lax.optimization_barrier((mixed, gains))
    grad_inputs = to_given(input_rows)
    layer_out = to_given(exchange(by_source(hidden + mixed.astype(jnp.float32))))
    layer_out = layer_out.astype(jnp.bfloat16)
    grad_output = jnp.transpose(grad_output)
    cuts = (width, 2 * width, 2 * width + HEAD)
    return (
        layer_out,
        grad_inputs,
        grad_query,
        grad_kv[:, :HEAD],
        grad_kv[:, HEAD:],
        grad_output,
        gains[: cuts[0]],
        gains[cuts[1] : cuts[2]],
        gains[cuts[2] :],
        gains[cuts[0] : cuts[1]],
        grad_gate[None],
        grad_up[None],
        grad_down[None],
    )


def solution(mesh):
    split = P(("ep", "tp"), None)
    experts = P(("ep", "tp"), None, None)
    columns = P(None, "tp")
    return jax.shard_map(
        on_device,
        mesh=mesh,
        in_specs=(
            split, split, P(), P(), split, split, P(), columns, columns, columns,
            P(), P(), P("tp", None), P(), experts, experts, experts,
        ),
        out_specs=(
            split, split, P("ep", "tp"), P("ep", "tp"), P("ep", "tp"), P("tp", "ep"),
            P(), P(), P(), P(), experts, experts, experts,
        ),
        check_vma=False,
    )
```

```python
import functools
import math

import jax
import jax.numpy as jnp
from jax import lax
from jax.experimental import pallas as pl
from jax.experimental.pallas import tpu as pltpu
from jax.sharding import PartitionSpec as P

TOP = 8
EPSILON = 1e-06
ROPE_BASE = 1000000.0
KEY_SPAN = 512
QUERY_TOKENS = 64
HEAD = 128
ROW_TILE = 256
MIB = 1 << 20
LOG2E = math.log2(math.e)
ROWS_BY_ROWS = (((0,), (0,)), ((), ()))
COLS_BY_COLS = (((1,), (1,)), ((), ()))


def dot(left, right):
    return jnp.dot(left, right, preferred_element_type=jnp.float32)


def dot_with(left, right, dims):
    return lax.dot_general(left, right, dims, preferred_element_type=jnp.float32)


def cost(flops, moved, transcendentals=0):
    return pl.CostEstimate(
        flops=int(flops), bytes_accessed=int(moved), transcendentals=int(transcendentals)
    )


def params(mib):
    return pltpu.CompilerParams(
        dimension_semantics=("arbitrary",), vmem_limit_bytes=mib * MIB
    )


def whole(shape, single=True):
    rank = len(shape)
    if single:
        return pl.BlockSpec(shape, lambda *ids: (0,) * rank, pipeline_mode=pl.Buffered(1))
    return pl.BlockSpec(shape, lambda *ids: (0,) * rank)


def rows_of(shape):
    rank = len(shape)
    return pl.BlockSpec(shape, lambda i, *ids: (i,) + (0,) * (rank - 1))


def rope_tables(positions, head_dim):
    freqs = ROPE_BASE ** (-jnp.arange(0, head_dim, 2, dtype=jnp.float32) / head_dim)
    angles = positions.astype(jnp.float32)[:, None] * freqs[None, :]
    cosine, sine = jnp.cos(angles), jnp.sin(angles)
    return (
        jnp.concatenate([cosine, cosine], axis=-1),
        jnp.concatenate([-sine, sine], axis=-1),
    )


def seq_starts(given, seq_lengths):
    ends = jnp.cumsum(seq_lengths)
    passed = given[:, None] >= ends[None, :]
    return jnp.sum(jnp.where(passed, seq_lengths[None, :], 0), axis=1)


def inverse_root(values):
    return lax.rsqrt(jnp.mean(values * values, axis=-1, keepdims=True) + EPSILON)


def front_kernel(
    x_ref, gain_ref, wq_ref, wk_ref, wv_ref, qg_ref, kg_ref, cos_ref, sin_ref,
    normed_ref, qraw_ref, q_ref, kraw_ref, kv_ref,
):
    x = x_ref[...].astype(jnp.float32)
    normed = (x * inverse_root(x) * gain_ref[...]).astype(jnp.bfloat16)
    normed_ref[...] = normed
    cosine, sine = cos_ref[...], sin_ref[...]

    def prepare(raw, gain):
        values = raw * inverse_root(raw) * gain
        return (values * cosine + pltpu.roll(values, HEAD // 2, 1) * sine).astype(jnp.bfloat16)

    raw = dot(normed, wq_ref[...])
    qraw_ref[...] = raw
    for head in range(raw.shape[1] // HEAD):
        part = slice(head * HEAD, (head + 1) * HEAD)
        q_ref[:, part] = prepare(raw[:, part], qg_ref[...])
    raw = dot(normed, wk_ref[...])
    kraw_ref[...] = raw
    kv_ref[:, :HEAD] = prepare(raw, kg_ref[...])
    kv_ref[:, HEAD:] = dot(normed, wv_ref[...]).astype(jnp.bfloat16)


def front(group_x, input_gain, wq, wk, wv, query_gain, key_gain, cosine, sine):
    rows, width = group_x.shape
    cols = wq.shape[1]
    tile = min(ROW_TILE, rows)
    out = [
        ((rows, width), jnp.bfloat16),
        ((rows, cols), jnp.float32),
        ((rows, cols), jnp.bfloat16),
        ((rows, HEAD), jnp.float32),
        ((rows, 2 * HEAD), jnp.bfloat16),
    ]
    return pl.pallas_call(
        front_kernel,
        grid=(rows // tile,),
        in_specs=[
            rows_of((tile, width)),
            whole((1, width)),
            whole(wq.shape),
            whole(wk.shape),
            whole(wv.shape),
            whole((1, HEAD)),
            whole((1, HEAD)),
            rows_of((tile, HEAD)),
            rows_of((tile, HEAD)),
        ],
        out_specs=[rows_of((tile, shape[1])) for shape, kind in out],
        out_shape=[jax.ShapeDtypeStruct(shape, kind) for shape, kind in out],
        compiler_params=params(40),
        cost_estimate=cost(2 * rows * width * (cols + 2 * HEAD), 20 * MIB),
        name="front",
    )(
        group_x,
        input_gain[None],
        wq,
        wk,
        wv,
        query_gain[None],
        key_gain[None],
        cosine,
        sine,
    )


def stack_heads(block):
    heads = block.shape[1] // HEAD
    return jnp.concatenate(
        [block[:, head * HEAD : (head + 1) * HEAD] for head in range(heads)], axis=0
    )


def attend_forward_kernel(
    bounds_ref, q_ref, ask_ref, key_given_ref, kv_ref, exact_ref, out_ref, lse_ref, acc, tot
):
    step = pl.program_id(0)
    tokens, cols = q_ref.shape
    heads = cols // HEAD
    query = stack_heads(q_ref[...])
    ask = ask_ref[...]
    last = jnp.concatenate([ask[:, 0:1]] * heads, axis=0)
    first = jnp.concatenate([ask[:, 1:2]] * heads, axis=0)
    acc[...] = jnp.zeros_like(acc)
    tot[...] = jnp.zeros_like(tot)

    def visit(span, masked):
        offset = pl.multiple_of(span * KEY_SPAN, KEY_SPAN)
        keys = kv_ref[pl.ds(offset, KEY_SPAN), :HEAD]
        values = kv_ref[pl.ds(offset, KEY_SPAN), HEAD:]
        scores = dot_with(query, keys, COLS_BY_COLS)
        weights = jnp.exp2(scores * (HEAD**-0.5 * LOG2E))
        if masked:
            key_given = key_given_ref[:, pl.ds(offset, KEY_SPAN)]
            weights = jnp.where((key_given <= last) & (key_given >= first), weights, 0.0)
        part = weights[:, :HEAD]
        for chunk in range(1, KEY_SPAN // HEAD):
            part = part + weights[:, chunk * HEAD : (chunk + 1) * HEAD]
        tot[...] += part
        acc[...] += dot(weights.astype(jnp.bfloat16), values)

    lowest, open_low = bounds_ref[0, step], bounds_ref[1, step]
    open_high, highest = bounds_ref[2, step], bounds_ref[3, step]

    @pl.loop(lowest, open_low)
    def _(span):
        visit(span, True)

    @pl.loop(open_low, open_high)
    def _(span):
        visit(span, False)

    @pl.loop(open_high, highest)
    def _(span):
        visit(span, True)

    total = tot[...]
    exact = acc[...] / jnp.sum(total, axis=1, keepdims=True)
    for head in range(heads):
        rows = exact[head * tokens : (head + 1) * tokens]
        exact_ref[:, head * HEAD : (head + 1) * HEAD] = rows
        out_ref[:, head * HEAD : (head + 1) * HEAD] = rows.astype(jnp.bfloat16)
    lse_ref[0] = jnp.log2(jnp.sum(total.T, axis=0, keepdims=True))


def attend_forward(bounds, query, ask, key_given, kv, pairs):
    rows, cols = query.shape
    heads = cols // HEAD
    steps = rows // QUERY_TOKENS
    stacked = heads * QUERY_TOKENS
    return pl.pallas_call(
        attend_forward_kernel,
        grid_spec=pltpu.PrefetchScalarGridSpec(
            num_scalar_prefetch=1,
            grid=(steps,),
            in_specs=[
                rows_of((QUERY_TOKENS, cols)),
                rows_of((QUERY_TOKENS, 2)),
                whole(key_given.shape),
                whole(kv.shape),
            ],
            out_specs=[
                rows_of((QUERY_TOKENS, cols)),
                rows_of((QUERY_TOKENS, cols)),
                rows_of((1, 1, stacked)),
            ],
            scratch_shapes=[
                pltpu.VMEM((stacked, HEAD), jnp.float32),
                pltpu.VMEM((stacked, HEAD), jnp.float32),
            ],
        ),
        out_shape=[
            jax.ShapeDtypeStruct((rows, cols), jnp.float32),
            jax.ShapeDtypeStruct((rows, cols), jnp.bfloat16),
            jax.ShapeDtypeStruct((steps, 1, stacked), jnp.float32),
        ],
        compiler_params=params(48),
        cost_estimate=cost(8 * pairs * HEAD, 16 * MIB, pairs),
        name="attend_forward",
    )(bounds, query, ask, key_given, kv)


def attend_backward_kernel(
    bounds_ref, q_ref, grad_ref, exact_ref, lse_ref, ask_ref, key_given_ref, kv_ref,
    dq_ref, rounded_ref, dkv_ref, acc,
):
    step = pl.program_id(0)
    tokens, cols = q_ref.shape
    heads = cols // HEAD

    @pl.when(step == 0)
    def _():
        dkv_ref[...] = jnp.zeros_like(dkv_ref)

    query = stack_heads(q_ref[...])
    grad = stack_heads(grad_ref[...])
    product = grad.astype(jnp.float32) * stack_heads(exact_ref[...])
    delta = jnp.sum(product.T, axis=0, keepdims=True)
    lse = lse_ref[0]
    last, first = ask_ref[0, 0:1, :], ask_ref[0, 1:2, :]
    acc[...] = jnp.zeros_like(acc)

    def visit(span, masked):
        offset = pl.multiple_of(span * KEY_SPAN, KEY_SPAN)
        place = pl.ds(offset, KEY_SPAN)
        keys = kv_ref[place, :HEAD]
        values = kv_ref[place, HEAD:]
        scores = dot_with(keys, query, COLS_BY_COLS)
        probs = jnp.exp2(scores * (HEAD**-0.5 * LOG2E) - lse)
        if masked:
            key_given = jnp.broadcast_to(key_given_ref[:, place], (8, KEY_SPAN)).T[:, 0:1]
            probs = jnp.where((key_given <= last) & (key_given >= first), probs, 0.0)
        prob_grad = dot_with(values, grad, COLS_BY_COLS)
        score_grad = (probs * (prob_grad - delta)).astype(jnp.bfloat16)
        dkv_ref[place, HEAD:] += dot(probs.astype(jnp.bfloat16), grad)
        dkv_ref[place, :HEAD] += dot(score_grad, query) * (HEAD**-0.5)
        acc[...] += dot_with(score_grad, keys, ROWS_BY_ROWS)

    lowest, open_low = bounds_ref[0, step], bounds_ref[1, step]
    open_high, highest = bounds_ref[2, step], bounds_ref[3, step]

    @pl.loop(lowest, open_low)
    def _(span):
        visit(span, True)

    @pl.loop(open_low, open_high)
    def _(span):
        visit(span, False)

    @pl.loop(open_high, highest)
    def _(span):
        visit(span, True)

    for head in range(heads):
        dq_ref[:, head * HEAD : (head + 1) * HEAD] = acc[
            head * tokens : (head + 1) * tokens
        ] * (HEAD**-0.5)

    @pl.when(step == pl.num_programs(0) - 1)
    def _():
        @pl.loop(0, dkv_ref.shape[0], step=KEY_SPAN)
        def _(row):
            place = pl.ds(row, KEY_SPAN)
            rounded_ref[place] = dkv_ref[place].astype(jnp.bfloat16)


def attend_backward(bounds, query, grad, exact, lse, ask_rows, key_given, kv, pairs):
    rows, cols = query.shape
    heads = cols // HEAD
    steps = rows // QUERY_TOKENS
    stacked = heads * QUERY_TOKENS
    return pl.pallas_call(
        attend_backward_kernel,
        grid_spec=pltpu.PrefetchScalarGridSpec(
            num_scalar_prefetch=1,
            grid=(steps,),
            in_specs=[
                rows_of((QUERY_TOKENS, cols)),
                rows_of((QUERY_TOKENS, cols)),
                rows_of((QUERY_TOKENS, cols)),
                rows_of((1, 1, stacked)),
                rows_of((1, 2, stacked)),
                whole(key_given.shape),
                whole(kv.shape),
            ],
            out_specs=[rows_of((QUERY_TOKENS, cols)), whole(kv.shape)],
            scratch_shapes=[
                pltpu.VMEM(kv.shape, jnp.float32),
                pltpu.VMEM((stacked, HEAD), jnp.float32),
            ],
        ),
        out_shape=[
            jax.ShapeDtypeStruct((rows, cols), jnp.float32),
            jax.ShapeDtypeStruct(kv.shape, jnp.bfloat16),
        ],
        compiler_params=params(56),
        cost_estimate=cost(20 * pairs * HEAD, 32 * MIB, pairs),
        name="attend_backward",
    )(bounds, query, grad, exact, lse, ask_rows, key_given, kv)


def selection(meta, expert, capacity):
    tokens = meta.shape[1]
    weight = jnp.sum(jnp.where(meta[:TOP] == expert, meta[TOP : 2 * TOP], 0.0), axis=0, keepdims=True)
    member = jnp.where(weight > 0.0, 1.0, 0.0)
    earlier = lax.broadcasted_iota(jnp.int32, (tokens, tokens), 0)
    later = lax.broadcasted_iota(jnp.int32, (tokens, tokens), 1)
    before = jnp.where(earlier < later, 1.0, 0.0).astype(jnp.bfloat16)
    rank = dot(jnp.broadcast_to(member, (16, tokens)).astype(jnp.bfloat16), before)[0:1]
    rank = jnp.where(weight > 0.0, rank, -1.0).astype(jnp.int32)
    hit = lax.broadcasted_iota(jnp.int32, (capacity, tokens), 0) == rank
    gate = jnp.sum(jnp.where(hit, weight, 0.0), axis=1, keepdims=True)
    return jnp.where(hit, 1.0, 0.0).astype(jnp.bfloat16), gate


def expert_kernel(
    expert_ref, meta_ref, x_ref, c_ref, wg_ref, wu_ref, wd_ref,
    mid_ref, out_ref, xs_ref, cs_ref, inner_ref, gg_ref, ug_ref,
):
    blocks, _, tokens = meta_ref.shape
    capacity = xs_ref.shape[0] // blocks
    expert = expert_ref[0].astype(jnp.float32)
    picks, gates = [], []
    for block in range(blocks):
        rows = slice(block * tokens, (block + 1) * tokens)
        slots = slice(block * capacity, (block + 1) * capacity)
        pick, gate = selection(meta_ref[block], expert, capacity)
        picks.append(pick)
        gates.append(gate)
        xs_ref[slots] = dot(pick, x_ref[rows]).astype(jnp.bfloat16)
        cs_ref[slots] = (dot(pick, c_ref[rows]) * gate).astype(jnp.bfloat16)
    gate_part = dot(xs_ref[...], wg_ref[0])
    up_part = dot(xs_ref[...], wu_ref[0])
    inner_grad = dot_with(cs_ref[...], wd_ref[0], COLS_BY_COLS)
    gate_sig = jax.nn.sigmoid(gate_part)
    activated = gate_part * gate_sig
    inner = (activated * up_part).astype(jnp.bfloat16)
    inner_ref[...] = inner
    gate_grad = (inner_grad * up_part * gate_sig * (1.0 + gate_part * (1.0 - gate_sig))).astype(
        jnp.bfloat16
    )
    up_grad = (inner_grad * activated).astype(jnp.bfloat16)
    gg_ref[...] = gate_grad
    ug_ref[...] = up_grad
    slot_grad = dot_with(gate_grad, wg_ref[0], COLS_BY_COLS)
    slot_grad = (slot_grad + dot_with(up_grad, wu_ref[0], COLS_BY_COLS)).astype(jnp.bfloat16)
    for block in range(blocks):
        rows = slice(block * tokens, (block + 1) * tokens)
        slots = slice(block * capacity, (block + 1) * capacity)
        mid_ref[rows] = dot_with(picks[block], slot_grad[slots], ROWS_BY_ROWS).astype(
            jnp.bfloat16
        )
    result = dot(inner, wd_ref[0]).astype(jnp.bfloat16).astype(jnp.float32)
    for block in range(blocks):
        rows = slice(block * tokens, (block + 1) * tokens)
        slots = slice(block * capacity, (block + 1) * capacity)
        scaled = (result[slots] * gates[block]).astype(jnp.bfloat16)
        out_ref[rows] = dot_with(picks[block], scaled, ROWS_BY_ROWS).astype(jnp.bfloat16)


def expert_pass(expert, meta, x_all, c_all, gate_w, up_w, down_w, capacity):
    blocks, lines, tokens = meta.shape
    width, hidden = gate_w.shape[1:]
    per = max(1, 512 // tokens)
    total = blocks * capacity
    slots = per * capacity
    shapes = [(blocks * tokens, width)] * 2 + [(total, width)] * 2 + [(total, hidden)] * 3
    return pl.pallas_call(
        expert_kernel,
        grid_spec=pltpu.PrefetchScalarGridSpec(
            num_scalar_prefetch=1,
            grid=(blocks // per,),
            in_specs=[
                rows_of((per, lines, tokens)),
                rows_of((per * tokens, width)),
                rows_of((per * tokens, width)),
                whole(gate_w.shape),
                whole(up_w.shape),
                whole(down_w.shape),
            ],
            out_specs=[rows_of((per * tokens, width))] * 2
            + [rows_of((slots, width))] * 2
            + [rows_of((slots, hidden))] * 3,
        ),
        out_shape=[jax.ShapeDtypeStruct(shape, jnp.bfloat16) for shape in shapes],
        compiler_params=params(56),
        cost_estimate=cost(10 * total * width * hidden, 150 * MIB, total * hidden),
        name="expert_pass",
    )(expert, meta, x_all, c_all, gate_w, up_w, down_w)


def head_back_kernel(raw_ref, grad_ref, gain_ref, cos_ref, sin_ref, out_ref, gain_grad_ref):
    @pl.when(pl.program_id(0) == 0)
    def _():
        gain_grad_ref[...] = jnp.zeros_like(gain_grad_ref)

    cosine, sine, gain = cos_ref[...], sin_ref[...], gain_ref[...]
    for head in range(raw_ref.shape[1] // HEAD):
        part = slice(head * HEAD, (head + 1) * HEAD)
        raw = raw_ref[:, part]
        grad = grad_ref[:, part].astype(jnp.float32)
        back = grad * cosine - pltpu.roll(grad, HEAD // 2, 1) * sine
        inverse = inverse_root(raw)
        hat = raw * inverse
        gain_grad_ref[...] += jnp.sum(back * hat, axis=0, keepdims=True)
        scaled = back * gain
        out_ref[:, part] = (
            inverse * (scaled - hat * jnp.mean(scaled * hat, axis=-1, keepdims=True))
        ).astype(jnp.bfloat16)


def head_back(raw, grad, gain, cosine, sine):
    rows, cols = raw.shape
    tile = min(ROW_TILE, rows)
    return pl.pallas_call(
        head_back_kernel,
        grid=(rows // tile,),
        in_specs=[
            rows_of((tile, cols)),
            rows_of((tile, cols)),
            whole((1, HEAD)),
            rows_of((tile, HEAD)),
            rows_of((tile, HEAD)),
        ],
        out_specs=[rows_of((tile, cols)), whole((1, HEAD))],
        out_shape=[
            jax.ShapeDtypeStruct((rows, cols), jnp.bfloat16),
            jax.ShapeDtypeStruct((1, HEAD), jnp.float32),
        ],
        compiler_params=params(24),
        cost_estimate=cost(rows * cols * 20, rows * cols * 10),
        name="head_back",
    )(raw, grad, gain[None], cosine, sine)


MESH_ID = pl.DeviceIdType.MESH


class Place:
    def __init__(self, send_sem, tp_size=4, nearest=False):
        self.tp_size, self.send_sem, self.sent = tp_size, send_sem, []
        self.nearest = nearest
        self.ep, self.tp = lax.axis_index("ep"), lax.axis_index("tp")
        self.z, self.y, self.x, self.core = self.ep // 2, self.ep % 2, self.tp // 2, self.tp % 2
        self.edge = 1 - (self.z + self.z // 2) % 2
        self.over_x = self.tp + 2 - 4 * self.x
        self.over_core = self.tp + 1 - 2 * self.core
        self.over_both = self.over_core + 2 - 4 * self.x

    def level(self, step):
        levels = [self.z, self.z + 1 - 2 * (self.z % 2), (self.z + 2) % 4, 3 - self.z]
        if self.nearest and step > 1:
            return self.edge * levels[step] + (1 - self.edge) * levels[5 - step]
        return levels[step]

    def across(self, step, over_y):
        return self.level(step) * 2 + self.y + over_y * (1 - 2 * self.y)

    def device(self, step, first, second, other=0):
        core = self.core + other * (1 - 2 * self.core)
        over_y = first * (1 - core) + second * core
        over_x = first * core + second * (1 - core)
        x = self.x + over_x * (1 - 2 * self.x)
        return self.across(step, over_y), x * 2 + core

    def slot(self, *where):
        ep, tp = self.device(*where)
        return ep * self.tp_size + tp

    def greet(self, partners):
        barrier = pltpu.get_barrier_semaphore()
        for partner in partners:
            pl.semaphore_signal(barrier, inc=1, device_id=partner, device_id_type=MESH_ID)
        pl.semaphore_wait(barrier, len(partners))

    def greet_all_ways(self):
        partners = [(1, 0, 0), (2, 0, 0), (3, 0, 0), (0, 1, 0), (0, 0, 1), (0, 0, 0, 1)]
        self.greet([self.device(*partner) for partner in partners])

    def send(self, src, dst, sem, device):
        copy = pltpu.make_async_remote_copy(
            src_ref=src,
            dst_ref=dst,
            send_sem=self.send_sem.at[len(self.sent)],
            recv_sem=sem,
            device_id=device,
            device_id_type=MESH_ID,
        )
        copy.start()
        self.sent.append(copy)

    def arrive(self, dst, sem):
        pltpu.make_async_remote_copy(
            src_ref=dst,
            dst_ref=dst,
            send_sem=self.send_sem.at[0],
            recv_sem=sem,
            device_id=(self.ep, self.over_core),
            device_id_type=MESH_ID,
        ).wait_recv()

    def finish(self):
        for copy in self.sent:
            copy.wait_send()


def reach(kernel, out, scratch, ident, *operands, vmem_out=False, mib=None):
    dma = [kind if not isinstance(kind, tuple) else pltpu.SemaphoreType.DMA(kind) for kind in scratch]
    spaces = vmem_out if isinstance(vmem_out, tuple) else jax.tree.map(lambda _: vmem_out, out)
    out_specs = jax.tree.map(
        lambda vmem: pl.BlockSpec(memory_space=pltpu.VMEM if vmem else pl.ANY), spaces
    )
    return pl.pallas_call(
        kernel,
        in_specs=[pl.BlockSpec(memory_space=pl.ANY)] * len(operands),
        out_specs=out_specs,
        out_shape=out,
        scratch_shapes=dma,
        compiler_params=pltpu.CompilerParams(
            collective_id=ident,
            has_side_effects=True,
            vmem_limit_bytes=(mib or 16) * MIB,
        ),
        cost_estimate=cost(1, 1),
        name=kernel.__name__ if not isinstance(kernel, functools.partial) else kernel.func.__name__,
    )(*operands)


NEAR = ((0, 0), (1, 0), (0, 1), (2, 0), (1, 1), (3, 0), (2, 1), (3, 1))
ORDER = ((0,0,0),(1,0,0),(0,0,1),(0,1,0),(2,0,0),(1,0,1),(1,1,0),(0,1,1),(3,0,0),(2,1,0),(2,0,1),(1,1,1),(3,1,0),(3,0,1),(2,1,1),(3,1,1))


def expert_all_kernel(
    x_ref, m_ref, c_ref, wg_ref, wu_ref, wd_ref,
    all_ref, mid_ref, out_ref, xs_ref, cs_ref, inner_ref, gg_ref, ug_ref,
    lines, wg, wu, wd, pair, xb, cb, midb, outb, xsb, csb, innerb, ggb, ugb,
    w_sem, own_sem, z_sem, z_line_sem, send_sem, line_send_sem, recv_sem, line_sem,
    load_sem, store_sem,
):
    place = Place(send_sem, nearest=True)
    rows = x_ref.shape[0]
    capacity = xsb.shape[1] // 2
    expert = (place.ep * 4 + place.tp).astype(jnp.float32)
    count = len(ORDER)
    slots = {(*where, other): place.slot(*where, other) for where in ORDER for other in (0, 1)}
    first, second, across = place.device(0, 1, 0), place.device(0, 0, 1), place.device(0, 0, 0, 1)

    def part(ref, slot):
        return ref.at[pl.ds(slot * rows, rows)]

    weights = [
        pltpu.make_async_copy(ref, held, w_sem.at[number])
        for number, (ref, held) in enumerate(((wg_ref, wg), (wu_ref, wu), (wd_ref, wd)))
    ]
    mine = slots[0, 0, 0, 0]
    own = [
        pltpu.make_async_copy(x_ref, part(all_ref, mine), own_sem.at[0]),
        pltpu.make_async_copy(m_ref, lines.at[mine], own_sem.at[1]),
    ]
    for copy in own + weights:
        copy.start()
    place.greet_all_ways()
    for copy in own:
        copy.wait()

    def copies(slot, device, rows_sem, words_sem):
        some = dict(device_id=device, device_id_type=MESH_ID)
        return (
            pltpu.make_async_remote_copy(
                src_ref=lines.at[slot], dst_ref=lines.at[slot],
                send_sem=words_sem, recv_sem=line_sem.at[slot], **some,
            ),
            pltpu.make_async_remote_copy(
                src_ref=part(all_ref, slot), dst_ref=part(all_ref, slot),
                send_sem=rows_sem, recv_sem=recv_sem.at[slot], **some,
            ),
        )

    def along_z(step):
        level, z = place.level(step), place.z
        up = (z < 3) if step == 0 else (level < z) & (z < 3)
        down = (z > 0) if step == 0 else (level > z) & (z > 0)
        return ((up, 2 * step, (place.ep + 2, place.tp)), (down, 2 * step + 1, (place.ep - 2, place.tp)))

    def z_copies(slot, number, device):
        return copies(slot, device, z_sem.at[number], z_line_sem.at[number])

    sends = []
    for where in ORDER:
        targets = [across]
        if where[2] == 0:
            targets = [second, *targets]
        if where[1:] == (0, 0):
            targets = [first, *targets]
        sends.append(targets)
    starts = [sum(len(targets) for targets in sends[:number]) for number in range(count)]

    def arrive(slot):
        for copy in copies(slot, across, send_sem.at[0], line_send_sem.at[0]):
            copy.wait_recv()

    def onward_z(step):
        for wanted, index, device in along_z(step):

            @pl.when(wanted)
            def _(index=index, device=device):
                for copy in z_copies(slots[step, 0, 0, 0], index, device):
                    copy.start()

    relays = {1: 2, 3: 3}

    def event(number):
        where = ORDER[number]
        slot = slots[(*where, 0)]
        if where[0] in relays.values() and where[1:] == (0, 0):

            @pl.when(place.edge == 1)
            def _():
                arrive(slot)

        elif number:
            arrive(slot)
        if where in ((0, 0, 0), (1, 0, 0)):
            onward_z(where[0])
        if number in relays:
            step = relays[number]

            @pl.when(place.edge == 0)
            def _():
                arrive(slots[step, 0, 0, 0])
                onward_z(step)

        for index, device in enumerate(sends[number], starts[number]):
            for copy in copies(slot, device, send_sem.at[index], line_send_sem.at[index]):
                copy.start()

    def load_copies(slot, parity, half):
        return (
            pltpu.make_async_copy(part(all_ref, slot), xb.at[parity, half], load_sem.at[parity, half]),
            pltpu.make_async_copy(part(c_ref, slot), cb.at[parity, half], load_sem.at[parity, 2 + half]),
        )

    def load(number):
        where, parity = ORDER[number], number % 2
        arrive(slots[(*where, 1)])
        for half in (0, 1):
            slot = slots[(*where, half)]
            pair[parity, half] = lines[slot]
            for copy in load_copies(slot, parity, half):
                copy.start()

    def store_copies(number, parity, both):
        kept = pl.ds(number * 2 * capacity, 2 * capacity)
        moves = [(held.at[parity], ref.at[kept]) for held, ref in (
            (xsb, xs_ref), (csb, cs_ref), (innerb, inner_ref), (ggb, gg_ref), (ugb, ug_ref),
        )]
        for half in (0, 1):
            moves.append((midb.at[parity, half], part(mid_ref, both[half])))
            slot = both[half]
            moves.append((outb.at[parity, half], out_ref.at[:, slot % 4, slot // 4]))
        return [
            pltpu.make_async_copy(held, ref, store_sem.at[parity, index])
            for index, (held, ref) in enumerate(moves)
        ]

    def compute(parity):
        picks, gates = [], []
        for half in (0, 1):
            pick, gate = selection(pair[parity, half], expert, capacity)
            picks.append(pick)
            gates.append(gate)
            some = slice(half * capacity, (half + 1) * capacity)
            xsb[parity, some] = dot(pick, xb[parity, half]).astype(jnp.bfloat16)
            csb[parity, some] = (dot(pick, cb[parity, half]) * gate).astype(jnp.bfloat16)
        expert_in, slot_cot = xsb[parity], csb[parity]
        gate_part = dot(expert_in, wg[0])
        up_part = dot(expert_in, wu[0])
        inner_grad = dot_with(slot_cot, wd[0], COLS_BY_COLS)
        gate_sig = jax.nn.sigmoid(gate_part)
        activated = gate_part * gate_sig
        inner = (activated * up_part).astype(jnp.bfloat16)
        innerb[parity] = inner
        gate_grad = inner_grad * up_part * gate_sig * (1.0 + gate_part * (1.0 - gate_sig))
        gate_grad = gate_grad.astype(jnp.bfloat16)
        up_grad = (inner_grad * activated).astype(jnp.bfloat16)
        ggb[parity] = gate_grad
        ugb[parity] = up_grad
        slot_grad = dot_with(gate_grad, wg[0], COLS_BY_COLS)
        slot_grad = (slot_grad + dot_with(up_grad, wu[0], COLS_BY_COLS)).astype(jnp.bfloat16)
        result = dot(inner, wd[0]).astype(jnp.bfloat16).astype(jnp.float32)
        for half in (0, 1):
            some = slice(half * capacity, (half + 1) * capacity)
            midb[parity, half] = dot_with(picks[half], slot_grad[some], ROWS_BY_ROWS).astype(
                jnp.bfloat16
            )
            scaled = (result[some] * gates[half]).astype(jnp.bfloat16)
            mixed = dot_with(picks[half], scaled, ROWS_BY_ROWS).astype(jnp.bfloat16)
            outb[parity, half] = mixed.reshape(outb.shape[2:])

    @pl.loop(0, count + 2)
    def _(turn):
        for number in range(count):

            @pl.when(turn == number)
            def _(number=number):
                event(number)

        for number in range(count):

            @pl.when(turn == number + 1)
            def _(number=number):
                load(number)

        @pl.when(turn == 2)
        def _():
            for copy in weights:
                copy.wait()

        @pl.when(turn >= 2)
        def _():
            parity = turn % 2
            for half in (0, 1):
                for copy in load_copies(0, parity, half):
                    copy.wait()

            @pl.when(turn >= 4)
            def _():
                for copy in store_copies(0, parity, (0, 0)):
                    copy.wait()

            compute(parity)

        for number in range(count):

            @pl.when(turn == number + 2)
            def _(number=number):
                both = [slots[(*ORDER[number], half)] for half in (0, 1)]
                for copy in store_copies(number, number % 2, both):
                    copy.start()

    for parity in (0, 1):
        for copy in store_copies(0, parity, (0, 0)):
            copy.wait()
    for index in range(sum(len(targets) for targets in sends)):
        for copy in copies(0, across, send_sem.at[index], line_send_sem.at[index]):
            copy.wait_send()
    for step in range(4):
        for wanted, index, device in along_z(step):

            @pl.when(wanted)
            def _(index=index, device=device):
                for copy in z_copies(0, index, device):
                    copy.wait_send()


def expert_all(x, lines, c_all, gate_w, up_w, down_w, capacity, ident):
    rows, width = x.shape
    blocks = c_all.shape[0] // rows
    hidden = gate_w.shape[2]
    total = blocks * capacity
    shapes = [c_all.shape] * 3 + [(total, width)] * 2 + [(total, hidden)] * 3
    ep_size = blocks // 4
    shapes[2] = (ep_size, 4, ep_size, rows // ep_size, width)
    out = [jax.ShapeDtypeStruct(shape, jnp.bfloat16) for shape in shapes]

    def buffer(*shape):
        return pltpu.VMEM(shape, jnp.bfloat16)

    scratch = [pltpu.VMEM((blocks, *lines.shape), jnp.float32)]
    scratch += [buffer(*gate_w.shape), buffer(*up_w.shape), buffer(*down_w.shape)]
    scratch += [pltpu.VMEM((2, 2, *lines.shape), jnp.float32)]
    scratch += [buffer(2, 2, rows, width)] * 3 + [buffer(2, 2, ep_size, rows // ep_size, width)]
    scratch += [buffer(2, 2 * capacity, width)] * 2
    scratch += [buffer(2, 2 * capacity, hidden)] * 3
    scratch += [(3,), (2,), (8,), (8,), (28,), (28,), (blocks,), (blocks,), (2, 4), (2, 9)]
    operands = (x, lines, c_all, gate_w, up_w, down_w)
    return reach(expert_all_kernel, out, scratch, ident, *operands, mib=58)[1:]


BUFFERS = 4


def scatter_all_kernel(
    p_ref, out_ref, held, over_second, over_first, over_z, own,
    own_sem, send_sem, core_sem, second_sem, first_sem, z_sem,
):
    place = Place(send_sem)
    rows = out_ref.shape[0]

    def add(total, other):
        @pl.loop(0, rows, step=64)
        def _(row):
            some = pl.ds(row, 64)
            total[some] = total[some] + other[some]

    def part(slot):
        return p_ref.at[pl.ds(slot * rows, rows)]

    order = [(step, first, second) for second in (1, 0) for step in (3, 2, 1, 0) for first in (1, 0)]
    loads = []

    def load(number):
        buffer = number % BUFFERS
        copy = pltpu.make_async_copy(
            part(place.slot(*order[number])), own.at[buffer], own_sem.at[buffer]
        )
        copy.start()
        loads.append(copy)

    for number in range(BUFFERS):
        load(number)
    place.greet_all_ways()
    for step, first, second in order:
        place.send(
            part(place.slot(step, first, second, 1)),
            held.at[step, first, second],
            core_sem.at[step, first, second],
            place.device(0, 0, 0, 1),
        )
    for number, (step, first, second) in enumerate(order):
        mine = held.at[step, first, second]
        place.arrive(mine, core_sem.at[step, first, second])
        loads[number].wait()
        add(mine, own.at[number % BUFFERS])
        if number + BUFFERS < len(order):
            load(number + BUFFERS)
        if second:
            place.send(
                mine, over_second.at[step, first], second_sem.at[step, first], place.device(0, 0, 1)
            )

    def onward(step):
        mine = held.at[step, 0, 0]
        place.arrive(over_first.at[step], first_sem.at[step])
        add(mine, over_first.at[step])
        if step == 2:
            place.arrive(over_z.at[3], z_sem.at[3])
            add(mine, over_z.at[3])
        if step:
            place.send(mine, over_z.at[step], z_sem.at[step], place.device(1 + (step == 2), 0, 0))

    for step in (3, 2, 1, 0):
        mine = held.at[step, 1, 0]
        place.arrive(over_second.at[step, 1], second_sem.at[step, 1])
        add(mine, over_second.at[step, 1])
        place.send(mine, over_first.at[step], first_sem.at[step], place.device(0, 1, 0))
        mine = held.at[step, 0, 0]
        place.arrive(over_second.at[step, 0], second_sem.at[step, 0])
        add(mine, over_second.at[step, 0])
        if step < 3:
            onward(step + 1)
    onward(0)
    for step in (2, 1):
        place.arrive(over_z.at[step], z_sem.at[step])

    @pl.loop(0, rows, step=32)
    def _(row):
        some = pl.ds(row, 32)
        total = held[0, 0, 0, some].astype(jnp.float32)
        for step in (1, 2):
            total = total + over_z[step, some].astype(jnp.float32)
        out_ref[some] = total

    place.finish()


def scatter_all(p, parts, ident):
    rows, width = p.shape[0] // parts, p.shape[1]

    def buffer(*lead):
        return pltpu.VMEM((*lead, rows, width), p.dtype)

    scratch = [buffer(4, 2, 2), buffer(4, 2), buffer(4), buffer(4), buffer(BUFFERS)]
    scratch += [(BUFFERS,), (parts - 1,), (4, 2, 2), (4, 2), (4,), (4,)]
    out = jax.ShapeDtypeStruct((rows, width), jnp.float32)
    return reach(scatter_all_kernel, out, scratch, ident, p, vmem_out=True, mib=56)


def enter_kernel(x_ref, c_ref, group_ref, cot_ref, own_sem, send_sem, x_sem, cot_sem):
    place = Place(send_sem)
    ep, tp = place.ep, place.tp
    others = [place.across(step, over) for step in range(4) for over in (0, 1)]
    own = [
        pltpu.make_async_copy(x_ref.at[ep], group_ref.at[ep, tp], own_sem.at[0]),
        pltpu.make_async_copy(c_ref.at[ep], cot_ref.at[ep], own_sem.at[1]),
    ]
    for copy in own:
        copy.start()
    place.greet(
        [(other, tp) for other in others[1:]] + [(ep, place.over_x), (ep, place.over_core)]
    )
    for other in others[1:]:
        place.send(x_ref.at[other], group_ref.at[ep, tp], x_sem.at[ep, tp], (other, tp))
    for number, other in enumerate(others):
        block = group_ref.at[other, tp]
        if number:
            place.arrive(block, x_sem.at[other, tp])
        source = block if number else x_ref.at[ep]
        place.send(source, block, x_sem.at[other, tp], (ep, place.over_x))
        place.send(source, block, x_sem.at[other, tp], (ep, place.over_core))
    for other in others[1:]:
        place.send(c_ref.at[other], cot_ref.at[ep], cot_sem.at[ep], (other, tp))
    for other in others:
        block = group_ref.at[other, place.over_x]
        place.arrive(block, x_sem.at[other, place.over_x])
        place.send(block, block, x_sem.at[other, place.over_x], (ep, place.over_core))
    for other in others:
        for source in (place.over_core, place.over_both):
            place.arrive(group_ref.at[other, source], x_sem.at[other, source])
    for other in others[1:]:
        place.arrive(cot_ref.at[other], cot_sem.at[other])
    for copy in own:
        copy.wait()
    place.finish()


def enter(x, c, tp_size, ident):
    ep_size, block, width = x.shape
    moves = (ep_size - 1) * 2 + ep_size * 3
    out = [
        jax.ShapeDtypeStruct((ep_size, tp_size, block, width), x.dtype),
        jax.ShapeDtypeStruct((ep_size, block, width), x.dtype),
    ]
    scratch = [(2,), (moves,), (ep_size, tp_size), (ep_size,)]
    return reach(enter_kernel, out, scratch, ident, x, c)


CHUNKS = 4


def gather_group_kernel(x_ref, group_ref, own_sem, send_sem, recv_sem):
    place = Place(send_sem)
    ep, tp = place.ep, place.tp
    some = x_ref.shape[0] // CHUNKS

    def piece(chunk, owner):
        return group_ref.at[pl.ds(chunk * some, some), owner]

    own = pltpu.make_async_copy(x_ref, group_ref.at[:, tp], own_sem)
    own.start()
    place.greet([(ep, place.over_x), (ep, place.over_core)])
    for partner in (place.over_x, place.over_core):
        for chunk in range(CHUNKS):
            place.send(
                x_ref.at[pl.ds(chunk * some, some)],
                piece(chunk, tp),
                recv_sem.at[chunk, tp],
                (ep, partner),
            )
    for chunk in range(CHUNKS):
        block = piece(chunk, place.over_x)
        place.arrive(block, recv_sem.at[chunk, place.over_x])
        place.send(block, block, recv_sem.at[chunk, place.over_x], (ep, place.over_core))
    for chunk in range(CHUNKS):
        for source in (place.over_core, place.over_both):
            place.arrive(piece(chunk, source), recv_sem.at[chunk, source])
    own.wait()
    place.finish()


def gather_group(x, tp_size, ident):
    ep_size, block, width = x.shape
    out = jax.ShapeDtypeStruct((ep_size, tp_size, block, width), x.dtype)
    scratch = [pltpu.SemaphoreType.DMA, (CHUNKS * 3,), (CHUNKS, tp_size)]
    return reach(gather_group_kernel, out, scratch, ident, x)


def scatter_group_kernel(
    p_ref, out_ref, own, held, over_x, own_sem, send_sem, core_sem, x_sem
):
    place = Place(send_sem)
    ep, tp = place.ep, place.tp
    some = p_ref.shape[0] // CHUNKS
    block, width = p_ref.shape[2:]

    def chunk_of(chunk):
        return pl.ds(chunk * some, some)

    loads = [
        pltpu.make_async_copy(p_ref.at[:, owner], own.at[number], own_sem.at[number])
        for number, owner in enumerate((place.over_x, tp))
    ]
    for copy in loads:
        copy.start()
    place.greet([(ep, place.over_x), (ep, place.over_core)])
    for number, owner in enumerate((place.over_both, place.over_core)):
        for chunk in range(CHUNKS):
            place.send(
                p_ref.at[chunk_of(chunk), owner],
                held.at[number, chunk_of(chunk)],
                core_sem.at[number, chunk],
                (ep, place.over_core),
            )

    def add(number, chunk):
        place.arrive(held.at[number, chunk_of(chunk)], core_sem.at[number, chunk])
        for row in range(chunk * some, (chunk + 1) * some):
            held[number, row] = held[number, row] + own[number, row]

    loads[0].wait()
    for chunk in range(CHUNKS):
        add(0, chunk)
        place.send(
            held.at[0, chunk_of(chunk)],
            over_x.at[chunk_of(chunk)],
            x_sem.at[chunk],
            (ep, place.over_x),
        )
    loads[1].wait()
    for chunk in range(CHUNKS):
        add(1, chunk)
    for chunk in range(CHUNKS):
        place.arrive(over_x.at[chunk_of(chunk)], x_sem.at[chunk])
        for row in range(chunk * some, (chunk + 1) * some):
            out_ref[row] = held[1, row].astype(jnp.float32) + over_x[row].astype(jnp.float32)
    place.finish()


def scatter_group(p, ident):
    ep_size, tp_size, block, width = p.shape

    def buffer(*lead):
        return pltpu.VMEM((*lead, ep_size, block, width), p.dtype)

    scratch = [buffer(2), buffer(2), buffer(), (2,), (CHUNKS * 3,), (2, CHUNKS), (CHUNKS,)]
    out = jax.ShapeDtypeStruct((ep_size, block, width), jnp.float32)
    return reach(scatter_group_kernel, out, scratch, ident, p, vmem_out=True, mib=24)


def gather_kv_kernel(kv_ref, out_ref, own_sem, send_sem, recv_sem):
    place = Place(send_sem)
    ep, tp = place.ep, place.tp
    own = pltpu.make_async_copy(kv_ref, out_ref.at[:, ep], own_sem)
    own.start()
    partners = [place.across(*where) for where in ((1, 0), (2, 0), (3, 0), (0, 1))]
    place.greet([(partner, tp) for partner in partners])
    for partner in (partners[3], *partners[:3]):
        place.send(kv_ref, out_ref.at[:, ep], recv_sem.at[ep], (partner, tp))
    for partner in partners[:3]:
        block = out_ref.at[:, partner]
        place.arrive(block, recv_sem.at[partner])
        place.send(block, block, recv_sem.at[partner], (partners[3], tp))
    for step in range(4):
        other = place.across(step, 1)
        place.arrive(out_ref.at[:, other], recv_sem.at[other])
    own.wait()
    place.finish()


def gather_kv(kv, ep_size, ident):
    blocks, rows, width = kv.shape
    out = jax.ShapeDtypeStruct((blocks, ep_size, rows, width), kv.dtype)
    scratch = [pltpu.SemaphoreType.DMA, (ep_size - 1,), (ep_size,)]
    return reach(gather_kv_kernel, out, scratch, ident, kv)


def scatter_kv_kernel(p_ref, out_ref, own, over_y, over_z, own_sem, send_sem, y_sem, z_sem):
    place = Place(send_sem)
    tp = place.tp
    blocks = out_ref.shape[0]
    order = (3, 2, 1, 0)
    loads = {}
    for step in order:
        loads[step] = pltpu.make_async_copy(
            p_ref.at[:, place.across(step, 0)], own.at[step], own_sem.at[step]
        )
        loads[step].start()
    place.greet([(place.across(*where), tp) for where in ((1, 0), (2, 0), (3, 0), (0, 1))])
    for step in order:
        place.send(
            p_ref.at[:, place.across(step, 1)],
            over_y.at[step],
            y_sem.at[step],
            (place.across(0, 1), tp),
        )
    for step in order:
        loads[step].wait()
        place.arrive(over_y.at[step], y_sem.at[step])

        @pl.loop(0, blocks)
        def _(block, step=step):
            own[step, block] = own[step, block] + over_y[step, block]

        if step == 2:
            place.arrive(over_z.at[3], z_sem.at[3])

            @pl.loop(0, blocks)
            def _(block):
                own[2, block] = own[2, block] + over_z[3, block]

        if step:
            device = (place.across(1 + (step == 2), 0), tp)
            place.send(own.at[step], over_z.at[step], z_sem.at[step], device)
    for step in (2, 1):
        place.arrive(over_z.at[step], z_sem.at[step])

    @pl.loop(0, blocks)
    def _(block):
        total = own[0, block].astype(jnp.float32)
        for step in (1, 2):
            total = total + over_z[step, block].astype(jnp.float32)
        out_ref[block] = total.astype(jnp.bfloat16)

    place.finish()


def scatter_kv(p, ident):
    blocks, ep_size, rows, width = p.shape
    buffer = pltpu.VMEM((4, blocks, rows, width), p.dtype)
    scratch = [buffer, buffer, buffer, (4,), (7,), (4,), (4,)]
    out = jax.ShapeDtypeStruct((blocks, rows, width), p.dtype)
    return reach(scatter_kv_kernel, out, scratch, ident, p, vmem_out=True, mib=24)


SLOTS = 1024


def finish_kernel(*refs):
    partials, gains_ref, rows_ref, experts = refs[:3], refs[3], refs[4], refs[5:10]
    outs, gain_out, rows_out, grads, refs = refs[10:13], refs[13], refs[14], refs[15:18], refs[18:]
    owns, overs_y, overs_z, stages, refs = refs[:3], refs[3:6], refs[6:9], refs[9:11], refs[11:]
    wide, narrow, sums, refs = refs[0], refs[1], refs[2:5], refs[5:]
    own_sem, send_sem, y_sem, z_sem, gain_sem, load_sem, grad_sem, rows_sem, rows_send_sem = refs
    place = Place(send_sem)
    ep, tp = place.ep, place.tp
    count = len(partials)
    total, arrived = stages
    ways = [(ep, place.over_core), (ep, place.over_x)]
    ways += [(place.across(step, 0), tp) for step in (1, 2, 3)]
    ways.append((place.across(0, 1), tp))
    moves = [(number, step) for step in (3, 2, 1, 0) for number in range(count)]
    gain_load = pltpu.make_async_copy(gains_ref, total.at[0], own_sem.at[count, 0])
    gain_load.start()

    def own_copy(number, step):
        return pltpu.make_async_copy(
            partials[number].at[place.across(step, 0)],
            owns[number].at[step],
            own_sem.at[number, step],
        )

    def to_y(number, step):
        return pltpu.make_async_remote_copy(
            src_ref=partials[number].at[place.across(step, 1)],
            dst_ref=overs_y[number].at[step],
            send_sem=send_sem.at[number, step],
            recv_sem=y_sem.at[number, step],
            device_id=(place.across(0, 1), tp),
            device_id_type=MESH_ID,
        )

    def to_z(number, step):
        return pltpu.make_async_remote_copy(
            src_ref=owns[number].at[step],
            dst_ref=overs_z[number].at[step],
            send_sem=send_sem.at[number, 3 + step],
            recv_sem=z_sem.at[number, step],
            device_id=(place.across(1 + (step == 2), 0), tp),
            device_id_type=MESH_ID,
        )

    def gain_copy(number):
        return pltpu.make_async_remote_copy(
            src_ref=total.at[(0, 1, 2, 2, 2, 3)[number]],
            dst_ref=arrived.at[number],
            send_sem=send_sem.at[count, number],
            recv_sem=gain_sem.at[number],
            device_id=ways[number],
            device_id_type=MESH_ID,
        )

    others = [(step, over) for step in range(4) for over in (0, 1)][1:]

    def row_copy(index):
        other = place.across(*others[index])
        return pltpu.make_async_remote_copy(
            src_ref=rows_ref.at[other],
            dst_ref=rows_out.at[ep],
            send_sem=rows_send_sem.at[index],
            recv_sem=rows_sem.at[ep],
            device_id=(other, tp),
            device_id_type=MESH_ID,
        )

    def row_arrival(index):
        other = place.across(*others[index])
        return pltpu.make_async_remote_copy(
            src_ref=rows_ref.at[other],
            dst_ref=rows_out.at[other],
            send_sem=rows_send_sem.at[index],
            recv_sem=rows_sem.at[other],
            device_id=(other, tp),
            device_id_type=MESH_ID,
        )

    own_rows = pltpu.make_async_copy(rows_ref.at[ep], rows_out.at[ep], rows_sem.at[ep])
    own_rows.start()
    for number, step in moves:
        own_copy(number, step).start()
    place.greet(ways[:2] + [(place.across(*other), tp) for other in others])
    gain_load.wait()
    gain_copy(0).start()
    for index in range(len(others)):
        row_copy(index).start()
    for number, step in moves:
        to_y(number, step).start()

    def event(index):
        number, step = moves[index]
        own, over = owns[number], overs_y[number]
        own_copy(number, step).wait()
        to_y(number, step).wait_recv()

        @pl.loop(0, own.shape[1], step=64)
        def _(row):
            some = pl.ds(row, 64)
            own[step, some] = own[step, some] + over[step, some]

        if step == 2:
            to_z(number, 3).wait_recv()

            @pl.loop(0, own.shape[1], step=64)
            def _(row):
                some = pl.ds(row, 64)
                own[2, some] = own[2, some] + overs_z[number][3, some]

        if step:
            to_z(number, step).start()
        if index < 2:
            gain_copy(index).wait_recv()
            total[index + 1] = total[index] + arrived[index]
            for later in (1,) if index == 0 else (2, 3, 4):
                gain_copy(later).start()
        if index == 2:
            for later in (2, 3, 4):
                gain_copy(later).wait_recv()
            total[3] = (total[2] + arrived[2]) + (arrived[3] + arrived[4])
            gain_copy(5).start()

    expert_in, slot_cot, inner, gate_grad, up_grad = experts
    pieces = expert_in.shape[0] // SLOTS
    jobs = ((expert_in, gate_grad), (expert_in, up_grad), (slot_cot, inner))
    steps = pieces * len(jobs)

    def load_copies(pair, piece, parity):
        some = pl.ds(piece * SLOTS, SLOTS)
        return [
            pltpu.make_async_copy(ref.at[some], held.at[parity], load_sem.at[parity, index])
            for index, (ref, held) in enumerate(zip(pair, (wide, narrow)))
        ]

    def grad_copy(job):
        return pltpu.make_async_copy(sums[job], grads[job], grad_sem.at[job])

    def multiply(job, parity):
        into = sums[job]
        left, right = (wide, narrow) if job < 2 else (narrow, wide)
        tile = 512 if into.shape[0] % 512 == 0 else 384

        @pl.loop(0, into.shape[0], step=tile)
        def _(row):
            some = pl.ds(pl.multiple_of(row, tile), tile)
            product = dot_with(left[parity, :, some], right[parity], ROWS_BY_ROWS)

            into[some] += product

    for into in sums:

        @pl.loop(0, into.shape[0], step=64)
        def _(row, into=into):
            into[pl.ds(row, 64)] = jnp.zeros((64, into.shape[1]), jnp.float32)

    @pl.loop(0, steps + 1)
    def _(turn):
        for index in range(len(moves)):

            @pl.when(turn == index)
            def _(index=index):
                event(index)

        for job, pair in enumerate(jobs):

            @pl.when((turn >= job * pieces) & (turn < (job + 1) * pieces))
            def _(job=job, pair=pair):
                for copy in load_copies(pair, turn - job * pieces, turn % 2):
                    copy.start()

        for job, pair in enumerate(jobs):

            @pl.when((turn > job * pieces) & (turn <= (job + 1) * pieces))
            def _(job=job, pair=pair):
                parity = (turn - 1) % 2
                for copy in load_copies(pair, 0, parity):
                    copy.wait()
                multiply(job, parity)

            @pl.when(turn == (job + 1) * pieces)
            def _(job=job):
                grad_copy(job).start()

    for number in range(count):
        own, over, out = owns[number], overs_z[number], outs[number]
        for step in (2, 1):
            to_z(number, step).wait_recv()

        @pl.loop(0, own.shape[1], step=64)
        def _(row, own=own, over=over, out=out):
            some = pl.ds(row, 64)
            sum_of = own[0, some].astype(jnp.float32)
            for step in (1, 2):
                sum_of = sum_of + over[step, some].astype(jnp.float32)
            out[some] = sum_of

    gain_copy(5).wait_recv()
    gain_out[...] = total[3] + arrived[5]
    for job in range(len(jobs)):
        grad_copy(job).wait()
    for number, step in moves:
        to_y(number, step).wait_send()
        if step:
            to_z(number, step).wait_send()
    for number in range(6):
        gain_copy(number).wait_send()
    own_rows.wait()
    for index in range(len(others)):
        row_copy(index).wait_send()
        row_arrival(index).wait_recv()


def finish(partials, gains, rows, expert_in, slot_cot, inner, gate_grad, up_grad, ident):
    count = len(partials)
    buffers = [pltpu.VMEM((4, *p.shape[1:]), p.dtype) for p in partials]
    width, hidden = expert_in.shape[1], inner.shape[1]
    grads = [(width, hidden), (width, hidden), (hidden, width)]
    scratch = buffers * 3
    scratch += [pltpu.VMEM((4, *gains.shape), gains.dtype), pltpu.VMEM((6, *gains.shape), gains.dtype)]
    scratch += [pltpu.VMEM((2, SLOTS, width), jnp.bfloat16), pltpu.VMEM((2, SLOTS, hidden), jnp.bfloat16)]
    scratch += [pltpu.VMEM(shape, jnp.float32) for shape in grads]
    scratch += [(count + 1, 4), (count + 1, 7), (count, 4), (count, 4), (6,), (2, 2), (3,), (8,), (7,)]
    out = [jax.ShapeDtypeStruct(p.shape[1:], jnp.float32) for p in partials]
    out.append(jax.ShapeDtypeStruct(gains.shape, jnp.float32))
    out.append(jax.ShapeDtypeStruct(rows.shape, rows.dtype))
    out += [jax.ShapeDtypeStruct(shape, jnp.float32) for shape in grads]
    operands = (*partials, gains, rows, expert_in, slot_cot, inner, gate_grad, up_grad)
    return reach(
        finish_kernel, out, scratch, ident, *operands, vmem_out=(True,) * 4 + (False,) * 4, mib=58
    )


def on_device(
    inputs,
    cotangent,
    arrangement,
    seq_lengths,
    routes,
    gate_values,
    input_gain,
    query_proj,
    key_projected,
    value_projected,
    query_gain,
    key_gain,
    output_proj,
    expert_gain,
    gate_weight,
    up_weight,
    down_weight,
):
    ep_size = lax.axis_size("ep")
    tp_size = lax.axis_size("tp")
    ep_index = lax.axis_index("ep")
    tp_index = lax.axis_index("tp")
    everyone = ("ep", "tp")
    own_rows, width = inputs.shape
    group_rows = own_rows * tp_size
    row_block = own_rows // ep_size
    token_total = arrangement.shape[0]
    expert_count = ep_size * tp_size
    capacity = 2 * own_rows * TOP // expert_count
    heads = query_proj.shape[1] // HEAD
    known = (ep_size, tp_size) == (8, 4)
    expert = (ep_index * tp_size + tp_index).astype(jnp.int32)[None]

    table = arrangement.reshape(ep_size, tp_size, ep_size, row_block)
    leaving_from = lax.dynamic_index_in_dim(table, tp_index, 1, keepdims=False)
    leaving_from = lax.dynamic_index_in_dim(leaving_from, ep_index, 1, keepdims=False)
    send_index = leaving_from - (ep_index * group_rows + tp_index * own_rows)
    mover = (
        send_index.reshape(-1)[:, None] == jnp.arange(own_rows, dtype=jnp.int32)[None, :]
    ).astype(jnp.bfloat16)

    def to_places(rows):
        return dot(mover, rows).astype(jnp.bfloat16).reshape(ep_size, row_block, width)

    def exchange(rows):
        return lax.all_to_all(rows, "ep", split_axis=0, concat_axis=0, tiled=True)

    def to_given(moved):
        return dot_with(mover, moved, ROWS_BY_ROWS)

    def group_sorted(rows, ident):
        blocks = rows.reshape(ep_size, row_block, width)
        if known:
            gathered = gather_group(blocks, tp_size, ident)
        else:
            gathered = lax.all_gather(blocks, "tp", axis=1)
        return gathered.reshape(group_rows, width)

    def sum_group(rows, ident):
        blocks = rows.astype(jnp.bfloat16).reshape(ep_size, tp_size, row_block, width)
        if known:
            return scatter_group(blocks, ident).reshape(own_rows, width)
        placed = jnp.swapaxes(blocks, 0, 1).reshape(group_rows, width)
        own = lax.psum_scatter(placed, "tp", scatter_dimension=0, tiled=True)
        return own.astype(jnp.float32)

    leaving_x, leaving_cot = to_places(inputs), to_places(cotangent)
    if known:
        group_x, own_cot = enter(leaving_x, leaving_cot, tp_size, 1)
        own_inputs = lax.dynamic_index_in_dim(group_x, tp_index, 1, keepdims=False)
    else:
        own_inputs, own_cot = exchange(leaving_x), exchange(leaving_cot)
        group_x = lax.all_gather(own_inputs, "tp", axis=1)
    own_inputs, own_cot = own_inputs.reshape(own_rows, width), own_cot.reshape(own_rows, width)
    group_x = group_x.reshape(group_rows, width)
    meta_own = jnp.concatenate([routes.astype(jnp.float32).T, gate_values.T], axis=0)
    cot_all = lax.all_gather(own_cot, everyone, axis=0, tiled=True)

    query_given = lax.dynamic_index_in_dim(table, ep_index, 0, keepdims=False)
    query_given = jnp.swapaxes(query_given, 0, 1).reshape(group_rows)
    query_first = seq_starts(query_given, seq_lengths)
    cosine, sine = rope_tables(query_given - query_first, HEAD)
    key_given = jnp.transpose(table, (2, 1, 0, 3)).reshape(token_total)
    by_step = (-1, QUERY_TOKENS)
    given_steps, first_steps = query_given.reshape(by_step), query_first.reshape(by_step)
    lowest = jnp.min(first_steps, axis=1) // KEY_SPAN
    highest = jnp.max(given_steps, axis=1) // KEY_SPAN + 1
    open_low = (jnp.max(first_steps, axis=1) + KEY_SPAN - 1) // KEY_SPAN
    open_low = jnp.minimum(open_low, highest)
    open_high = jnp.clip((jnp.min(given_steps, axis=1) + 1) // KEY_SPAN, open_low, highest)
    bounds = jnp.stack([lowest, open_low, open_high, highest]).astype(jnp.int32)
    ask = jnp.stack([query_given, query_first], axis=1)
    ask_rows = jnp.stack(
        [jnp.tile(given_steps, (1, heads)), jnp.tile(first_steps, (1, heads))], axis=1
    )

    normed_in, query_raw, query_rows, key_raw, kv_rows = front(
        group_x, input_gain, query_proj, key_projected, value_projected,
        query_gain, key_gain, cosine, sine,
    )
    kv_blocks = kv_rows.reshape(expert_count, row_block, 2 * HEAD)
    if known:
        kv_all = gather_kv(kv_blocks, ep_size, 2)
    else:
        kv_all = lax.all_gather(kv_blocks, "ep", axis=1)
    kv_all = kv_all.reshape(token_total, 2 * HEAD)
    pairs = group_rows * heads * 1536
    exact, out_rows, lse = attend_forward(
        bounds, query_rows, ask, key_given[None], kv_all, pairs
    )
    branch = sum_group(dot(out_rows, output_proj), 5)
    hidden = own_inputs.astype(jnp.float32) + branch
    mid_scale = inverse_root(hidden)
    normed_mid = (hidden * mid_scale * expert_gain).astype(jnp.bfloat16)

    experts = (gate_weight, up_weight, down_weight, capacity)
    if known:
        results = expert_all(normed_mid, meta_own, cot_all, *experts, 3)
    else:
        mid_all = lax.all_gather(normed_mid, everyone, axis=0, tiled=True)
        meta = lax.all_gather(meta_own, everyone, axis=0)
        results = list(expert_pass(expert, meta, mid_all, cot_all, *experts))
        results[1] = jnp.transpose(
            results[1].reshape(ep_size, tp_size, ep_size, row_block, width), (2, 1, 0, 3, 4)
        )
    mid_partial, out_partial, expert_in, slot_cot, inner, gate_grad, up_grad = results
    def sum_over_all(partial):
        return lax.psum_scatter(partial, everyone, scatter_dimension=0, tiled=True)

    if known:
        mid_grad = scatter_all(mid_partial, expert_count, 4)
    else:
        mid_grad = sum_over_all(mid_partial).astype(jnp.float32)
    mid_grad, out_partial = lax.optimization_barrier((mid_grad, out_partial))
    mixed = sum_over_all(out_partial.reshape(token_total, width))

    mid_hat = hidden * mid_scale
    grad_expert_gain = jnp.sum(mid_grad * mid_hat, axis=0)
    mid_scaled = mid_grad * expert_gain
    hidden_grad = own_cot.astype(jnp.float32) + mid_scale * (
        mid_scaled - mid_hat * jnp.mean(mid_scaled * mid_hat, axis=-1, keepdims=True)
    )
    branch_grad = group_sorted(hidden_grad.astype(jnp.bfloat16), 6)
    out_grad = dot_with(branch_grad, output_proj, COLS_BY_COLS).astype(jnp.bfloat16)
    query_grad, kv_grad = attend_backward(
        bounds, query_rows, out_grad, exact, lse, ask_rows, key_given[None], kv_all, pairs
    )
    kv_grad = kv_grad.reshape(expert_count, ep_size, row_block, 2 * HEAD)
    if known:
        kv_own = scatter_kv(kv_grad, 7)
    else:
        kv_own = lax.psum_scatter(kv_grad, "ep", scatter_dimension=1)
    kv_own = kv_own.reshape(group_rows, 2 * HEAD)
    value_grad = kv_own[:, HEAD:]
    raw_query_grad, grad_query_gain = head_back(query_raw, query_grad, query_gain, cosine, sine)
    raw_key_grad, grad_key_gain = head_back(key_raw, kv_own[:, :HEAD], key_gain, cosine, sine)
    normed_grad = (
        dot_with(raw_query_grad, query_proj, COLS_BY_COLS)
        + dot_with(raw_key_grad, key_projected, COLS_BY_COLS)
        + dot_with(value_grad, value_projected, COLS_BY_COLS)
    )
    normed_grad = sum_group(normed_grad, 8)
    own_float = own_inputs.astype(jnp.float32)
    in_scale = inverse_root(own_float)
    in_hat = own_float * in_scale
    grad_input_gain = jnp.sum(normed_grad * in_hat, axis=0)
    in_scaled = normed_grad * input_gain
    input_rows = hidden_grad + in_scale * (
        in_scaled - in_hat * jnp.mean(in_scaled * in_hat, axis=-1, keepdims=True)
    )
    leaving = jnp.concatenate([input_rows, hidden], axis=1).astype(jnp.bfloat16)
    leaving = leaving.reshape(ep_size, row_block, 2 * width)

    weights = [
        dot_with(branch_grad, out_rows, ROWS_BY_ROWS),
        dot_with(normed_in, raw_query_grad, ROWS_BY_ROWS),
        dot_with(normed_in, jnp.concatenate([raw_key_grad, value_grad], axis=1), ROWS_BY_ROWS),
    ]
    weights = [array.astype(jnp.bfloat16).reshape(ep_size, -1, array.shape[1]) for array in weights]
    gains = jnp.concatenate(
        [grad_input_gain, grad_expert_gain, grad_query_gain[0], grad_key_gain[0]]
    )
    if known:
        experts = (expert_in, slot_cot, inner, gate_grad, up_grad)
        results = finish(weights, gains.reshape(-1, HEAD), leaving, *experts, 10)
        grad_output, grad_query, grad_kv, gains, leaving = results[:5]
        grad_gate, grad_up, grad_down = results[5:]
        gains = gains.reshape(-1)
    else:
        grad_output, grad_query, grad_kv = [
            lax.psum_scatter(array, "ep", scatter_dimension=0).astype(jnp.float32)
            for array in weights
        ]
        gains, leaving = lax.psum(gains, everyone), exchange(leaving)
        grad_gate = dot_with(expert_in, gate_grad, ROWS_BY_ROWS)
        grad_up = dot_with(expert_in, up_grad, ROWS_BY_ROWS)
        grad_down = dot_with(inner, slot_cot, ROWS_BY_ROWS)
    mixed, gains = lax.optimization_barrier((mixed, gains))
    leaving = leaving.reshape(own_rows, 2 * width)
    grad_inputs = to_given(leaving[:, :width])
    layer_out = leaving[:, width:].astype(jnp.float32) + mixed.astype(jnp.float32)
    layer_out = to_given(layer_out.astype(jnp.bfloat16)).astype(jnp.bfloat16)
    grad_output = jnp.transpose(grad_output)
    cuts = (width, 2 * width, 2 * width + HEAD)
    return (
        layer_out,
        grad_inputs,
        grad_query,
        grad_kv[:, :HEAD],
        grad_kv[:, HEAD:],
        grad_output,
        gains[: cuts[0]],
        gains[cuts[1] : cuts[2]],
        gains[cuts[2] :],
        gains[cuts[0] : cuts[1]],
        grad_gate[None],
        grad_up[None],
        grad_down[None],
    )


def solution(mesh):
    split = P(("ep", "tp"), None)
    experts = P(("ep", "tp"), None, None)
    columns = P(None, "tp")
    return jax.shard_map(
        on_device,
        mesh=mesh,
        in_specs=(
            split, split, P(), P(), split, split, P(), columns, columns, columns,
            P(), P(), P("tp", None), P(), experts, experts, experts,
        ),
        out_specs=(
            split, split, P("ep", "tp"), P("ep", "tp"), P("ep", "tp"), P("tp", "ep"),
            P(), P(), P(), P(), experts, experts, experts,
        ),
        check_vma=False,
    )
```

```python
import functools
import math

import jax
import jax.numpy as jnp
from jax import lax
from jax.experimental import pallas as pl
from jax.experimental.pallas import tpu as pltpu
from jax.sharding import PartitionSpec as P

TOP = 8
EPSILON = 1e-06
ROPE_BASE = 1000000.0
KEY_SPAN = 512
QUERY_TOKENS = 64
HEAD = 128
ROW_TILE = 256
MIB = 1 << 20
LOG2E = math.log2(math.e)
ROWS_BY_ROWS = (((0,), (0,)), ((), ()))
COLS_BY_COLS = (((1,), (1,)), ((), ()))


def dot(left, right):
    return jnp.dot(left, right, preferred_element_type=jnp.float32)


def dot_with(left, right, dims):
    return lax.dot_general(left, right, dims, preferred_element_type=jnp.float32)


def cost(flops, moved, transcendentals=0):
    return pl.CostEstimate(
        flops=int(flops), bytes_accessed=int(moved), transcendentals=int(transcendentals)
    )


def params(mib):
    return pltpu.CompilerParams(
        dimension_semantics=("arbitrary",), vmem_limit_bytes=mib * MIB
    )


def whole(shape, single=True):
    rank = len(shape)
    if single:
        return pl.BlockSpec(shape, lambda *ids: (0,) * rank, pipeline_mode=pl.Buffered(1))
    return pl.BlockSpec(shape, lambda *ids: (0,) * rank)


def rows_of(shape):
    rank = len(shape)
    return pl.BlockSpec(shape, lambda i, *ids: (i,) + (0,) * (rank - 1))


def rope_tables(positions, head_dim):
    freqs = ROPE_BASE ** (-jnp.arange(0, head_dim, 2, dtype=jnp.float32) / head_dim)
    angles = positions.astype(jnp.float32)[:, None] * freqs[None, :]
    cosine, sine = jnp.cos(angles), jnp.sin(angles)
    return (
        jnp.concatenate([cosine, cosine], axis=-1),
        jnp.concatenate([-sine, sine], axis=-1),
    )


def seq_starts(given, seq_lengths):
    ends = jnp.cumsum(seq_lengths)
    passed = given[:, None] >= ends[None, :]
    return jnp.sum(jnp.where(passed, seq_lengths[None, :], 0), axis=1)


def inverse_root(values):
    return lax.rsqrt(jnp.mean(values * values, axis=-1, keepdims=True) + EPSILON)


def front_kernel(
    x_ref, gain_ref, wq_ref, wk_ref, wv_ref, qg_ref, kg_ref, cos_ref, sin_ref,
    normed_ref, qraw_ref, q_ref, kraw_ref, kv_ref,
):
    x = x_ref[...].astype(jnp.float32)
    normed = (x * inverse_root(x) * gain_ref[...]).astype(jnp.bfloat16)
    normed_ref[...] = normed
    cosine, sine = cos_ref[...], sin_ref[...]

    def prepare(raw, gain):
        values = raw * inverse_root(raw) * gain
        return (values * cosine + pltpu.roll(values, HEAD // 2, 1) * sine).astype(jnp.bfloat16)

    raw = dot(normed, wq_ref[...])
    qraw_ref[...] = raw
    for head in range(raw.shape[1] // HEAD):
        part = slice(head * HEAD, (head + 1) * HEAD)
        q_ref[:, part] = prepare(raw[:, part], qg_ref[...])
    raw = dot(normed, wk_ref[...])
    kraw_ref[...] = raw
    kv_ref[:, :HEAD] = prepare(raw, kg_ref[...])
    kv_ref[:, HEAD:] = dot(normed, wv_ref[...]).astype(jnp.bfloat16)


def front(group_x, input_gain, wq, wk, wv, query_gain, key_gain, cosine, sine):
    rows, width = group_x.shape
    cols = wq.shape[1]
    tile = min(ROW_TILE, rows)
    out = [
        ((rows, width), jnp.bfloat16),
        ((rows, cols), jnp.float32),
        ((rows, cols), jnp.bfloat16),
        ((rows, HEAD), jnp.float32),
        ((rows, 2 * HEAD), jnp.bfloat16),
    ]
    return pl.pallas_call(
        front_kernel,
        grid=(rows // tile,),
        in_specs=[
            rows_of((tile, width)),
            whole((1, width)),
            whole(wq.shape),
            whole(wk.shape),
            whole(wv.shape),
            whole((1, HEAD)),
            whole((1, HEAD)),
            rows_of((tile, HEAD)),
            rows_of((tile, HEAD)),
        ],
        out_specs=[rows_of((tile, shape[1])) for shape, kind in out],
        out_shape=[jax.ShapeDtypeStruct(shape, kind) for shape, kind in out],
        compiler_params=params(40),
        cost_estimate=cost(2 * rows * width * (cols + 2 * HEAD), 20 * MIB),
        name="front",
    )(
        group_x,
        input_gain[None],
        wq,
        wk,
        wv,
        query_gain[None],
        key_gain[None],
        cosine,
        sine,
    )


def stack_heads(block):
    heads = block.shape[1] // HEAD
    return jnp.concatenate(
        [block[:, head * HEAD : (head + 1) * HEAD] for head in range(heads)], axis=0
    )


def attend_forward_kernel(
    bounds_ref, q_ref, ask_ref, key_given_ref, kv_ref, exact_ref, out_ref, lse_ref, acc, tot
):
    step = pl.program_id(0)
    tokens, cols = q_ref.shape
    heads = cols // HEAD
    query = stack_heads(q_ref[...])
    ask = ask_ref[...]
    last = jnp.concatenate([ask[:, 0:1]] * heads, axis=0)
    first = jnp.concatenate([ask[:, 1:2]] * heads, axis=0)
    acc[...] = jnp.zeros_like(acc)
    tot[...] = jnp.zeros_like(tot)

    def visit(span, masked):
        offset = pl.multiple_of(span * KEY_SPAN, KEY_SPAN)
        keys = kv_ref[pl.ds(offset, KEY_SPAN), :HEAD]
        values = kv_ref[pl.ds(offset, KEY_SPAN), HEAD:]
        scores = dot_with(query, keys, COLS_BY_COLS)
        weights = jnp.exp2(scores * (HEAD**-0.5 * LOG2E))
        if masked:
            key_given = key_given_ref[:, pl.ds(offset, KEY_SPAN)]
            weights = jnp.where((key_given <= last) & (key_given >= first), weights, 0.0)
        part = weights[:, :HEAD]
        for chunk in range(1, KEY_SPAN // HEAD):
            part = part + weights[:, chunk * HEAD : (chunk + 1) * HEAD]
        tot[...] += part
        acc[...] += dot(weights.astype(jnp.bfloat16), values)

    lowest, open_low = bounds_ref[0, step], bounds_ref[1, step]
    open_high, highest = bounds_ref[2, step], bounds_ref[3, step]

    @pl.loop(lowest, open_low)
    def _(span):
        visit(span, True)

    @pl.loop(open_low, open_high)
    def _(span):
        visit(span, False)

    @pl.loop(open_high, highest)
    def _(span):
        visit(span, True)

    total = tot[...]
    exact = acc[...] / jnp.sum(total, axis=1, keepdims=True)
    for head in range(heads):
        rows = exact[head * tokens : (head + 1) * tokens]
        exact_ref[:, head * HEAD : (head + 1) * HEAD] = rows
        out_ref[:, head * HEAD : (head + 1) * HEAD] = rows.astype(jnp.bfloat16)
    lse_ref[0] = jnp.log2(jnp.sum(total.T, axis=0, keepdims=True))


def attend_forward(bounds, query, ask, key_given, kv, pairs):
    rows, cols = query.shape
    heads = cols // HEAD
    steps = rows // QUERY_TOKENS
    stacked = heads * QUERY_TOKENS
    return pl.pallas_call(
        attend_forward_kernel,
        grid_spec=pltpu.PrefetchScalarGridSpec(
            num_scalar_prefetch=1,
            grid=(steps,),
            in_specs=[
                rows_of((QUERY_TOKENS, cols)),
                rows_of((QUERY_TOKENS, 2)),
                whole(key_given.shape),
                whole(kv.shape),
            ],
            out_specs=[
                rows_of((QUERY_TOKENS, cols)),
                rows_of((QUERY_TOKENS, cols)),
                rows_of((1, 1, stacked)),
            ],
            scratch_shapes=[
                pltpu.VMEM((stacked, HEAD), jnp.float32),
                pltpu.VMEM((stacked, HEAD), jnp.float32),
            ],
        ),
        out_shape=[
            jax.ShapeDtypeStruct((rows, cols), jnp.float32),
            jax.ShapeDtypeStruct((rows, cols), jnp.bfloat16),
            jax.ShapeDtypeStruct((steps, 1, stacked), jnp.float32),
        ],
        compiler_params=params(48),
        cost_estimate=cost(8 * pairs * HEAD, 16 * MIB, pairs),
        name="attend_forward",
    )(bounds, query, ask, key_given, kv)


def attend_backward_kernel(
    bounds_ref, q_ref, grad_ref, exact_ref, lse_ref, ask_ref, key_given_ref, kv_ref,
    dq_ref, rounded_ref, dkv_ref, acc,
):
    step = pl.program_id(0)
    tokens, cols = q_ref.shape
    heads = cols // HEAD

    @pl.when(step == 0)
    def _():
        dkv_ref[...] = jnp.zeros_like(dkv_ref)

    query = stack_heads(q_ref[...])
    grad = stack_heads(grad_ref[...])
    product = grad.astype(jnp.float32) * stack_heads(exact_ref[...])
    delta = jnp.sum(product.T, axis=0, keepdims=True)
    lse = lse_ref[0]
    last, first = ask_ref[0, 0:1, :], ask_ref[0, 1:2, :]
    acc[...] = jnp.zeros_like(acc)

    def visit(span, masked):
        offset = pl.multiple_of(span * KEY_SPAN, KEY_SPAN)
        place = pl.ds(offset, KEY_SPAN)
        keys = kv_ref[place, :HEAD]
        values = kv_ref[place, HEAD:]
        scores = dot_with(keys, query, COLS_BY_COLS)
        probs = jnp.exp2(scores * (HEAD**-0.5 * LOG2E) - lse)
        if masked:
            key_given = jnp.broadcast_to(key_given_ref[:, place], (8, KEY_SPAN)).T[:, 0:1]
            probs = jnp.where((key_given <= last) & (key_given >= first), probs, 0.0)
        prob_grad = dot_with(values, grad, COLS_BY_COLS)
        score_grad = (probs * (prob_grad - delta)).astype(jnp.bfloat16)
        dkv_ref[place, HEAD:] += dot(probs.astype(jnp.bfloat16), grad)
        dkv_ref[place, :HEAD] += dot(score_grad, query) * (HEAD**-0.5)
        acc[...] += dot_with(score_grad, keys, ROWS_BY_ROWS)

    lowest, open_low = bounds_ref[0, step], bounds_ref[1, step]
    open_high, highest = bounds_ref[2, step], bounds_ref[3, step]

    @pl.loop(lowest, open_low)
    def _(span):
        visit(span, True)

    @pl.loop(open_low, open_high)
    def _(span):
        visit(span, False)

    @pl.loop(open_high, highest)
    def _(span):
        visit(span, True)

    for head in range(heads):
        dq_ref[:, head * HEAD : (head + 1) * HEAD] = acc[
            head * tokens : (head + 1) * tokens
        ] * (HEAD**-0.5)

    @pl.when(step == pl.num_programs(0) - 1)
    def _():
        @pl.loop(0, dkv_ref.shape[0], step=KEY_SPAN)
        def _(row):
            place = pl.ds(row, KEY_SPAN)
            rounded_ref[place] = dkv_ref[place].astype(jnp.bfloat16)


def attend_backward(bounds, query, grad, exact, lse, ask_rows, key_given, kv, pairs):
    rows, cols = query.shape
    heads = cols // HEAD
    steps = rows // QUERY_TOKENS
    stacked = heads * QUERY_TOKENS
    return pl.pallas_call(
        attend_backward_kernel,
        grid_spec=pltpu.PrefetchScalarGridSpec(
            num_scalar_prefetch=1,
            grid=(steps,),
            in_specs=[
                rows_of((QUERY_TOKENS, cols)),
                rows_of((QUERY_TOKENS, cols)),
                rows_of((QUERY_TOKENS, cols)),
                rows_of((1, 1, stacked)),
                rows_of((1, 2, stacked)),
                whole(key_given.shape),
                whole(kv.shape),
            ],
            out_specs=[rows_of((QUERY_TOKENS, cols)), whole(kv.shape)],
            scratch_shapes=[
                pltpu.VMEM(kv.shape, jnp.float32),
                pltpu.VMEM((stacked, HEAD), jnp.float32),
            ],
        ),
        out_shape=[
            jax.ShapeDtypeStruct((rows, cols), jnp.float32),
            jax.ShapeDtypeStruct(kv.shape, jnp.bfloat16),
        ],
        compiler_params=params(56),
        cost_estimate=cost(20 * pairs * HEAD, 32 * MIB, pairs),
        name="attend_backward",
    )(bounds, query, grad, exact, lse, ask_rows, key_given, kv)


def selection(meta, expert, capacity):
    tokens = meta.shape[1]
    weight = jnp.sum(jnp.where(meta[:TOP] == expert, meta[TOP : 2 * TOP], 0.0), axis=0, keepdims=True)
    member = jnp.where(weight > 0.0, 1.0, 0.0)
    earlier = lax.broadcasted_iota(jnp.int32, (tokens, tokens), 0)
    later = lax.broadcasted_iota(jnp.int32, (tokens, tokens), 1)
    before = jnp.where(earlier < later, 1.0, 0.0).astype(jnp.bfloat16)
    rank = dot(jnp.broadcast_to(member, (16, tokens)).astype(jnp.bfloat16), before)[0:1]
    rank = jnp.where(weight > 0.0, rank, -1.0).astype(jnp.int32)
    hit = lax.broadcasted_iota(jnp.int32, (capacity, tokens), 0) == rank
    gate = jnp.sum(jnp.where(hit, weight, 0.0), axis=1, keepdims=True)
    return jnp.where(hit, 1.0, 0.0).astype(jnp.bfloat16), gate


def expert_kernel(
    expert_ref, meta_ref, x_ref, c_ref, wg_ref, wu_ref, wd_ref,
    mid_ref, out_ref, xs_ref, cs_ref, inner_ref, gg_ref, ug_ref,
):
    blocks, _, tokens = meta_ref.shape
    capacity = xs_ref.shape[0] // blocks
    expert = expert_ref[0].astype(jnp.float32)
    picks, gates = [], []
    for block in range(blocks):
        rows = slice(block * tokens, (block + 1) * tokens)
        slots = slice(block * capacity, (block + 1) * capacity)
        pick, gate = selection(meta_ref[block], expert, capacity)
        picks.append(pick)
        gates.append(gate)
        xs_ref[slots] = dot(pick, x_ref[rows]).astype(jnp.bfloat16)
        cs_ref[slots] = (dot(pick, c_ref[rows]) * gate).astype(jnp.bfloat16)
    gate_part = dot(xs_ref[...], wg_ref[0])
    up_part = dot(xs_ref[...], wu_ref[0])
    inner_grad = dot_with(cs_ref[...], wd_ref[0], COLS_BY_COLS)
    gate_sig = jax.nn.sigmoid(gate_part)
    activated = gate_part * gate_sig
    inner = (activated * up_part).astype(jnp.bfloat16)
    inner_ref[...] = inner
    gate_grad = (inner_grad * up_part * gate_sig * (1.0 + gate_part * (1.0 - gate_sig))).astype(
        jnp.bfloat16
    )
    up_grad = (inner_grad * activated).astype(jnp.bfloat16)
    gg_ref[...] = gate_grad
    ug_ref[...] = up_grad
    slot_grad = dot_with(gate_grad, wg_ref[0], COLS_BY_COLS)
    slot_grad = (slot_grad + dot_with(up_grad, wu_ref[0], COLS_BY_COLS)).astype(jnp.bfloat16)
    for block in range(blocks):
        rows = slice(block * tokens, (block + 1) * tokens)
        slots = slice(block * capacity, (block + 1) * capacity)
        mid_ref[rows] = dot_with(picks[block], slot_grad[slots], ROWS_BY_ROWS).astype(
            jnp.bfloat16
        )
    result = dot(inner, wd_ref[0]).astype(jnp.bfloat16).astype(jnp.float32)
    for block in range(blocks):
        rows = slice(block * tokens, (block + 1) * tokens)
        slots = slice(block * capacity, (block + 1) * capacity)
        scaled = (result[slots] * gates[block]).astype(jnp.bfloat16)
        out_ref[rows] = dot_with(picks[block], scaled, ROWS_BY_ROWS).astype(jnp.bfloat16)


def expert_pass(expert, meta, x_all, c_all, gate_w, up_w, down_w, capacity):
    blocks, lines, tokens = meta.shape
    width, hidden = gate_w.shape[1:]
    per = max(1, 512 // tokens)
    total = blocks * capacity
    slots = per * capacity
    shapes = [(blocks * tokens, width)] * 2 + [(total, width)] * 2 + [(total, hidden)] * 3
    return pl.pallas_call(
        expert_kernel,
        grid_spec=pltpu.PrefetchScalarGridSpec(
            num_scalar_prefetch=1,
            grid=(blocks // per,),
            in_specs=[
                rows_of((per, lines, tokens)),
                rows_of((per * tokens, width)),
                rows_of((per * tokens, width)),
                whole(gate_w.shape),
                whole(up_w.shape),
                whole(down_w.shape),
            ],
            out_specs=[rows_of((per * tokens, width))] * 2
            + [rows_of((slots, width))] * 2
            + [rows_of((slots, hidden))] * 3,
        ),
        out_shape=[jax.ShapeDtypeStruct(shape, jnp.bfloat16) for shape in shapes],
        compiler_params=params(56),
        cost_estimate=cost(10 * total * width * hidden, 150 * MIB, total * hidden),
        name="expert_pass",
    )(expert, meta, x_all, c_all, gate_w, up_w, down_w)


def head_back_kernel(raw_ref, grad_ref, gain_ref, cos_ref, sin_ref, out_ref, gain_grad_ref):
    @pl.when(pl.program_id(0) == 0)
    def _():
        gain_grad_ref[...] = jnp.zeros_like(gain_grad_ref)

    cosine, sine, gain = cos_ref[...], sin_ref[...], gain_ref[...]
    for head in range(raw_ref.shape[1] // HEAD):
        part = slice(head * HEAD, (head + 1) * HEAD)
        raw = raw_ref[:, part]
        grad = grad_ref[:, part].astype(jnp.float32)
        back = grad * cosine - pltpu.roll(grad, HEAD // 2, 1) * sine
        inverse = inverse_root(raw)
        hat = raw * inverse
        gain_grad_ref[...] += jnp.sum(back * hat, axis=0, keepdims=True)
        scaled = back * gain
        out_ref[:, part] = (
            inverse * (scaled - hat * jnp.mean(scaled * hat, axis=-1, keepdims=True))
        ).astype(jnp.bfloat16)


def head_back(raw, grad, gain, cosine, sine):
    rows, cols = raw.shape
    tile = min(ROW_TILE, rows)
    return pl.pallas_call(
        head_back_kernel,
        grid=(rows // tile,),
        in_specs=[
            rows_of((tile, cols)),
            rows_of((tile, cols)),
            whole((1, HEAD)),
            rows_of((tile, HEAD)),
            rows_of((tile, HEAD)),
        ],
        out_specs=[rows_of((tile, cols)), whole((1, HEAD))],
        out_shape=[
            jax.ShapeDtypeStruct((rows, cols), jnp.bfloat16),
            jax.ShapeDtypeStruct((1, HEAD), jnp.float32),
        ],
        compiler_params=params(24),
        cost_estimate=cost(rows * cols * 20, rows * cols * 10),
        name="head_back",
    )(raw, grad, gain[None], cosine, sine)


MESH_ID = pl.DeviceIdType.MESH


class Place:
    def __init__(self, send_sem, tp_size=4, nearest=False):
        self.tp_size, self.send_sem, self.sent = tp_size, send_sem, []
        self.nearest = nearest
        self.ep, self.tp = lax.axis_index("ep"), lax.axis_index("tp")
        self.z, self.y, self.x, self.core = self.ep // 2, self.ep % 2, self.tp // 2, self.tp % 2
        self.edge = 1 - (self.z + self.z // 2) % 2
        self.over_x = self.tp + 2 - 4 * self.x
        self.over_core = self.tp + 1 - 2 * self.core
        self.over_both = self.over_core + 2 - 4 * self.x

    def level(self, step):
        levels = [self.z, self.z + 1 - 2 * (self.z % 2), (self.z + 2) % 4, 3 - self.z]
        if self.nearest and step > 1:
            return self.edge * levels[step] + (1 - self.edge) * levels[5 - step]
        return levels[step]

    def across(self, step, over_y):
        return self.level(step) * 2 + self.y + over_y * (1 - 2 * self.y)

    def device(self, step, first, second, other=0):
        core = self.core + other * (1 - 2 * self.core)
        over_y = first * (1 - core) + second * core
        over_x = first * core + second * (1 - core)
        x = self.x + over_x * (1 - 2 * self.x)
        return self.across(step, over_y), x * 2 + core

    def slot(self, *where):
        ep, tp = self.device(*where)
        return ep * self.tp_size + tp

    def greet(self, partners):
        barrier = pltpu.get_barrier_semaphore()
        for partner in partners:
            pl.semaphore_signal(barrier, inc=1, device_id=partner, device_id_type=MESH_ID)
        pl.semaphore_wait(barrier, len(partners))

    def greet_all_ways(self):
        partners = [(1, 0, 0), (2, 0, 0), (3, 0, 0), (0, 1, 0), (0, 0, 1), (0, 0, 0, 1)]
        self.greet([self.device(*partner) for partner in partners])

    def send(self, src, dst, sem, device):
        copy = pltpu.make_async_remote_copy(
            src_ref=src,
            dst_ref=dst,
            send_sem=self.send_sem.at[len(self.sent)],
            recv_sem=sem,
            device_id=device,
            device_id_type=MESH_ID,
        )
        copy.start()
        self.sent.append(copy)

    def arrive(self, dst, sem):
        pltpu.make_async_remote_copy(
            src_ref=dst,
            dst_ref=dst,
            send_sem=self.send_sem.at[0],
            recv_sem=sem,
            device_id=(self.ep, self.over_core),
            device_id_type=MESH_ID,
        ).wait_recv()

    def finish(self):
        for copy in self.sent:
            copy.wait_send()


def reach(kernel, out, scratch, ident, *operands, vmem_out=False, mib=None):
    dma = [kind if not isinstance(kind, tuple) else pltpu.SemaphoreType.DMA(kind) for kind in scratch]
    spaces = vmem_out if isinstance(vmem_out, tuple) else jax.tree.map(lambda _: vmem_out, out)
    out_specs = jax.tree.map(
        lambda vmem: pl.BlockSpec(memory_space=pltpu.VMEM if vmem else pl.ANY), spaces
    )
    return pl.pallas_call(
        kernel,
        in_specs=[pl.BlockSpec(memory_space=pl.ANY)] * len(operands),
        out_specs=out_specs,
        out_shape=out,
        scratch_shapes=dma,
        compiler_params=pltpu.CompilerParams(
            collective_id=ident,
            has_side_effects=True,
            vmem_limit_bytes=(mib or 16) * MIB,
        ),
        cost_estimate=cost(1, 1),
        name=kernel.__name__ if not isinstance(kernel, functools.partial) else kernel.func.__name__,
    )(*operands)


NEAR = ((0, 0), (1, 0), (0, 1), (2, 0), (1, 1), (3, 0), (2, 1), (3, 1))
ORDER = ((0,0,0),(1,0,0),(0,0,1),(0,1,0),(2,0,0),(1,0,1),(1,1,0),(0,1,1),(3,0,0),(2,1,0),(2,0,1),(1,1,1),(3,1,0),(3,0,1),(2,1,1),(3,1,1))


def expert_all_kernel(
    x_ref, m_ref, c_ref, wg_ref, wu_ref, wd_ref,
    all_ref, mid_ref, out_ref, xs_ref, cs_ref, inner_ref, gg_ref, ug_ref,
    lines, wg, wu, wd, pair, xb, cb, midb, outb, xsb, csb, innerb, ggb, ugb,
    w_sem, own_sem, z_sem, z_line_sem, send_sem, line_send_sem, recv_sem, line_sem,
    load_sem, store_sem,
):
    place = Place(send_sem, nearest=True)
    rows = x_ref.shape[0]
    capacity = xsb.shape[1] // 2
    expert = (place.ep * 4 + place.tp).astype(jnp.float32)
    count = len(ORDER)
    slots = {(*where, other): place.slot(*where, other) for where in ORDER for other in (0, 1)}
    first, second, across = place.device(0, 1, 0), place.device(0, 0, 1), place.device(0, 0, 0, 1)

    def part(ref, slot):
        return ref.at[pl.ds(slot * rows, rows)]

    weights = [
        pltpu.make_async_copy(ref, held, w_sem.at[number])
        for number, (ref, held) in enumerate(((wg_ref, wg), (wu_ref, wu), (wd_ref, wd)))
    ]
    mine = slots[0, 0, 0, 0]
    own = [
        pltpu.make_async_copy(x_ref, part(all_ref, mine), own_sem.at[0]),
        pltpu.make_async_copy(m_ref, lines.at[mine], own_sem.at[1]),
    ]
    for copy in own + weights:
        copy.start()
    place.greet_all_ways()
    for copy in own:
        copy.wait()

    def copies(slot, device, rows_sem, words_sem):
        some = dict(device_id=device, device_id_type=MESH_ID)
        return (
            pltpu.make_async_remote_copy(
                src_ref=lines.at[slot], dst_ref=lines.at[slot],
                send_sem=words_sem, recv_sem=line_sem.at[slot], **some,
            ),
            pltpu.make_async_remote_copy(
                src_ref=part(all_ref, slot), dst_ref=part(all_ref, slot),
                send_sem=rows_sem, recv_sem=recv_sem.at[slot], **some,
            ),
        )

    def along_z(step):
        level, z = place.level(step), place.z
        up = (z < 3) if step == 0 else (level < z) & (z < 3)
        down = (z > 0) if step == 0 else (level > z) & (z > 0)
        return ((up, 2 * step, (place.ep + 2, place.tp)), (down, 2 * step + 1, (place.ep - 2, place.tp)))

    def z_copies(slot, number, device):
        return copies(slot, device, z_sem.at[number], z_line_sem.at[number])

    sends = []
    for where in ORDER:
        targets = [across]
        if where[2] == 0:
            targets = [second, *targets]
        if where[1:] == (0, 0):
            targets = [first, *targets]
        sends.append(targets)
    starts = [sum(len(targets) for targets in sends[:number]) for number in range(count)]

    def arrive(slot):
        for copy in copies(slot, across, send_sem.at[0], line_send_sem.at[0]):
            copy.wait_recv()

    def onward_z(step):
        for wanted, index, device in along_z(step):

            @pl.when(wanted)
            def _(index=index, device=device):
                for copy in z_copies(slots[step, 0, 0, 0], index, device):
                    copy.start()

    relays = {1: 2, 3: 3}

    def event(number):
        where = ORDER[number]
        slot = slots[(*where, 0)]
        if where[0] in relays.values() and where[1:] == (0, 0):

            @pl.when(place.edge == 1)
            def _():
                arrive(slot)

        elif number:
            arrive(slot)
        if where in ((0, 0, 0), (1, 0, 0)):
            onward_z(where[0])
        if number in relays:
            step = relays[number]

            @pl.when(place.edge == 0)
            def _():
                arrive(slots[step, 0, 0, 0])
                onward_z(step)

        for index, device in enumerate(sends[number], starts[number]):
            for copy in copies(slot, device, send_sem.at[index], line_send_sem.at[index]):
                copy.start()

    def load_copies(slot, parity, half):
        return (
            pltpu.make_async_copy(part(all_ref, slot), xb.at[parity, half], load_sem.at[parity, half]),
            pltpu.make_async_copy(
                c_ref.at[:, slot % 4, slot // 4], cb.at[parity, half], load_sem.at[parity, 2 + half]
            ),
        )

    def load(number):
        where, parity = ORDER[number], number % 2
        arrive(slots[(*where, 1)])
        for half in (0, 1):
            slot = slots[(*where, half)]
            pair[parity, half] = lines[slot]
            for copy in load_copies(slot, parity, half):
                copy.start()

    def store_copies(number, parity, both):
        kept = pl.ds(number * 2 * capacity, 2 * capacity)
        moves = [(held.at[parity], ref.at[kept]) for held, ref in (
            (xsb, xs_ref), (csb, cs_ref), (innerb, inner_ref), (ggb, gg_ref), (ugb, ug_ref),
        )]
        for half in (0, 1):
            moves.append((midb.at[parity, half], part(mid_ref, both[half])))
            slot = both[half]
            moves.append((outb.at[parity, half], out_ref.at[:, slot % 4, slot // 4]))
        return [
            pltpu.make_async_copy(held, ref, store_sem.at[parity, index])
            for index, (held, ref) in enumerate(moves)
        ]

    def compute(parity):
        picks, gates = [], []
        for half in (0, 1):
            pick, gate = selection(pair[parity, half], expert, capacity)
            picks.append(pick)
            gates.append(gate)
            some = slice(half * capacity, (half + 1) * capacity)
            xsb[parity, some] = dot(pick, xb[parity, half]).astype(jnp.bfloat16)
            cot = cb[parity, half].reshape(rows, -1)
            csb[parity, some] = (dot(pick, cot) * gate).astype(jnp.bfloat16)
        expert_in, slot_cot = xsb[parity], csb[parity]
        gate_part = dot(expert_in, wg[0])
        up_part = dot(expert_in, wu[0])
        inner_grad = dot_with(slot_cot, wd[0], COLS_BY_COLS)
        gate_sig = jax.nn.sigmoid(gate_part)
        activated = gate_part * gate_sig
        inner = (activated * up_part).astype(jnp.bfloat16)
        innerb[parity] = inner
        gate_grad = inner_grad * up_part * gate_sig * (1.0 + gate_part * (1.0 - gate_sig))
        gate_grad = gate_grad.astype(jnp.bfloat16)
        up_grad = (inner_grad * activated).astype(jnp.bfloat16)
        ggb[parity] = gate_grad
        ugb[parity] = up_grad
        slot_grad = dot_with(gate_grad, wg[0], COLS_BY_COLS)
        slot_grad = (slot_grad + dot_with(up_grad, wu[0], COLS_BY_COLS)).astype(jnp.bfloat16)
        result = dot(inner, wd[0]).astype(jnp.bfloat16).astype(jnp.float32)
        for half in (0, 1):
            some = slice(half * capacity, (half + 1) * capacity)
            midb[parity, half] = dot_with(picks[half], slot_grad[some], ROWS_BY_ROWS).astype(
                jnp.bfloat16
            )
            scaled = (result[some] * gates[half]).astype(jnp.bfloat16)
            mixed = dot_with(picks[half], scaled, ROWS_BY_ROWS).astype(jnp.bfloat16)
            outb[parity, half] = mixed.reshape(outb.shape[2:])

    @pl.loop(0, count + 2)
    def _(turn):
        for number in range(count):

            @pl.when(turn == number)
            def _(number=number):
                event(number)

        for number in range(count):

            @pl.when(turn == number + 1)
            def _(number=number):
                load(number)

        @pl.when(turn == 2)
        def _():
            for copy in weights:
                copy.wait()

        @pl.when(turn >= 2)
        def _():
            parity = turn % 2
            for half in (0, 1):
                for copy in load_copies(0, parity, half):
                    copy.wait()

            @pl.when(turn >= 4)
            def _():
                for copy in store_copies(0, parity, (0, 0)):
                    copy.wait()

            compute(parity)

        for number in range(count):

            @pl.when(turn == number + 2)
            def _(number=number):
                both = [slots[(*ORDER[number], half)] for half in (0, 1)]
                for copy in store_copies(number, number % 2, both):
                    copy.start()

    for parity in (0, 1):
        for copy in store_copies(0, parity, (0, 0)):
            copy.wait()
    for index in range(sum(len(targets) for targets in sends)):
        for copy in copies(0, across, send_sem.at[index], line_send_sem.at[index]):
            copy.wait_send()
    for step in range(4):
        for wanted, index, device in along_z(step):

            @pl.when(wanted)
            def _(index=index, device=device):
                for copy in z_copies(0, index, device):
                    copy.wait_send()


def expert_all(x, lines, c_all, gate_w, up_w, down_w, capacity, ident):
    rows, width = x.shape
    ep_size, tp_size = c_all.shape[:2]
    blocks = ep_size * tp_size
    hidden = gate_w.shape[2]
    total = blocks * capacity
    shapes = [(blocks * rows, width)] * 2 + [c_all.shape]
    shapes += [(total, width)] * 2 + [(total, hidden)] * 3
    out = [jax.ShapeDtypeStruct(shape, jnp.bfloat16) for shape in shapes]

    def buffer(*shape):
        return pltpu.VMEM(shape, jnp.bfloat16)

    scratch = [pltpu.VMEM((blocks, *lines.shape), jnp.float32)]
    scratch += [buffer(*gate_w.shape), buffer(*up_w.shape), buffer(*down_w.shape)]
    scratch += [pltpu.VMEM((2, 2, *lines.shape), jnp.float32)]
    by_source = buffer(2, 2, ep_size, rows // ep_size, width)
    scratch += [buffer(2, 2, rows, width), by_source, buffer(2, 2, rows, width), by_source]
    scratch += [buffer(2, 2 * capacity, width)] * 2
    scratch += [buffer(2, 2 * capacity, hidden)] * 3
    scratch += [(3,), (2,), (8,), (8,), (28,), (28,), (blocks,), (blocks,), (2, 4), (2, 9)]
    operands = (x, lines, c_all, gate_w, up_w, down_w)
    return reach(expert_all_kernel, out, scratch, ident, *operands, mib=58)[1:]


BUFFERS = 4


def scatter_all_kernel(
    p_ref, out_ref, held, over_second, over_first, over_z, own,
    own_sem, send_sem, core_sem, second_sem, first_sem, z_sem,
):
    place = Place(send_sem)
    rows = out_ref.shape[0]

    def add(total, other):
        @pl.loop(0, rows, step=64)
        def _(row):
            some = pl.ds(row, 64)
            total[some] = total[some] + other[some]

    def part(slot):
        return p_ref.at[pl.ds(slot * rows, rows)]

    order = [(step, first, second) for second in (1, 0) for step in (3, 2, 1, 0) for first in (1, 0)]
    loads = []

    def load(number):
        buffer = number % BUFFERS
        copy = pltpu.make_async_copy(
            part(place.slot(*order[number])), own.at[buffer], own_sem.at[buffer]
        )
        copy.start()
        loads.append(copy)

    for number in range(BUFFERS):
        load(number)
    place.greet_all_ways()
    for step, first, second in order:
        place.send(
            part(place.slot(step, first, second, 1)),
            held.at[step, first, second],
            core_sem.at[step, first, second],
            place.device(0, 0, 0, 1),
        )
    for number, (step, first, second) in enumerate(order):
        mine = held.at[step, first, second]
        place.arrive(mine, core_sem.at[step, first, second])
        loads[number].wait()
        add(mine, own.at[number % BUFFERS])
        if number + BUFFERS < len(order):
            load(number + BUFFERS)
        if second:
            place.send(
                mine, over_second.at[step, first], second_sem.at[step, first], place.device(0, 0, 1)
            )

    def onward(step):
        mine = held.at[step, 0, 0]
        place.arrive(over_first.at[step], first_sem.at[step])
        add(mine, over_first.at[step])
        if step == 2:
            place.arrive(over_z.at[3], z_sem.at[3])
            add(mine, over_z.at[3])
        if step:
            place.send(mine, over_z.at[step], z_sem.at[step], place.device(1 + (step == 2), 0, 0))

    for step in (3, 2, 1, 0):
        mine = held.at[step, 1, 0]
        place.arrive(over_second.at[step, 1], second_sem.at[step, 1])
        add(mine, over_second.at[step, 1])
        place.send(mine, over_first.at[step], first_sem.at[step], place.device(0, 1, 0))
        mine = held.at[step, 0, 0]
        place.arrive(over_second.at[step, 0], second_sem.at[step, 0])
        add(mine, over_second.at[step, 0])
        if step < 3:
            onward(step + 1)
    onward(0)
    for step in (2, 1):
        place.arrive(over_z.at[step], z_sem.at[step])

    @pl.loop(0, rows, step=32)
    def _(row):
        some = pl.ds(row, 32)
        total = held[0, 0, 0, some].astype(jnp.float32)
        for step in (1, 2):
            total = total + over_z[step, some].astype(jnp.float32)
        out_ref[some] = total

    place.finish()


def scatter_all(p, parts, ident):
    rows, width = p.shape[0] // parts, p.shape[1]

    def buffer(*lead):
        return pltpu.VMEM((*lead, rows, width), p.dtype)

    scratch = [buffer(4, 2, 2), buffer(4, 2), buffer(4), buffer(4), buffer(BUFFERS)]
    scratch += [(BUFFERS,), (parts - 1,), (4, 2, 2), (4, 2), (4,), (4,)]
    out = jax.ShapeDtypeStruct((rows, width), jnp.float32)
    return reach(scatter_all_kernel, out, scratch, ident, p, vmem_out=True, mib=56)


def enter_kernel(x_ref, group_ref, own_sem, send_sem, x_sem):
    place = Place(send_sem)
    ep, tp = place.ep, place.tp
    others = [place.across(step, over) for step in range(4) for over in (0, 1)]
    own = pltpu.make_async_copy(x_ref.at[ep], group_ref.at[ep, tp], own_sem)
    own.start()
    place.greet(
        [(other, tp) for other in others[1:]] + [(ep, place.over_x), (ep, place.over_core)]
    )
    for other in others[1:]:
        place.send(x_ref.at[other], group_ref.at[ep, tp], x_sem.at[ep, tp], (other, tp))
    for number, other in enumerate(others):
        block = group_ref.at[other, tp]
        if number:
            place.arrive(block, x_sem.at[other, tp])
        source = block if number else x_ref.at[ep]
        place.send(source, block, x_sem.at[other, tp], (ep, place.over_x))
        place.send(source, block, x_sem.at[other, tp], (ep, place.over_core))
    for other in others:
        block = group_ref.at[other, place.over_x]
        place.arrive(block, x_sem.at[other, place.over_x])
        place.send(block, block, x_sem.at[other, place.over_x], (ep, place.over_core))
    for other in others:
        for source in (place.over_core, place.over_both):
            place.arrive(group_ref.at[other, source], x_sem.at[other, source])
    own.wait()
    place.finish()


def enter(x, tp_size, ident):
    ep_size, block, width = x.shape
    moves = ep_size - 1 + ep_size * 3
    out = jax.ShapeDtypeStruct((ep_size, tp_size, block, width), x.dtype)
    scratch = [pltpu.SemaphoreType.DMA, (moves,), (ep_size, tp_size)]
    return reach(enter_kernel, out, scratch, ident, x)


CHUNKS = 4


def gather_group_kernel(x_ref, group_ref, own_sem, send_sem, recv_sem):
    place = Place(send_sem)
    ep, tp = place.ep, place.tp
    some = x_ref.shape[0] // CHUNKS

    def piece(chunk, owner):
        return group_ref.at[pl.ds(chunk * some, some), owner]

    own = pltpu.make_async_copy(x_ref, group_ref.at[:, tp], own_sem)
    own.start()
    place.greet([(ep, place.over_x), (ep, place.over_core)])
    for partner in (place.over_x, place.over_core):
        for chunk in range(CHUNKS):
            place.send(
                x_ref.at[pl.ds(chunk * some, some)],
                piece(chunk, tp),
                recv_sem.at[chunk, tp],
                (ep, partner),
            )
    for chunk in range(CHUNKS):
        block = piece(chunk, place.over_x)
        place.arrive(block, recv_sem.at[chunk, place.over_x])
        place.send(block, block, recv_sem.at[chunk, place.over_x], (ep, place.over_core))
    for chunk in range(CHUNKS):
        for source in (place.over_core, place.over_both):
            place.arrive(piece(chunk, source), recv_sem.at[chunk, source])
    own.wait()
    place.finish()


def gather_group(x, tp_size, ident):
    ep_size, block, width = x.shape
    out = jax.ShapeDtypeStruct((ep_size, tp_size, block, width), x.dtype)
    scratch = [pltpu.SemaphoreType.DMA, (CHUNKS * 3,), (CHUNKS, tp_size)]
    return reach(gather_group_kernel, out, scratch, ident, x)


def scatter_group_kernel(
    p_ref, out_ref, own, held, over_x, own_sem, send_sem, core_sem, x_sem
):
    place = Place(send_sem)
    ep, tp = place.ep, place.tp
    some = p_ref.shape[0] // CHUNKS
    block, width = p_ref.shape[2:]

    def chunk_of(chunk):
        return pl.ds(chunk * some, some)

    loads = [
        pltpu.make_async_copy(p_ref.at[:, owner], own.at[number], own_sem.at[number])
        for number, owner in enumerate((place.over_x, tp))
    ]
    for copy in loads:
        copy.start()
    place.greet([(ep, place.over_x), (ep, place.over_core)])
    for number, owner in enumerate((place.over_both, place.over_core)):
        for chunk in range(CHUNKS):
            place.send(
                p_ref.at[chunk_of(chunk), owner],
                held.at[number, chunk_of(chunk)],
                core_sem.at[number, chunk],
                (ep, place.over_core),
            )

    def add(number, chunk):
        place.arrive(held.at[number, chunk_of(chunk)], core_sem.at[number, chunk])
        for row in range(chunk * some, (chunk + 1) * some):
            held[number, row] = held[number, row] + own[number, row]

    loads[0].wait()
    for chunk in range(CHUNKS):
        add(0, chunk)
        place.send(
            held.at[0, chunk_of(chunk)],
            over_x.at[chunk_of(chunk)],
            x_sem.at[chunk],
            (ep, place.over_x),
        )
    loads[1].wait()
    for chunk in range(CHUNKS):
        add(1, chunk)
    for chunk in range(CHUNKS):
        place.arrive(over_x.at[chunk_of(chunk)], x_sem.at[chunk])
        for row in range(chunk * some, (chunk + 1) * some):
            out_ref[row] = held[1, row].astype(jnp.float32) + over_x[row].astype(jnp.float32)
    place.finish()


def scatter_group(p, ident):
    ep_size, tp_size, block, width = p.shape

    def buffer(*lead):
        return pltpu.VMEM((*lead, ep_size, block, width), p.dtype)

    scratch = [buffer(2), buffer(2), buffer(), (2,), (CHUNKS * 3,), (2, CHUNKS), (CHUNKS,)]
    out = jax.ShapeDtypeStruct((ep_size, block, width), jnp.float32)
    return reach(scatter_group_kernel, out, scratch, ident, p, vmem_out=True, mib=24)


def gather_kv_kernel(kv_ref, out_ref, own_sem, send_sem, recv_sem):
    place = Place(send_sem)
    ep, tp = place.ep, place.tp
    own = pltpu.make_async_copy(kv_ref, out_ref.at[:, ep], own_sem)
    own.start()
    partners = [place.across(*where) for where in ((1, 0), (2, 0), (3, 0), (0, 1))]
    place.greet([(partner, tp) for partner in partners])
    for partner in (partners[3], *partners[:3]):
        place.send(kv_ref, out_ref.at[:, ep], recv_sem.at[ep], (partner, tp))
    for partner in partners[:3]:
        block = out_ref.at[:, partner]
        place.arrive(block, recv_sem.at[partner])
        place.send(block, block, recv_sem.at[partner], (partners[3], tp))
    for step in range(4):
        other = place.across(step, 1)
        place.arrive(out_ref.at[:, other], recv_sem.at[other])
    own.wait()
    place.finish()


def gather_kv(kv, ep_size, ident):
    blocks, rows, width = kv.shape
    out = jax.ShapeDtypeStruct((blocks, ep_size, rows, width), kv.dtype)
    scratch = [pltpu.SemaphoreType.DMA, (ep_size - 1,), (ep_size,)]
    return reach(gather_kv_kernel, out, scratch, ident, kv)


def scatter_kv_kernel(p_ref, out_ref, own, over_y, over_z, own_sem, send_sem, y_sem, z_sem):
    place = Place(send_sem)
    tp = place.tp
    blocks = out_ref.shape[0]
    order = (3, 2, 1, 0)
    loads = {}
    for step in order:
        loads[step] = pltpu.make_async_copy(
            p_ref.at[:, place.across(step, 0)], own.at[step], own_sem.at[step]
        )
        loads[step].start()
    place.greet([(place.across(*where), tp) for where in ((1, 0), (2, 0), (3, 0), (0, 1))])
    for step in order:
        place.send(
            p_ref.at[:, place.across(step, 1)],
            over_y.at[step],
            y_sem.at[step],
            (place.across(0, 1), tp),
        )
    for step in order:
        loads[step].wait()
        place.arrive(over_y.at[step], y_sem.at[step])

        @pl.loop(0, blocks)
        def _(block, step=step):
            own[step, block] = own[step, block] + over_y[step, block]

        if step == 2:
            place.arrive(over_z.at[3], z_sem.at[3])

            @pl.loop(0, blocks)
            def _(block):
                own[2, block] = own[2, block] + over_z[3, block]

        if step:
            device = (place.across(1 + (step == 2), 0), tp)
            place.send(own.at[step], over_z.at[step], z_sem.at[step], device)
    for step in (2, 1):
        place.arrive(over_z.at[step], z_sem.at[step])

    @pl.loop(0, blocks)
    def _(block):
        total = own[0, block].astype(jnp.float32)
        for step in (1, 2):
            total = total + over_z[step, block].astype(jnp.float32)
        out_ref[block] = total.astype(jnp.bfloat16)

    place.finish()


def scatter_kv(p, ident):
    blocks, ep_size, rows, width = p.shape
    buffer = pltpu.VMEM((4, blocks, rows, width), p.dtype)
    scratch = [buffer, buffer, buffer, (4,), (7,), (4,), (4,)]
    out = jax.ShapeDtypeStruct((blocks, rows, width), p.dtype)
    return reach(scatter_kv_kernel, out, scratch, ident, p, vmem_out=True, mib=24)


SLOTS = 1024


def finish_kernel(*refs):
    partials, gains_ref, rows_ref, experts = refs[:3], refs[3], refs[4], refs[5:10]
    outs, gain_out, rows_out, grads, refs = refs[10:13], refs[13], refs[14], refs[15:18], refs[18:]
    owns, overs_y, overs_z, stages, refs = refs[:3], refs[3:6], refs[6:9], refs[9:11], refs[11:]
    wide, narrow, sums, refs = refs[0], refs[1], refs[2:5], refs[5:]
    own_sem, send_sem, y_sem, z_sem, gain_sem, load_sem, grad_sem, rows_sem, rows_send_sem = refs
    place = Place(send_sem)
    ep, tp = place.ep, place.tp
    count = len(partials)
    total, arrived = stages
    ways = [(ep, place.over_core), (ep, place.over_x)]
    ways += [(place.across(step, 0), tp) for step in (1, 2, 3)]
    ways.append((place.across(0, 1), tp))
    moves = [(number, step) for step in (3, 2, 1, 0) for number in range(count)]
    gain_load = pltpu.make_async_copy(gains_ref, total.at[0], own_sem.at[count, 0])
    gain_load.start()

    def own_copy(number, step):
        return pltpu.make_async_copy(
            partials[number].at[place.across(step, 0)],
            owns[number].at[step],
            own_sem.at[number, step],
        )

    def to_y(number, step):
        return pltpu.make_async_remote_copy(
            src_ref=partials[number].at[place.across(step, 1)],
            dst_ref=overs_y[number].at[step],
            send_sem=send_sem.at[number, step],
            recv_sem=y_sem.at[number, step],
            device_id=(place.across(0, 1), tp),
            device_id_type=MESH_ID,
        )

    def to_z(number, step):
        return pltpu.make_async_remote_copy(
            src_ref=owns[number].at[step],
            dst_ref=overs_z[number].at[step],
            send_sem=send_sem.at[number, 3 + step],
            recv_sem=z_sem.at[number, step],
            device_id=(place.across(1 + (step == 2), 0), tp),
            device_id_type=MESH_ID,
        )

    def gain_copy(number):
        return pltpu.make_async_remote_copy(
            src_ref=total.at[(0, 1, 2, 2, 2, 3)[number]],
            dst_ref=arrived.at[number],
            send_sem=send_sem.at[count, number],
            recv_sem=gain_sem.at[number],
            device_id=ways[number],
            device_id_type=MESH_ID,
        )

    others = [(step, over) for step in range(4) for over in (0, 1)][1:]

    def row_copy(index):
        other = place.across(*others[index])
        return pltpu.make_async_remote_copy(
            src_ref=rows_ref.at[other],
            dst_ref=rows_out.at[ep],
            send_sem=rows_send_sem.at[index],
            recv_sem=rows_sem.at[ep],
            device_id=(other, tp),
            device_id_type=MESH_ID,
        )

    def row_arrival(index):
        other = place.across(*others[index])
        return pltpu.make_async_remote_copy(
            src_ref=rows_ref.at[other],
            dst_ref=rows_out.at[other],
            send_sem=rows_send_sem.at[index],
            recv_sem=rows_sem.at[other],
            device_id=(other, tp),
            device_id_type=MESH_ID,
        )

    own_rows = pltpu.make_async_copy(rows_ref.at[ep], rows_out.at[ep], rows_sem.at[ep])
    own_rows.start()
    for number, step in moves:
        own_copy(number, step).start()
    place.greet(ways[:2] + [(place.across(*other), tp) for other in others])
    gain_load.wait()
    gain_copy(0).start()
    for index in range(len(others)):
        row_copy(index).start()
    for number, step in moves:
        to_y(number, step).start()

    def event(index):
        number, step = moves[index]
        own, over = owns[number], overs_y[number]
        own_copy(number, step).wait()
        to_y(number, step).wait_recv()

        @pl.loop(0, own.shape[1], step=64)
        def _(row):
            some = pl.ds(row, 64)
            own[step, some] = own[step, some] + over[step, some]

        if step == 2:
            to_z(number, 3).wait_recv()

            @pl.loop(0, own.shape[1], step=64)
            def _(row):
                some = pl.ds(row, 64)
                own[2, some] = own[2, some] + overs_z[number][3, some]

        if step:
            to_z(number, step).start()
        if index < 2:
            gain_copy(index).wait_recv()
            total[index + 1] = total[index] + arrived[index]
            for later in (1,) if index == 0 else (2, 3, 4):
                gain_copy(later).start()
        if index == 2:
            for later in (2, 3, 4):
                gain_copy(later).wait_recv()
            total[3] = (total[2] + arrived[2]) + (arrived[3] + arrived[4])
            gain_copy(5).start()

    expert_in, slot_cot, inner, gate_grad, up_grad = experts
    pieces = expert_in.shape[0] // SLOTS
    jobs = ((expert_in, gate_grad), (expert_in, up_grad), (slot_cot, inner))
    steps = pieces * len(jobs)

    def load_copies(pair, piece, parity):
        some = pl.ds(piece * SLOTS, SLOTS)
        return [
            pltpu.make_async_copy(ref.at[some], held.at[parity], load_sem.at[parity, index])
            for index, (ref, held) in enumerate(zip(pair, (wide, narrow)))
        ]

    def grad_copy(job):
        return pltpu.make_async_copy(sums[job], grads[job], grad_sem.at[job])

    def multiply(job, parity):
        into = sums[job]
        left, right = (wide, narrow) if job < 2 else (narrow, wide)
        tile = 512 if into.shape[0] % 512 == 0 else 384

        @pl.loop(0, into.shape[0], step=tile)
        def _(row):
            some = pl.ds(pl.multiple_of(row, tile), tile)
            product = dot_with(left[parity, :, some], right[parity], ROWS_BY_ROWS)

            into[some] += product

    for into in sums:

        @pl.loop(0, into.shape[0], step=64)
        def _(row, into=into):
            into[pl.ds(row, 64)] = jnp.zeros((64, into.shape[1]), jnp.float32)

    @pl.loop(0, steps + 1)
    def _(turn):
        for index in range(len(moves)):

            @pl.when(turn == index)
            def _(index=index):
                event(index)

        for job, pair in enumerate(jobs):

            @pl.when((turn >= job * pieces) & (turn < (job + 1) * pieces))
            def _(job=job, pair=pair):
                for copy in load_copies(pair, turn - job * pieces, turn % 2):
                    copy.start()

        for job, pair in enumerate(jobs):

            @pl.when((turn > job * pieces) & (turn <= (job + 1) * pieces))
            def _(job=job, pair=pair):
                parity = (turn - 1) % 2
                for copy in load_copies(pair, 0, parity):
                    copy.wait()
                multiply(job, parity)

            @pl.when(turn == (job + 1) * pieces)
            def _(job=job):
                grad_copy(job).start()

    for number in range(count):
        own, over, out = owns[number], overs_z[number], outs[number]
        for step in (2, 1):
            to_z(number, step).wait_recv()

        @pl.loop(0, own.shape[1], step=64)
        def _(row, own=own, over=over, out=out):
            some = pl.ds(row, 64)
            sum_of = own[0, some].astype(jnp.float32)
            for step in (1, 2):
                sum_of = sum_of + over[step, some].astype(jnp.float32)
            out[some] = sum_of

    gain_copy(5).wait_recv()
    gain_out[...] = total[3] + arrived[5]
    for job in range(len(jobs)):
        grad_copy(job).wait()
    for number, step in moves:
        to_y(number, step).wait_send()
        if step:
            to_z(number, step).wait_send()
    for number in range(6):
        gain_copy(number).wait_send()
    own_rows.wait()
    for index in range(len(others)):
        row_copy(index).wait_send()
        row_arrival(index).wait_recv()


def finish(partials, gains, rows, expert_in, slot_cot, inner, gate_grad, up_grad, ident):
    count = len(partials)
    buffers = [pltpu.VMEM((4, *p.shape[1:]), p.dtype) for p in partials]
    width, hidden = expert_in.shape[1], inner.shape[1]
    grads = [(width, hidden), (width, hidden), (hidden, width)]
    scratch = buffers * 3
    scratch += [pltpu.VMEM((4, *gains.shape), gains.dtype), pltpu.VMEM((6, *gains.shape), gains.dtype)]
    scratch += [pltpu.VMEM((2, SLOTS, width), jnp.bfloat16), pltpu.VMEM((2, SLOTS, hidden), jnp.bfloat16)]
    scratch += [pltpu.VMEM(shape, jnp.float32) for shape in grads]
    scratch += [(count + 1, 4), (count + 1, 7), (count, 4), (count, 4), (6,), (2, 2), (3,), (8,), (7,)]
    out = [jax.ShapeDtypeStruct(p.shape[1:], jnp.float32) for p in partials]
    out.append(jax.ShapeDtypeStruct(gains.shape, jnp.float32))
    out.append(jax.ShapeDtypeStruct(rows.shape, rows.dtype))
    out += [jax.ShapeDtypeStruct(shape, jnp.float32) for shape in grads]
    operands = (*partials, gains, rows, expert_in, slot_cot, inner, gate_grad, up_grad)
    return reach(
        finish_kernel, out, scratch, ident, *operands, vmem_out=(True,) * 4 + (False,) * 4, mib=58
    )


def on_device(
    inputs,
    cotangent,
    arrangement,
    seq_lengths,
    routes,
    gate_values,
    input_gain,
    query_proj,
    key_projected,
    value_projected,
    query_gain,
    key_gain,
    output_proj,
    expert_gain,
    gate_weight,
    up_weight,
    down_weight,
):
    ep_size = lax.axis_size("ep")
    tp_size = lax.axis_size("tp")
    ep_index = lax.axis_index("ep")
    tp_index = lax.axis_index("tp")
    everyone = ("ep", "tp")
    own_rows, width = inputs.shape
    group_rows = own_rows * tp_size
    row_block = own_rows // ep_size
    token_total = arrangement.shape[0]
    expert_count = ep_size * tp_size
    capacity = 2 * own_rows * TOP // expert_count
    heads = query_proj.shape[1] // HEAD
    known = (ep_size, tp_size) == (8, 4)
    expert = (ep_index * tp_size + tp_index).astype(jnp.int32)[None]

    table = arrangement.reshape(ep_size, tp_size, ep_size, row_block)
    leaving_from = lax.dynamic_index_in_dim(table, tp_index, 1, keepdims=False)
    leaving_from = lax.dynamic_index_in_dim(leaving_from, ep_index, 1, keepdims=False)
    send_index = leaving_from - (ep_index * group_rows + tp_index * own_rows)
    mover = (
        send_index.reshape(-1)[:, None] == jnp.arange(own_rows, dtype=jnp.int32)[None, :]
    ).astype(jnp.bfloat16)

    def to_places(rows):
        return dot(mover, rows).astype(jnp.bfloat16).reshape(ep_size, row_block, width)

    def exchange(rows):
        return lax.all_to_all(rows, "ep", split_axis=0, concat_axis=0, tiled=True)

    def to_given(moved):
        return dot_with(mover, moved, ROWS_BY_ROWS)

    def group_sorted(rows, ident):
        blocks = rows.reshape(ep_size, row_block, width)
        if known:
            gathered = gather_group(blocks, tp_size, ident)
        else:
            gathered = lax.all_gather(blocks, "tp", axis=1)
        return gathered.reshape(group_rows, width)

    def sum_group(rows, ident):
        blocks = rows.astype(jnp.bfloat16).reshape(ep_size, tp_size, row_block, width)
        if known:
            return scatter_group(blocks, ident).reshape(own_rows, width)
        placed = jnp.swapaxes(blocks, 0, 1).reshape(group_rows, width)
        own = lax.psum_scatter(placed, "tp", scatter_dimension=0, tiled=True)
        return own.astype(jnp.float32)

    leaving_x, leaving_cot = to_places(inputs), to_places(cotangent)
    if known:
        cot_all = lax.all_gather(leaving_cot, everyone, axis=0, tiled=True)
        cot_all = cot_all.reshape(ep_size, tp_size, ep_size, row_block, width)
        own_cot = lax.dynamic_index_in_dim(cot_all, tp_index, 1, keepdims=False)
        own_cot = lax.dynamic_index_in_dim(own_cot, ep_index, 1, keepdims=False)
        group_x = enter(leaving_x, tp_size, 1)
        own_inputs = lax.dynamic_index_in_dim(group_x, tp_index, 1, keepdims=False)
    else:
        own_inputs, own_cot = exchange(leaving_x), exchange(leaving_cot)
        group_x = lax.all_gather(own_inputs, "tp", axis=1)
        cot_all = lax.all_gather(own_cot.reshape(own_rows, width), everyone, axis=0, tiled=True)
    own_inputs, own_cot = own_inputs.reshape(own_rows, width), own_cot.reshape(own_rows, width)
    group_x = group_x.reshape(group_rows, width)
    meta_own = jnp.concatenate([routes.astype(jnp.float32).T, gate_values.T], axis=0)

    query_given = lax.dynamic_index_in_dim(table, ep_index, 0, keepdims=False)
    query_given = jnp.swapaxes(query_given, 0, 1).reshape(group_rows)
    query_first = seq_starts(query_given, seq_lengths)
    cosine, sine = rope_tables(query_given - query_first, HEAD)
    key_given = jnp.transpose(table, (2, 1, 0, 3)).reshape(token_total)
    by_step = (-1, QUERY_TOKENS)
    given_steps, first_steps = query_given.reshape(by_step), query_first.reshape(by_step)
    lowest = jnp.min(first_steps, axis=1) // KEY_SPAN
    highest = jnp.max(given_steps, axis=1) // KEY_SPAN + 1
    open_low = (jnp.max(first_steps, axis=1) + KEY_SPAN - 1) // KEY_SPAN
    open_low = jnp.minimum(open_low, highest)
    open_high = jnp.clip((jnp.min(given_steps, axis=1) + 1) // KEY_SPAN, open_low, highest)
    bounds = jnp.stack([lowest, open_low, open_high, highest]).astype(jnp.int32)
    ask = jnp.stack([query_given, query_first], axis=1)
    ask_rows = jnp.stack(
        [jnp.tile(given_steps, (1, heads)), jnp.tile(first_steps, (1, heads))], axis=1
    )

    normed_in, query_raw, query_rows, key_raw, kv_rows = front(
        group_x, input_gain, query_proj, key_projected, value_projected,
        query_gain, key_gain, cosine, sine,
    )
    kv_blocks = kv_rows.reshape(expert_count, row_block, 2 * HEAD)
    if known:
        kv_all = gather_kv(kv_blocks, ep_size, 2)
    else:
        kv_all = lax.all_gather(kv_blocks, "ep", axis=1)
    kv_all = kv_all.reshape(token_total, 2 * HEAD)
    pairs = group_rows * heads * 1536
    exact, out_rows, lse = attend_forward(
        bounds, query_rows, ask, key_given[None], kv_all, pairs
    )
    branch = sum_group(dot(out_rows, output_proj), 5)
    hidden = own_inputs.astype(jnp.float32) + branch
    mid_scale = inverse_root(hidden)
    normed_mid = (hidden * mid_scale * expert_gain).astype(jnp.bfloat16)

    experts = (gate_weight, up_weight, down_weight, capacity)
    if known:
        results = expert_all(normed_mid, meta_own, cot_all, *experts, 3)
    else:
        mid_all = lax.all_gather(normed_mid, everyone, axis=0, tiled=True)
        meta = lax.all_gather(meta_own, everyone, axis=0)
        results = list(expert_pass(expert, meta, mid_all, cot_all, *experts))
        results[1] = jnp.transpose(
            results[1].reshape(ep_size, tp_size, ep_size, row_block, width), (2, 1, 0, 3, 4)
        )
    mid_partial, out_partial, expert_in, slot_cot, inner, gate_grad, up_grad = results
    def sum_over_all(partial):
        return lax.psum_scatter(partial, everyone, scatter_dimension=0, tiled=True)

    if known:
        mid_grad = scatter_all(mid_partial, expert_count, 4)
    else:
        mid_grad = sum_over_all(mid_partial).astype(jnp.float32)
    mid_grad, out_partial = lax.optimization_barrier((mid_grad, out_partial))
    mixed = sum_over_all(out_partial.reshape(token_total, width))

    mid_hat = hidden * mid_scale
    grad_expert_gain = jnp.sum(mid_grad * mid_hat, axis=0)
    mid_scaled = mid_grad * expert_gain
    hidden_grad = own_cot.astype(jnp.float32) + mid_scale * (
        mid_scaled - mid_hat * jnp.mean(mid_scaled * mid_hat, axis=-1, keepdims=True)
    )
    branch_grad = group_sorted(hidden_grad.astype(jnp.bfloat16), 6)
    out_grad = dot_with(branch_grad, output_proj, COLS_BY_COLS).astype(jnp.bfloat16)
    query_grad, kv_grad = attend_backward(
        bounds, query_rows, out_grad, exact, lse, ask_rows, key_given[None], kv_all, pairs
    )
    kv_grad = kv_grad.reshape(expert_count, ep_size, row_block, 2 * HEAD)
    if known:
        kv_own = scatter_kv(kv_grad, 7)
    else:
        kv_own = lax.psum_scatter(kv_grad, "ep", scatter_dimension=1)
    kv_own = kv_own.reshape(group_rows, 2 * HEAD)
    value_grad = kv_own[:, HEAD:]
    raw_query_grad, grad_query_gain = head_back(query_raw, query_grad, query_gain, cosine, sine)
    raw_key_grad, grad_key_gain = head_back(key_raw, kv_own[:, :HEAD], key_gain, cosine, sine)
    normed_grad = (
        dot_with(raw_query_grad, query_proj, COLS_BY_COLS)
        + dot_with(raw_key_grad, key_projected, COLS_BY_COLS)
        + dot_with(value_grad, value_projected, COLS_BY_COLS)
    )
    normed_grad = sum_group(normed_grad, 8)
    own_float = own_inputs.astype(jnp.float32)
    in_scale = inverse_root(own_float)
    in_hat = own_float * in_scale
    grad_input_gain = jnp.sum(normed_grad * in_hat, axis=0)
    in_scaled = normed_grad * input_gain
    input_rows = hidden_grad + in_scale * (
        in_scaled - in_hat * jnp.mean(in_scaled * in_hat, axis=-1, keepdims=True)
    )
    leaving = jnp.concatenate([input_rows, hidden], axis=1).astype(jnp.bfloat16)
    leaving = leaving.reshape(ep_size, row_block, 2 * width)

    weights = [
        dot_with(branch_grad, out_rows, ROWS_BY_ROWS),
        dot_with(normed_in, raw_query_grad, ROWS_BY_ROWS),
        dot_with(normed_in, jnp.concatenate([raw_key_grad, value_grad], axis=1), ROWS_BY_ROWS),
    ]
    weights = [array.astype(jnp.bfloat16).reshape(ep_size, -1, array.shape[1]) for array in weights]
    gains = jnp.concatenate(
        [grad_input_gain, grad_expert_gain, grad_query_gain[0], grad_key_gain[0]]
    )
    if known:
        experts = (expert_in, slot_cot, inner, gate_grad, up_grad)
        results = finish(weights, gains.reshape(-1, HEAD), leaving, *experts, 10)
        grad_output, grad_query, grad_kv, gains, leaving = results[:5]
        grad_gate, grad_up, grad_down = results[5:]
        gains = gains.reshape(-1)
    else:
        grad_output, grad_query, grad_kv = [
            lax.psum_scatter(array, "ep", scatter_dimension=0).astype(jnp.float32)
            for array in weights
        ]
        gains, leaving = lax.psum(gains, everyone), exchange(leaving)
        grad_gate = dot_with(expert_in, gate_grad, ROWS_BY_ROWS)
        grad_up = dot_with(expert_in, up_grad, ROWS_BY_ROWS)
        grad_down = dot_with(inner, slot_cot, ROWS_BY_ROWS)
    mixed, gains = lax.optimization_barrier((mixed, gains))
    leaving = leaving.reshape(own_rows, 2 * width)
    grad_inputs = to_given(leaving[:, :width])
    layer_out = leaving[:, width:].astype(jnp.float32) + mixed.astype(jnp.float32)
    layer_out = to_given(layer_out.astype(jnp.bfloat16)).astype(jnp.bfloat16)
    grad_output = jnp.transpose(grad_output)
    cuts = (width, 2 * width, 2 * width + HEAD)
    return (
        layer_out,
        grad_inputs,
        grad_query,
        grad_kv[:, :HEAD],
        grad_kv[:, HEAD:],
        grad_output,
        gains[: cuts[0]],
        gains[cuts[1] : cuts[2]],
        gains[cuts[2] :],
        gains[cuts[0] : cuts[1]],
        grad_gate[None],
        grad_up[None],
        grad_down[None],
    )


def solution(mesh):
    split = P(("ep", "tp"), None)
    experts = P(("ep", "tp"), None, None)
    columns = P(None, "tp")
    return jax.shard_map(
        on_device,
        mesh=mesh,
        in_specs=(
            split, split, P(), P(), split, split, P(), columns, columns, columns,
            P(), P(), P("tp", None), P(), experts, experts, experts,
        ),
        out_specs=(
            split, split, P("ep", "tp"), P("ep", "tp"), P("ep", "tp"), P("tp", "ep"),
            P(), P(), P(), P(), experts, experts, experts,
        ),
        check_vma=False,
    )
```

```python
import functools
import math

import jax
import jax.numpy as jnp
from jax import lax
from jax.experimental import pallas as pl
from jax.experimental.pallas import tpu as pltpu
from jax.sharding import PartitionSpec as P

TOP = 8
EPSILON = 1e-06
ROPE_BASE = 1000000.0
KEY_SPAN = 512
QUERY_TOKENS = 64
HEAD = 128
ROW_TILE = 256
MIB = 1 << 20
LOG2E = math.log2(math.e)
ROWS_BY_ROWS = (((0,), (0,)), ((), ()))
COLS_BY_COLS = (((1,), (1,)), ((), ()))


def dot(left, right):
    return jnp.dot(left, right, preferred_element_type=jnp.float32)


def dot_with(left, right, dims):
    return lax.dot_general(left, right, dims, preferred_element_type=jnp.float32)


def cost(flops, moved, transcendentals=0):
    return pl.CostEstimate(
        flops=int(flops), bytes_accessed=int(moved), transcendentals=int(transcendentals)
    )


def params(mib):
    return pltpu.CompilerParams(
        dimension_semantics=("arbitrary",), vmem_limit_bytes=mib * MIB
    )


def whole(shape, single=True):
    rank = len(shape)
    if single:
        return pl.BlockSpec(shape, lambda *ids: (0,) * rank, pipeline_mode=pl.Buffered(1))
    return pl.BlockSpec(shape, lambda *ids: (0,) * rank)


def rows_of(shape):
    rank = len(shape)
    return pl.BlockSpec(shape, lambda i, *ids: (i,) + (0,) * (rank - 1))


def rope_tables(positions, head_dim):
    freqs = ROPE_BASE ** (-jnp.arange(0, head_dim, 2, dtype=jnp.float32) / head_dim)
    angles = positions.astype(jnp.float32)[:, None] * freqs[None, :]
    cosine, sine = jnp.cos(angles), jnp.sin(angles)
    return (
        jnp.concatenate([cosine, cosine], axis=-1),
        jnp.concatenate([-sine, sine], axis=-1),
    )


def seq_starts(given, seq_lengths):
    ends = jnp.cumsum(seq_lengths)
    passed = given[:, None] >= ends[None, :]
    return jnp.sum(jnp.where(passed, seq_lengths[None, :], 0), axis=1)


def inverse_root(values):
    return lax.rsqrt(jnp.mean(values * values, axis=-1, keepdims=True) + EPSILON)


def front_kernel(
    x_ref, gain_ref, wq_ref, wk_ref, wv_ref, qg_ref, kg_ref, cos_ref, sin_ref,
    normed_ref, qraw_ref, q_ref, kraw_ref, kv_ref,
):
    x = x_ref[...].astype(jnp.float32)
    normed = (x * inverse_root(x) * gain_ref[...]).astype(jnp.bfloat16)
    normed_ref[...] = normed
    cosine, sine = cos_ref[...], sin_ref[...]

    def prepare(raw, gain):
        values = raw * inverse_root(raw) * gain
        return (values * cosine + pltpu.roll(values, HEAD // 2, 1) * sine).astype(jnp.bfloat16)

    raw = dot(normed, wq_ref[...])
    qraw_ref[...] = raw
    for head in range(raw.shape[1] // HEAD):
        part = slice(head * HEAD, (head + 1) * HEAD)
        q_ref[:, part] = prepare(raw[:, part], qg_ref[...])
    raw = dot(normed, wk_ref[...])
    kraw_ref[...] = raw
    kv_ref[:, :HEAD] = prepare(raw, kg_ref[...])
    kv_ref[:, HEAD:] = dot(normed, wv_ref[...]).astype(jnp.bfloat16)


def front(group_x, input_gain, wq, wk, wv, query_gain, key_gain, cosine, sine):
    rows, width = group_x.shape
    cols = wq.shape[1]
    tile = min(ROW_TILE, rows)
    out = [
        ((rows, width), jnp.bfloat16),
        ((rows, cols), jnp.float32),
        ((rows, cols), jnp.bfloat16),
        ((rows, HEAD), jnp.float32),
        ((rows, 2 * HEAD), jnp.bfloat16),
    ]
    return pl.pallas_call(
        front_kernel,
        grid=(rows // tile,),
        in_specs=[
            rows_of((tile, width)),
            whole((1, width)),
            whole(wq.shape),
            whole(wk.shape),
            whole(wv.shape),
            whole((1, HEAD)),
            whole((1, HEAD)),
            rows_of((tile, HEAD)),
            rows_of((tile, HEAD)),
        ],
        out_specs=[rows_of((tile, shape[1])) for shape, kind in out],
        out_shape=[jax.ShapeDtypeStruct(shape, kind) for shape, kind in out],
        compiler_params=params(40),
        cost_estimate=cost(2 * rows * width * (cols + 2 * HEAD), 20 * MIB),
        name="front",
    )(
        group_x,
        input_gain[None],
        wq,
        wk,
        wv,
        query_gain[None],
        key_gain[None],
        cosine,
        sine,
    )


def stack_heads(block):
    heads = block.shape[1] // HEAD
    return jnp.concatenate(
        [block[:, head * HEAD : (head + 1) * HEAD] for head in range(heads)], axis=0
    )


def attend_forward_kernel(
    bounds_ref, q_ref, ask_ref, key_given_ref, kv_ref, exact_ref, out_ref, lse_ref, acc, tot
):
    step = pl.program_id(0)
    tokens, cols = q_ref.shape
    heads = cols // HEAD
    query = stack_heads(q_ref[...])
    ask = ask_ref[...]
    last = jnp.concatenate([ask[:, 0:1]] * heads, axis=0)
    first = jnp.concatenate([ask[:, 1:2]] * heads, axis=0)
    acc[...] = jnp.zeros_like(acc)
    tot[...] = jnp.zeros_like(tot)

    def visit(span, masked):
        offset = pl.multiple_of(span * KEY_SPAN, KEY_SPAN)
        keys = kv_ref[pl.ds(offset, KEY_SPAN), :HEAD]
        values = kv_ref[pl.ds(offset, KEY_SPAN), HEAD:]
        scores = dot_with(query, keys, COLS_BY_COLS)
        weights = jnp.exp2(scores * (HEAD**-0.5 * LOG2E))
        if masked:
            key_given = key_given_ref[:, pl.ds(offset, KEY_SPAN)]
            weights = jnp.where((key_given <= last) & (key_given >= first), weights, 0.0)
        part = weights[:, :HEAD]
        for chunk in range(1, KEY_SPAN // HEAD):
            part = part + weights[:, chunk * HEAD : (chunk + 1) * HEAD]
        tot[...] += part
        acc[...] += dot(weights.astype(jnp.bfloat16), values)

    lowest, open_low = bounds_ref[0, step], bounds_ref[1, step]
    open_high, highest = bounds_ref[2, step], bounds_ref[3, step]

    @pl.loop(lowest, open_low)
    def _(span):
        visit(span, True)

    @pl.loop(open_low, open_high)
    def _(span):
        visit(span, False)

    @pl.loop(open_high, highest)
    def _(span):
        visit(span, True)

    total = tot[...]
    exact = acc[...] / jnp.sum(total, axis=1, keepdims=True)
    for head in range(heads):
        rows = exact[head * tokens : (head + 1) * tokens]
        exact_ref[:, head * HEAD : (head + 1) * HEAD] = rows
        out_ref[:, head * HEAD : (head + 1) * HEAD] = rows.astype(jnp.bfloat16)
    lse_ref[0] = jnp.log2(jnp.sum(total.T, axis=0, keepdims=True))


def attend_forward(bounds, query, ask, key_given, kv, pairs):
    rows, cols = query.shape
    heads = cols // HEAD
    steps = rows // QUERY_TOKENS
    stacked = heads * QUERY_TOKENS
    return pl.pallas_call(
        attend_forward_kernel,
        grid_spec=pltpu.PrefetchScalarGridSpec(
            num_scalar_prefetch=1,
            grid=(steps,),
            in_specs=[
                rows_of((QUERY_TOKENS, cols)),
                rows_of((QUERY_TOKENS, 2)),
                whole(key_given.shape),
                whole(kv.shape),
            ],
            out_specs=[
                rows_of((QUERY_TOKENS, cols)),
                rows_of((QUERY_TOKENS, cols)),
                rows_of((1, 1, stacked)),
            ],
            scratch_shapes=[
                pltpu.VMEM((stacked, HEAD), jnp.float32),
                pltpu.VMEM((stacked, HEAD), jnp.float32),
            ],
        ),
        out_shape=[
            jax.ShapeDtypeStruct((rows, cols), jnp.float32),
            jax.ShapeDtypeStruct((rows, cols), jnp.bfloat16),
            jax.ShapeDtypeStruct((steps, 1, stacked), jnp.float32),
        ],
        compiler_params=params(48),
        cost_estimate=cost(8 * pairs * HEAD, 16 * MIB, pairs),
        name="attend_forward",
    )(bounds, query, ask, key_given, kv)


def attend_backward_kernel(
    bounds_ref, q_ref, grad_ref, exact_ref, lse_ref, ask_ref, key_given_ref, kv_ref,
    dq_ref, rounded_ref, dkv_ref, acc,
):
    step = pl.program_id(0)
    tokens, cols = q_ref.shape
    heads = cols // HEAD

    @pl.when(step == 0)
    def _():
        dkv_ref[...] = jnp.zeros_like(dkv_ref)

    query = stack_heads(q_ref[...])
    grad = stack_heads(grad_ref[...])
    product = grad.astype(jnp.float32) * stack_heads(exact_ref[...])
    delta = jnp.sum(product.T, axis=0, keepdims=True)
    lse = lse_ref[0]
    last, first = ask_ref[0, 0:1, :], ask_ref[0, 1:2, :]
    acc[...] = jnp.zeros_like(acc)

    def visit(span, masked):
        offset = pl.multiple_of(span * KEY_SPAN, KEY_SPAN)
        place = pl.ds(offset, KEY_SPAN)
        keys = kv_ref[place, :HEAD]
        values = kv_ref[place, HEAD:]
        scores = dot_with(keys, query, COLS_BY_COLS)
        probs = jnp.exp2(scores * (HEAD**-0.5 * LOG2E) - lse)
        if masked:
            key_given = jnp.broadcast_to(key_given_ref[:, place], (8, KEY_SPAN)).T[:, 0:1]
            probs = jnp.where((key_given <= last) & (key_given >= first), probs, 0.0)
        prob_grad = dot_with(values, grad, COLS_BY_COLS)
        score_grad = (probs * (prob_grad - delta)).astype(jnp.bfloat16)
        dkv_ref[place, HEAD:] += dot(probs.astype(jnp.bfloat16), grad)
        dkv_ref[place, :HEAD] += dot(score_grad, query) * (HEAD**-0.5)
        acc[...] += dot_with(score_grad, keys, ROWS_BY_ROWS)

    lowest, open_low = bounds_ref[0, step], bounds_ref[1, step]
    open_high, highest = bounds_ref[2, step], bounds_ref[3, step]

    @pl.loop(lowest, open_low)
    def _(span):
        visit(span, True)

    @pl.loop(open_low, open_high)
    def _(span):
        visit(span, False)

    @pl.loop(open_high, highest)
    def _(span):
        visit(span, True)

    for head in range(heads):
        dq_ref[:, head * HEAD : (head + 1) * HEAD] = acc[
            head * tokens : (head + 1) * tokens
        ] * (HEAD**-0.5)

    @pl.when(step == pl.num_programs(0) - 1)
    def _():
        @pl.loop(0, dkv_ref.shape[0], step=KEY_SPAN)
        def _(row):
            place = pl.ds(row, KEY_SPAN)
            rounded_ref[place] = dkv_ref[place].astype(jnp.bfloat16)


def attend_backward(bounds, query, grad, exact, lse, ask_rows, key_given, kv, pairs):
    rows, cols = query.shape
    heads = cols // HEAD
    steps = rows // QUERY_TOKENS
    stacked = heads * QUERY_TOKENS
    return pl.pallas_call(
        attend_backward_kernel,
        grid_spec=pltpu.PrefetchScalarGridSpec(
            num_scalar_prefetch=1,
            grid=(steps,),
            in_specs=[
                rows_of((QUERY_TOKENS, cols)),
                rows_of((QUERY_TOKENS, cols)),
                rows_of((QUERY_TOKENS, cols)),
                rows_of((1, 1, stacked)),
                rows_of((1, 2, stacked)),
                whole(key_given.shape),
                whole(kv.shape),
            ],
            out_specs=[rows_of((QUERY_TOKENS, cols)), whole(kv.shape)],
            scratch_shapes=[
                pltpu.VMEM(kv.shape, jnp.float32),
                pltpu.VMEM((stacked, HEAD), jnp.float32),
            ],
        ),
        out_shape=[
            jax.ShapeDtypeStruct((rows, cols), jnp.float32),
            jax.ShapeDtypeStruct(kv.shape, jnp.bfloat16),
        ],
        compiler_params=params(56),
        cost_estimate=cost(20 * pairs * HEAD, 32 * MIB, pairs),
        name="attend_backward",
    )(bounds, query, grad, exact, lse, ask_rows, key_given, kv)


def selection(meta, expert, capacity):
    tokens = meta.shape[1]
    weight = jnp.sum(jnp.where(meta[:TOP] == expert, meta[TOP : 2 * TOP], 0.0), axis=0, keepdims=True)
    member = jnp.where(weight > 0.0, 1.0, 0.0)
    earlier = lax.broadcasted_iota(jnp.int32, (tokens, tokens), 0)
    later = lax.broadcasted_iota(jnp.int32, (tokens, tokens), 1)
    before = jnp.where(earlier < later, 1.0, 0.0).astype(jnp.bfloat16)
    rank = dot(jnp.broadcast_to(member, (16, tokens)).astype(jnp.bfloat16), before)[0:1]
    rank = jnp.where(weight > 0.0, rank, -1.0).astype(jnp.int32)
    hit = lax.broadcasted_iota(jnp.int32, (capacity, tokens), 0) == rank
    gate = jnp.sum(jnp.where(hit, weight, 0.0), axis=1, keepdims=True)
    return jnp.where(hit, 1.0, 0.0).astype(jnp.bfloat16), gate


def expert_kernel(
    expert_ref, meta_ref, x_ref, c_ref, wg_ref, wu_ref, wd_ref,
    mid_ref, out_ref, xs_ref, cs_ref, inner_ref, gg_ref, ug_ref,
):
    blocks, _, tokens = meta_ref.shape
    capacity = xs_ref.shape[0] // blocks
    expert = expert_ref[0].astype(jnp.float32)
    picks, gates = [], []
    for block in range(blocks):
        rows = slice(block * tokens, (block + 1) * tokens)
        slots = slice(block * capacity, (block + 1) * capacity)
        pick, gate = selection(meta_ref[block], expert, capacity)
        picks.append(pick)
        gates.append(gate)
        xs_ref[slots] = dot(pick, x_ref[rows]).astype(jnp.bfloat16)
        cs_ref[slots] = (dot(pick, c_ref[rows]) * gate).astype(jnp.bfloat16)
    gate_part = dot(xs_ref[...], wg_ref[0])
    up_part = dot(xs_ref[...], wu_ref[0])
    inner_grad = dot_with(cs_ref[...], wd_ref[0], COLS_BY_COLS)
    gate_sig = jax.nn.sigmoid(gate_part)
    activated = gate_part * gate_sig
    inner = (activated * up_part).astype(jnp.bfloat16)
    inner_ref[...] = inner
    gate_grad = (inner_grad * up_part * gate_sig * (1.0 + gate_part * (1.0 - gate_sig))).astype(
        jnp.bfloat16
    )
    up_grad = (inner_grad * activated).astype(jnp.bfloat16)
    gg_ref[...] = gate_grad
    ug_ref[...] = up_grad
    slot_grad = dot_with(gate_grad, wg_ref[0], COLS_BY_COLS)
    slot_grad = (slot_grad + dot_with(up_grad, wu_ref[0], COLS_BY_COLS)).astype(jnp.bfloat16)
    for block in range(blocks):
        rows = slice(block * tokens, (block + 1) * tokens)
        slots = slice(block * capacity, (block + 1) * capacity)
        mid_ref[rows] = dot_with(picks[block], slot_grad[slots], ROWS_BY_ROWS).astype(
            jnp.bfloat16
        )
    result = dot(inner, wd_ref[0]).astype(jnp.bfloat16).astype(jnp.float32)
    for block in range(blocks):
        rows = slice(block * tokens, (block + 1) * tokens)
        slots = slice(block * capacity, (block + 1) * capacity)
        scaled = (result[slots] * gates[block]).astype(jnp.bfloat16)
        out_ref[rows] = dot_with(picks[block], scaled, ROWS_BY_ROWS).astype(jnp.bfloat16)


def expert_pass(expert, meta, x_all, c_all, gate_w, up_w, down_w, capacity):
    blocks, lines, tokens = meta.shape
    width, hidden = gate_w.shape[1:]
    per = max(1, 512 // tokens)
    total = blocks * capacity
    slots = per * capacity
    shapes = [(blocks * tokens, width)] * 2 + [(total, width)] * 2 + [(total, hidden)] * 3
    return pl.pallas_call(
        expert_kernel,
        grid_spec=pltpu.PrefetchScalarGridSpec(
            num_scalar_prefetch=1,
            grid=(blocks // per,),
            in_specs=[
                rows_of((per, lines, tokens)),
                rows_of((per * tokens, width)),
                rows_of((per * tokens, width)),
                whole(gate_w.shape),
                whole(up_w.shape),
                whole(down_w.shape),
            ],
            out_specs=[rows_of((per * tokens, width))] * 2
            + [rows_of((slots, width))] * 2
            + [rows_of((slots, hidden))] * 3,
        ),
        out_shape=[jax.ShapeDtypeStruct(shape, jnp.bfloat16) for shape in shapes],
        compiler_params=params(56),
        cost_estimate=cost(10 * total * width * hidden, 150 * MIB, total * hidden),
        name="expert_pass",
    )(expert, meta, x_all, c_all, gate_w, up_w, down_w)


def head_back_kernel(raw_ref, grad_ref, gain_ref, cos_ref, sin_ref, out_ref, gain_grad_ref):
    @pl.when(pl.program_id(0) == 0)
    def _():
        gain_grad_ref[...] = jnp.zeros_like(gain_grad_ref)

    cosine, sine, gain = cos_ref[...], sin_ref[...], gain_ref[...]
    for head in range(raw_ref.shape[1] // HEAD):
        part = slice(head * HEAD, (head + 1) * HEAD)
        raw = raw_ref[:, part]
        grad = grad_ref[:, part].astype(jnp.float32)
        back = grad * cosine - pltpu.roll(grad, HEAD // 2, 1) * sine
        inverse = inverse_root(raw)
        hat = raw * inverse
        gain_grad_ref[...] += jnp.sum(back * hat, axis=0, keepdims=True)
        scaled = back * gain
        out_ref[:, part] = (
            inverse * (scaled - hat * jnp.mean(scaled * hat, axis=-1, keepdims=True))
        ).astype(jnp.bfloat16)


def head_back(raw, grad, gain, cosine, sine):
    rows, cols = raw.shape
    tile = min(ROW_TILE, rows)
    return pl.pallas_call(
        head_back_kernel,
        grid=(rows // tile,),
        in_specs=[
            rows_of((tile, cols)),
            rows_of((tile, cols)),
            whole((1, HEAD)),
            rows_of((tile, HEAD)),
            rows_of((tile, HEAD)),
        ],
        out_specs=[rows_of((tile, cols)), whole((1, HEAD))],
        out_shape=[
            jax.ShapeDtypeStruct((rows, cols), jnp.bfloat16),
            jax.ShapeDtypeStruct((1, HEAD), jnp.float32),
        ],
        compiler_params=params(24),
        cost_estimate=cost(rows * cols * 20, rows * cols * 10),
        name="head_back",
    )(raw, grad, gain[None], cosine, sine)


MESH_ID = pl.DeviceIdType.MESH


class Place:
    def __init__(self, send_sem, tp_size=4, nearest=False):
        self.tp_size, self.send_sem, self.sent = tp_size, send_sem, []
        self.nearest = nearest
        self.ep, self.tp = lax.axis_index("ep"), lax.axis_index("tp")
        self.z, self.y, self.x, self.core = self.ep // 2, self.ep % 2, self.tp // 2, self.tp % 2
        self.edge = 1 - (self.z + self.z // 2) % 2
        self.over_x = self.tp + 2 - 4 * self.x
        self.over_core = self.tp + 1 - 2 * self.core
        self.over_both = self.over_core + 2 - 4 * self.x

    def level(self, step):
        levels = [self.z, self.z + 1 - 2 * (self.z % 2), (self.z + 2) % 4, 3 - self.z]
        if self.nearest and step > 1:
            return self.edge * levels[step] + (1 - self.edge) * levels[5 - step]
        return levels[step]

    def across(self, step, over_y):
        return self.level(step) * 2 + self.y + over_y * (1 - 2 * self.y)

    def device(self, step, first, second, other=0):
        core = self.core + other * (1 - 2 * self.core)
        over_y = first * (1 - core) + second * core
        over_x = first * core + second * (1 - core)
        x = self.x + over_x * (1 - 2 * self.x)
        return self.across(step, over_y), x * 2 + core

    def slot(self, *where):
        ep, tp = self.device(*where)
        return ep * self.tp_size + tp

    def greet(self, partners):
        barrier = pltpu.get_barrier_semaphore()
        for partner in partners:
            pl.semaphore_signal(barrier, inc=1, device_id=partner, device_id_type=MESH_ID)
        pl.semaphore_wait(barrier, len(partners))

    def greet_all_ways(self):
        partners = [(1, 0, 0), (2, 0, 0), (3, 0, 0), (0, 1, 0), (0, 0, 1), (0, 0, 0, 1)]
        self.greet([self.device(*partner) for partner in partners])

    def send(self, src, dst, sem, device):
        copy = pltpu.make_async_remote_copy(
            src_ref=src,
            dst_ref=dst,
            send_sem=self.send_sem.at[len(self.sent)],
            recv_sem=sem,
            device_id=device,
            device_id_type=MESH_ID,
        )
        copy.start()
        self.sent.append(copy)

    def arrive(self, dst, sem):
        pltpu.make_async_remote_copy(
            src_ref=dst,
            dst_ref=dst,
            send_sem=self.send_sem.at[0],
            recv_sem=sem,
            device_id=(self.ep, self.over_core),
            device_id_type=MESH_ID,
        ).wait_recv()

    def finish(self):
        for copy in self.sent:
            copy.wait_send()


def reach(kernel, out, scratch, ident, *operands, vmem_out=False, mib=None):
    dma = [kind if not isinstance(kind, tuple) else pltpu.SemaphoreType.DMA(kind) for kind in scratch]
    spaces = vmem_out if isinstance(vmem_out, tuple) else jax.tree.map(lambda _: vmem_out, out)
    out_specs = jax.tree.map(
        lambda vmem: pl.BlockSpec(memory_space=pltpu.VMEM if vmem else pl.ANY), spaces
    )
    return pl.pallas_call(
        kernel,
        in_specs=[pl.BlockSpec(memory_space=pl.ANY)] * len(operands),
        out_specs=out_specs,
        out_shape=out,
        scratch_shapes=dma,
        compiler_params=pltpu.CompilerParams(
            collective_id=ident,
            has_side_effects=True,
            vmem_limit_bytes=(mib or 16) * MIB,
        ),
        cost_estimate=cost(1, 1),
        name=kernel.__name__ if not isinstance(kernel, functools.partial) else kernel.func.__name__,
    )(*operands)


NEAR = ((0, 0), (1, 0), (0, 1), (2, 0), (1, 1), (3, 0), (2, 1), (3, 1))
ORDER = ((0,0,0),(1,0,0),(0,0,1),(0,1,0),(2,0,0),(1,0,1),(1,1,0),(0,1,1),(3,0,0),(2,1,0),(2,0,1),(1,1,1),(3,1,0),(3,0,1),(2,1,1),(3,1,1))


def expert_all_kernel(
    x_ref, m_ref, c_ref, wg_ref, wu_ref, wd_ref,
    all_ref, mid_ref, out_ref, xs_ref, cs_ref, inner_ref, gg_ref, ug_ref,
    lines, wg, wu, wd, pair, xb, cb, midb, outb, xsb, csb, innerb, ggb, ugb,
    w_sem, own_sem, z_sem, z_line_sem, send_sem, line_send_sem, recv_sem, line_sem,
    load_sem, store_sem,
):
    place = Place(send_sem, nearest=True)
    rows = x_ref.shape[0]
    capacity = xsb.shape[1] // 2
    expert = (place.ep * 4 + place.tp).astype(jnp.float32)
    count = len(ORDER)
    slots = {(*where, other): place.slot(*where, other) for where in ORDER for other in (0, 1)}
    first, second, across = place.device(0, 1, 0), place.device(0, 0, 1), place.device(0, 0, 0, 1)

    def part(ref, slot):
        return ref.at[pl.ds(slot * rows, rows)]

    weights = [
        pltpu.make_async_copy(ref, held, w_sem.at[number])
        for number, (ref, held) in enumerate(((wg_ref, wg), (wu_ref, wu), (wd_ref, wd)))
    ]
    mine = slots[0, 0, 0, 0]
    own = [
        pltpu.make_async_copy(x_ref, part(all_ref, mine), own_sem.at[0]),
        pltpu.make_async_copy(m_ref, lines.at[mine], own_sem.at[1]),
    ]
    for copy in own + weights:
        copy.start()
    place.greet_all_ways()
    for copy in own:
        copy.wait()

    def copies(slot, device, rows_sem, words_sem):
        some = dict(device_id=device, device_id_type=MESH_ID)
        return (
            pltpu.make_async_remote_copy(
                src_ref=lines.at[slot], dst_ref=lines.at[slot],
                send_sem=words_sem, recv_sem=line_sem.at[slot], **some,
            ),
            pltpu.make_async_remote_copy(
                src_ref=part(all_ref, slot), dst_ref=part(all_ref, slot),
                send_sem=rows_sem, recv_sem=recv_sem.at[slot], **some,
            ),
        )

    def along_z(step):
        level, z = place.level(step), place.z
        up = (z < 3) if step == 0 else (level < z) & (z < 3)
        down = (z > 0) if step == 0 else (level > z) & (z > 0)
        return ((up, 2 * step, (place.ep + 2, place.tp)), (down, 2 * step + 1, (place.ep - 2, place.tp)))

    def z_copies(slot, number, device):
        return copies(slot, device, z_sem.at[number], z_line_sem.at[number])

    sends = []
    for where in ORDER:
        targets = [across]
        if where[2] == 0:
            targets = [second, *targets]
        if where[1:] == (0, 0):
            targets = [first, *targets]
        sends.append(targets)
    starts = [sum(len(targets) for targets in sends[:number]) for number in range(count)]

    def arrive(slot):
        for copy in copies(slot, across, send_sem.at[0], line_send_sem.at[0]):
            copy.wait_recv()

    def onward_z(step):
        for wanted, index, device in along_z(step):

            @pl.when(wanted)
            def _(index=index, device=device):
                for copy in z_copies(slots[step, 0, 0, 0], index, device):
                    copy.start()

    relays = {1: 2, 3: 3}

    def event(number):
        where = ORDER[number]
        slot = slots[(*where, 0)]
        if where[0] in relays.values() and where[1:] == (0, 0):

            @pl.when(place.edge == 1)
            def _():
                arrive(slot)

        elif number:
            arrive(slot)
        if where in ((0, 0, 0), (1, 0, 0)):
            onward_z(where[0])
        if number in relays:
            step = relays[number]

            @pl.when(place.edge == 0)
            def _():
                arrive(slots[step, 0, 0, 0])
                onward_z(step)

        for index, device in enumerate(sends[number], starts[number]):
            for copy in copies(slot, device, send_sem.at[index], line_send_sem.at[index]):
                copy.start()

    def load_copies(slot, parity, half):
        return (
            pltpu.make_async_copy(part(all_ref, slot), xb.at[parity, half], load_sem.at[parity, half]),
            pltpu.make_async_copy(
                c_ref.at[:, slot % 4, slot // 4], cb.at[parity, half], load_sem.at[parity, 2 + half]
            ),
        )

    def load(number):
        where, parity = ORDER[number], number % 2
        arrive(slots[(*where, 1)])
        for half in (0, 1):
            slot = slots[(*where, half)]
            pair[parity, half] = lines[slot]
            for copy in load_copies(slot, parity, half):
                copy.start()

    def store_copies(number, parity, both):
        kept = pl.ds(number * 2 * capacity, 2 * capacity)
        moves = [(held.at[parity], ref.at[kept]) for held, ref in (
            (xsb, xs_ref), (csb, cs_ref), (innerb, inner_ref), (ggb, gg_ref), (ugb, ug_ref),
        )]
        for half in (0, 1):
            moves.append((midb.at[parity, half], part(mid_ref, both[half])))
            slot = both[half]
            moves.append((outb.at[parity, half], out_ref.at[:, slot % 4, slot // 4]))
        return [
            pltpu.make_async_copy(held, ref, store_sem.at[parity, index])
            for index, (held, ref) in enumerate(moves)
        ]

    def compute(parity):
        picks, gates = [], []
        for half in (0, 1):
            pick, gate = selection(pair[parity, half], expert, capacity)
            picks.append(pick)
            gates.append(gate)
            some = slice(half * capacity, (half + 1) * capacity)
            xsb[parity, some] = dot(pick, xb[parity, half]).astype(jnp.bfloat16)
            cot = cb[parity, half].reshape(rows, -1)
            csb[parity, some] = (dot(pick, cot) * gate).astype(jnp.bfloat16)
        expert_in, slot_cot = xsb[parity], csb[parity]
        gate_part = dot(expert_in, wg[0])
        up_part = dot(expert_in, wu[0])
        inner_grad = dot_with(slot_cot, wd[0], COLS_BY_COLS)
        gate_sig = jax.nn.sigmoid(gate_part)
        activated = gate_part * gate_sig
        inner = (activated * up_part).astype(jnp.bfloat16)
        innerb[parity] = inner
        gate_grad = inner_grad * up_part * gate_sig * (1.0 + gate_part * (1.0 - gate_sig))
        gate_grad = gate_grad.astype(jnp.bfloat16)
        up_grad = (inner_grad * activated).astype(jnp.bfloat16)
        ggb[parity] = gate_grad
        ugb[parity] = up_grad
        slot_grad = dot_with(gate_grad, wg[0], COLS_BY_COLS)
        slot_grad = (slot_grad + dot_with(up_grad, wu[0], COLS_BY_COLS)).astype(jnp.bfloat16)
        result = dot(inner, wd[0]).astype(jnp.bfloat16).astype(jnp.float32)
        for half in (0, 1):
            some = slice(half * capacity, (half + 1) * capacity)
            midb[parity, half] = dot_with(picks[half], slot_grad[some], ROWS_BY_ROWS).astype(
                jnp.bfloat16
            )
            scaled = (result[some] * gates[half]).astype(jnp.bfloat16)
            mixed = dot_with(picks[half], scaled, ROWS_BY_ROWS).astype(jnp.bfloat16)
            outb[parity, half] = mixed.reshape(outb.shape[2:])

    @pl.loop(0, count + 2)
    def _(turn):
        for number in range(count):

            @pl.when(turn == number)
            def _(number=number):
                event(number)

        for number in range(count):

            @pl.when(turn == number + 1)
            def _(number=number):
                load(number)

        @pl.when(turn == 2)
        def _():
            for copy in weights:
                copy.wait()

        @pl.when(turn >= 2)
        def _():
            parity = turn % 2
            for half in (0, 1):
                for copy in load_copies(0, parity, half):
                    copy.wait()

            @pl.when(turn >= 4)
            def _():
                for copy in store_copies(0, parity, (0, 0)):
                    copy.wait()

            compute(parity)

        for number in range(count):

            @pl.when(turn == number + 2)
            def _(number=number):
                both = [slots[(*ORDER[number], half)] for half in (0, 1)]
                for copy in store_copies(number, number % 2, both):
                    copy.start()

    for parity in (0, 1):
        for copy in store_copies(0, parity, (0, 0)):
            copy.wait()
    for index in range(sum(len(targets) for targets in sends)):
        for copy in copies(0, across, send_sem.at[index], line_send_sem.at[index]):
            copy.wait_send()
    for step in range(4):
        for wanted, index, device in along_z(step):

            @pl.when(wanted)
            def _(index=index, device=device):
                for copy in z_copies(0, index, device):
                    copy.wait_send()


def expert_all(x, lines, c_all, gate_w, up_w, down_w, capacity, ident):
    rows, width = x.shape
    ep_size, tp_size = c_all.shape[:2]
    blocks = ep_size * tp_size
    hidden = gate_w.shape[2]
    total = blocks * capacity
    shapes = [(blocks * rows, width)] * 2 + [c_all.shape]
    shapes += [(total, width)] * 2 + [(total, hidden)] * 3
    out = [jax.ShapeDtypeStruct(shape, jnp.bfloat16) for shape in shapes]

    def buffer(*shape):
        return pltpu.VMEM(shape, jnp.bfloat16)

    scratch = [pltpu.VMEM((blocks, *lines.shape), jnp.float32)]
    scratch += [buffer(*gate_w.shape), buffer(*up_w.shape), buffer(*down_w.shape)]
    scratch += [pltpu.VMEM((2, 2, *lines.shape), jnp.float32)]
    by_source = buffer(2, 2, ep_size, rows // ep_size, width)
    scratch += [buffer(2, 2, rows, width), by_source, buffer(2, 2, rows, width), by_source]
    scratch += [buffer(2, 2 * capacity, width)] * 2
    scratch += [buffer(2, 2 * capacity, hidden)] * 3
    scratch += [(3,), (2,), (8,), (8,), (28,), (28,), (blocks,), (blocks,), (2, 4), (2, 9)]
    operands = (x, lines, c_all, gate_w, up_w, down_w)
    return reach(expert_all_kernel, out, scratch, ident, *operands, mib=58)[1:]


BUFFERS = 4
LEAD = 2


def scatter_all_kernel(
    p_ref, out_ref, held, over_second, over_first, over_z, own,
    own_sem, send_sem, core_sem, second_sem, first_sem, z_sem,
):
    place = Place(send_sem)
    rows = out_ref.shape[0]

    def add(total, other):
        @pl.loop(0, rows, step=64)
        def _(row):
            some = pl.ds(row, 64)
            total[some] = total[some] + other[some]

    def part(slot):
        return p_ref.at[pl.ds(slot * rows, rows)]

    pairs = [(step, first) for step in (3, 2, 1, 0) for first in (1, 0)]
    order = [(*pairs[number], 1) for number in range(LEAD)]
    for number, where in enumerate(pairs):
        if number + LEAD < len(pairs):
            order.append((*pairs[number + LEAD], 1))
        order.append((*where, 0))
    loads = []

    def load(number):
        buffer = number % BUFFERS
        copy = pltpu.make_async_copy(
            part(place.slot(*order[number])), own.at[buffer], own_sem.at[buffer]
        )
        copy.start()
        loads.append(copy)

    for number in range(BUFFERS):
        load(number)
    place.greet_all_ways()
    for where in order:
        place.send(
            part(place.slot(*where, 1)), held.at[where], core_sem.at[where], place.device(0, 0, 0, 1)
        )

    def onward(step):
        mine = held.at[step, 0, 0]
        place.arrive(over_first.at[step], first_sem.at[step])
        add(mine, over_first.at[step])
        if step == 2:
            place.arrive(over_z.at[3], z_sem.at[3])
            add(mine, over_z.at[3])
        if step:
            place.send(mine, over_z.at[step], z_sem.at[step], place.device(1 + (step == 2), 0, 0))

    for number, where in enumerate(order):
        step, first, second = where
        mine = held.at[where]
        place.arrive(mine, core_sem.at[where])
        loads[number].wait()
        add(mine, own.at[number % BUFFERS])
        if number + BUFFERS < len(order):
            load(number + BUFFERS)
        if second:
            place.send(
                mine, over_second.at[step, first], second_sem.at[step, first], place.device(0, 0, 1)
            )
            continue
        place.arrive(over_second.at[step, first], second_sem.at[step, first])
        add(mine, over_second.at[step, first])
        if first:
            place.send(mine, over_first.at[step], first_sem.at[step], place.device(0, 1, 0))
        else:
            onward(step)
    for step in (2, 1):
        place.arrive(over_z.at[step], z_sem.at[step])

    @pl.loop(0, rows, step=32)
    def _(row):
        some = pl.ds(row, 32)
        total = held[0, 0, 0, some].astype(jnp.float32)
        for step in (1, 2):
            total = total + over_z[step, some].astype(jnp.float32)
        out_ref[some] = total

    place.finish()


def scatter_all(p, parts, ident):
    rows, width = p.shape[0] // parts, p.shape[1]

    def buffer(*lead):
        return pltpu.VMEM((*lead, rows, width), p.dtype)

    scratch = [buffer(4, 2, 2), buffer(4, 2), buffer(4), buffer(4), buffer(BUFFERS)]
    scratch += [(BUFFERS,), (parts - 1,), (4, 2, 2), (4, 2), (4,), (4,)]
    out = jax.ShapeDtypeStruct((rows, width), jnp.float32)
    return reach(scatter_all_kernel, out, scratch, ident, p, vmem_out=True, mib=56)


def enter_kernel(x_ref, group_ref, own_sem, send_sem, x_sem):
    place = Place(send_sem)
    ep, tp = place.ep, place.tp
    others = [place.across(step, over) for step in range(4) for over in (0, 1)]
    own = pltpu.make_async_copy(x_ref.at[ep], group_ref.at[ep, tp], own_sem)
    own.start()
    place.greet(
        [(other, tp) for other in others[1:]] + [(ep, place.over_x), (ep, place.over_core)]
    )
    for other in others[1:]:
        place.send(x_ref.at[other], group_ref.at[ep, tp], x_sem.at[ep, tp], (other, tp))
    for number, other in enumerate(others):
        block = group_ref.at[other, tp]
        if number:
            place.arrive(block, x_sem.at[other, tp])
        source = block if number else x_ref.at[ep]
        place.send(source, block, x_sem.at[other, tp], (ep, place.over_x))
        place.send(source, block, x_sem.at[other, tp], (ep, place.over_core))
    for other in others:
        block = group_ref.at[other, place.over_x]
        place.arrive(block, x_sem.at[other, place.over_x])
        place.send(block, block, x_sem.at[other, place.over_x], (ep, place.over_core))
    for other in others:
        for source in (place.over_core, place.over_both):
            place.arrive(group_ref.at[other, source], x_sem.at[other, source])
    own.wait()
    place.finish()


def enter(x, tp_size, ident):
    ep_size, block, width = x.shape
    moves = ep_size - 1 + ep_size * 3
    out = jax.ShapeDtypeStruct((ep_size, tp_size, block, width), x.dtype)
    scratch = [pltpu.SemaphoreType.DMA, (moves,), (ep_size, tp_size)]
    return reach(enter_kernel, out, scratch, ident, x)


CHUNKS = 4


def gather_group_kernel(x_ref, group_ref, own_sem, send_sem, recv_sem):
    place = Place(send_sem)
    ep, tp = place.ep, place.tp
    some = x_ref.shape[0] // CHUNKS

    def piece(chunk, owner):
        return group_ref.at[pl.ds(chunk * some, some), owner]

    own = pltpu.make_async_copy(x_ref, group_ref.at[:, tp], own_sem)
    own.start()
    place.greet([(ep, place.over_x), (ep, place.over_core)])
    for partner in (place.over_x, place.over_core):
        for chunk in range(CHUNKS):
            place.send(
                x_ref.at[pl.ds(chunk * some, some)],
                piece(chunk, tp),
                recv_sem.at[chunk, tp],
                (ep, partner),
            )
    for chunk in range(CHUNKS):
        block = piece(chunk, place.over_x)
        place.arrive(block, recv_sem.at[chunk, place.over_x])
        place.send(block, block, recv_sem.at[chunk, place.over_x], (ep, place.over_core))
    for chunk in range(CHUNKS):
        for source in (place.over_core, place.over_both):
            place.arrive(piece(chunk, source), recv_sem.at[chunk, source])
    own.wait()
    place.finish()


def gather_group(x, tp_size, ident):
    ep_size, block, width = x.shape
    out = jax.ShapeDtypeStruct((ep_size, tp_size, block, width), x.dtype)
    scratch = [pltpu.SemaphoreType.DMA, (CHUNKS * 3,), (CHUNKS, tp_size)]
    return reach(gather_group_kernel, out, scratch, ident, x)


def scatter_group_kernel(
    p_ref, out_ref, own, held, over_x, own_sem, send_sem, core_sem, x_sem
):
    place = Place(send_sem)
    ep, tp = place.ep, place.tp
    some = p_ref.shape[0] // CHUNKS
    block, width = p_ref.shape[2:]

    def chunk_of(chunk):
        return pl.ds(chunk * some, some)

    loads = [
        pltpu.make_async_copy(p_ref.at[:, owner], own.at[number], own_sem.at[number])
        for number, owner in enumerate((place.over_x, tp))
    ]
    for copy in loads:
        copy.start()
    place.greet([(ep, place.over_x), (ep, place.over_core)])
    for number, owner in enumerate((place.over_both, place.over_core)):
        for chunk in range(CHUNKS):
            place.send(
                p_ref.at[chunk_of(chunk), owner],
                held.at[number, chunk_of(chunk)],
                core_sem.at[number, chunk],
                (ep, place.over_core),
            )

    def add(number, chunk):
        place.arrive(held.at[number, chunk_of(chunk)], core_sem.at[number, chunk])
        for row in range(chunk * some, (chunk + 1) * some):
            held[number, row] = held[number, row] + own[number, row]

    loads[0].wait()
    for chunk in range(CHUNKS):
        add(0, chunk)
        place.send(
            held.at[0, chunk_of(chunk)],
            over_x.at[chunk_of(chunk)],
            x_sem.at[chunk],
            (ep, place.over_x),
        )
    loads[1].wait()
    for chunk in range(CHUNKS):
        add(1, chunk)
    for chunk in range(CHUNKS):
        place.arrive(over_x.at[chunk_of(chunk)], x_sem.at[chunk])
        for row in range(chunk * some, (chunk + 1) * some):
            out_ref[row] = held[1, row].astype(jnp.float32) + over_x[row].astype(jnp.float32)
    place.finish()


def scatter_group(p, ident):
    ep_size, tp_size, block, width = p.shape

    def buffer(*lead):
        return pltpu.VMEM((*lead, ep_size, block, width), p.dtype)

    scratch = [buffer(2), buffer(2), buffer(), (2,), (CHUNKS * 3,), (2, CHUNKS), (CHUNKS,)]
    out = jax.ShapeDtypeStruct((ep_size, block, width), jnp.float32)
    return reach(scatter_group_kernel, out, scratch, ident, p, vmem_out=True, mib=24)


def gather_kv_kernel(kv_ref, out_ref, own_sem, send_sem, recv_sem):
    place = Place(send_sem)
    ep, tp = place.ep, place.tp
    own = pltpu.make_async_copy(kv_ref, out_ref.at[:, ep], own_sem)
    own.start()
    partners = [place.across(*where) for where in ((1, 0), (2, 0), (3, 0), (0, 1))]
    place.greet([(partner, tp) for partner in partners])
    for partner in (partners[3], *partners[:3]):
        place.send(kv_ref, out_ref.at[:, ep], recv_sem.at[ep], (partner, tp))
    for partner in partners[:3]:
        block = out_ref.at[:, partner]
        place.arrive(block, recv_sem.at[partner])
        place.send(block, block, recv_sem.at[partner], (partners[3], tp))
    for step in range(4):
        other = place.across(step, 1)
        place.arrive(out_ref.at[:, other], recv_sem.at[other])
    own.wait()
    place.finish()


def gather_kv(kv, ep_size, ident):
    blocks, rows, width = kv.shape
    out = jax.ShapeDtypeStruct((blocks, ep_size, rows, width), kv.dtype)
    scratch = [pltpu.SemaphoreType.DMA, (ep_size - 1,), (ep_size,)]
    return reach(gather_kv_kernel, out, scratch, ident, kv)


def scatter_kv_kernel(p_ref, out_ref, own, over_y, over_z, own_sem, send_sem, y_sem, z_sem):
    place = Place(send_sem)
    tp = place.tp
    blocks = out_ref.shape[0]
    order = (3, 2, 1, 0)
    loads = {}
    for step in order:
        loads[step] = pltpu.make_async_copy(
            p_ref.at[:, place.across(step, 0)], own.at[step], own_sem.at[step]
        )
        loads[step].start()
    place.greet([(place.across(*where), tp) for where in ((1, 0), (2, 0), (3, 0), (0, 1))])
    for step in order:
        place.send(
            p_ref.at[:, place.across(step, 1)],
            over_y.at[step],
            y_sem.at[step],
            (place.across(0, 1), tp),
        )
    for step in order:
        loads[step].wait()
        place.arrive(over_y.at[step], y_sem.at[step])

        @pl.loop(0, blocks)
        def _(block, step=step):
            own[step, block] = own[step, block] + over_y[step, block]

        if step == 2:
            place.arrive(over_z.at[3], z_sem.at[3])

            @pl.loop(0, blocks)
            def _(block):
                own[2, block] = own[2, block] + over_z[3, block]

        if step:
            device = (place.across(1 + (step == 2), 0), tp)
            place.send(own.at[step], over_z.at[step], z_sem.at[step], device)
    for step in (2, 1):
        place.arrive(over_z.at[step], z_sem.at[step])

    @pl.loop(0, blocks)
    def _(block):
        total = own[0, block].astype(jnp.float32)
        for step in (1, 2):
            total = total + over_z[step, block].astype(jnp.float32)
        out_ref[block] = total.astype(jnp.bfloat16)

    place.finish()


def scatter_kv(p, ident):
    blocks, ep_size, rows, width = p.shape
    buffer = pltpu.VMEM((4, blocks, rows, width), p.dtype)
    scratch = [buffer, buffer, buffer, (4,), (7,), (4,), (4,)]
    out = jax.ShapeDtypeStruct((blocks, rows, width), p.dtype)
    return reach(scatter_kv_kernel, out, scratch, ident, p, vmem_out=True, mib=24)


SLOTS = 1024


def finish_kernel(*refs):
    partials, gains_ref, rows_ref, experts = refs[:3], refs[3], refs[4], refs[5:10]
    outs, gain_out, rows_out, grads, refs = refs[10:13], refs[13], refs[14], refs[15:18], refs[18:]
    owns, overs_y, overs_z, stages, refs = refs[:3], refs[3:6], refs[6:9], refs[9:11], refs[11:]
    wide, narrow, sums, refs = refs[0], refs[1], refs[2:5], refs[5:]
    own_sem, send_sem, y_sem, z_sem, gain_sem, load_sem, grad_sem, rows_sem, rows_send_sem = refs
    place = Place(send_sem)
    ep, tp = place.ep, place.tp
    count = len(partials)
    total, arrived = stages
    ways = [(ep, place.over_core), (ep, place.over_x)]
    ways += [(place.across(step, 0), tp) for step in (1, 2, 3)]
    ways.append((place.across(0, 1), tp))
    moves = [(number, step) for step in (3, 2, 1, 0) for number in range(count)]
    gain_load = pltpu.make_async_copy(gains_ref, total.at[0], own_sem.at[count, 0])
    gain_load.start()

    def own_copy(number, step):
        return pltpu.make_async_copy(
            partials[number].at[place.across(step, 0)],
            owns[number].at[step],
            own_sem.at[number, step],
        )

    def to_y(number, step):
        return pltpu.make_async_remote_copy(
            src_ref=partials[number].at[place.across(step, 1)],
            dst_ref=overs_y[number].at[step],
            send_sem=send_sem.at[number, step],
            recv_sem=y_sem.at[number, step],
            device_id=(place.across(0, 1), tp),
            device_id_type=MESH_ID,
        )

    def to_z(number, step):
        return pltpu.make_async_remote_copy(
            src_ref=owns[number].at[step],
            dst_ref=overs_z[number].at[step],
            send_sem=send_sem.at[number, 3 + step],
            recv_sem=z_sem.at[number, step],
            device_id=(place.across(1 + (step == 2), 0), tp),
            device_id_type=MESH_ID,
        )

    def gain_copy(number):
        return pltpu.make_async_remote_copy(
            src_ref=total.at[(0, 1, 2, 2, 2, 3)[number]],
            dst_ref=arrived.at[number],
            send_sem=send_sem.at[count, number],
            recv_sem=gain_sem.at[number],
            device_id=ways[number],
            device_id_type=MESH_ID,
        )

    others = [(step, over) for step in range(4) for over in (0, 1)][1:]

    def row_copy(index):
        other = place.across(*others[index])
        return pltpu.make_async_remote_copy(
            src_ref=rows_ref.at[other],
            dst_ref=rows_out.at[ep],
            send_sem=rows_send_sem.at[index],
            recv_sem=rows_sem.at[ep],
            device_id=(other, tp),
            device_id_type=MESH_ID,
        )

    def row_arrival(index):
        other = place.across(*others[index])
        return pltpu.make_async_remote_copy(
            src_ref=rows_ref.at[other],
            dst_ref=rows_out.at[other],
            send_sem=rows_send_sem.at[index],
            recv_sem=rows_sem.at[other],
            device_id=(other, tp),
            device_id_type=MESH_ID,
        )

    own_rows = pltpu.make_async_copy(rows_ref.at[ep], rows_out.at[ep], rows_sem.at[ep])
    own_rows.start()
    for number, step in moves:
        own_copy(number, step).start()
    place.greet(ways[:2] + [(place.across(*other), tp) for other in others])
    gain_load.wait()
    gain_copy(0).start()
    for index in range(len(others)):
        row_copy(index).start()
    for number, step in moves:
        to_y(number, step).start()

    def event(index):
        number, step = moves[index]
        own, over = owns[number], overs_y[number]
        own_copy(number, step).wait()
        to_y(number, step).wait_recv()

        @pl.loop(0, own.shape[1], step=64)
        def _(row):
            some = pl.ds(row, 64)
            own[step, some] = own[step, some] + over[step, some]

        if step == 2:
            to_z(number, 3).wait_recv()

            @pl.loop(0, own.shape[1], step=64)
            def _(row):
                some = pl.ds(row, 64)
                own[2, some] = own[2, some] + overs_z[number][3, some]

        if step:
            to_z(number, step).start()
        if index < 2:
            gain_copy(index).wait_recv()
            total[index + 1] = total[index] + arrived[index]
            for later in (1,) if index == 0 else (2, 3, 4):
                gain_copy(later).start()
        if index == 2:
            for later in (2, 3, 4):
                gain_copy(later).wait_recv()
            total[3] = (total[2] + arrived[2]) + (arrived[3] + arrived[4])
            gain_copy(5).start()

    expert_in, slot_cot, inner, gate_grad, up_grad = experts
    pieces = expert_in.shape[0] // SLOTS
    jobs = ((expert_in, gate_grad), (expert_in, up_grad), (slot_cot, inner))
    steps = pieces * len(jobs)

    def load_copies(pair, piece, parity):
        some = pl.ds(piece * SLOTS, SLOTS)
        return [
            pltpu.make_async_copy(ref.at[some], held.at[parity], load_sem.at[parity, index])
            for index, (ref, held) in enumerate(zip(pair, (wide, narrow)))
        ]

    def grad_copy(job):
        return pltpu.make_async_copy(sums[job], grads[job], grad_sem.at[job])

    def multiply(job, parity):
        into = sums[job]
        left, right = (wide, narrow) if job < 2 else (narrow, wide)
        tile = 512 if into.shape[0] % 512 == 0 else 384

        @pl.loop(0, into.shape[0], step=tile)
        def _(row):
            some = pl.ds(pl.multiple_of(row, tile), tile)
            product = dot_with(left[parity, :, some], right[parity], ROWS_BY_ROWS)

            into[some] += product

    for into in sums:

        @pl.loop(0, into.shape[0], step=64)
        def _(row, into=into):
            into[pl.ds(row, 64)] = jnp.zeros((64, into.shape[1]), jnp.float32)

    @pl.loop(0, steps + 1)
    def _(turn):
        for index in range(len(moves)):

            @pl.when(turn == index)
            def _(index=index):
                event(index)

        for job, pair in enumerate(jobs):

            @pl.when((turn >= job * pieces) & (turn < (job + 1) * pieces))
            def _(job=job, pair=pair):
                for copy in load_copies(pair, turn - job * pieces, turn % 2):
                    copy.start()

        for job, pair in enumerate(jobs):

            @pl.when((turn > job * pieces) & (turn <= (job + 1) * pieces))
            def _(job=job, pair=pair):
                parity = (turn - 1) % 2
                for copy in load_copies(pair, 0, parity):
                    copy.wait()
                multiply(job, parity)

            @pl.when(turn == (job + 1) * pieces)
            def _(job=job):
                grad_copy(job).start()

    for number in range(count):
        own, over, out = owns[number], overs_z[number], outs[number]
        for step in (2, 1):
            to_z(number, step).wait_recv()

        @pl.loop(0, own.shape[1], step=64)
        def _(row, own=own, over=over, out=out):
            some = pl.ds(row, 64)
            sum_of = own[0, some].astype(jnp.float32)
            for step in (1, 2):
                sum_of = sum_of + over[step, some].astype(jnp.float32)
            out[some] = sum_of

    gain_copy(5).wait_recv()
    gain_out[...] = total[3] + arrived[5]
    for job in range(len(jobs)):
        grad_copy(job).wait()
    for number, step in moves:
        to_y(number, step).wait_send()
        if step:
            to_z(number, step).wait_send()
    for number in range(6):
        gain_copy(number).wait_send()
    own_rows.wait()
    for index in range(len(others)):
        row_copy(index).wait_send()
        row_arrival(index).wait_recv()


def finish(partials, gains, rows, expert_in, slot_cot, inner, gate_grad, up_grad, ident):
    count = len(partials)
    buffers = [pltpu.VMEM((4, *p.shape[1:]), p.dtype) for p in partials]
    width, hidden = expert_in.shape[1], inner.shape[1]
    grads = [(width, hidden), (width, hidden), (hidden, width)]
    scratch = buffers * 3
    scratch += [pltpu.VMEM((4, *gains.shape), gains.dtype), pltpu.VMEM((6, *gains.shape), gains.dtype)]
    scratch += [pltpu.VMEM((2, SLOTS, width), jnp.bfloat16), pltpu.VMEM((2, SLOTS, hidden), jnp.bfloat16)]
    scratch += [pltpu.VMEM(shape, jnp.float32) for shape in grads]
    scratch += [(count + 1, 4), (count + 1, 7), (count, 4), (count, 4), (6,), (2, 2), (3,), (8,), (7,)]
    out = [jax.ShapeDtypeStruct(p.shape[1:], jnp.float32) for p in partials]
    out.append(jax.ShapeDtypeStruct(gains.shape, jnp.float32))
    out.append(jax.ShapeDtypeStruct(rows.shape, rows.dtype))
    out += [jax.ShapeDtypeStruct(shape, jnp.float32) for shape in grads]
    operands = (*partials, gains, rows, expert_in, slot_cot, inner, gate_grad, up_grad)
    return reach(
        finish_kernel, out, scratch, ident, *operands, vmem_out=(True,) * 4 + (False,) * 4, mib=58
    )


def on_device(
    inputs,
    cotangent,
    arrangement,
    seq_lengths,
    routes,
    gate_values,
    input_gain,
    query_proj,
    key_projected,
    value_projected,
    query_gain,
    key_gain,
    output_proj,
    expert_gain,
    gate_weight,
    up_weight,
    down_weight,
):
    ep_size = lax.axis_size("ep")
    tp_size = lax.axis_size("tp")
    ep_index = lax.axis_index("ep")
    tp_index = lax.axis_index("tp")
    everyone = ("ep", "tp")
    own_rows, width = inputs.shape
    group_rows = own_rows * tp_size
    row_block = own_rows // ep_size
    token_total = arrangement.shape[0]
    expert_count = ep_size * tp_size
    capacity = 2 * own_rows * TOP // expert_count
    heads = query_proj.shape[1] // HEAD
    known = (ep_size, tp_size) == (8, 4)
    expert = (ep_index * tp_size + tp_index).astype(jnp.int32)[None]

    table = arrangement.reshape(ep_size, tp_size, ep_size, row_block)
    leaving_from = lax.dynamic_index_in_dim(table, tp_index, 1, keepdims=False)
    leaving_from = lax.dynamic_index_in_dim(leaving_from, ep_index, 1, keepdims=False)
    send_index = leaving_from - (ep_index * group_rows + tp_index * own_rows)
    mover = (
        send_index.reshape(-1)[:, None] == jnp.arange(own_rows, dtype=jnp.int32)[None, :]
    ).astype(jnp.bfloat16)

    def to_places(rows):
        return dot(mover, rows).astype(jnp.bfloat16).reshape(ep_size, row_block, width)

    def exchange(rows):
        return lax.all_to_all(rows, "ep", split_axis=0, concat_axis=0, tiled=True)

    def to_given(moved):
        return dot_with(mover, moved, ROWS_BY_ROWS)

    def group_sorted(rows, ident):
        blocks = rows.reshape(ep_size, row_block, width)
        if known:
            gathered = gather_group(blocks, tp_size, ident)
        else:
            gathered = lax.all_gather(blocks, "tp", axis=1)
        return gathered.reshape(group_rows, width)

    def sum_group(rows, ident):
        blocks = rows.astype(jnp.bfloat16).reshape(ep_size, tp_size, row_block, width)
        if known:
            return scatter_group(blocks, ident).reshape(own_rows, width)
        placed = jnp.swapaxes(blocks, 0, 1).reshape(group_rows, width)
        own = lax.psum_scatter(placed, "tp", scatter_dimension=0, tiled=True)
        return own.astype(jnp.float32)

    leaving_x, leaving_cot = to_places(inputs), to_places(cotangent)
    if known:
        cot_all = lax.all_gather(leaving_cot, everyone, axis=0, tiled=True)
        cot_all = cot_all.reshape(ep_size, tp_size, ep_size, row_block, width)
        own_cot = lax.dynamic_index_in_dim(cot_all, tp_index, 1, keepdims=False)
        own_cot = lax.dynamic_index_in_dim(own_cot, ep_index, 1, keepdims=False)
        group_x = enter(leaving_x, tp_size, 1)
        own_inputs = lax.dynamic_index_in_dim(group_x, tp_index, 1, keepdims=False)
    else:
        own_inputs, own_cot = exchange(leaving_x), exchange(leaving_cot)
        group_x = lax.all_gather(own_inputs, "tp", axis=1)
        cot_all = lax.all_gather(own_cot.reshape(own_rows, width), everyone, axis=0, tiled=True)
    own_inputs, own_cot = own_inputs.reshape(own_rows, width), own_cot.reshape(own_rows, width)
    group_x = group_x.reshape(group_rows, width)
    meta_own = jnp.concatenate([routes.astype(jnp.float32).T, gate_values.T], axis=0)

    query_given = lax.dynamic_index_in_dim(table, ep_index, 0, keepdims=False)
    query_given = jnp.swapaxes(query_given, 0, 1).reshape(group_rows)
    query_first = seq_starts(query_given, seq_lengths)
    cosine, sine = rope_tables(query_given - query_first, HEAD)
    key_given = jnp.transpose(table, (2, 1, 0, 3)).reshape(token_total)
    by_step = (-1, QUERY_TOKENS)
    given_steps, first_steps = query_given.reshape(by_step), query_first.reshape(by_step)
    lowest = jnp.min(first_steps, axis=1) // KEY_SPAN
    highest = jnp.max(given_steps, axis=1) // KEY_SPAN + 1
    open_low = (jnp.max(first_steps, axis=1) + KEY_SPAN - 1) // KEY_SPAN
    open_low = jnp.minimum(open_low, highest)
    open_high = jnp.clip((jnp.min(given_steps, axis=1) + 1) // KEY_SPAN, open_low, highest)
    bounds = jnp.stack([lowest, open_low, open_high, highest]).astype(jnp.int32)
    ask = jnp.stack([query_given, query_first], axis=1)
    ask_rows = jnp.stack(
        [jnp.tile(given_steps, (1, heads)), jnp.tile(first_steps, (1, heads))], axis=1
    )

    normed_in, query_raw, query_rows, key_raw, kv_rows = front(
        group_x, input_gain, query_proj, key_projected, value_projected,
        query_gain, key_gain, cosine, sine,
    )
    kv_blocks = kv_rows.reshape(expert_count, row_block, 2 * HEAD)
    if known:
        kv_all = gather_kv(kv_blocks, ep_size, 2)
    else:
        kv_all = lax.all_gather(kv_blocks, "ep", axis=1)
    kv_all = kv_all.reshape(token_total, 2 * HEAD)
    pairs = group_rows * heads * 1536
    exact, out_rows, lse = attend_forward(
        bounds, query_rows, ask, key_given[None], kv_all, pairs
    )
    branch = sum_group(dot(out_rows, output_proj), 5)
    hidden = own_inputs.astype(jnp.float32) + branch
    mid_scale = inverse_root(hidden)
    normed_mid = (hidden * mid_scale * expert_gain).astype(jnp.bfloat16)

    experts = (gate_weight, up_weight, down_weight, capacity)
    if known:
        results = expert_all(normed_mid, meta_own, cot_all, *experts, 3)
    else:
        mid_all = lax.all_gather(normed_mid, everyone, axis=0, tiled=True)
        meta = lax.all_gather(meta_own, everyone, axis=0)
        results = list(expert_pass(expert, meta, mid_all, cot_all, *experts))
        results[1] = jnp.transpose(
            results[1].reshape(ep_size, tp_size, ep_size, row_block, width), (2, 1, 0, 3, 4)
        )
    mid_partial, out_partial, expert_in, slot_cot, inner, gate_grad, up_grad = results
    def sum_over_all(partial):
        return lax.psum_scatter(partial, everyone, scatter_dimension=0, tiled=True)

    if known:
        mid_grad = scatter_all(mid_partial, expert_count, 4)
    else:
        mid_grad = sum_over_all(mid_partial).astype(jnp.float32)
    mid_grad, out_partial = lax.optimization_barrier((mid_grad, out_partial))
    mixed = sum_over_all(out_partial.reshape(token_total, width))

    mid_hat = hidden * mid_scale
    grad_expert_gain = jnp.sum(mid_grad * mid_hat, axis=0)
    mid_scaled = mid_grad * expert_gain
    hidden_grad = own_cot.astype(jnp.float32) + mid_scale * (
        mid_scaled - mid_hat * jnp.mean(mid_scaled * mid_hat, axis=-1, keepdims=True)
    )
    branch_grad = group_sorted(hidden_grad.astype(jnp.bfloat16), 6)
    out_grad = dot_with(branch_grad, output_proj, COLS_BY_COLS).astype(jnp.bfloat16)
    query_grad, kv_grad = attend_backward(
        bounds, query_rows, out_grad, exact, lse, ask_rows, key_given[None], kv_all, pairs
    )
    kv_grad = kv_grad.reshape(expert_count, ep_size, row_block, 2 * HEAD)
    if known:
        kv_own = scatter_kv(kv_grad, 7)
    else:
        kv_own = lax.psum_scatter(kv_grad, "ep", scatter_dimension=1)
    kv_own = kv_own.reshape(group_rows, 2 * HEAD)
    value_grad = kv_own[:, HEAD:]
    raw_query_grad, grad_query_gain = head_back(query_raw, query_grad, query_gain, cosine, sine)
    raw_key_grad, grad_key_gain = head_back(key_raw, kv_own[:, :HEAD], key_gain, cosine, sine)
    normed_grad = (
        dot_with(raw_query_grad, query_proj, COLS_BY_COLS)
        + dot_with(raw_key_grad, key_projected, COLS_BY_COLS)
        + dot_with(value_grad, value_projected, COLS_BY_COLS)
    )
    normed_grad = sum_group(normed_grad, 8)
    own_float = own_inputs.astype(jnp.float32)
    in_scale = inverse_root(own_float)
    in_hat = own_float * in_scale
    grad_input_gain = jnp.sum(normed_grad * in_hat, axis=0)
    in_scaled = normed_grad * input_gain
    input_rows = hidden_grad + in_scale * (
        in_scaled - in_hat * jnp.mean(in_scaled * in_hat, axis=-1, keepdims=True)
    )
    leaving = jnp.concatenate([input_rows, hidden], axis=1).astype(jnp.bfloat16)
    leaving = leaving.reshape(ep_size, row_block, 2 * width)

    weights = [
        dot_with(branch_grad, out_rows, ROWS_BY_ROWS),
        dot_with(normed_in, raw_query_grad, ROWS_BY_ROWS),
        dot_with(normed_in, jnp.concatenate([raw_key_grad, value_grad], axis=1), ROWS_BY_ROWS),
    ]
    weights = [array.astype(jnp.bfloat16).reshape(ep_size, -1, array.shape[1]) for array in weights]
    gains = jnp.concatenate(
        [grad_input_gain, grad_expert_gain, grad_query_gain[0], grad_key_gain[0]]
    )
    if known:
        experts = (expert_in, slot_cot, inner, gate_grad, up_grad)
        results = finish(weights, gains.reshape(-1, HEAD), leaving, *experts, 10)
        grad_output, grad_query, grad_kv, gains, leaving = results[:5]
        grad_gate, grad_up, grad_down = results[5:]
        gains = gains.reshape(-1)
    else:
        grad_output, grad_query, grad_kv = [
            lax.psum_scatter(array, "ep", scatter_dimension=0).astype(jnp.float32)
            for array in weights
        ]
        gains, leaving = lax.psum(gains, everyone), exchange(leaving)
        grad_gate = dot_with(expert_in, gate_grad, ROWS_BY_ROWS)
        grad_up = dot_with(expert_in, up_grad, ROWS_BY_ROWS)
        grad_down = dot_with(inner, slot_cot, ROWS_BY_ROWS)
    mixed, gains = lax.optimization_barrier((mixed, gains))
    leaving = leaving.reshape(own_rows, 2 * width)
    grad_inputs = to_given(leaving[:, :width])
    layer_out = leaving[:, width:].astype(jnp.float32) + mixed.astype(jnp.float32)
    layer_out = to_given(layer_out.astype(jnp.bfloat16)).astype(jnp.bfloat16)
    grad_output = jnp.transpose(grad_output)
    cuts = (width, 2 * width, 2 * width + HEAD)
    return (
        layer_out,
        grad_inputs,
        grad_query,
        grad_kv[:, :HEAD],
        grad_kv[:, HEAD:],
        grad_output,
        gains[: cuts[0]],
        gains[cuts[1] : cuts[2]],
        gains[cuts[2] :],
        gains[cuts[0] : cuts[1]],
        grad_gate[None],
        grad_up[None],
        grad_down[None],
    )


def solution(mesh):
    split = P(("ep", "tp"), None)
    experts = P(("ep", "tp"), None, None)
    columns = P(None, "tp")
    return jax.shard_map(
        on_device,
        mesh=mesh,
        in_specs=(
            split, split, P(), P(), split, split, P(), columns, columns, columns,
            P(), P(), P("tp", None), P(), experts, experts, experts,
        ),
        out_specs=(
            split, split, P("ep", "tp"), P("ep", "tp"), P("ep", "tp"), P("tp", "ep"),
            P(), P(), P(), P(), experts, experts, experts,
        ),
        check_vma=False,
    )
```

```python
import functools
import math

import jax
import jax.numpy as jnp
from jax import lax
from jax.experimental import pallas as pl
from jax.experimental.pallas import tpu as pltpu
from jax.sharding import PartitionSpec as P

TOP = 8
EPSILON = 1e-06
ROPE_BASE = 1000000.0
KEY_SPAN = 512
QUERY_TOKENS = 64
HEAD = 128
ROW_TILE = 256
MIB = 1 << 20
LOG2E = math.log2(math.e)
ROWS_BY_ROWS = (((0,), (0,)), ((), ()))
COLS_BY_COLS = (((1,), (1,)), ((), ()))


def dot(left, right):
    return jnp.dot(left, right, preferred_element_type=jnp.float32)


def dot_with(left, right, dims):
    return lax.dot_general(left, right, dims, preferred_element_type=jnp.float32)


def cost(flops, moved, transcendentals=0):
    return pl.CostEstimate(
        flops=int(flops), bytes_accessed=int(moved), transcendentals=int(transcendentals)
    )


def params(mib):
    return pltpu.CompilerParams(
        dimension_semantics=("arbitrary",), vmem_limit_bytes=mib * MIB
    )


def whole(shape, single=True):
    rank = len(shape)
    if single:
        return pl.BlockSpec(shape, lambda *ids: (0,) * rank, pipeline_mode=pl.Buffered(1))
    return pl.BlockSpec(shape, lambda *ids: (0,) * rank)


def rows_of(shape):
    rank = len(shape)
    return pl.BlockSpec(shape, lambda i, *ids: (i,) + (0,) * (rank - 1))


def rope_tables(positions, head_dim):
    freqs = ROPE_BASE ** (-jnp.arange(0, head_dim, 2, dtype=jnp.float32) / head_dim)
    angles = positions.astype(jnp.float32)[:, None] * freqs[None, :]
    cosine, sine = jnp.cos(angles), jnp.sin(angles)
    return (
        jnp.concatenate([cosine, cosine], axis=-1),
        jnp.concatenate([-sine, sine], axis=-1),
    )


def seq_starts(given, seq_lengths):
    ends = jnp.cumsum(seq_lengths)
    passed = given[:, None] >= ends[None, :]
    return jnp.sum(jnp.where(passed, seq_lengths[None, :], 0), axis=1)


def inverse_root(values):
    return lax.rsqrt(jnp.mean(values * values, axis=-1, keepdims=True) + EPSILON)


def front_kernel(
    x_ref, gain_ref, wq_ref, wk_ref, wv_ref, qg_ref, kg_ref, cos_ref, sin_ref,
    normed_ref, qraw_ref, q_ref, kraw_ref, kv_ref,
):
    x = x_ref[...].astype(jnp.float32)
    normed = (x * inverse_root(x) * gain_ref[...]).astype(jnp.bfloat16)
    normed_ref[...] = normed
    cosine, sine = cos_ref[...], sin_ref[...]

    def prepare(raw, gain):
        values = raw * inverse_root(raw) * gain
        return (values * cosine + pltpu.roll(values, HEAD // 2, 1) * sine).astype(jnp.bfloat16)

    raw = dot(normed, wq_ref[...])
    qraw_ref[...] = raw
    for head in range(raw.shape[1] // HEAD):
        part = slice(head * HEAD, (head + 1) * HEAD)
        q_ref[:, part] = prepare(raw[:, part], qg_ref[...])
    raw = dot(normed, wk_ref[...])
    kraw_ref[...] = raw
    kv_ref[:, :HEAD] = prepare(raw, kg_ref[...])
    kv_ref[:, HEAD:] = dot(normed, wv_ref[...]).astype(jnp.bfloat16)


def front(group_x, input_gain, wq, wk, wv, query_gain, key_gain, cosine, sine):
    rows, width = group_x.shape
    cols = wq.shape[1]
    tile = min(ROW_TILE, rows)
    out = [
        ((rows, width), jnp.bfloat16),
        ((rows, cols), jnp.float32),
        ((rows, cols), jnp.bfloat16),
        ((rows, HEAD), jnp.float32),
        ((rows, 2 * HEAD), jnp.bfloat16),
    ]
    return pl.pallas_call(
        front_kernel,
        grid=(rows // tile,),
        in_specs=[
            rows_of((tile, width)),
            whole((1, width)),
            whole(wq.shape),
            whole(wk.shape),
            whole(wv.shape),
            whole((1, HEAD)),
            whole((1, HEAD)),
            rows_of((tile, HEAD)),
            rows_of((tile, HEAD)),
        ],
        out_specs=[rows_of((tile, shape[1])) for shape, kind in out],
        out_shape=[jax.ShapeDtypeStruct(shape, kind) for shape, kind in out],
        compiler_params=params(40),
        cost_estimate=cost(2 * rows * width * (cols + 2 * HEAD), 20 * MIB),
        name="front",
    )(
        group_x,
        input_gain[None],
        wq,
        wk,
        wv,
        query_gain[None],
        key_gain[None],
        cosine,
        sine,
    )


def stack_heads(block):
    heads = block.shape[1] // HEAD
    return jnp.concatenate(
        [block[:, head * HEAD : (head + 1) * HEAD] for head in range(heads)], axis=0
    )


def attend_forward_kernel(
    bounds_ref, q_ref, ask_ref, key_given_ref, kv_ref, exact_ref, out_ref, lse_ref, acc, tot
):
    step = pl.program_id(0)
    tokens, cols = q_ref.shape
    heads = cols // HEAD
    query = stack_heads(q_ref[...])
    ask = ask_ref[...]
    last = jnp.concatenate([ask[:, 0:1]] * heads, axis=0)
    first = jnp.concatenate([ask[:, 1:2]] * heads, axis=0)
    acc[...] = jnp.zeros_like(acc)
    tot[...] = jnp.zeros_like(tot)

    def visit(span, masked):
        offset = pl.multiple_of(span * KEY_SPAN, KEY_SPAN)
        keys = kv_ref[pl.ds(offset, KEY_SPAN), :HEAD]
        values = kv_ref[pl.ds(offset, KEY_SPAN), HEAD:]
        scores = dot_with(query, keys, COLS_BY_COLS)
        weights = jnp.exp2(scores * (HEAD**-0.5 * LOG2E))
        if masked:
            key_given = key_given_ref[:, pl.ds(offset, KEY_SPAN)]
            weights = jnp.where((key_given <= last) & (key_given >= first), weights, 0.0)
        part = weights[:, :HEAD]
        for chunk in range(1, KEY_SPAN // HEAD):
            part = part + weights[:, chunk * HEAD : (chunk + 1) * HEAD]
        tot[...] += part
        acc[...] += dot(weights.astype(jnp.bfloat16), values)

    lowest, open_low = bounds_ref[0, step], bounds_ref[1, step]
    open_high, highest = bounds_ref[2, step], bounds_ref[3, step]

    @pl.loop(lowest, open_low)
    def _(span):
        visit(span, True)

    @pl.loop(open_low, open_high)
    def _(span):
        visit(span, False)

    @pl.loop(open_high, highest)
    def _(span):
        visit(span, True)

    total = tot[...]
    exact = acc[...] / jnp.sum(total, axis=1, keepdims=True)
    for head in range(heads):
        rows = exact[head * tokens : (head + 1) * tokens]
        exact_ref[:, head * HEAD : (head + 1) * HEAD] = rows
        out_ref[:, head * HEAD : (head + 1) * HEAD] = rows.astype(jnp.bfloat16)
    lse_ref[0] = jnp.log2(jnp.sum(total.T, axis=0, keepdims=True))


def attend_forward(bounds, query, ask, key_given, kv, pairs):
    rows, cols = query.shape
    heads = cols // HEAD
    steps = rows // QUERY_TOKENS
    stacked = heads * QUERY_TOKENS
    return pl.pallas_call(
        attend_forward_kernel,
        grid_spec=pltpu.PrefetchScalarGridSpec(
            num_scalar_prefetch=1,
            grid=(steps,),
            in_specs=[
                rows_of((QUERY_TOKENS, cols)),
                rows_of((QUERY_TOKENS, 2)),
                whole(key_given.shape),
                whole(kv.shape),
            ],
            out_specs=[
                rows_of((QUERY_TOKENS, cols)),
                rows_of((QUERY_TOKENS, cols)),
                rows_of((1, 1, stacked)),
            ],
            scratch_shapes=[
                pltpu.VMEM((stacked, HEAD), jnp.float32),
                pltpu.VMEM((stacked, HEAD), jnp.float32),
            ],
        ),
        out_shape=[
            jax.ShapeDtypeStruct((rows, cols), jnp.float32),
            jax.ShapeDtypeStruct((rows, cols), jnp.bfloat16),
            jax.ShapeDtypeStruct((steps, 1, stacked), jnp.float32),
        ],
        compiler_params=params(48),
        cost_estimate=cost(8 * pairs * HEAD, 16 * MIB, pairs),
        name="attend_forward",
    )(bounds, query, ask, key_given, kv)


def attend_backward_kernel(
    bounds_ref, q_ref, grad_ref, exact_ref, lse_ref, ask_ref, key_given_ref, kv_ref,
    dq_ref, rounded_ref, dkv_ref, acc,
):
    step = pl.program_id(0)
    tokens, cols = q_ref.shape
    heads = cols // HEAD

    @pl.when(step == 0)
    def _():
        dkv_ref[...] = jnp.zeros_like(dkv_ref)

    query = stack_heads(q_ref[...])
    grad = stack_heads(grad_ref[...])
    product = grad.astype(jnp.float32) * stack_heads(exact_ref[...])
    delta = jnp.sum(product.T, axis=0, keepdims=True)
    lse = lse_ref[0]
    last, first = ask_ref[0, 0:1, :], ask_ref[0, 1:2, :]
    acc[...] = jnp.zeros_like(acc)

    def visit(span, masked):
        offset = pl.multiple_of(span * KEY_SPAN, KEY_SPAN)
        place = pl.ds(offset, KEY_SPAN)
        keys = kv_ref[place, :HEAD]
        values = kv_ref[place, HEAD:]
        scores = dot_with(keys, query, COLS_BY_COLS)
        probs = jnp.exp2(scores * (HEAD**-0.5 * LOG2E) - lse)
        if masked:
            key_given = jnp.broadcast_to(key_given_ref[:, place], (8, KEY_SPAN)).T[:, 0:1]
            probs = jnp.where((key_given <= last) & (key_given >= first), probs, 0.0)
        prob_grad = dot_with(values, grad, COLS_BY_COLS)
        score_grad = (probs * (prob_grad - delta)).astype(jnp.bfloat16)
        dkv_ref[place, HEAD:] += dot(probs.astype(jnp.bfloat16), grad)
        dkv_ref[place, :HEAD] += dot(score_grad, query) * (HEAD**-0.5)
        acc[...] += dot_with(score_grad, keys, ROWS_BY_ROWS)

    lowest, open_low = bounds_ref[0, step], bounds_ref[1, step]
    open_high, highest = bounds_ref[2, step], bounds_ref[3, step]

    @pl.loop(lowest, open_low)
    def _(span):
        visit(span, True)

    @pl.loop(open_low, open_high)
    def _(span):
        visit(span, False)

    @pl.loop(open_high, highest)
    def _(span):
        visit(span, True)

    for head in range(heads):
        dq_ref[:, head * HEAD : (head + 1) * HEAD] = acc[
            head * tokens : (head + 1) * tokens
        ] * (HEAD**-0.5)

    @pl.when(step == pl.num_programs(0) - 1)
    def _():
        @pl.loop(0, dkv_ref.shape[0], step=KEY_SPAN)
        def _(row):
            place = pl.ds(row, KEY_SPAN)
            rounded_ref[place] = dkv_ref[place].astype(jnp.bfloat16)


def attend_backward(bounds, query, grad, exact, lse, ask_rows, key_given, kv, pairs):
    rows, cols = query.shape
    heads = cols // HEAD
    steps = rows // QUERY_TOKENS
    stacked = heads * QUERY_TOKENS
    return pl.pallas_call(
        attend_backward_kernel,
        grid_spec=pltpu.PrefetchScalarGridSpec(
            num_scalar_prefetch=1,
            grid=(steps,),
            in_specs=[
                rows_of((QUERY_TOKENS, cols)),
                rows_of((QUERY_TOKENS, cols)),
                rows_of((QUERY_TOKENS, cols)),
                rows_of((1, 1, stacked)),
                rows_of((1, 2, stacked)),
                whole(key_given.shape),
                whole(kv.shape),
            ],
            out_specs=[rows_of((QUERY_TOKENS, cols)), whole(kv.shape)],
            scratch_shapes=[
                pltpu.VMEM(kv.shape, jnp.float32),
                pltpu.VMEM((stacked, HEAD), jnp.float32),
            ],
        ),
        out_shape=[
            jax.ShapeDtypeStruct((rows, cols), jnp.float32),
            jax.ShapeDtypeStruct(kv.shape, jnp.bfloat16),
        ],
        compiler_params=params(56),
        cost_estimate=cost(20 * pairs * HEAD, 32 * MIB, pairs),
        name="attend_backward",
    )(bounds, query, grad, exact, lse, ask_rows, key_given, kv)


def selection(meta, expert, capacity):
    tokens = meta.shape[1]
    weight = jnp.sum(jnp.where(meta[:TOP] == expert, meta[TOP : 2 * TOP], 0.0), axis=0, keepdims=True)
    member = jnp.where(weight > 0.0, 1.0, 0.0)
    earlier = lax.broadcasted_iota(jnp.int32, (tokens, tokens), 0)
    later = lax.broadcasted_iota(jnp.int32, (tokens, tokens), 1)
    before = jnp.where(earlier < later, 1.0, 0.0).astype(jnp.bfloat16)
    rank = dot(jnp.broadcast_to(member, (16, tokens)).astype(jnp.bfloat16), before)[0:1]
    rank = jnp.where(weight > 0.0, rank, -1.0).astype(jnp.int32)
    hit = lax.broadcasted_iota(jnp.int32, (capacity, tokens), 0) == rank
    gate = jnp.sum(jnp.where(hit, weight, 0.0), axis=1, keepdims=True)
    return jnp.where(hit, 1.0, 0.0).astype(jnp.bfloat16), gate


def expert_kernel(
    expert_ref, meta_ref, x_ref, c_ref, wg_ref, wu_ref, wd_ref,
    mid_ref, out_ref, xs_ref, cs_ref, inner_ref, gg_ref, ug_ref,
):
    blocks, _, tokens = meta_ref.shape
    capacity = xs_ref.shape[0] // blocks
    expert = expert_ref[0].astype(jnp.float32)
    picks, gates = [], []
    for block in range(blocks):
        rows = slice(block * tokens, (block + 1) * tokens)
        slots = slice(block * capacity, (block + 1) * capacity)
        pick, gate = selection(meta_ref[block], expert, capacity)
        picks.append(pick)
        gates.append(gate)
        xs_ref[slots] = dot(pick, x_ref[rows]).astype(jnp.bfloat16)
        cs_ref[slots] = (dot(pick, c_ref[rows]) * gate).astype(jnp.bfloat16)
    gate_part = dot(xs_ref[...], wg_ref[0])
    up_part = dot(xs_ref[...], wu_ref[0])
    inner_grad = dot_with(cs_ref[...], wd_ref[0], COLS_BY_COLS)
    gate_sig = jax.nn.sigmoid(gate_part)
    activated = gate_part * gate_sig
    inner = (activated * up_part).astype(jnp.bfloat16)
    inner_ref[...] = inner
    gate_grad = (inner_grad * up_part * gate_sig * (1.0 + gate_part * (1.0 - gate_sig))).astype(
        jnp.bfloat16
    )
    up_grad = (inner_grad * activated).astype(jnp.bfloat16)
    gg_ref[...] = gate_grad
    ug_ref[...] = up_grad
    slot_grad = dot_with(gate_grad, wg_ref[0], COLS_BY_COLS)
    slot_grad = (slot_grad + dot_with(up_grad, wu_ref[0], COLS_BY_COLS)).astype(jnp.bfloat16)
    for block in range(blocks):
        rows = slice(block * tokens, (block + 1) * tokens)
        slots = slice(block * capacity, (block + 1) * capacity)
        mid_ref[rows] = dot_with(picks[block], slot_grad[slots], ROWS_BY_ROWS).astype(
            jnp.bfloat16
        )
    result = dot(inner, wd_ref[0]).astype(jnp.bfloat16).astype(jnp.float32)
    for block in range(blocks):
        rows = slice(block * tokens, (block + 1) * tokens)
        slots = slice(block * capacity, (block + 1) * capacity)
        scaled = (result[slots] * gates[block]).astype(jnp.bfloat16)
        out_ref[rows] = dot_with(picks[block], scaled, ROWS_BY_ROWS).astype(jnp.bfloat16)


def expert_pass(expert, meta, x_all, c_all, gate_w, up_w, down_w, capacity):
    blocks, lines, tokens = meta.shape
    width, hidden = gate_w.shape[1:]
    per = max(1, 512 // tokens)
    total = blocks * capacity
    slots = per * capacity
    shapes = [(blocks * tokens, width)] * 2 + [(total, width)] * 2 + [(total, hidden)] * 3
    return pl.pallas_call(
        expert_kernel,
        grid_spec=pltpu.PrefetchScalarGridSpec(
            num_scalar_prefetch=1,
            grid=(blocks // per,),
            in_specs=[
                rows_of((per, lines, tokens)),
                rows_of((per * tokens, width)),
                rows_of((per * tokens, width)),
                whole(gate_w.shape),
                whole(up_w.shape),
                whole(down_w.shape),
            ],
            out_specs=[rows_of((per * tokens, width))] * 2
            + [rows_of((slots, width))] * 2
            + [rows_of((slots, hidden))] * 3,
        ),
        out_shape=[jax.ShapeDtypeStruct(shape, jnp.bfloat16) for shape in shapes],
        compiler_params=params(56),
        cost_estimate=cost(10 * total * width * hidden, 150 * MIB, total * hidden),
        name="expert_pass",
    )(expert, meta, x_all, c_all, gate_w, up_w, down_w)


def head_back_kernel(raw_ref, grad_ref, gain_ref, cos_ref, sin_ref, out_ref, gain_grad_ref):
    @pl.when(pl.program_id(0) == 0)
    def _():
        gain_grad_ref[...] = jnp.zeros_like(gain_grad_ref)

    cosine, sine, gain = cos_ref[...], sin_ref[...], gain_ref[...]
    for head in range(raw_ref.shape[1] // HEAD):
        part = slice(head * HEAD, (head + 1) * HEAD)
        raw = raw_ref[:, part]
        grad = grad_ref[:, part].astype(jnp.float32)
        back = grad * cosine - pltpu.roll(grad, HEAD // 2, 1) * sine
        inverse = inverse_root(raw)
        hat = raw * inverse
        gain_grad_ref[...] += jnp.sum(back * hat, axis=0, keepdims=True)
        scaled = back * gain
        out_ref[:, part] = (
            inverse * (scaled - hat * jnp.mean(scaled * hat, axis=-1, keepdims=True))
        ).astype(jnp.bfloat16)


def head_back(raw, grad, gain, cosine, sine):
    rows, cols = raw.shape
    tile = min(ROW_TILE, rows)
    return pl.pallas_call(
        head_back_kernel,
        grid=(rows // tile,),
        in_specs=[
            rows_of((tile, cols)),
            rows_of((tile, cols)),
            whole((1, HEAD)),
            rows_of((tile, HEAD)),
            rows_of((tile, HEAD)),
        ],
        out_specs=[rows_of((tile, cols)), whole((1, HEAD))],
        out_shape=[
            jax.ShapeDtypeStruct((rows, cols), jnp.bfloat16),
            jax.ShapeDtypeStruct((1, HEAD), jnp.float32),
        ],
        compiler_params=params(24),
        cost_estimate=cost(rows * cols * 20, rows * cols * 10),
        name="head_back",
    )(raw, grad, gain[None], cosine, sine)


MESH_ID = pl.DeviceIdType.MESH


class Place:
    def __init__(self, send_sem, tp_size=4, nearest=False):
        self.tp_size, self.send_sem, self.sent = tp_size, send_sem, []
        self.nearest = nearest
        self.ep, self.tp = lax.axis_index("ep"), lax.axis_index("tp")
        self.z, self.y, self.x, self.core = self.ep // 2, self.ep % 2, self.tp // 2, self.tp % 2
        self.edge = 1 - (self.z + self.z // 2) % 2
        self.over_x = self.tp + 2 - 4 * self.x
        self.over_core = self.tp + 1 - 2 * self.core
        self.over_both = self.over_core + 2 - 4 * self.x

    def level(self, step):
        levels = [self.z, self.z + 1 - 2 * (self.z % 2), (self.z + 2) % 4, 3 - self.z]
        if self.nearest and step > 1:
            return self.edge * levels[step] + (1 - self.edge) * levels[5 - step]
        return levels[step]

    def across(self, step, over_y):
        return self.level(step) * 2 + self.y + over_y * (1 - 2 * self.y)

    def device(self, step, first, second, other=0):
        core = self.core + other * (1 - 2 * self.core)
        over_y = first * (1 - core) + second * core
        over_x = first * core + second * (1 - core)
        x = self.x + over_x * (1 - 2 * self.x)
        return self.across(step, over_y), x * 2 + core

    def slot(self, *where):
        ep, tp = self.device(*where)
        return ep * self.tp_size + tp

    def greet(self, partners):
        barrier = pltpu.get_barrier_semaphore()
        for partner in partners:
            pl.semaphore_signal(barrier, inc=1, device_id=partner, device_id_type=MESH_ID)
        pl.semaphore_wait(barrier, len(partners))

    def greet_all_ways(self):
        partners = [(1, 0, 0), (2, 0, 0), (3, 0, 0), (0, 1, 0), (0, 0, 1), (0, 0, 0, 1)]
        self.greet([self.device(*partner) for partner in partners])

    def send(self, src, dst, sem, device):
        copy = pltpu.make_async_remote_copy(
            src_ref=src,
            dst_ref=dst,
            send_sem=self.send_sem.at[len(self.sent)],
            recv_sem=sem,
            device_id=device,
            device_id_type=MESH_ID,
        )
        copy.start()
        self.sent.append(copy)

    def arrive(self, dst, sem):
        pltpu.make_async_remote_copy(
            src_ref=dst,
            dst_ref=dst,
            send_sem=self.send_sem.at[0],
            recv_sem=sem,
            device_id=(self.ep, self.over_core),
            device_id_type=MESH_ID,
        ).wait_recv()

    def finish(self):
        for copy in self.sent:
            copy.wait_send()


def reach(kernel, out, scratch, ident, *operands, vmem_out=False, mib=None):
    dma = [kind if not isinstance(kind, tuple) else pltpu.SemaphoreType.DMA(kind) for kind in scratch]
    spaces = vmem_out if isinstance(vmem_out, tuple) else jax.tree.map(lambda _: vmem_out, out)
    out_specs = jax.tree.map(
        lambda vmem: pl.BlockSpec(memory_space=pltpu.VMEM if vmem else pl.ANY), spaces
    )
    return pl.pallas_call(
        kernel,
        in_specs=[pl.BlockSpec(memory_space=pl.ANY)] * len(operands),
        out_specs=out_specs,
        out_shape=out,
        scratch_shapes=dma,
        compiler_params=pltpu.CompilerParams(
            collective_id=ident,
            has_side_effects=True,
            vmem_limit_bytes=(mib or 16) * MIB,
        ),
        cost_estimate=cost(1, 1),
        name=kernel.__name__ if not isinstance(kernel, functools.partial) else kernel.func.__name__,
    )(*operands)


NEAR = ((0, 0), (1, 0), (0, 1), (2, 0), (1, 1), (3, 0), (2, 1), (3, 1))
ORDER = ((0,0,0),(1,0,0),(0,0,1),(0,1,0),(2,0,0),(1,0,1),(1,1,0),(0,1,1),(3,0,0),(2,1,0),(2,0,1),(1,1,1),(3,1,0),(3,0,1),(2,1,1),(3,1,1))


def expert_all_kernel(
    x_ref, m_ref, c_ref, wg_ref, wu_ref, wd_ref,
    all_ref, mid_ref, out_ref, xs_ref, cs_ref, inner_ref, gg_ref, ug_ref,
    lines, wg, wu, wd, pair, xb, cb, midb, outb, xsb, csb, innerb, ggb, ugb,
    w_sem, own_sem, z_sem, z_line_sem, send_sem, line_send_sem, recv_sem, line_sem,
    load_sem, store_sem,
):
    place = Place(send_sem, nearest=True)
    rows = x_ref.shape[0]
    capacity = xsb.shape[1] // 2
    expert = (place.ep * 4 + place.tp).astype(jnp.float32)
    count = len(ORDER)
    slots = {(*where, other): place.slot(*where, other) for where in ORDER for other in (0, 1)}
    first, second, across = place.device(0, 1, 0), place.device(0, 0, 1), place.device(0, 0, 0, 1)

    def part(ref, slot):
        return ref.at[pl.ds(slot * rows, rows)]

    weights = [
        pltpu.make_async_copy(ref, held, w_sem.at[number])
        for number, (ref, held) in enumerate(((wg_ref, wg), (wu_ref, wu), (wd_ref, wd)))
    ]
    mine = slots[0, 0, 0, 0]
    own = [
        pltpu.make_async_copy(x_ref, part(all_ref, mine), own_sem.at[0]),
        pltpu.make_async_copy(m_ref, lines.at[mine], own_sem.at[1]),
    ]
    for copy in own + weights:
        copy.start()
    place.greet_all_ways()
    for copy in own:
        copy.wait()

    def copies(slot, device, rows_sem, words_sem):
        some = dict(device_id=device, device_id_type=MESH_ID)
        return (
            pltpu.make_async_remote_copy(
                src_ref=lines.at[slot], dst_ref=lines.at[slot],
                send_sem=words_sem, recv_sem=line_sem.at[slot], **some,
            ),
            pltpu.make_async_remote_copy(
                src_ref=part(all_ref, slot), dst_ref=part(all_ref, slot),
                send_sem=rows_sem, recv_sem=recv_sem.at[slot], **some,
            ),
        )

    def along_z(step):
        level, z = place.level(step), place.z
        up = (z < 3) if step == 0 else (level < z) & (z < 3)
        down = (z > 0) if step == 0 else (level > z) & (z > 0)
        return ((up, 2 * step, (place.ep + 2, place.tp)), (down, 2 * step + 1, (place.ep - 2, place.tp)))

    def z_copies(slot, number, device):
        return copies(slot, device, z_sem.at[number], z_line_sem.at[number])

    sends = []
    for where in ORDER:
        targets = [across]
        if where[2] == 0:
            targets = [second, *targets]
        if where[1:] == (0, 0):
            targets = [first, *targets]
        sends.append(targets)
    starts = [sum(len(targets) for targets in sends[:number]) for number in range(count)]

    def arrive(slot):
        for copy in copies(slot, across, send_sem.at[0], line_send_sem.at[0]):
            copy.wait_recv()

    def onward_z(step):
        for wanted, index, device in along_z(step):

            @pl.when(wanted)
            def _(index=index, device=device):
                for copy in z_copies(slots[step, 0, 0, 0], index, device):
                    copy.start()

    relays = {1: 2, 4: 3}

    def event(number):
        where = ORDER[number]
        slot = slots[(*where, 0)]
        if where[0] in relays.values() and where[1:] == (0, 0):

            @pl.when(place.edge == 1)
            def _():
                arrive(slot)

        elif number:
            arrive(slot)
        if where in ((0, 0, 0), (1, 0, 0)):
            onward_z(where[0])
        if number in relays:
            step = relays[number]

            @pl.when(place.edge == 0)
            def _():
                arrive(slots[step, 0, 0, 0])
                onward_z(step)

        for index, device in enumerate(sends[number], starts[number]):
            for copy in copies(slot, device, send_sem.at[index], line_send_sem.at[index]):
                copy.start()

    def load_copies(slot, parity, half):
        return (
            pltpu.make_async_copy(part(all_ref, slot), xb.at[parity, half], load_sem.at[parity, half]),
            pltpu.make_async_copy(
                c_ref.at[:, slot % 4, slot // 4], cb.at[parity, half], load_sem.at[parity, 2 + half]
            ),
        )

    def load(number):
        where, parity = ORDER[number], number % 2
        arrive(slots[(*where, 1)])
        for half in (0, 1):
            slot = slots[(*where, half)]
            pair[parity, half] = lines[slot]
            for copy in load_copies(slot, parity, half):
                copy.start()

    def store_copies(number, parity, both):
        kept = pl.ds(number * 2 * capacity, 2 * capacity)
        moves = [(held.at[parity], ref.at[kept]) for held, ref in (
            (xsb, xs_ref), (csb, cs_ref), (innerb, inner_ref), (ggb, gg_ref), (ugb, ug_ref),
        )]
        for half in (0, 1):
            moves.append((midb.at[parity, half], part(mid_ref, both[half])))
            slot = both[half]
            moves.append((outb.at[parity, half], out_ref.at[:, slot % 4, slot // 4]))
        return [
            pltpu.make_async_copy(held, ref, store_sem.at[parity, index])
            for index, (held, ref) in enumerate(moves)
        ]

    def compute(parity):
        picks, gates = [], []
        for half in (0, 1):
            pick, gate = selection(pair[parity, half], expert, capacity)
            picks.append(pick)
            gates.append(gate)
            some = slice(half * capacity, (half + 1) * capacity)
            xsb[parity, some] = dot(pick, xb[parity, half]).astype(jnp.bfloat16)
            cot = cb[parity, half].reshape(rows, -1)
            csb[parity, some] = (dot(pick, cot) * gate).astype(jnp.bfloat16)
        expert_in, slot_cot = xsb[parity], csb[parity]
        gate_part = dot(expert_in, wg[0])
        up_part = dot(expert_in, wu[0])
        inner_grad = dot_with(slot_cot, wd[0], COLS_BY_COLS)
        gate_sig = jax.nn.sigmoid(gate_part)
        activated = gate_part * gate_sig
        inner = (activated * up_part).astype(jnp.bfloat16)
        innerb[parity] = inner
        gate_grad = inner_grad * up_part * gate_sig * (1.0 + gate_part * (1.0 - gate_sig))
        gate_grad = gate_grad.astype(jnp.bfloat16)
        up_grad = (inner_grad * activated).astype(jnp.bfloat16)
        ggb[parity] = gate_grad
        ugb[parity] = up_grad
        slot_grad = dot_with(gate_grad, wg[0], COLS_BY_COLS)
        slot_grad = (slot_grad + dot_with(up_grad, wu[0], COLS_BY_COLS)).astype(jnp.bfloat16)
        result = dot(inner, wd[0]).astype(jnp.bfloat16).astype(jnp.float32)
        for half in (0, 1):
            some = slice(half * capacity, (half + 1) * capacity)
            midb[parity, half] = dot_with(picks[half], slot_grad[some], ROWS_BY_ROWS).astype(
                jnp.bfloat16
            )
            scaled = (result[some] * gates[half]).astype(jnp.bfloat16)
            mixed = dot_with(picks[half], scaled, ROWS_BY_ROWS).astype(jnp.bfloat16)
            outb[parity, half] = mixed.reshape(outb.shape[2:])

    @pl.loop(0, count + 2)
    def _(turn):
        for number in range(count):

            @pl.when(turn == number)
            def _(number=number):
                event(number)

        for number in range(count):

            @pl.when(turn == number + 1)
            def _(number=number):
                load(number)

        @pl.when(turn == 2)
        def _():
            for copy in weights:
                copy.wait()

        @pl.when(turn >= 2)
        def _():
            parity = turn % 2
            for half in (0, 1):
                for copy in load_copies(0, parity, half):
                    copy.wait()

            @pl.when(turn >= 4)
            def _():
                for copy in store_copies(0, parity, (0, 0)):
                    copy.wait()

            compute(parity)

        for number in range(count):

            @pl.when(turn == number + 2)
            def _(number=number):
                both = [slots[(*ORDER[number], half)] for half in (0, 1)]
                for copy in store_copies(number, number % 2, both):
                    copy.start()

    for parity in (0, 1):
        for copy in store_copies(0, parity, (0, 0)):
            copy.wait()
    for index in range(sum(len(targets) for targets in sends)):
        for copy in copies(0, across, send_sem.at[index], line_send_sem.at[index]):
            copy.wait_send()
    for step in range(4):
        for wanted, index, device in along_z(step):

            @pl.when(wanted)
            def _(index=index, device=device):
                for copy in z_copies(0, index, device):
                    copy.wait_send()


def expert_all(x, lines, c_all, gate_w, up_w, down_w, capacity, ident):
    rows, width = x.shape
    ep_size, tp_size = c_all.shape[:2]
    blocks = ep_size * tp_size
    hidden = gate_w.shape[2]
    total = blocks * capacity
    shapes = [(blocks * rows, width)] * 2 + [c_all.shape]
    shapes += [(total, width)] * 2 + [(total, hidden)] * 3
    out = [jax.ShapeDtypeStruct(shape, jnp.bfloat16) for shape in shapes]

    def buffer(*shape):
        return pltpu.VMEM(shape, jnp.bfloat16)

    scratch = [pltpu.VMEM((blocks, *lines.shape), jnp.float32)]
    scratch += [buffer(*gate_w.shape), buffer(*up_w.shape), buffer(*down_w.shape)]
    scratch += [pltpu.VMEM((2, 2, *lines.shape), jnp.float32)]
    by_source = buffer(2, 2, ep_size, rows // ep_size, width)
    scratch += [buffer(2, 2, rows, width), by_source, buffer(2, 2, rows, width), by_source]
    scratch += [buffer(2, 2 * capacity, width)] * 2
    scratch += [buffer(2, 2 * capacity, hidden)] * 3
    scratch += [(3,), (2,), (8,), (8,), (28,), (28,), (blocks,), (blocks,), (2, 4), (2, 9)]
    operands = (x, lines, c_all, gate_w, up_w, down_w)
    return reach(expert_all_kernel, out, scratch, ident, *operands, mib=58)[1:]


BUFFERS = 4
LEAD = 2


def scatter_all_kernel(
    p_ref, out_ref, held, over_second, over_first, over_z, own,
    own_sem, send_sem, core_sem, second_sem, first_sem, z_sem,
):
    place = Place(send_sem)
    rows = out_ref.shape[0]

    def add(total, other):
        @pl.loop(0, rows, step=64)
        def _(row):
            some = pl.ds(row, 64)
            total[some] = total[some] + other[some]

    def part(slot):
        return p_ref.at[pl.ds(slot * rows, rows)]

    pairs = [(step, first) for step in (3, 2, 1, 0) for first in (1, 0)]
    order = [(*pairs[number], 1) for number in range(LEAD)]
    for number, where in enumerate(pairs):
        if number + LEAD < len(pairs):
            order.append((*pairs[number + LEAD], 1))
        order.append((*where, 0))
    loads = []

    def load(number):
        buffer = number % BUFFERS
        copy = pltpu.make_async_copy(
            part(place.slot(*order[number])), own.at[buffer], own_sem.at[buffer]
        )
        copy.start()
        loads.append(copy)

    for number in range(BUFFERS):
        load(number)
    place.greet_all_ways()
    for where in order:
        place.send(
            part(place.slot(*where, 1)), held.at[where], core_sem.at[where], place.device(0, 0, 0, 1)
        )

    def onward(step):
        mine = held.at[step, 0, 0]
        place.arrive(over_first.at[step], first_sem.at[step])
        add(mine, over_first.at[step])
        if step == 2:
            place.arrive(over_z.at[3], z_sem.at[3])
            add(mine, over_z.at[3])
        if step:
            place.send(mine, over_z.at[step], z_sem.at[step], place.device(1 + (step == 2), 0, 0))

    for number, where in enumerate(order):
        step, first, second = where
        mine = held.at[where]
        place.arrive(mine, core_sem.at[where])
        loads[number].wait()
        add(mine, own.at[number % BUFFERS])
        if number + BUFFERS < len(order):
            load(number + BUFFERS)
        if second:
            place.send(
                mine, over_second.at[step, first], second_sem.at[step, first], place.device(0, 0, 1)
            )
            continue
        place.arrive(over_second.at[step, first], second_sem.at[step, first])
        add(mine, over_second.at[step, first])
        if first:
            place.send(mine, over_first.at[step], first_sem.at[step], place.device(0, 1, 0))
        else:
            onward(step)
    for step in (2, 1):
        place.arrive(over_z.at[step], z_sem.at[step])

    @pl.loop(0, rows, step=32)
    def _(row):
        some = pl.ds(row, 32)
        total = held[0, 0, 0, some].astype(jnp.float32)
        for step in (1, 2):
            total = total + over_z[step, some].astype(jnp.float32)
        out_ref[some] = total

    place.finish()


def scatter_all(p, parts, ident):
    rows, width = p.shape[0] // parts, p.shape[1]

    def buffer(*lead):
        return pltpu.VMEM((*lead, rows, width), p.dtype)

    scratch = [buffer(4, 2, 2), buffer(4, 2), buffer(4), buffer(4), buffer(BUFFERS)]
    scratch += [(BUFFERS,), (parts - 1,), (4, 2, 2), (4, 2), (4,), (4,)]
    out = jax.ShapeDtypeStruct((rows, width), jnp.float32)
    return reach(scatter_all_kernel, out, scratch, ident, p, vmem_out=True, mib=56)


def enter_kernel(x_ref, group_ref, own_sem, send_sem, x_sem):
    place = Place(send_sem)
    ep, tp = place.ep, place.tp
    others = [place.across(step, over) for step in range(4) for over in (0, 1)]
    own = pltpu.make_async_copy(x_ref.at[ep], group_ref.at[ep, tp], own_sem)
    own.start()
    place.greet(
        [(other, tp) for other in others[1:]] + [(ep, place.over_x), (ep, place.over_core)]
    )
    for other in others[1:]:
        place.send(x_ref.at[other], group_ref.at[ep, tp], x_sem.at[ep, tp], (other, tp))
    for number, other in enumerate(others):
        block = group_ref.at[other, tp]
        if number:
            place.arrive(block, x_sem.at[other, tp])
        source = block if number else x_ref.at[ep]
        place.send(source, block, x_sem.at[other, tp], (ep, place.over_x))
        place.send(source, block, x_sem.at[other, tp], (ep, place.over_core))
    for other in others:
        block = group_ref.at[other, place.over_x]
        place.arrive(block, x_sem.at[other, place.over_x])
        place.send(block, block, x_sem.at[other, place.over_x], (ep, place.over_core))
    for other in others:
        for source in (place.over_core, place.over_both):
            place.arrive(group_ref.at[other, source], x_sem.at[other, source])
    own.wait()
    place.finish()


def enter(x, tp_size, ident):
    ep_size, block, width = x.shape
    moves = ep_size - 1 + ep_size * 3
    out = jax.ShapeDtypeStruct((ep_size, tp_size, block, width), x.dtype)
    scratch = [pltpu.SemaphoreType.DMA, (moves,), (ep_size, tp_size)]
    return reach(enter_kernel, out, scratch, ident, x)


CHUNKS = 4


def gather_group_kernel(x_ref, group_ref, own_sem, send_sem, recv_sem):
    place = Place(send_sem)
    ep, tp = place.ep, place.tp
    some = x_ref.shape[0] // CHUNKS

    def piece(chunk, owner):
        return group_ref.at[pl.ds(chunk * some, some), owner]

    own = pltpu.make_async_copy(x_ref, group_ref.at[:, tp], own_sem)
    own.start()
    place.greet([(ep, place.over_x), (ep, place.over_core)])
    for partner in (place.over_x, place.over_core):
        for chunk in range(CHUNKS):
            place.send(
                x_ref.at[pl.ds(chunk * some, some)],
                piece(chunk, tp),
                recv_sem.at[chunk, tp],
                (ep, partner),
            )
    for chunk in range(CHUNKS):
        block = piece(chunk, place.over_x)
        place.arrive(block, recv_sem.at[chunk, place.over_x])
        place.send(block, block, recv_sem.at[chunk, place.over_x], (ep, place.over_core))
    for chunk in range(CHUNKS):
        for source in (place.over_core, place.over_both):
            place.arrive(piece(chunk, source), recv_sem.at[chunk, source])
    own.wait()
    place.finish()


def gather_group(x, tp_size, ident):
    ep_size, block, width = x.shape
    out = jax.ShapeDtypeStruct((ep_size, tp_size, block, width), x.dtype)
    scratch = [pltpu.SemaphoreType.DMA, (CHUNKS * 3,), (CHUNKS, tp_size)]
    return reach(gather_group_kernel, out, scratch, ident, x)


def scatter_group_kernel(
    p_ref, out_ref, own, held, over_x, own_sem, send_sem, core_sem, x_sem
):
    place = Place(send_sem)
    ep, tp = place.ep, place.tp
    some = p_ref.shape[0] // CHUNKS
    block, width = p_ref.shape[2:]

    def chunk_of(chunk):
        return pl.ds(chunk * some, some)

    loads = [
        pltpu.make_async_copy(p_ref.at[:, owner], own.at[number], own_sem.at[number])
        for number, owner in enumerate((place.over_x, tp))
    ]
    for copy in loads:
        copy.start()
    place.greet([(ep, place.over_x), (ep, place.over_core)])
    for number, owner in enumerate((place.over_both, place.over_core)):
        for chunk in range(CHUNKS):
            place.send(
                p_ref.at[chunk_of(chunk), owner],
                held.at[number, chunk_of(chunk)],
                core_sem.at[number, chunk],
                (ep, place.over_core),
            )

    def add(number, chunk):
        place.arrive(held.at[number, chunk_of(chunk)], core_sem.at[number, chunk])
        for row in range(chunk * some, (chunk + 1) * some):
            held[number, row] = held[number, row] + own[number, row]

    loads[0].wait()
    for chunk in range(CHUNKS):
        add(0, chunk)
        place.send(
            held.at[0, chunk_of(chunk)],
            over_x.at[chunk_of(chunk)],
            x_sem.at[chunk],
            (ep, place.over_x),
        )
    loads[1].wait()
    for chunk in range(CHUNKS):
        add(1, chunk)
    for chunk in range(CHUNKS):
        place.arrive(over_x.at[chunk_of(chunk)], x_sem.at[chunk])
        for row in range(chunk * some, (chunk + 1) * some):
            out_ref[row] = held[1, row].astype(jnp.float32) + over_x[row].astype(jnp.float32)
    place.finish()


def scatter_group(p, ident):
    ep_size, tp_size, block, width = p.shape

    def buffer(*lead):
        return pltpu.VMEM((*lead, ep_size, block, width), p.dtype)

    scratch = [buffer(2), buffer(2), buffer(), (2,), (CHUNKS * 3,), (2, CHUNKS), (CHUNKS,)]
    out = jax.ShapeDtypeStruct((ep_size, block, width), jnp.float32)
    return reach(scatter_group_kernel, out, scratch, ident, p, vmem_out=True, mib=24)


def gather_kv_kernel(kv_ref, out_ref, own_sem, send_sem, recv_sem):
    place = Place(send_sem)
    ep, tp = place.ep, place.tp
    own = pltpu.make_async_copy(kv_ref, out_ref.at[:, ep], own_sem)
    own.start()
    partners = [place.across(*where) for where in ((1, 0), (2, 0), (3, 0), (0, 1))]
    place.greet([(partner, tp) for partner in partners])
    for partner in (partners[3], *partners[:3]):
        place.send(kv_ref, out_ref.at[:, ep], recv_sem.at[ep], (partner, tp))
    for partner in partners[:3]:
        block = out_ref.at[:, partner]
        place.arrive(block, recv_sem.at[partner])
        place.send(block, block, recv_sem.at[partner], (partners[3], tp))
    for step in range(4):
        other = place.across(step, 1)
        place.arrive(out_ref.at[:, other], recv_sem.at[other])
    own.wait()
    place.finish()


def gather_kv(kv, ep_size, ident):
    blocks, rows, width = kv.shape
    out = jax.ShapeDtypeStruct((blocks, ep_size, rows, width), kv.dtype)
    scratch = [pltpu.SemaphoreType.DMA, (ep_size - 1,), (ep_size,)]
    return reach(gather_kv_kernel, out, scratch, ident, kv)


def scatter_kv_kernel(p_ref, out_ref, own, over_y, over_z, own_sem, send_sem, y_sem, z_sem):
    place = Place(send_sem)
    tp = place.tp
    blocks = out_ref.shape[0]
    order = (3, 2, 1, 0)
    loads = {}
    for step in order:
        loads[step] = pltpu.make_async_copy(
            p_ref.at[:, place.across(step, 0)], own.at[step], own_sem.at[step]
        )
        loads[step].start()
    place.greet([(place.across(*where), tp) for where in ((1, 0), (2, 0), (3, 0), (0, 1))])
    for step in order:
        place.send(
            p_ref.at[:, place.across(step, 1)],
            over_y.at[step],
            y_sem.at[step],
            (place.across(0, 1), tp),
        )
    for step in order:
        loads[step].wait()
        place.arrive(over_y.at[step], y_sem.at[step])

        @pl.loop(0, blocks)
        def _(block, step=step):
            own[step, block] = own[step, block] + over_y[step, block]

        if step == 2:
            place.arrive(over_z.at[3], z_sem.at[3])

            @pl.loop(0, blocks)
            def _(block):
                own[2, block] = own[2, block] + over_z[3, block]

        if step:
            device = (place.across(1 + (step == 2), 0), tp)
            place.send(own.at[step], over_z.at[step], z_sem.at[step], device)
    for step in (2, 1):
        place.arrive(over_z.at[step], z_sem.at[step])

    @pl.loop(0, blocks)
    def _(block):
        total = own[0, block].astype(jnp.float32)
        for step in (1, 2):
            total = total + over_z[step, block].astype(jnp.float32)
        out_ref[block] = total.astype(jnp.bfloat16)

    place.finish()


def scatter_kv(p, ident):
    blocks, ep_size, rows, width = p.shape
    buffer = pltpu.VMEM((4, blocks, rows, width), p.dtype)
    scratch = [buffer, buffer, buffer, (4,), (7,), (4,), (4,)]
    out = jax.ShapeDtypeStruct((blocks, rows, width), p.dtype)
    return reach(scatter_kv_kernel, out, scratch, ident, p, vmem_out=True, mib=24)


SLOTS = 1024


def finish_kernel(*refs):
    partials, gains_ref, rows_ref, experts = refs[:3], refs[3], refs[4], refs[5:10]
    outs, gain_out, rows_out, grads, refs = refs[10:13], refs[13], refs[14], refs[15:18], refs[18:]
    owns, overs_y, overs_z, stages, refs = refs[:3], refs[3:6], refs[6:9], refs[9:11], refs[11:]
    wide, narrow, sums, refs = refs[0], refs[1], refs[2:5], refs[5:]
    own_sem, send_sem, y_sem, z_sem, gain_sem, load_sem, grad_sem, rows_sem, rows_send_sem = refs
    place = Place(send_sem)
    ep, tp = place.ep, place.tp
    count = len(partials)
    total, arrived = stages
    ways = [(ep, place.over_core), (ep, place.over_x)]
    ways += [(place.across(step, 0), tp) for step in (1, 2, 3)]
    ways.append((place.across(0, 1), tp))
    moves = [(number, step) for step in (3, 2, 1, 0) for number in range(count)]
    gain_load = pltpu.make_async_copy(gains_ref, total.at[0], own_sem.at[count, 0])
    gain_load.start()

    def own_copy(number, step):
        return pltpu.make_async_copy(
            partials[number].at[place.across(step, 0)],
            owns[number].at[step],
            own_sem.at[number, step],
        )

    def to_y(number, step):
        return pltpu.make_async_remote_copy(
            src_ref=partials[number].at[place.across(step, 1)],
            dst_ref=overs_y[number].at[step],
            send_sem=send_sem.at[number, step],
            recv_sem=y_sem.at[number, step],
            device_id=(place.across(0, 1), tp),
            device_id_type=MESH_ID,
        )

    def to_z(number, step):
        return pltpu.make_async_remote_copy(
            src_ref=owns[number].at[step],
            dst_ref=overs_z[number].at[step],
            send_sem=send_sem.at[number, 3 + step],
            recv_sem=z_sem.at[number, step],
            device_id=(place.across(1 + (step == 2), 0), tp),
            device_id_type=MESH_ID,
        )

    def gain_copy(number):
        return pltpu.make_async_remote_copy(
            src_ref=total.at[(0, 1, 2, 2, 2, 3)[number]],
            dst_ref=arrived.at[number],
            send_sem=send_sem.at[count, number],
            recv_sem=gain_sem.at[number],
            device_id=ways[number],
            device_id_type=MESH_ID,
        )

    others = [(step, over) for step in range(4) for over in (0, 1)][1:]

    def row_copy(index):
        other = place.across(*others[index])
        return pltpu.make_async_remote_copy(
            src_ref=rows_ref.at[other],
            dst_ref=rows_out.at[ep],
            send_sem=rows_send_sem.at[index],
            recv_sem=rows_sem.at[ep],
            device_id=(other, tp),
            device_id_type=MESH_ID,
        )

    def row_arrival(index):
        other = place.across(*others[index])
        return pltpu.make_async_remote_copy(
            src_ref=rows_ref.at[other],
            dst_ref=rows_out.at[other],
            send_sem=rows_send_sem.at[index],
            recv_sem=rows_sem.at[other],
            device_id=(other, tp),
            device_id_type=MESH_ID,
        )

    own_rows = pltpu.make_async_copy(rows_ref.at[ep], rows_out.at[ep], rows_sem.at[ep])
    own_rows.start()
    for number, step in moves:
        own_copy(number, step).start()
    place.greet(ways[:2] + [(place.across(*other), tp) for other in others])
    gain_load.wait()
    gain_copy(0).start()
    for index in range(len(others)):
        row_copy(index).start()
    for number, step in moves:
        to_y(number, step).start()

    def event(index):
        number, step = moves[index]
        own, over = owns[number], overs_y[number]
        own_copy(number, step).wait()
        to_y(number, step).wait_recv()

        @pl.loop(0, own.shape[1], step=64)
        def _(row):
            some = pl.ds(row, 64)
            own[step, some] = own[step, some] + over[step, some]

        if step == 2:
            to_z(number, 3).wait_recv()

            @pl.loop(0, own.shape[1], step=64)
            def _(row):
                some = pl.ds(row, 64)
                own[2, some] = own[2, some] + overs_z[number][3, some]

        if step:
            to_z(number, step).start()
        if index < 2:
            gain_copy(index).wait_recv()
            total[index + 1] = total[index] + arrived[index]
            for later in (1,) if index == 0 else (2, 3, 4):
                gain_copy(later).start()
        if index == 2:
            for later in (2, 3, 4):
                gain_copy(later).wait_recv()
            total[3] = (total[2] + arrived[2]) + (arrived[3] + arrived[4])
            gain_copy(5).start()

    expert_in, slot_cot, inner, gate_grad, up_grad = experts
    pieces = expert_in.shape[0] // SLOTS
    jobs = ((expert_in, gate_grad), (expert_in, up_grad), (slot_cot, inner))
    steps = pieces * len(jobs)

    def load_copies(pair, piece, parity):
        some = pl.ds(piece * SLOTS, SLOTS)
        return [
            pltpu.make_async_copy(ref.at[some], held.at[parity], load_sem.at[parity, index])
            for index, (ref, held) in enumerate(zip(pair, (wide, narrow)))
        ]

    def grad_copy(job):
        return pltpu.make_async_copy(sums[job], grads[job], grad_sem.at[job])

    def multiply(job, parity):
        into = sums[job]
        left, right = (wide, narrow) if job < 2 else (narrow, wide)
        tile = 512 if into.shape[0] % 512 == 0 else 384

        @pl.loop(0, into.shape[0], step=tile)
        def _(row):
            some = pl.ds(pl.multiple_of(row, tile), tile)
            product = dot_with(left[parity, :, some], right[parity], ROWS_BY_ROWS)

            into[some] += product

    for into in sums:

        @pl.loop(0, into.shape[0], step=64)
        def _(row, into=into):
            into[pl.ds(row, 64)] = jnp.zeros((64, into.shape[1]), jnp.float32)

    @pl.loop(0, steps + 1)
    def _(turn):
        for index in range(len(moves)):

            @pl.when(turn == index)
            def _(index=index):
                event(index)

        for job, pair in enumerate(jobs):

            @pl.when((turn >= job * pieces) & (turn < (job + 1) * pieces))
            def _(job=job, pair=pair):
                for copy in load_copies(pair, turn - job * pieces, turn % 2):
                    copy.start()

        for job, pair in enumerate(jobs):

            @pl.when((turn > job * pieces) & (turn <= (job + 1) * pieces))
            def _(job=job, pair=pair):
                parity = (turn - 1) % 2
                for copy in load_copies(pair, 0, parity):
                    copy.wait()
                multiply(job, parity)

            @pl.when(turn == (job + 1) * pieces)
            def _(job=job):
                grad_copy(job).start()

    for number in range(count):
        own, over, out = owns[number], overs_z[number], outs[number]
        for step in (2, 1):
            to_z(number, step).wait_recv()

        @pl.loop(0, own.shape[1], step=64)
        def _(row, own=own, over=over, out=out):
            some = pl.ds(row, 64)
            sum_of = own[0, some].astype(jnp.float32)
            for step in (1, 2):
                sum_of = sum_of + over[step, some].astype(jnp.float32)
            out[some] = sum_of

    gain_copy(5).wait_recv()
    gain_out[...] = total[3] + arrived[5]
    for job in range(len(jobs)):
        grad_copy(job).wait()
    for number, step in moves:
        to_y(number, step).wait_send()
        if step:
            to_z(number, step).wait_send()
    for number in range(6):
        gain_copy(number).wait_send()
    own_rows.wait()
    for index in range(len(others)):
        row_copy(index).wait_send()
        row_arrival(index).wait_recv()


def finish(partials, gains, rows, expert_in, slot_cot, inner, gate_grad, up_grad, ident):
    count = len(partials)
    buffers = [pltpu.VMEM((4, *p.shape[1:]), p.dtype) for p in partials]
    width, hidden = expert_in.shape[1], inner.shape[1]
    grads = [(width, hidden), (width, hidden), (hidden, width)]
    scratch = buffers * 3
    scratch += [pltpu.VMEM((4, *gains.shape), gains.dtype), pltpu.VMEM((6, *gains.shape), gains.dtype)]
    scratch += [pltpu.VMEM((2, SLOTS, width), jnp.bfloat16), pltpu.VMEM((2, SLOTS, hidden), jnp.bfloat16)]
    scratch += [pltpu.VMEM(shape, jnp.float32) for shape in grads]
    scratch += [(count + 1, 4), (count + 1, 7), (count, 4), (count, 4), (6,), (2, 2), (3,), (8,), (7,)]
    out = [jax.ShapeDtypeStruct(p.shape[1:], jnp.float32) for p in partials]
    out.append(jax.ShapeDtypeStruct(gains.shape, jnp.float32))
    out.append(jax.ShapeDtypeStruct(rows.shape, rows.dtype))
    out += [jax.ShapeDtypeStruct(shape, jnp.float32) for shape in grads]
    operands = (*partials, gains, rows, expert_in, slot_cot, inner, gate_grad, up_grad)
    return reach(
        finish_kernel, out, scratch, ident, *operands, vmem_out=(True,) * 4 + (False,) * 4, mib=58
    )


def on_device(
    inputs,
    cotangent,
    arrangement,
    seq_lengths,
    routes,
    gate_values,
    input_gain,
    query_proj,
    key_projected,
    value_projected,
    query_gain,
    key_gain,
    output_proj,
    expert_gain,
    gate_weight,
    up_weight,
    down_weight,
):
    ep_size = lax.axis_size("ep")
    tp_size = lax.axis_size("tp")
    ep_index = lax.axis_index("ep")
    tp_index = lax.axis_index("tp")
    everyone = ("ep", "tp")
    own_rows, width = inputs.shape
    group_rows = own_rows * tp_size
    row_block = own_rows // ep_size
    token_total = arrangement.shape[0]
    expert_count = ep_size * tp_size
    capacity = 2 * own_rows * TOP // expert_count
    heads = query_proj.shape[1] // HEAD
    known = (ep_size, tp_size) == (8, 4)
    expert = (ep_index * tp_size + tp_index).astype(jnp.int32)[None]

    table = arrangement.reshape(ep_size, tp_size, ep_size, row_block)
    leaving_from = lax.dynamic_index_in_dim(table, tp_index, 1, keepdims=False)
    leaving_from = lax.dynamic_index_in_dim(leaving_from, ep_index, 1, keepdims=False)
    send_index = leaving_from - (ep_index * group_rows + tp_index * own_rows)
    mover = (
        send_index.reshape(-1)[:, None] == jnp.arange(own_rows, dtype=jnp.int32)[None, :]
    ).astype(jnp.bfloat16)

    def to_places(rows):
        return dot(mover, rows).astype(jnp.bfloat16).reshape(ep_size, row_block, width)

    def exchange(rows):
        return lax.all_to_all(rows, "ep", split_axis=0, concat_axis=0, tiled=True)

    def to_given(moved):
        return dot_with(mover, moved, ROWS_BY_ROWS)

    def group_sorted(rows, ident):
        blocks = rows.reshape(ep_size, row_block, width)
        if known:
            gathered = gather_group(blocks, tp_size, ident)
        else:
            gathered = lax.all_gather(blocks, "tp", axis=1)
        return gathered.reshape(group_rows, width)

    def sum_group(rows, ident):
        blocks = rows.astype(jnp.bfloat16).reshape(ep_size, tp_size, row_block, width)
        if known:
            return scatter_group(blocks, ident).reshape(own_rows, width)
        placed = jnp.swapaxes(blocks, 0, 1).reshape(group_rows, width)
        own = lax.psum_scatter(placed, "tp", scatter_dimension=0, tiled=True)
        return own.astype(jnp.float32)

    leaving_x, leaving_cot = to_places(inputs), to_places(cotangent)
    if known:
        cot_all = lax.all_gather(leaving_cot, everyone, axis=0, tiled=True)
        cot_all = cot_all.reshape(ep_size, tp_size, ep_size, row_block, width)
        own_cot = lax.dynamic_index_in_dim(cot_all, tp_index, 1, keepdims=False)
        own_cot = lax.dynamic_index_in_dim(own_cot, ep_index, 1, keepdims=False)
        group_x = enter(leaving_x, tp_size, 1)
        own_inputs = lax.dynamic_index_in_dim(group_x, tp_index, 1, keepdims=False)
    else:
        own_inputs, own_cot = exchange(leaving_x), exchange(leaving_cot)
        group_x = lax.all_gather(own_inputs, "tp", axis=1)
        cot_all = lax.all_gather(own_cot.reshape(own_rows, width), everyone, axis=0, tiled=True)
    own_inputs, own_cot = own_inputs.reshape(own_rows, width), own_cot.reshape(own_rows, width)
    group_x = group_x.reshape(group_rows, width)
    meta_own = jnp.concatenate([routes.astype(jnp.float32).T, gate_values.T], axis=0)

    query_given = lax.dynamic_index_in_dim(table, ep_index, 0, keepdims=False)
    query_given = jnp.swapaxes(query_given, 0, 1).reshape(group_rows)
    query_first = seq_starts(query_given, seq_lengths)
    cosine, sine = rope_tables(query_given - query_first, HEAD)
    key_given = jnp.transpose(table, (2, 1, 0, 3)).reshape(token_total)
    by_step = (-1, QUERY_TOKENS)
    given_steps, first_steps = query_given.reshape(by_step), query_first.reshape(by_step)
    lowest = jnp.min(first_steps, axis=1) // KEY_SPAN
    highest = jnp.max(given_steps, axis=1) // KEY_SPAN + 1
    open_low = (jnp.max(first_steps, axis=1) + KEY_SPAN - 1) // KEY_SPAN
    open_low = jnp.minimum(open_low, highest)
    open_high = jnp.clip((jnp.min(given_steps, axis=1) + 1) // KEY_SPAN, open_low, highest)
    bounds = jnp.stack([lowest, open_low, open_high, highest]).astype(jnp.int32)
    ask = jnp.stack([query_given, query_first], axis=1)
    ask_rows = jnp.stack(
        [jnp.tile(given_steps, (1, heads)), jnp.tile(first_steps, (1, heads))], axis=1
    )

    normed_in, query_raw, query_rows, key_raw, kv_rows = front(
        group_x, input_gain, query_proj, key_projected, value_projected,
        query_gain, key_gain, cosine, sine,
    )
    kv_blocks = kv_rows.reshape(expert_count, row_block, 2 * HEAD)
    if known:
        kv_all = gather_kv(kv_blocks, ep_size, 2)
    else:
        kv_all = lax.all_gather(kv_blocks, "ep", axis=1)
    kv_all = kv_all.reshape(token_total, 2 * HEAD)
    pairs = group_rows * heads * 1536
    exact, out_rows, lse = attend_forward(
        bounds, query_rows, ask, key_given[None], kv_all, pairs
    )
    branch = sum_group(dot(out_rows, output_proj), 5)
    hidden = own_inputs.astype(jnp.float32) + branch
    mid_scale = inverse_root(hidden)
    normed_mid = (hidden * mid_scale * expert_gain).astype(jnp.bfloat16)

    experts = (gate_weight, up_weight, down_weight, capacity)
    if known:
        results = expert_all(normed_mid, meta_own, cot_all, *experts, 3)
    else:
        mid_all = lax.all_gather(normed_mid, everyone, axis=0, tiled=True)
        meta = lax.all_gather(meta_own, everyone, axis=0)
        results = list(expert_pass(expert, meta, mid_all, cot_all, *experts))
        results[1] = jnp.transpose(
            results[1].reshape(ep_size, tp_size, ep_size, row_block, width), (2, 1, 0, 3, 4)
        )
    mid_partial, out_partial, expert_in, slot_cot, inner, gate_grad, up_grad = results
    def sum_over_all(partial):
        return lax.psum_scatter(partial, everyone, scatter_dimension=0, tiled=True)

    if known:
        mid_grad = scatter_all(mid_partial, expert_count, 4)
    else:
        mid_grad = sum_over_all(mid_partial).astype(jnp.float32)
    mid_grad, out_partial = lax.optimization_barrier((mid_grad, out_partial))
    mixed = sum_over_all(out_partial.reshape(token_total, width))

    mid_hat = hidden * mid_scale
    grad_expert_gain = jnp.sum(mid_grad * mid_hat, axis=0)
    mid_scaled = mid_grad * expert_gain
    hidden_grad = own_cot.astype(jnp.float32) + mid_scale * (
        mid_scaled - mid_hat * jnp.mean(mid_scaled * mid_hat, axis=-1, keepdims=True)
    )
    branch_grad = group_sorted(hidden_grad.astype(jnp.bfloat16), 6)
    out_grad = dot_with(branch_grad, output_proj, COLS_BY_COLS).astype(jnp.bfloat16)
    query_grad, kv_grad = attend_backward(
        bounds, query_rows, out_grad, exact, lse, ask_rows, key_given[None], kv_all, pairs
    )
    kv_grad = kv_grad.reshape(expert_count, ep_size, row_block, 2 * HEAD)
    if known:
        kv_own = scatter_kv(kv_grad, 7)
    else:
        kv_own = lax.psum_scatter(kv_grad, "ep", scatter_dimension=1)
    kv_own = kv_own.reshape(group_rows, 2 * HEAD)
    value_grad = kv_own[:, HEAD:]
    raw_query_grad, grad_query_gain = head_back(query_raw, query_grad, query_gain, cosine, sine)
    raw_key_grad, grad_key_gain = head_back(key_raw, kv_own[:, :HEAD], key_gain, cosine, sine)
    normed_grad = (
        dot_with(raw_query_grad, query_proj, COLS_BY_COLS)
        + dot_with(raw_key_grad, key_projected, COLS_BY_COLS)
        + dot_with(value_grad, value_projected, COLS_BY_COLS)
    )
    normed_grad = sum_group(normed_grad, 8)
    own_float = own_inputs.astype(jnp.float32)
    in_scale = inverse_root(own_float)
    in_hat = own_float * in_scale
    grad_input_gain = jnp.sum(normed_grad * in_hat, axis=0)
    in_scaled = normed_grad * input_gain
    input_rows = hidden_grad + in_scale * (
        in_scaled - in_hat * jnp.mean(in_scaled * in_hat, axis=-1, keepdims=True)
    )
    leaving = jnp.concatenate([input_rows, hidden], axis=1).astype(jnp.bfloat16)
    leaving = leaving.reshape(ep_size, row_block, 2 * width)

    weights = [
        dot_with(branch_grad, out_rows, ROWS_BY_ROWS),
        dot_with(normed_in, raw_query_grad, ROWS_BY_ROWS),
        dot_with(normed_in, jnp.concatenate([raw_key_grad, value_grad], axis=1), ROWS_BY_ROWS),
    ]
    weights = [array.astype(jnp.bfloat16).reshape(ep_size, -1, array.shape[1]) for array in weights]
    gains = jnp.concatenate(
        [grad_input_gain, grad_expert_gain, grad_query_gain[0], grad_key_gain[0]]
    )
    if known:
        experts = (expert_in, slot_cot, inner, gate_grad, up_grad)
        results = finish(weights, gains.reshape(-1, HEAD), leaving, *experts, 10)
        grad_output, grad_query, grad_kv, gains, leaving = results[:5]
        grad_gate, grad_up, grad_down = results[5:]
        gains = gains.reshape(-1)
    else:
        grad_output, grad_query, grad_kv = [
            lax.psum_scatter(array, "ep", scatter_dimension=0).astype(jnp.float32)
            for array in weights
        ]
        gains, leaving = lax.psum(gains, everyone), exchange(leaving)
        grad_gate = dot_with(expert_in, gate_grad, ROWS_BY_ROWS)
        grad_up = dot_with(expert_in, up_grad, ROWS_BY_ROWS)
        grad_down = dot_with(inner, slot_cot, ROWS_BY_ROWS)
    mixed, gains = lax.optimization_barrier((mixed, gains))
    leaving = leaving.reshape(own_rows, 2 * width)
    grad_inputs = to_given(leaving[:, :width])
    layer_out = leaving[:, width:].astype(jnp.float32) + mixed.astype(jnp.float32)
    layer_out = to_given(layer_out.astype(jnp.bfloat16)).astype(jnp.bfloat16)
    grad_output = jnp.transpose(grad_output)
    cuts = (width, 2 * width, 2 * width + HEAD)
    return (
        layer_out,
        grad_inputs,
        grad_query,
        grad_kv[:, :HEAD],
        grad_kv[:, HEAD:],
        grad_output,
        gains[: cuts[0]],
        gains[cuts[1] : cuts[2]],
        gains[cuts[2] :],
        gains[cuts[0] : cuts[1]],
        grad_gate[None],
        grad_up[None],
        grad_down[None],
    )


def solution(mesh):
    split = P(("ep", "tp"), None)
    experts = P(("ep", "tp"), None, None)
    columns = P(None, "tp")
    return jax.shard_map(
        on_device,
        mesh=mesh,
        in_specs=(
            split, split, P(), P(), split, split, P(), columns, columns, columns,
            P(), P(), P("tp", None), P(), experts, experts, experts,
        ),
        out_specs=(
            split, split, P("ep", "tp"), P("ep", "tp"), P("ep", "tp"), P("tp", "ep"),
            P(), P(), P(), P(), experts, experts, experts,
        ),
        check_vma=False,
    )
```
